32 devices in a mesh: ch: 2 (over core), lat: 4 (over y, x), lon: 4 (over z).
Axes of the slice: x: 2, y: 2, z: 4, core: 2. Of those that a mesh axis runs over, the one named last changes fastest.
Arguments:
- inputs: bfloat16 [512, 4, 16, 192], P('ch', None, 'lat', 'lon'), may hold values from -6 to 6
- weights: bfloat16 [512, 27, 512], P('ch'), may hold values from -0.0546875 to 0.0546875
- out_grad: bfloat16 [512, 4, 16, 192], P('ch', None, 'lat', 'lon'), may hold values from -6 to 6
Outputs:
- input_grad: bfloat16 [512, 4, 16, 192], P('ch', None, 'lat', 'lon')
- weight_grad: float32 [512, 27, 512], P('ch')
The draws below stay inside these ranges and needn't reach their ends.
All inputs are finite; a program needn't handle non-finite values.
Results may differ from the reference program's by a relative error of at most 0.001.
Values may be sent and summed in bfloat16 or wider, within the bound.
No kernel may reach another device: no remote copies, remote signals or barrier semaphores. Data moves between devices by JAX's collectives and lax.ppermute only.
A program may use at most 320 MiB of HBM per device.

```python
import math
import jax
import jax.numpy as jnp

C = 512
F = 512
LEV = 4
NLON = 192
NLAT = 16


def block_scale(rng, shape, shards, low, largest):
    gain, own = 1.0, jax.random.fold_in(rng, 6)
    for axis_at, parts in shards:
        draws = jnp.exp(jax.random.uniform(jax.random.fold_in(own, axis_at), (parts,), jnp.float32, low / len(shards), largest / len(shards)))
        gain = gain * jnp.repeat(draws, shape[axis_at] // parts).reshape([-1 if axis == axis_at else 1 for axis in range(len(shape))])
    return gain


def scatter_about(rng, dims, scale, most, shards=(), kind=jnp.bfloat16):
    level = block_scale(rng, dims, shards, -0.22, 0.18) if shards else 1.0
    values = jax.random.normal(rng, dims, jnp.float32) * scale * level
    return jnp.minimum(jnp.maximum(values, -most), most).astype(kind)


def setup_inputs(seed: int = 0) -> dict:
    splits = jax.random.split(jax.random.key(seed), 4)
    inputs = scatter_about(splits[0], (C, LEV, NLAT, NLON), 1.0, 6.0, ((0, 2), (2, 4), (3, 4)))
    weights = scatter_about(splits[1], (C, 27, F), (27 * C) ** -0.5, 0.0546875, ((0, 2),))
    out_grad = scatter_about(splits[2], (F, LEV, NLAT, NLON), 1.0, 6.0, ((0, 2), (2, 4), (3, 4)))
    return {"inputs": inputs, "weights": weights, "out_grad": out_grad}


def pad_field(field):
    field = jnp.concatenate([field[..., -1:], field, field[..., :1]], axis=3)
    return jnp.pad(field, ((0, 0), (1, 1), (1, 1), (0, 0)))

def reference(inputs, weights, out_grad):
    input_pad = pad_field(inputs.astype(jnp.float32))
    grad_pad = pad_field(out_grad.astype(jnp.float32))
    grad_full = out_grad.astype(jnp.float32)
    taps = weights.astype(jnp.float32)
    levels, height, width = (inputs.shape[1], inputs.shape[2], inputs.shape[3])
    total = jnp.zeros(inputs.shape, jnp.float32)
    pieces = []
    for tap in range(27):
        shift_lev = tap // 9 - 1
        shift_lat = tap // 3 % 3 - 1
        shift_lon = tap % 3 - 1
        shifted = grad_pad[:, 1 - shift_lev:1 - shift_lev + levels, 1 - shift_lat:1 - shift_lat + height, 1 - shift_lon:1 - shift_lon + width]
        total = total + jnp.einsum('cf,flhw->clhw', taps[:, tap, :], shifted)
        moved = input_pad[:, 1 + shift_lev:1 + shift_lev + levels, 1 + shift_lat:1 + shift_lat + height, 1 + shift_lon:1 + shift_lon + width]
        pieces.append(jnp.einsum('clhw,flhw->cf', moved, grad_full))
    raw = jnp.stack(pieces, axis=1)
    weight_grad = raw * (1.0 / math.sqrt(LEV * NLAT * NLON))
    return (total.astype(jnp.bfloat16), weight_grad)
```

```python
import math

import jax
import jax.numpy as jnp
from jax import lax
from jax.experimental import pallas as pl
from jax.experimental.pallas import tpu as pltpu
from jax.sharding import PartitionSpec as P

VMEM = pltpu.VMEM
SMEM = pltpu.SMEM
AXES = ("ch", "lat", "lon")
LIMIT = 56 * 1024 * 1024


def padded_2(cells, sides, width):
    for axis, dim in sides:
        count = lax.axis_size(axis)
        head = lax.slice_in_dim(cells, 0, width, axis=dim)
        tail = lax.slice_in_dim(cells, cells.shape[dim] - width, cells.shape[dim], axis=dim)
        cells = jnp.concatenate(
            [
                lax.ppermute(tail, axis, [(i, (i + 1) % count) for i in range(count)]),
                cells,
                lax.ppermute(head, axis, [((i + 1) % count, i) for i in range(count)]),
            ],
            axis=dim,
        )
    return cells


def mask_rims(padded):
    count = lax.axis_size("lat")
    where_lat = lax.axis_index("lat")
    lines = jnp.arange(padded.shape[2])
    drop = (lines == 0) & (where_lat == 0) | (lines == padded.shape[2] - 1) & (
        where_lat == count - 1
    )
    return jnp.where(drop[None, None, :, None], jnp.zeros((), padded.dtype), padded)


def pad_levels(field):
    return jnp.pad(field, ((0, 0), (1, 1), (0, 0), (0, 0)))


def plain_body(inputs, weights, out_grad):
    chans, levels, height, width = inputs.shape
    input_pad = pad_levels(mask_rims(padded_2(inputs, (("lat", 2), ("lon", 3)), 1)))
    grad_inner = lax.all_gather(out_grad, "ch", axis=0, tiled=True)
    grad_pad = pad_levels(mask_rims(padded_2(grad_inner, (("lat", 2), ("lon", 3)), 1)))
    filters = grad_pad.shape[0]
    products = jnp.dot(
        weights.reshape(chans * 27, filters),
        grad_pad.reshape(filters, -1),
        preferred_element_type=jnp.float32,
    )
    products = products.reshape((chans, 27) + tuple(grad_pad.shape[1:]))
    total = jnp.zeros((chans, levels, height, width), jnp.float32)
    pieces = []
    for tap in range(27):
        lev, lat, lon = tap // 9 - 1, tap // 3 % 3 - 1, tap % 3 - 1
        total = (
            total
            + products[
                :,
                tap,
                1 - lev : 1 - lev + levels,
                1 - lat : 1 - lat + height,
                1 - lon : 1 - lon + width,
            ]
        )
        pieces.append(
            input_pad[
                :,
                1 + lev : 1 + lev + levels,
                1 + lat : 1 + lat + height,
                1 + lon : 1 + lon + width,
            ]
        )
    columns = jnp.stack(pieces, axis=1).reshape(chans * 27, -1)
    partial_grad = lax.dot_general(
        columns,
        grad_inner.reshape(filters, -1),
        (((1,), (1,)), ((), ())),
        preferred_element_type=jnp.float32,
    )
    summed = lax.psum(partial_grad, ("lat", "lon"))
    cells = levels * height * width * lax.axis_size("lat") * lax.axis_size("lon")
    weight_grad = (summed * (1.0 / math.sqrt(cells))).reshape(chans, 27, filters)
    return (total.astype(jnp.bfloat16), weight_grad)


def move(x, target):
    pairs = []
    for i in range(32):
        to = target(i // 16, i // 4 % 4, i % 4)
        if to is not None:
            pairs.append((i, (to[0] * 4 + to[1]) * 4 + to[2]))
    return lax.ppermute(x, AXES, pairs)


def lon_by(step):
    return lambda c, a, o: (c, a, (o + step) % 4)


def lat_xor(mask):
    return lambda c, a, o: (c, a ^ mask, o)


def sibling(c, a, o):
    return (1 - c, a, o)


def north(c, a, o):
    return (c, a + 1, o) if a < 3 else None


def south(c, a, o):
    return (c, a - 1, o) if a > 0 else None


def call(kernel, outs, ins, scratch, flops, name, **kw):
    moved = sum(math.prod(x.shape) * x.dtype.itemsize for x in list(ins[1:]) + list(outs))
    return pl.pallas_call(
        kernel,
        out_shape=outs,
        in_specs=[pl.BlockSpec(memory_space=SMEM)] + [pl.BlockSpec(memory_space=VMEM)] * (len(ins) - 1),
        out_specs=[pl.BlockSpec(memory_space=VMEM)] * len(outs),
        scratch_shapes=scratch,
        cost_estimate=pl.CostEstimate(flops=flops, bytes_accessed=moved, transcendentals=0),
        compiler_params=pltpu.CompilerParams(vmem_limit_bytes=LIMIT),
        name=name,
    )(*ins)


def pack_kernel(pos, x, g, x0, x1, x2, x3, g_same, g_other, rim_lo, rim_hi, held):
    levels, height, width, chans = x.shape
    half = levels // 2
    for block in range(4):
        at = block * (chans // 4)
        lo = x[0:half, :, :, at : at + chans // 4]
        hi = x[half:levels, :, :, at : at + chans // 4]
        both = jnp.concatenate([lo, hi], axis=-1)
        held[block] = both.reshape(held.shape[1:])
    lon = pos[2]
    for step, out in enumerate((x0, x1, x2, x3)):
        out[...] = held[lax.rem(lon + step, 4)]
    right = lax.rem(pos[1], 2)
    wide = chans // 2
    g_same[...] = g[:, :, :, pl.ds(pl.multiple_of(right * wide, wide), wide)].reshape(g_same.shape)
    g_other[...] = g[:, :, :, pl.ds(pl.multiple_of((1 - right) * wide, wide), wide)].reshape(
        g_other.shape
    )
    rim_lo[...] = g[:, 0]
    rim_hi[...] = g[:, height - 1]


def taps_kernel(
    pos, x_own, x_x, x_y, x_d1, x_d2, g0, g1, g3, g2a, g2b, s0, s1, s3, s2a, s2b, out, xs, gs, gt, acc
):
    lat, core = pos[1], pos[0]
    levels, rows, circle, _ = gs.shape
    width = circle // 4
    height = rows // 4
    half = levels // 2
    span = 64

    def place(piece, lat_at, lon_at):
        gs[:, pl.ds(lat_at * height, height), lon_at * width : (lon_at + 1) * width, :] = (
            piece.reshape(levels, height, width, piece.shape[-1])
        )

    right = lax.rem(lat, 2)
    for which, sets in ((core, (g0, g1, g3, g2a, g2b)), (1 - core, (s0, s1, s3, s2a, s2b))):
        same, other = 2 * which + right, 2 * which + 1 - right
        for part, lon_at in ((sets[0], 0), (sets[1], 3), (sets[2], 1)):
            place(part[0], same, lon_at)
            place(part[1], other, lon_at)
        place(sets[3][...], same, 2)
        place(sets[4][...], other, 2)
    filters = gs.shape[-1]

    @pl.loop(0, levels * (rows // 2))
    def _(step):
        lev, pair = step // (rows // 2), lax.rem(step, rows // 2)
        block = gs[lev, pl.ds(2 * pair, 2)].reshape(2 * circle, filters)
        gt[
            pl.ds(pl.multiple_of(lev * filters, filters), filters),
            pl.ds(pl.multiple_of(pair * 2 * circle, 2 * circle), 2 * circle),
        ] = block.T

    xs[:, 0] = jnp.zeros_like(xs[:, 0])
    xs[:, rows + 1] = jnp.zeros_like(xs[:, rows + 1])
    low = lax.broadcasted_iota(jnp.int32, (circle, 2 * span), 1) < span
    for tag in range(4):
        start = (lat ^ tag) * height

        def piece(lon_from, tag=tag):
            ref, at = ((x_own, lon_from), (x_x, lon_from), (x_y, lon_from), (x_d1, lon_from))[tag]
            if tag == 3 and lon_from > 1:
                ref, at = x_d2, lon_from - 2
            return ref.at[at].reshape(half, height, width, 2 * span)

        strips = [piece((4 - at) % 4) for at in range(4)]

        @pl.loop(0, half * height)
        def _(step, strips=strips, start=start):
            lev, row = step // height, lax.rem(step, height)
            line = jnp.concatenate([s[lev, row] for s in strips], axis=0).astype(jnp.float32)
            turned = pltpu.roll(line, span, 1)
            for upper in range(2):
                same = jnp.where(low, turned, line) if upper else jnp.where(low, line, turned)
                before = pltpu.roll(same, 1, 0)
                after = pltpu.roll(same, circle - 1, 0)
                at = upper * half + lev
                xs[at, 1 + start + row, :, 0 : 2 * span] = jnp.where(low, before, same).astype(xs.dtype)
                xs[at, 1 + start + row, :, 2 * span : 4 * span] = after.astype(xs.dtype)

    acc[...] = jnp.zeros_like(acc)

    @pl.loop(0, 3)
    def _(lat_by):
        for lev in range(levels):
            first, last = max(lev - 1, 0), min(lev + 1, levels - 1)
            to = (first - lev + 1) * filters
            many = (last - first + 1) * filters
            acc[lat_by, to : to + many, :] += jnp.dot(
                gt[first * filters : (last + 1) * filters, :],
                xs[lev, pl.ds(lat_by, rows)].reshape(rows * circle, 4 * span),
                preferred_element_type=jnp.float32,
            )

    scale = 1.0 / math.sqrt(levels * rows * circle)
    most = jnp.zeros((span, filters), jnp.float32)
    for lat_by in range(3):
        for lev_at in range(3):
            block = acc[lat_by, lev_at * filters : (lev_at + 1) * filters, :].T * scale
            for lon_by_ in range(3):
                tap = (2 - lev_at) * 9 + lat_by * 3 + lon_by_
                value = block[lon_by_ * span : (lon_by_ + 1) * span]
                out[tap * span : (tap + 1) * span, :] = value
                most = jnp.maximum(most, jnp.abs(value))
    top = jnp.maximum(jnp.max(most, axis=(0, 1), keepdims=True), 1e-30)
    power = jnp.broadcast_to(jnp.ceil(jnp.log(top) * (1.0 / math.log(2.0))), (16, filters))
    out[27 * span :, :] = power
    out[0 : 27 * span, :] = out[0 : 27 * span, :] * jnp.exp2(14.0 - power[0:1])


def field_kernel(pos, after, mine, theirs, w, out, copies, acc):
    del after
    tap = pl.program_id(0)
    levels, height, width, chans = out.shape
    many = mine.shape[-1]

    @pl.when(tap == 0)
    def _():
        copies[:, 0] = jnp.zeros_like(copies[:, 0])
        copies[:, levels + 1] = jnp.zeros_like(copies[:, levels + 1])
        line_at = lax.broadcasted_iota(jnp.int32, (width, many), 0)
        for which, field in ((pos[0], mine), (1 - pos[0], theirs)):
            lanes = pl.ds(pl.multiple_of(which * many, many), many)
            for lev in range(levels):
                for row in range(height + 2):
                    line = field[lev, row, 0:width].astype(jnp.float32)
                    west = field[lev, row, width : width + 1].astype(jnp.float32)
                    east = field[lev, row, width + 8 : width + 9].astype(jnp.float32)
                    before = jnp.where(line_at == 0, west, pltpu.roll(line, 1, 0))
                    later = jnp.where(line_at == width - 1, east, pltpu.roll(line, width - 1, 0))
                    copies[0, lev + 1, row, :, lanes] = later.astype(copies.dtype)
                    copies[1, lev + 1, row, :, lanes] = field[lev, row, 0:width]
                    copies[2, lev + 1, row, :, lanes] = before.astype(copies.dtype)
        acc[...] = jnp.zeros_like(acc)

    lev_by, lat_by, lon_by_ = tap // 9, lax.rem(tap // 3, 3), lax.rem(tap, 3)
    cells = copies[lon_by_, pl.ds(2 - lev_by, levels), pl.ds(2 - lat_by, height)]
    acc[...] += lax.dot_general(
        cells.reshape(levels * height * width, 2 * many),
        w[0],
        (((1,), (1,)), ((), ())),
        preferred_element_type=jnp.float32,
    )

    @pl.when(tap == 26)
    def _():
        out[...] = acc[...].reshape(out.shape).astype(out.dtype)


def blocked_body(inputs, weights, out_grad):
    chans, levels, height, width = inputs.shape
    filters = weights.shape[2]
    bf16, f32 = jnp.bfloat16, jnp.float32
    lat, lon = lax.axis_index("lat"), lax.axis_index("lon")
    pos = jnp.stack([lax.axis_index("ch"), lat, lon]).astype(jnp.int32)
    x_cells = jnp.transpose(inputs, (1, 2, 3, 0))
    g_cells = jnp.transpose(out_grad, (1, 2, 3, 0))
    taps = jnp.transpose(weights, (1, 0, 2))
    cells = levels * height * width
    span, wide = chans // 4, filters // 4
    packed = jax.ShapeDtypeStruct((cells // 2, 2 * span), bf16)
    block = jax.ShapeDtypeStruct((cells, wide), bf16)
    rim = jax.ShapeDtypeStruct((levels, width, chans), bf16)
    x0, x1, x2, x3, g_same, g_other, rim_lo, rim_hi = call(
        pack_kernel,
        [packed] * 4 + [block] * 2 + [rim] * 2,
        (pos, x_cells, g_cells),
        [VMEM((4,) + packed.shape, bf16)],
        0,
        "pack",
    )

    to_same = lambda c, a, o: (a // 2, 2 * c + a % 2, o)
    to_other = lambda c, a, o: (a // 2, 2 * c + 1 - a % 2, o)
    g_s = move(g_same, to_same)
    g_o = move(g_other, to_other)
    x_r1 = move(x1, lon_by(1))
    x_r3 = move(x3, lon_by(-1))
    x_r2 = move(x2, lon_by(2))
    g0 = jnp.stack([g_s, g_o])
    g1 = move(g0, lon_by(1))
    g3 = move(g0, lon_by(-1))
    s0 = move(g0, sibling)
    x_own = jnp.stack([x0, x_r1, x_r2, x_r3])
    x_x = move(x_own, lat_xor(1))
    x_y = move(x_own, lat_xor(2))
    x_d1 = move(x_y[0:2], lat_xor(1))
    x_d2 = move(x_x[2:4], lat_xor(2))
    g2a = move(g1[0], lon_by(1))
    g2b = move(g3[1], lon_by(-1))
    s1 = move(g1, sibling)
    s3 = move(g3, sibling)
    s2a = move(g2a, sibling)
    s2b = move(g2b, sibling)

    from_lo = move(rim_hi, north)
    from_hi = move(rim_lo, south)
    tall = jnp.concatenate([from_lo[:, None], g_cells, from_hi[:, None]], axis=1)
    west = move(tall[:, :, width - 1], lon_by(1))
    east = move(tall[:, :, 0], lon_by(-1))
    rims = jnp.stack([jnp.broadcast_to(r[:, :, None], r.shape[:2] + (8,) + r.shape[2:]) for r in (west, east)], 2)
    mine = jnp.concatenate([tall, rims.reshape(levels, height + 2, 16, chans)], axis=2)
    theirs = move(mine, sibling)

    rows, circle = 4 * height, 4 * width
    (grads,) = call(
        taps_kernel,
        [jax.ShapeDtypeStruct((27 * span + 16, wide), f32)],
        (pos, x_own, x_x, x_y, x_d1, x_d2, g0, g1, g3, g2a, g2b, s0, s1, s3, s2a, s2b),
        [
            VMEM((levels, rows + 2, circle, 4 * span), bf16),
            VMEM((levels, rows, circle, wide), bf16),
            VMEM((levels * wide, rows * circle), bf16),
            VMEM((3, 3 * wide, 4 * span), f32),
        ],
        2 * 27 * span * wide * rows * circle * levels,
        "taps",
    )
    own = grads.astype(jnp.float16)

    weight_grad = jnp.zeros((27, chans, filters), f32)
    cut = 14 * span

    def put(total, top, bottom, lat_from, lon_from):
        factor = jnp.exp2(bottom[-1:, :].astype(f32) - 14.0)
        for piece, first, last in ((top, 0, 14), (bottom, 14, 27)):
            value = piece[0 : (last - first) * span].reshape(last - first, span, wide)
            total = lax.dynamic_update_slice(
                total, value.astype(f32) * factor[None], (first, lon_from * span, lat_from * wide)
            )
        return total

    def put_whole(total, piece, lat_from, lon_from):
        factor = jnp.exp2(piece[-1:, :].astype(f32) - 14.0)
        value = piece[0 : 27 * span].reshape(27, span, wide).astype(f32) * factor[None]
        return lax.dynamic_update_slice(total, value, (0, lon_from * span, lat_from * wide))

    from_1 = move(own, lon_by(1))
    from_3 = move(own, lon_by(-1))
    shares = {0: own, 3: from_1, 1: from_3}
    opp_top = move(from_1[:cut], lon_by(1))
    opp_bottom = move(from_3[cut:], lon_by(-1))
    for step in (0, 3, 1, 2):
        share = shares[step] if step != 2 else jnp.concatenate([opp_top, opp_bottom])
        there = lax.rem(lon + step, 4)
        weight_grad = put_whole(weight_grad, share, lat, there)
        by_x = move(share, lat_xor(1))
        by_y = move(share, lat_xor(2))
        top = move(by_y[:cut], lat_xor(1))
        bottom = move(by_x[cut:], lat_xor(2))
        weight_grad = put_whole(weight_grad, by_x, lat ^ 1, there)
        weight_grad = put_whole(weight_grad, by_y, lat ^ 2, there)
        weight_grad = put(weight_grad, top, bottom, lat ^ 3, there)

    whole = lambda t: (0, 0, 0, 0)
    field = pl.pallas_call(
        field_kernel,
        out_shape=jax.ShapeDtypeStruct((levels, height, width, chans), bf16),
        grid=(27,),
        in_specs=[
            pl.BlockSpec(memory_space=SMEM),
            pl.BlockSpec(memory_space=pl.ANY),
            pl.BlockSpec(mine.shape, whole),
            pl.BlockSpec(mine.shape, whole),
            pl.BlockSpec((1, chans, filters), lambda t: (t, 0, 0)),
        ],
        out_specs=pl.BlockSpec((levels, height, width, chans), whole),
        scratch_shapes=[
            VMEM((3, levels + 2, height + 2, width, filters), bf16),
            VMEM((cells, chans), f32),
        ],
        cost_estimate=pl.CostEstimate(
            flops=2 * 27 * chans * filters * cells, bytes_accessed=27 * chans * filters * 2, transcendentals=0
        ),
        compiler_params=pltpu.CompilerParams(vmem_limit_bytes=LIMIT),
        name="field",
    )(pos, grads, mine, theirs, taps)
    return (jnp.transpose(field, (3, 0, 1, 2)), jnp.transpose(weight_grad, (1, 0, 2)))


def body(inputs, weights, out_grad):
    chans, levels, height, width = inputs.shape
    shape = tuple(lax.axis_size(axis) for axis in AXES)
    fits = (
        shape == (2, 4, 4)
        and chans == out_grad.shape[0] == 256
        and weights.shape[2] == 512
        and levels % 2 == 0
        and height % 2 == 0
        and width % 16 == 0
    )
    return (blocked_body if fits else plain_body)(inputs, weights, out_grad)


def solution(mesh):
    in_specs = (P("ch", None, "lat", "lon"), P("ch", None, None), P("ch", None, "lat", "lon"))
    out_specs = (P("ch", None, "lat", "lon"), P("ch", None, None))
    return jax.shard_map(body, mesh=mesh, in_specs=in_specs, out_specs=out_specs, check_vma=False)
```

```python
import math

import jax
import jax.numpy as jnp
from jax import lax
from jax.experimental import pallas as pl
from jax.experimental.pallas import tpu as pltpu
from jax.sharding import PartitionSpec as P

VMEM = pltpu.VMEM
SMEM = pltpu.SMEM
AXES = ("ch", "lat", "lon")


def padded_2(cells, sides, width):
    for axis, dim in sides:
        count = lax.axis_size(axis)
        head = lax.slice_in_dim(cells, 0, width, axis=dim)
        tail = lax.slice_in_dim(cells, cells.shape[dim] - width, cells.shape[dim], axis=dim)
        cells = jnp.concatenate(
            [
                lax.ppermute(tail, axis, [(i, (i + 1) % count) for i in range(count)]),
                cells,
                lax.ppermute(head, axis, [((i + 1) % count, i) for i in range(count)]),
            ],
            axis=dim,
        )
    return cells


def mask_rims(padded):
    count = lax.axis_size("lat")
    where_lat = lax.axis_index("lat")
    lines = jnp.arange(padded.shape[2])
    drop = (lines == 0) & (where_lat == 0) | (lines == padded.shape[2] - 1) & (
        where_lat == count - 1
    )
    return jnp.where(drop[None, None, :, None], jnp.zeros((), padded.dtype), padded)


def pad_levels(field):
    return jnp.pad(field, ((0, 0), (1, 1), (0, 0), (0, 0)))


def plain_body(inputs, weights, out_grad):
    chans, levels, height, width = inputs.shape
    input_pad = pad_levels(mask_rims(padded_2(inputs, (("lat", 2), ("lon", 3)), 1)))
    grad_inner = lax.all_gather(out_grad, "ch", axis=0, tiled=True)
    grad_pad = pad_levels(mask_rims(padded_2(grad_inner, (("lat", 2), ("lon", 3)), 1)))
    filters = grad_pad.shape[0]
    products = jnp.dot(
        weights.reshape(chans * 27, filters),
        grad_pad.reshape(filters, -1),
        preferred_element_type=jnp.float32,
    )
    products = products.reshape((chans, 27) + tuple(grad_pad.shape[1:]))
    total = jnp.zeros((chans, levels, height, width), jnp.float32)
    pieces = []
    for tap in range(27):
        lev, lat, lon = tap // 9 - 1, tap // 3 % 3 - 1, tap % 3 - 1
        total = (
            total
            + products[
                :,
                tap,
                1 - lev : 1 - lev + levels,
                1 - lat : 1 - lat + height,
                1 - lon : 1 - lon + width,
            ]
        )
        pieces.append(
            input_pad[
                :,
                1 + lev : 1 + lev + levels,
                1 + lat : 1 + lat + height,
                1 + lon : 1 + lon + width,
            ]
        )
    columns = jnp.stack(pieces, axis=1).reshape(chans * 27, -1)
    partial_grad = lax.dot_general(
        columns,
        grad_inner.reshape(filters, -1),
        (((1,), (1,)), ((), ())),
        preferred_element_type=jnp.float32,
    )
    summed = lax.psum(partial_grad, ("lat", "lon"))
    cells = levels * height * width * lax.axis_size("lat") * lax.axis_size("lon")
    weight_grad = (summed * (1.0 / math.sqrt(cells))).reshape(chans, 27, filters)
    return (total.astype(jnp.bfloat16), weight_grad)


def move(x, target):
    pairs = []
    for i in range(32):
        to = target(i // 16, i // 4 % 4, i % 4)
        if to is not None:
            pairs.append((i, (to[0] * 4 + to[1]) * 4 + to[2]))
    return lax.ppermute(x, AXES, pairs)


def lon_by(step):
    return lambda c, a, o: (c, a, (o + step) % 4)


def lat_xor(mask):
    return lambda c, a, o: (c, a ^ mask, o)


def sibling(c, a, o):
    return (1 - c, a, o)


def north(c, a, o):
    return (c, a + 1, o) if a < 3 else None


def south(c, a, o):
    return (c, a - 1, o) if a > 0 else None


def call(kernel, outs, ins, scratch, flops, name, limit, held=0):
    read = len(ins) - 1 - held
    moved = sum(math.prod(x.shape) * x.dtype.itemsize for x in list(ins[1 : 1 + read]) + list(outs))
    return pl.pallas_call(
        kernel,
        out_shape=outs,
        in_specs=[pl.BlockSpec(memory_space=SMEM)]
        + [pl.BlockSpec(memory_space=VMEM)] * read
        + [pl.BlockSpec(memory_space=pl.ANY)] * held,
        out_specs=[pl.BlockSpec(memory_space=VMEM)] * len(outs),
        scratch_shapes=scratch,
        cost_estimate=pl.CostEstimate(flops=flops, bytes_accessed=moved, transcendentals=0),
        compiler_params=pltpu.CompilerParams(vmem_limit_bytes=limit * 1024 * 1024),
        name=name,
    )(*ins)


def pack_grad_kernel(pos, g, g_same, g_other):
    right = lax.rem(pos[1], 2)
    wide = g.shape[-1] // 2
    for out, half in ((g_same, right), (g_other, 1 - right)):
        out[...] = g[:, :, :, pl.ds(pl.multiple_of(half * wide, wide), wide)].reshape(out.shape)


def pack_input_kernel(pos, x, g, after, x0, x1, x2, x3, held):
    del after
    levels, height, width, chans = x.shape
    half = levels // 2
    many = x0.shape[0]
    for block in range(4):
        at = block * (chans // 4)
        lo = x[0:half, :, :, at : at + chans // 4]
        hi = x[half:levels, :, :, at : at + chans // 4]
        held[block] = jnp.concatenate([lo, hi], axis=-1).reshape(held.shape[1:])
    lon = pos[2]
    for step, out in enumerate((x0, x1, x2, x3)):
        out[0:many, :] = held[lax.rem(lon + step, 4)]
    wide = chans // 2
    for out, column in ((x1, width - 1), (x3, 0)):
        rim = g[:, :, column, :].reshape(levels * height, chans)
        out[many : many + levels * height, :] = rim[:, 0:wide]
        out[many + levels * height :, :] = rim[:, wide:]


def lines_kernel(pos, x_own, x_x, x_y, x_d, xs, blank):
    del blank
    lat = pos[1]
    levels, rows, circle, lanes = xs.shape
    rows, width, span, half = rows - 2, circle // 4, lanes // 4, levels // 2
    height = rows // 4
    xs[:, 0] = jnp.zeros_like(xs[:, 0])
    xs[:, rows + 1] = jnp.zeros_like(xs[:, rows + 1])
    low = lax.broadcasted_iota(jnp.int32, (circle, 2 * span), 1) < span
    for tag, ref in enumerate((x_own, x_x, x_y, x_d)):
        start = (lat ^ tag) * height
        strips = [ref.at[(4 - at) % 4].reshape(half, height, width, 2 * span) for at in range(4)]

        @pl.loop(0, half * height)
        def _(step, strips=strips, start=start):
            lev, row = step // height, lax.rem(step, height)
            line = jnp.concatenate([s[lev, row] for s in strips], axis=0).astype(jnp.float32)
            turned = pltpu.roll(line, span, 1)
            for upper in range(2):
                same = jnp.where(low, turned, line) if upper else jnp.where(low, line, turned)
                before = pltpu.roll(same, 1, 0)
                after = pltpu.roll(same, circle - 1, 0)
                at = upper * half + lev
                xs[at, 1 + start + row, :, 0 : 2 * span] = jnp.where(low, before, same).astype(xs.dtype)
                xs[at, 1 + start + row, :, 2 * span : 4 * span] = after.astype(xs.dtype)


def turn(gt, slot, core, first, second, levels):
    many, filters = first.shape
    line = many // levels
    for lev in range(levels):
        block = jnp.concatenate([first[lev * line : (lev + 1) * line], second[lev * line : (lev + 1) * line]], axis=0)
        gt[
            lev * filters : (lev + 1) * filters,
            pl.ds(pl.multiple_of((2 * slot + core) * 2 * line, 2 * line), 2 * line),
        ] = block.T


def add_taps(acc, gt, xs, places):
    levels, rows, circle, lanes = xs.shape
    rows, width = rows - 2, circle // 4
    filters = gt.shape[0] // levels
    deep = rows * width

    @pl.loop(0, 3)
    def _(lat_by):
        for lev in range(levels):
            first, last = max(lev - 1, 0), min(lev + 1, levels - 1)
            to = (first - lev + 1) * filters
            many = (last - first + 1) * filters
            total = acc[lat_by, to : to + many, :]
            for slot, place in enumerate(places):
                total += jnp.dot(
                    gt[first * filters : (last + 1) * filters, slot * deep : (slot + 1) * deep],
                    xs[lev, pl.ds(lat_by, rows), place * width : (place + 1) * width].reshape(deep, lanes),
                    preferred_element_type=jnp.float32,
                )
            acc[lat_by, to : to + many, :] = total


def near_kernel(pos, xs, g0, g1, g3, s0, s1, s3, after, acc, gt):
    del after
    levels = xs.shape[0]
    right = lax.rem(pos[1], 2)
    for core, parts in ((pos[0], (g0, g3, g1)), (1 - pos[0], (s0, s3, s1))):
        for slot, part in enumerate(parts):
            turn(gt, slot, core, part[right], part[1 - right], levels)
    acc[...] = jnp.zeros_like(acc)
    add_taps(acc, gt, xs, (0, 1, 3))


def far_kernel(pos, xs, part, g2a, g2b, s2a, s2b, out, gt, acc, *, early):
    levels, rows, circle, lanes = xs.shape
    span = lanes // 4
    filters = out.shape[1]
    right = lax.rem(pos[1], 2) == 0
    for core, same, other in ((pos[0], g2a, g2b), (1 - pos[0], s2a, s2b)):
        one, two = same[...], other[...]
        turn(gt, 0, core, jnp.where(right, one, two), jnp.where(right, two, one), levels)
    acc[...] = part[...]
    add_taps(acc, gt, xs, (2,))
    scale = 1.0 / math.sqrt(levels * (rows - 2) * circle)

    def place(tap):
        return tap * span + (16 if tap >= early else 0)

    most = jnp.zeros((span, filters), jnp.float32)
    for lat_by in range(3):
        for lev_at in range(3):
            block = acc[lat_by, lev_at * filters : (lev_at + 1) * filters, :].T * scale
            for lon_at in range(3):
                at = place((2 - lev_at) * 9 + lat_by * 3 + lon_at)
                value = block[lon_at * span : (lon_at + 1) * span]
                out[at : at + span, :] = value
                most = jnp.maximum(most, jnp.abs(value))
    top = jnp.maximum(jnp.max(most, axis=(0, 1), keepdims=True), 1e-30)
    power = jnp.broadcast_to(jnp.ceil(jnp.log(top) * (1.0 / math.log(2.0))), (16, filters))
    factor = jnp.exp2(14.0 - power[0:1])
    out[0 : early * span, :] = out[0 : early * span, :] * factor
    out[early * span + 16 :, :] = out[early * span + 16 :, :] * factor
    out[early * span : early * span + 16, :] = power


def field_kernel(pos, mine, theirs, w, out, copies, acc):
    step = pl.program_id(0)
    levels, height, width, chans = out.shape
    many = mine.shape[-1]

    @pl.when(step == 0)
    def _():
        copies[:, 0] = jnp.zeros_like(copies[:, 0])
        copies[:, levels + 1] = jnp.zeros_like(copies[:, levels + 1])
        line_at = lax.broadcasted_iota(jnp.int32, (width, many), 0)
        for which, field in ((pos[0], mine), (1 - pos[0], theirs)):
            lanes = pl.ds(pl.multiple_of(which * many, many), many)
            for lev in range(levels):
                for row in range(height + 2):
                    line = field[lev, row, 0:width].astype(jnp.float32)
                    west = field[lev, row, width : width + 1].astype(jnp.float32)
                    east = field[lev, row, width + 8 : width + 9].astype(jnp.float32)
                    before = jnp.where(line_at == 0, west, pltpu.roll(line, 1, 0))
                    later = jnp.where(line_at == width - 1, east, pltpu.roll(line, width - 1, 0))
                    copies[0, lev + 1, row, :, lanes] = later.astype(copies.dtype)
                    copies[1, lev + 1, row, :, lanes] = field[lev, row, 0:width]
                    copies[2, lev + 1, row, :, lanes] = before.astype(copies.dtype)
        acc[...] = jnp.zeros_like(acc)

    lev_by, lat_by = step // 3, lax.rem(step, 3)
    cells = [
        copies[at, pl.ds(2 - lev_by, levels), pl.ds(2 - lat_by, height)].reshape(
            levels * height * width, 2 * many
        )
        for at in range(3)
    ]
    acc[...] += lax.dot_general(
        jnp.concatenate(cells, axis=1),
        jnp.concatenate([w[at] for at in range(3)], axis=1),
        (((1,), (1,)), ((), ())),
        preferred_element_type=jnp.float32,
    )

    @pl.when(step == 8)
    def _():
        out[...] = acc[...].reshape(out.shape).astype(out.dtype)


def blocked_body(inputs, weights, out_grad):
    chans, levels, height, width = inputs.shape
    filters = weights.shape[2]
    bf16, f32 = jnp.bfloat16, jnp.float32
    lat, lon = lax.axis_index("lat"), lax.axis_index("lon")
    pos = jnp.stack([lax.axis_index("ch"), lat, lon]).astype(jnp.int32)
    x_cells = jnp.transpose(inputs, (1, 2, 3, 0))
    g_cells = jnp.transpose(out_grad, (1, 2, 3, 0))
    taps = jnp.transpose(weights, (1, 0, 2))
    cells = levels * height * width
    span, wide = chans // 4, filters // 4
    rows, circle = 4 * height, 4 * width
    edge = levels * height

    to_same = lambda c, a, o: (a // 2, 2 * c + a % 2, o)
    to_other = lambda c, a, o: (a // 2, 2 * c + 1 - a % 2, o)
    g_same, g_other = call(
        pack_grad_kernel, [jax.ShapeDtypeStruct((cells, wide), bf16)] * 2, (pos, g_cells), [], 0, "pack_grad", 16
    )
    g_s = move(g_same, to_same)
    g_o = move(g_other, to_other)
    many = cells // 2
    x0, x1, x2, x3 = call(
        pack_input_kernel,
        [jax.ShapeDtypeStruct((many + extra, 2 * span), bf16) for extra in (0, 2 * edge, 0, 2 * edge)],
        (pos, x_cells, g_cells, g_same),
        [VMEM((4, many, 2 * span), bf16)],
        0,
        "pack_input",
        16,
        held=1,
    )
    x_r1 = move(x1, lon_by(1))
    x_r3 = move(x3, lon_by(-1))
    x_r2 = move(x2, lon_by(2))
    g0 = jnp.stack([g_s, g_o])
    g1 = move(g0, lon_by(1))
    g3 = move(g0, lon_by(-1))

    def column(message):
        rim = message[many:].reshape(2, edge, span * 2)
        rim = jnp.concatenate([rim[0], rim[1]], axis=-1).reshape(levels, height, 1, chans)
        return jnp.broadcast_to(rim, (levels, height, 8, chans))

    broad = jnp.concatenate([g_cells, column(x_r1), column(x_r3)], axis=2)
    from_lo = move(broad[:, height - 1], north)
    from_hi = move(broad[:, 0], south)
    mine = jnp.concatenate([from_lo[:, None], broad, from_hi[:, None]], axis=1)
    theirs = move(mine, sibling)

    s0 = move(g0, sibling)
    x_own = jnp.stack([x0, x_r1[:many], x_r2, x_r3[:many]])
    x_x = move(x_own, lat_xor(1))
    x_y = move(x_own, lat_xor(2))
    x_d = move(x_own, lat_xor(3))
    g2a = move(g1[0], lon_by(1))
    g2b = move(g3[1], lon_by(-1))
    s1 = move(g1, sibling)
    s3 = move(g3, sibling)
    s2a = move(g2a, sibling)
    s2b = move(g2b, sibling)

    xs, total = pl.pallas_call(
        lines_kernel,
        out_shape=[
            jax.ShapeDtypeStruct((levels, rows + 2, circle, 4 * span), bf16),
            jax.ShapeDtypeStruct((27, chans, filters), f32),
        ],
        in_specs=[pl.BlockSpec(memory_space=SMEM)] + [pl.BlockSpec(memory_space=VMEM)] * 4,
        out_specs=[pl.BlockSpec(memory_space=VMEM), pl.BlockSpec(memory_space=pl.ANY)],
        cost_estimate=pl.CostEstimate(flops=0, bytes_accessed=12 * 2**20, transcendentals=0),
        compiler_params=pltpu.CompilerParams(vmem_limit_bytes=24 * 1024 * 1024),
        name="lines",
    )(pos, x_own, x_x, x_y, x_d)

    whole = lambda t: (0, 0, 0, 0)
    field = pl.pallas_call(
        field_kernel,
        out_shape=jax.ShapeDtypeStruct((levels, height, width, chans), bf16),
        grid=(9,),
        in_specs=[
            pl.BlockSpec(memory_space=SMEM),
            pl.BlockSpec(mine.shape, whole),
            pl.BlockSpec(mine.shape, whole),
            pl.BlockSpec((3, chans, filters), lambda t: (t, 0, 0)),
        ],
        out_specs=pl.BlockSpec((levels, height, width, chans), whole),
        scratch_shapes=[
            VMEM((3, levels + 2, height + 2, width, filters), bf16),
            VMEM((cells, chans), f32),
        ],
        cost_estimate=pl.CostEstimate(
            flops=4 * 27 * chans * filters * cells, bytes_accessed=27 * chans * filters * 2, transcendentals=0
        ),
        compiler_params=pltpu.CompilerParams(vmem_limit_bytes=32 * 1024 * 1024),
        name="field",
    )(pos, mine, theirs, taps)

    work = 2 * 27 * span * wide * rows * circle * levels
    (part,) = call(
        near_kernel,
        [jax.ShapeDtypeStruct((3, 3 * wide, 4 * span), f32)],
        (pos, xs, g0, g1, g3, s0, s1, s3, field),
        [VMEM((levels * wide, 3 * rows * width), bf16)],
        work,
        "near",
        28,
        held=1,
    )
    early = 6
    (grads,) = call(
        lambda *refs: far_kernel(*refs, early=early),
        [jax.ShapeDtypeStruct((27 * span + 16, wide), f32)],
        (pos, xs, part, g2a, g2b, s2a, s2b),
        [VMEM((levels * wide, rows * width), bf16), VMEM((3, 3 * wide, 4 * span), f32)],
        work // 3,
        "far",
        28,
    )
    own = grads.astype(jnp.float16)

    front, back = early * span + 16, early * span
    middle = 16 + 10 * span

    def put(total, piece, power, first, last, lat_from, lon_from):
        factor = jnp.exp2(power.astype(f32) - 14.0)
        value = piece.reshape(last - first, span, wide).astype(f32) * factor[None]
        return lax.dynamic_update_slice(total, value, (first, lon_from * span, lat_from * wide))

    def put_late(total, piece, lat_from, lon_from):
        return put(total, piece[16:], piece[0:1], early, 27, lat_from, lon_from)

    def put_split(total, top, bottom, lat_from, lon_from):
        total = put(total, top[16:], top[0:1], early, early + 10, lat_from, lon_from)
        return put(total, bottom, top[0:1], early + 10, 27, lat_from, lon_from)

    def put_whole(total, piece, lat_from, lon_from):
        total = put(total, piece[:back], piece[back : back + 1], 0, early, lat_from, lon_from)
        return put_late(total, piece[back:], lat_from, lon_from)

    late = own[back:]
    from_1 = move(late, lon_by(1))
    from_3 = move(late, lon_by(-1))
    by_x = move(own, lat_xor(1))
    by_y = move(own, lat_xor(2))
    cut = back + middle
    top = move(by_y[:cut], lat_xor(1))
    bottom = move(by_x[cut:], lat_xor(2))
    opp_top = move(from_1[:middle], lon_by(1))
    opp_bottom = move(from_3[middle:], lon_by(-1))

    def exchange(share):
        to_x = move(share, lat_xor(1))
        to_y = move(share, lat_xor(2))
        return to_x, to_y, move(to_y[:middle], lat_xor(1)), move(to_x[middle:], lat_xor(2))

    block = jnp.concatenate([own[:front], by_x[:front], by_y[:front], top[:front]])
    near_1 = exchange(from_1)
    near_3 = exchange(from_3)
    early_1 = move(block, lon_by(1))
    early_3 = move(block, lon_by(-1))
    from_2 = jnp.concatenate([opp_top, opp_bottom])
    across = exchange(from_2)
    early_2a = move(early_1[: 2 * front], lon_by(1))
    early_2b = move(early_3[2 * front :], lon_by(-1))

    total = put_whole(total, own, lat, lon)
    total = put_whole(total, by_x, lat ^ 1, lon)
    total = put_whole(total, by_y, lat ^ 2, lon)
    total = put(total, top[:back], top[back : back + 1], 0, early, lat ^ 3, lon)
    total = put_split(total, top[back:], bottom, lat ^ 3, lon)

    def put_early(total, pieces, tags, lon_from):
        for at, tag in enumerate(tags):
            piece = pieces[at * front : (at + 1) * front]
            total = put(total, piece[:back], piece[back : back + 1], 0, early, lat ^ tag, lon_from)
        return total

    for share, (to_x, to_y, upper, lower), step in ((from_1, near_1, 3), (from_3, near_3, 1)):
        there = lax.rem(lon + step, 4)
        total = put_late(total, share, lat, there)
        total = put_late(total, to_x, lat ^ 1, there)
        total = put_late(total, to_y, lat ^ 2, there)
        total = put_split(total, upper, lower, lat ^ 3, there)
    there = lax.rem(lon + 2, 4)
    total = put_early(total, early_1, (0, 1, 2, 3), lax.rem(lon + 3, 4))
    total = put_early(total, early_3, (0, 1, 2, 3), lax.rem(lon + 1, 4))
    total = put_late(total, from_2, lat, there)
    total = put_late(total, across[0], lat ^ 1, there)
    total = put_late(total, across[1], lat ^ 2, there)
    total = put_early(total, early_2a, (0, 1), there)
    total = put_early(total, early_2b, (2, 3), there)
    total = put_split(total, across[2], across[3], lat ^ 3, there)
    return (jnp.transpose(field, (3, 0, 1, 2)), jnp.transpose(total, (1, 0, 2)))


def body(inputs, weights, out_grad):
    chans, levels, height, width = inputs.shape
    shape = tuple(lax.axis_size(axis) for axis in AXES)
    fits = (
        shape == (2, 4, 4)
        and chans == out_grad.shape[0] == 256
        and weights.shape[2] == 512
        and levels % 2 == 0
        and height % 2 == 0
        and width % 16 == 0
    )
    return (blocked_body if fits else plain_body)(inputs, weights, out_grad)


def solution(mesh):
    in_specs = (P("ch", None, "lat", "lon"), P("ch", None, None), P("ch", None, "lat", "lon"))
    out_specs = (P("ch", None, "lat", "lon"), P("ch", None, None))
    return jax.shard_map(body, mesh=mesh, in_specs=in_specs, out_specs=out_specs, check_vma=False)
```

```python
import math

import jax
import jax.numpy as jnp
from jax import lax
from jax.experimental import pallas as pl
from jax.experimental.pallas import tpu as pltpu
from jax.sharding import PartitionSpec as P

VMEM = pltpu.VMEM
SMEM = pltpu.SMEM
AXES = ("ch", "lat", "lon")


def padded_2(cells, sides, width):
    for axis, dim in sides:
        count = lax.axis_size(axis)
        head = lax.slice_in_dim(cells, 0, width, axis=dim)
        tail = lax.slice_in_dim(cells, cells.shape[dim] - width, cells.shape[dim], axis=dim)
        cells = jnp.concatenate(
            [
                lax.ppermute(tail, axis, [(i, (i + 1) % count) for i in range(count)]),
                cells,
                lax.ppermute(head, axis, [((i + 1) % count, i) for i in range(count)]),
            ],
            axis=dim,
        )
    return cells


def mask_rims(padded):
    count = lax.axis_size("lat")
    where_lat = lax.axis_index("lat")
    lines = jnp.arange(padded.shape[2])
    drop = (lines == 0) & (where_lat == 0) | (lines == padded.shape[2] - 1) & (
        where_lat == count - 1
    )
    return jnp.where(drop[None, None, :, None], jnp.zeros((), padded.dtype), padded)


def pad_levels(field):
    return jnp.pad(field, ((0, 0), (1, 1), (0, 0), (0, 0)))


def plain_body(inputs, weights, out_grad):
    chans, levels, height, width = inputs.shape
    input_pad = pad_levels(mask_rims(padded_2(inputs, (("lat", 2), ("lon", 3)), 1)))
    grad_inner = lax.all_gather(out_grad, "ch", axis=0, tiled=True)
    grad_pad = pad_levels(mask_rims(padded_2(grad_inner, (("lat", 2), ("lon", 3)), 1)))
    filters = grad_pad.shape[0]
    products = jnp.dot(
        weights.reshape(chans * 27, filters),
        grad_pad.reshape(filters, -1),
        preferred_element_type=jnp.float32,
    )
    products = products.reshape((chans, 27) + tuple(grad_pad.shape[1:]))
    total = jnp.zeros((chans, levels, height, width), jnp.float32)
    pieces = []
    for tap in range(27):
        lev, lat, lon = tap // 9 - 1, tap // 3 % 3 - 1, tap % 3 - 1
        total = (
            total
            + products[
                :,
                tap,
                1 - lev : 1 - lev + levels,
                1 - lat : 1 - lat + height,
                1 - lon : 1 - lon + width,
            ]
        )
        pieces.append(
            input_pad[
                :,
                1 + lev : 1 + lev + levels,
                1 + lat : 1 + lat + height,
                1 + lon : 1 + lon + width,
            ]
        )
    columns = jnp.stack(pieces, axis=1).reshape(chans * 27, -1)
    partial_grad = lax.dot_general(
        columns,
        grad_inner.reshape(filters, -1),
        (((1,), (1,)), ((), ())),
        preferred_element_type=jnp.float32,
    )
    summed = lax.psum(partial_grad, ("lat", "lon"))
    cells = levels * height * width * lax.axis_size("lat") * lax.axis_size("lon")
    weight_grad = (summed * (1.0 / math.sqrt(cells))).reshape(chans, 27, filters)
    return (total.astype(jnp.bfloat16), weight_grad)


def move(x, target):
    pairs = []
    for i in range(32):
        to = target(i // 16, i // 4 % 4, i % 4)
        if to is not None:
            pairs.append((i, (to[0] * 4 + to[1]) * 4 + to[2]))
    return lax.ppermute(x, AXES, pairs)


def lon_by(step):
    return lambda c, a, o: (c, a, (o + step) % 4)


def lat_xor(mask):
    return lambda c, a, o: (c, a ^ mask, o)


def sibling(c, a, o):
    return (1 - c, a, o)


def north(c, a, o):
    return (c, a + 1, o) if a < 3 else None


def south(c, a, o):
    return (c, a - 1, o) if a > 0 else None


def call(kernel, outs, ins, scratch, flops, name, limit, held=0):
    read = len(ins) - 1 - held
    moved = sum(math.prod(x.shape) * x.dtype.itemsize for x in list(ins[1 : 1 + read]) + list(outs))
    return pl.pallas_call(
        kernel,
        out_shape=outs,
        in_specs=[pl.BlockSpec(memory_space=SMEM)]
        + [pl.BlockSpec(memory_space=VMEM)] * read
        + [pl.BlockSpec(memory_space=pl.ANY)] * held,
        out_specs=[pl.BlockSpec(memory_space=VMEM)] * len(outs),
        scratch_shapes=scratch,
        cost_estimate=pl.CostEstimate(flops=flops, bytes_accessed=moved, transcendentals=0),
        compiler_params=pltpu.CompilerParams(vmem_limit_bytes=limit * 1024 * 1024),
        name=name,
    )(*ins)


def pack_grad_kernel(pos, g, g_same, g_other):
    right = lax.rem(pos[1], 2)
    wide = g.shape[-1] // 2
    for out, half in ((g_same, right), (g_other, 1 - right)):
        out[...] = g[:, :, :, pl.ds(pl.multiple_of(half * wide, wide), wide)].reshape(out.shape)


def pack_input_kernel(pos, x, g, after, x0, x1, x2, x3, held):
    del after
    levels, height, width, chans = x.shape
    half = levels // 2
    many = x0.shape[0]
    for block in range(4):
        at = block * (chans // 4)
        lo = x[0:half, :, :, at : at + chans // 4]
        hi = x[half:levels, :, :, at : at + chans // 4]
        held[block] = jnp.concatenate([lo, hi], axis=-1).reshape(held.shape[1:])
    lon = pos[2]
    for step, out in enumerate((x0, x1, x2, x3)):
        out[0:many, :] = held[lax.rem(lon + step, 4)]
    wide = chans // 2
    for out, column in ((x1, width - 1), (x3, 0)):
        rim = g[:, :, column, :].reshape(levels * height, chans)
        out[many : many + levels * height, :] = rim[:, 0:wide]
        out[many + levels * height :, :] = rim[:, wide:]


def rims_kernel(pos, g, from_west, from_east, after1, after2, broad, low, high):
    del after1, after2
    levels, height, width, chans = g.shape
    many = from_west.shape[0] - 2 * levels * height
    wide = chans // 2
    broad[:, :, 0:width, :] = g[...]
    for message, at in ((from_west, width), (from_east, width + 8)):
        for half in range(2):
            first = many + half * levels * height
            rim = message[first : first + levels * height, :].reshape(levels, height, 1, wide)
            broad[:, :, at : at + 8, half * wide : (half + 1) * wide] = jnp.broadcast_to(
                rim, (levels, height, 8, wide)
            )
    low[...] = broad[:, 0]
    high[...] = broad[:, height - 1]


def lines_kernel(pos, x_own, x_x, x_y, x_d, xs, blank):
    del blank
    lat = pos[1]
    levels, rows, circle, lanes = xs.shape
    rows, width, span, half = rows - 2, circle // 4, lanes // 4, levels // 2
    height = rows // 4
    xs[:, 0] = jnp.zeros_like(xs[:, 0])
    xs[:, rows + 1] = jnp.zeros_like(xs[:, rows + 1])
    low = lax.broadcasted_iota(jnp.int32, (circle, 2 * span), 1) < span
    for tag, ref in enumerate((x_own, x_x, x_y, x_d)):
        start = (lat ^ tag) * height
        strips = [ref.at[(4 - at) % 4].reshape(half, height, width, 2 * span) for at in range(4)]

        @pl.loop(0, half * height)
        def _(step, strips=strips, start=start):
            lev, row = step // height, lax.rem(step, height)
            line = jnp.concatenate([s[lev, row] for s in strips], axis=0).astype(jnp.float32)
            turned = pltpu.roll(line, span, 1)
            for upper in range(2):
                same = jnp.where(low, turned, line) if upper else jnp.where(low, line, turned)
                before = pltpu.roll(same, 1, 0)
                after = pltpu.roll(same, circle - 1, 0)
                at = upper * half + lev
                xs[at, 1 + start + row, :, 0 : 2 * span] = jnp.where(low, before, same).astype(xs.dtype)
                xs[at, 1 + start + row, :, 2 * span : 4 * span] = after.astype(xs.dtype)


def turn(gt, slot, core, first, second, levels):
    many, filters = first.shape
    line = many // levels
    for lev in range(levels):
        block = jnp.concatenate([first[lev * line : (lev + 1) * line], second[lev * line : (lev + 1) * line]], axis=0)
        gt[
            lev * filters : (lev + 1) * filters,
            pl.ds(pl.multiple_of((2 * slot + core) * 2 * line, 2 * line), 2 * line),
        ] = block.T


def add_taps(acc, gt, xs, places):
    levels, rows, circle, lanes = xs.shape
    rows, width = rows - 2, circle // 4
    filters = gt.shape[0] // levels
    deep = rows * width

    @pl.loop(0, 3)
    def _(lat_by):
        for lev in range(levels):
            first, last = max(lev - 1, 0), min(lev + 1, levels - 1)
            to = (first - lev + 1) * filters
            many = (last - first + 1) * filters
            total = acc[lat_by, to : to + many, :]
            for slot, place in enumerate(places):
                total += jnp.dot(
                    gt[first * filters : (last + 1) * filters, slot * deep : (slot + 1) * deep],
                    xs[lev, pl.ds(lat_by, rows), place * width : (place + 1) * width].reshape(deep, lanes),
                    preferred_element_type=jnp.float32,
                )
            acc[lat_by, to : to + many, :] = total


def near_kernel(pos, xs, g0, g1, g3, s0, s1, s3, acc, gt):
    levels = xs.shape[0]
    right = lax.rem(pos[1], 2)
    for core, parts in ((pos[0], (g0, g3, g1)), (1 - pos[0], (s0, s3, s1))):
        for slot, part in enumerate(parts):
            turn(gt, slot, core, part[right], part[1 - right], levels)
    acc[...] = jnp.zeros_like(acc)
    add_taps(acc, gt, xs, (0, 1, 3))


def far_kernel(pos, xs, part, g2a, g2b, s2a, s2b, after, out, gt, acc):
    del after
    levels, rows, circle, lanes = xs.shape
    span = lanes // 4
    filters = out.shape[1]
    right = lax.rem(pos[1], 2) == 0
    for core, same, other in ((pos[0], g2a, g2b), (1 - pos[0], s2a, s2b)):
        one, two = same[...], other[...]
        turn(gt, 0, core, jnp.where(right, one, two), jnp.where(right, two, one), levels)
    acc[...] = part[...]
    add_taps(acc, gt, xs, (2,))
    scale = 1.0 / math.sqrt(levels * (rows - 2) * circle)

    most = jnp.zeros((span, filters), jnp.float32)
    for lat_by in range(3):
        for lev_at in range(3):
            block = acc[lat_by, lev_at * filters : (lev_at + 1) * filters, :].T * scale
            for lon_at in range(3):
                at = ((2 - lev_at) * 9 + lat_by * 3 + lon_at) * span
                value = block[lon_at * span : (lon_at + 1) * span]
                out[at : at + span, :] = value
                most = jnp.maximum(most, jnp.abs(value))
    top = jnp.maximum(jnp.max(most, axis=(0, 1), keepdims=True), 1e-30)
    power = jnp.broadcast_to(jnp.ceil(jnp.log(top) * (1.0 / math.log(2.0))), (16, filters))
    out[27 * span :, :] = power
    out[0 : 27 * span, :] = out[0 : 27 * span, :] * jnp.exp2(14.0 - power[0:1])


def field_kernel(pos, after, mine, theirs, w, out, copies, acc):
    del after
    step = pl.program_id(0)
    levels, height, width, chans = out.shape
    many = mine.shape[-1]

    @pl.when(step == 0)
    def _():
        copies[:, 0] = jnp.zeros_like(copies[:, 0])
        copies[:, levels + 1] = jnp.zeros_like(copies[:, levels + 1])
        line_at = lax.broadcasted_iota(jnp.int32, (width, many), 0)
        for which, field in ((pos[0], mine), (1 - pos[0], theirs)):
            lanes = pl.ds(pl.multiple_of(which * many, many), many)
            for lev in range(levels):
                for row in range(height + 2):
                    line = field[lev, row, 0:width].astype(jnp.float32)
                    west = field[lev, row, width : width + 1].astype(jnp.float32)
                    east = field[lev, row, width + 8 : width + 9].astype(jnp.float32)
                    before = jnp.where(line_at == 0, west, pltpu.roll(line, 1, 0))
                    later = jnp.where(line_at == width - 1, east, pltpu.roll(line, width - 1, 0))
                    copies[0, lev + 1, row, :, lanes] = later.astype(copies.dtype)
                    copies[1, lev + 1, row, :, lanes] = field[lev, row, 0:width]
                    copies[2, lev + 1, row, :, lanes] = before.astype(copies.dtype)
        acc[...] = jnp.zeros_like(acc)

    lev_by, lat_by = step // 3, lax.rem(step, 3)
    cells = [
        copies[at, pl.ds(2 - lev_by, levels), pl.ds(2 - lat_by, height)].reshape(
            levels * height * width, 2 * many
        )
        for at in range(3)
    ]
    acc[...] += lax.dot_general(
        jnp.concatenate(cells, axis=1),
        jnp.concatenate([w[at] for at in range(3)], axis=1),
        (((1,), (1,)), ((), ())),
        preferred_element_type=jnp.float32,
    )

    @pl.when(step == 8)
    def _():
        out[...] = acc[...].reshape(out.shape).astype(out.dtype)


def blocked_body(inputs, weights, out_grad):
    chans, levels, height, width = inputs.shape
    filters = weights.shape[2]
    bf16, f32 = jnp.bfloat16, jnp.float32
    lat, lon = lax.axis_index("lat"), lax.axis_index("lon")
    pos = jnp.stack([lax.axis_index("ch"), lat, lon]).astype(jnp.int32)
    x_cells = jnp.transpose(inputs, (1, 2, 3, 0))
    g_cells = jnp.transpose(out_grad, (1, 2, 3, 0))
    taps = jnp.transpose(weights, (1, 0, 2))
    cells = levels * height * width
    span, wide = chans // 4, filters // 4
    rows, circle = 4 * height, 4 * width
    edge = levels * height

    to_same = lambda c, a, o: (a // 2, 2 * c + a % 2, o)
    to_other = lambda c, a, o: (a // 2, 2 * c + 1 - a % 2, o)
    g_same, g_other = call(
        pack_grad_kernel, [jax.ShapeDtypeStruct((cells, wide), bf16)] * 2, (pos, g_cells), [], 0, "pack_grad", 16
    )
    g_s = move(g_same, to_same)
    g_o = move(g_other, to_other)
    many = cells // 2
    x0, x1, x2, x3 = call(
        pack_input_kernel,
        [jax.ShapeDtypeStruct((many + extra, 2 * span), bf16) for extra in (0, 2 * edge, 0, 2 * edge)],
        (pos, x_cells, g_cells, g_same),
        [VMEM((4, many, 2 * span), bf16)],
        0,
        "pack_input",
        16,
        held=1,
    )
    x_r1 = move(x1, lon_by(1))
    x_r3 = move(x3, lon_by(-1))
    x_r2 = move(x2, lon_by(2))
    g0 = jnp.stack([g_s, g_o])
    g1 = move(g0, lon_by(1))
    g3 = move(g0, lon_by(-1))

    s0 = move(g0, sibling)
    x_own = jnp.stack([x0, x_r1[:many], x_r2, x_r3[:many]])
    x_x = move(x_own, lat_xor(1))
    x_y = move(x_own, lat_xor(2))
    x_d = move(x_own, lat_xor(3))
    g2a = move(g1[0], lon_by(1))
    g2b = move(g3[1], lon_by(-1))
    s1 = move(g1, sibling)
    s3 = move(g3, sibling)
    s2a = move(g2a, sibling)
    s2b = move(g2b, sibling)

    strip = jax.ShapeDtypeStruct((levels, width + 16, chans), bf16)
    broad, low, high = call(
        rims_kernel,
        [jax.ShapeDtypeStruct((levels, height, width + 16, chans), bf16), strip, strip],
        (pos, g_cells, x_r1, x_r3, x_x, x_d),
        [],
        0,
        "rims",
        16,
        held=2,
    )
    from_lo = move(high, north)
    from_hi = move(low, south)
    mine = jnp.concatenate([from_lo[:, None], broad, from_hi[:, None]], axis=1)
    theirs = move(mine, sibling)

    xs, total = pl.pallas_call(
        lines_kernel,
        out_shape=[
            jax.ShapeDtypeStruct((levels, rows + 2, circle, 4 * span), bf16),
            jax.ShapeDtypeStruct((27, chans, filters), f32),
        ],
        in_specs=[pl.BlockSpec(memory_space=SMEM)] + [pl.BlockSpec(memory_space=VMEM)] * 4,
        out_specs=[pl.BlockSpec(memory_space=VMEM), pl.BlockSpec(memory_space=pl.ANY)],
        cost_estimate=pl.CostEstimate(flops=0, bytes_accessed=12 * 2**20, transcendentals=0),
        compiler_params=pltpu.CompilerParams(vmem_limit_bytes=24 * 1024 * 1024),
        name="lines",
    )(pos, x_own, x_x, x_y, x_d)

    work = 2 * 27 * span * wide * rows * circle * levels
    (part,) = call(
        near_kernel,
        [jax.ShapeDtypeStruct((3, 3 * wide, 4 * span), f32)],
        (pos, xs, g0, g1, g3, s0, s1, s3),
        [VMEM((levels * wide, 3 * rows * width), bf16)],
        work,
        "near",
        28,
    )
    (grads,) = call(
        far_kernel,
        [jax.ShapeDtypeStruct((27 * span + 16, wide), f32)],
        (pos, xs, part, g2a, g2b, s2a, s2b, theirs),
        [VMEM((levels * wide, rows * width), bf16), VMEM((3, 3 * wide, 4 * span), f32)],
        work // 3,
        "far",
        28,
        held=1,
    )
    own = grads.astype(jnp.float16)

    early = 7
    cut, end = early * span, 27 * span
    size = own.shape[0] - cut
    half = size // 32 * 16
    step_rows = cut + 16

    def to_plane(share):
        return [move(share, lat_xor(tag)) for tag in (1, 2, 3)]

    late = own[cut:]
    from_3 = move(late, lon_by(1))
    from_1 = move(late, lon_by(-1))
    plane = [own] + to_plane(own)
    block = [x for p in plane for x in (p[:cut], p[end:])]
    both = to_plane(jnp.concatenate([from_3, from_1]))
    by_3 = move(jnp.concatenate([from_3[:half]] + block), lon_by(1))
    by_1 = move(jnp.concatenate([from_1[half:]] + block), lon_by(-1))
    from_2 = jnp.concatenate([by_3[:half], by_1[: size - half]])
    across = to_plane(from_2)
    early_3, early_1 = by_3[half:], by_1[size - half :]
    early_2a = move(early_3[: 2 * step_rows], lon_by(1))
    early_2b = move(early_1[2 * step_rows :], lon_by(-1))

    whole = lambda t: (0, 0, 0, 0)
    field = pl.pallas_call(
        field_kernel,
        out_shape=jax.ShapeDtypeStruct((levels, height, width, chans), bf16),
        grid=(9,),
        in_specs=[
            pl.BlockSpec(memory_space=SMEM),
            pl.BlockSpec(memory_space=pl.ANY),
            pl.BlockSpec(mine.shape, whole),
            pl.BlockSpec(mine.shape, whole),
            pl.BlockSpec((3, chans, filters), lambda t: (t, 0, 0)),
        ],
        out_specs=pl.BlockSpec((levels, height, width, chans), whole),
        scratch_shapes=[
            VMEM((3, levels + 2, height + 2, width, filters), bf16),
            VMEM((cells, chans), f32),
        ],
        cost_estimate=pl.CostEstimate(
            flops=4 * 27 * chans * filters * cells, bytes_accessed=27 * chans * filters * 2, transcendentals=0
        ),
        compiler_params=pltpu.CompilerParams(vmem_limit_bytes=56 * 1024 * 1024),
        name="field",
    )(pos, grads, mine, theirs, taps)

    def put(total, piece, power, first, last, tag, step):
        factor = jnp.exp2(power[0:1].astype(f32) - 14.0)
        value = piece.reshape(last - first, span, wide).astype(f32) * factor[None]
        at = (first, lax.rem(lon + step, 4) * span, (lat ^ tag) * wide)
        return lax.dynamic_update_slice(total, value, at)

    def put_late(total, piece, tag, step):
        return put(total, piece[: end - cut], piece[end - cut :], early, 27, tag, step)

    def put_early(total, pieces, tags, step):
        for at, tag in enumerate(tags):
            piece = pieces[at * step_rows : (at + 1) * step_rows]
            total = put(total, piece[:cut], piece[cut:], 0, early, tag, step)
        return total

    for tag, piece in enumerate(plane):
        total = put(total, piece[:end], piece[end:], 0, 27, tag, 0)
    total = put_late(total, from_3, 0, 3)
    total = put_late(total, from_1, 0, 1)
    for tag, piece in enumerate(both):
        total = put_late(total, piece[:size], tag + 1, 3)
        total = put_late(total, piece[size:], tag + 1, 1)
    total = put_early(total, early_3, (0, 1, 2, 3), 3)
    total = put_early(total, early_1, (0, 1, 2, 3), 1)
    total = put_late(total, from_2, 0, 2)
    total = put_early(total, early_2a, (0, 1), 2)
    total = put_early(total, early_2b, (2, 3), 2)
    for tag, piece in enumerate(across):
        total = put_late(total, piece, tag + 1, 2)
    return (jnp.transpose(field, (3, 0, 1, 2)), jnp.transpose(total, (1, 0, 2)))


def body(inputs, weights, out_grad):
    chans, levels, height, width = inputs.shape
    shape = tuple(lax.axis_size(axis) for axis in AXES)
    fits = (
        shape == (2, 4, 4)
        and chans == out_grad.shape[0] == 256
        and weights.shape[2] == 512
        and levels % 2 == 0
        and height % 2 == 0
        and width % 16 == 0
    )
    return (blocked_body if fits else plain_body)(inputs, weights, out_grad)


def solution(mesh):
    in_specs = (P("ch", None, "lat", "lon"), P("ch", None, None), P("ch", None, "lat", "lon"))
    out_specs = (P("ch", None, "lat", "lon"), P("ch", None, None))
    return jax.shard_map(body, mesh=mesh, in_specs=in_specs, out_specs=out_specs, check_vma=False)
```

```python
import math

import jax
import jax.numpy as jnp
from jax import lax
from jax.experimental import pallas as pl
from jax.experimental.pallas import tpu as pltpu
from jax.sharding import PartitionSpec as P

VMEM = pltpu.VMEM
SMEM = pltpu.SMEM
AXES = ("ch", "lat", "lon")


def padded_2(cells, sides, width):
    for axis, dim in sides:
        count = lax.axis_size(axis)
        head = lax.slice_in_dim(cells, 0, width, axis=dim)
        tail = lax.slice_in_dim(cells, cells.shape[dim] - width, cells.shape[dim], axis=dim)
        cells = jnp.concatenate(
            [
                lax.ppermute(tail, axis, [(i, (i + 1) % count) for i in range(count)]),
                cells,
                lax.ppermute(head, axis, [((i + 1) % count, i) for i in range(count)]),
            ],
            axis=dim,
        )
    return cells


def mask_rims(padded):
    count = lax.axis_size("lat")
    where_lat = lax.axis_index("lat")
    lines = jnp.arange(padded.shape[2])
    drop = (lines == 0) & (where_lat == 0) | (lines == padded.shape[2] - 1) & (
        where_lat == count - 1
    )
    return jnp.where(drop[None, None, :, None], jnp.zeros((), padded.dtype), padded)


def pad_levels(field):
    return jnp.pad(field, ((0, 0), (1, 1), (0, 0), (0, 0)))


def plain_body(inputs, weights, out_grad):
    chans, levels, height, width = inputs.shape
    input_pad = pad_levels(mask_rims(padded_2(inputs, (("lat", 2), ("lon", 3)), 1)))
    grad_inner = lax.all_gather(out_grad, "ch", axis=0, tiled=True)
    grad_pad = pad_levels(mask_rims(padded_2(grad_inner, (("lat", 2), ("lon", 3)), 1)))
    filters = grad_pad.shape[0]
    products = jnp.dot(
        weights.reshape(chans * 27, filters),
        grad_pad.reshape(filters, -1),
        preferred_element_type=jnp.float32,
    )
    products = products.reshape((chans, 27) + tuple(grad_pad.shape[1:]))
    total = jnp.zeros((chans, levels, height, width), jnp.float32)
    pieces = []
    for tap in range(27):
        lev, lat, lon = tap // 9 - 1, tap // 3 % 3 - 1, tap % 3 - 1
        total = (
            total
            + products[
                :,
                tap,
                1 - lev : 1 - lev + levels,
                1 - lat : 1 - lat + height,
                1 - lon : 1 - lon + width,
            ]
        )
        pieces.append(
            input_pad[
                :,
                1 + lev : 1 + lev + levels,
                1 + lat : 1 + lat + height,
                1 + lon : 1 + lon + width,
            ]
        )
    columns = jnp.stack(pieces, axis=1).reshape(chans * 27, -1)
    partial_grad = lax.dot_general(
        columns,
        grad_inner.reshape(filters, -1),
        (((1,), (1,)), ((), ())),
        preferred_element_type=jnp.float32,
    )
    summed = lax.psum(partial_grad, ("lat", "lon"))
    cells = levels * height * width * lax.axis_size("lat") * lax.axis_size("lon")
    weight_grad = (summed * (1.0 / math.sqrt(cells))).reshape(chans, 27, filters)
    return (total.astype(jnp.bfloat16), weight_grad)


def move(x, target):
    pairs = []
    for i in range(32):
        to = target(i // 16, i // 4 % 4, i % 4)
        if to is not None:
            pairs.append((i, (to[0] * 4 + to[1]) * 4 + to[2]))
    return lax.ppermute(x, AXES, pairs)


def lon_by(step):
    return lambda c, a, o: (c, a, (o + step) % 4)


def lat_xor(mask):
    return lambda c, a, o: (c, a ^ mask, o)


def sibling(c, a, o):
    return (1 - c, a, o)


def call(kernel, outs, ins, scratch, flops, name, limit, held=0):
    read = len(ins) - 1 - held
    moved = sum(math.prod(x.shape) * x.dtype.itemsize for x in list(ins[1 : 1 + read]) + list(outs))
    return pl.pallas_call(
        kernel,
        out_shape=outs,
        in_specs=[pl.BlockSpec(memory_space=SMEM)]
        + [pl.BlockSpec(memory_space=VMEM)] * read
        + [pl.BlockSpec(memory_space=pl.ANY)] * held,
        out_specs=[pl.BlockSpec(memory_space=VMEM)] * len(outs),
        scratch_shapes=scratch,
        cost_estimate=pl.CostEstimate(flops=flops, bytes_accessed=moved, transcendentals=0),
        compiler_params=pltpu.CompilerParams(vmem_limit_bytes=limit * 1024 * 1024),
        name=name,
    )(*ins)


def pack_grad_kernel(pos, g, g_same, g_other):
    right = lax.rem(pos[1], 2)
    wide = g.shape[-1] // 2
    for out, half in ((g_same, right), (g_other, 1 - right)):
        out[...] = g[:, :, :, pl.ds(pl.multiple_of(half * wide, wide), wide)].reshape(out.shape)


def pack_input_kernel(pos, x, g, after, x0, x1, x2, x3, held):
    del after
    levels, height, width, chans = x.shape
    half = levels // 2
    many = x0.shape[0]
    for block in range(4):
        at = block * (chans // 4)
        lo = x[0:half, :, :, at : at + chans // 4]
        hi = x[half:levels, :, :, at : at + chans // 4]
        held[block] = jnp.concatenate([lo, hi], axis=-1).reshape(held.shape[1:])
    lon = pos[2]
    for step, out in enumerate((x0, x1, x2, x3)):
        out[0:many, :] = held[lax.rem(lon + step, 4)]
    wide = chans // 2
    for out, column in ((x1, width - 1), (x3, 0)):
        rim = g[:, :, column, :].reshape(levels * height, chans)
        out[many : many + levels * height, :] = rim[:, 0:wide]
        out[many + levels * height :, :] = rim[:, wide:]


def pair_kernel(pos, one, two, out):
    del pos
    out[0] = one[...]
    out[1] = two[...]


def split_kernel(pos, here, west, east, first, second, near):
    del pos
    first[...] = west[0]
    second[...] = east[1]
    for at, part in enumerate((here, west, east)):
        near[2 * at : 2 * at + 2] = part[...]


def spread_kernel(pos, x0, x1, x2, x3, g, by_x, by_y, by_d):
    levels, height, width, chans = g.shape
    many, wide = x0.shape[0], chans // 2
    line, edge = levels * width, levels * height
    for out in (by_x, by_y, by_d):
        for at, piece in enumerate((x0, x1, x2, x3)):
            out[at * many : (at + 1) * many, :] = piece[0:many, :]
    even = lax.rem(pos[1], 2) == 0
    low, high = g[:, 0], g[:, height - 1]
    for out, upward in ((by_x, even), (by_d, jnp.logical_not(even))):
        facing = jnp.where(upward, high, low).reshape(line, chans)
        for half in range(2):
            first = 4 * many + half * line
            out[first : first + line, :] = facing[:, half * wide : (half + 1) * wide]
        first = 4 * many + 2 * line
        out[first : first + 2 * edge, :] = x1[many : many + 2 * edge, :]
        out[first + 2 * edge : first + 4 * edge, :] = x3[many : many + 2 * edge, :]


def rims_kernel(pos, g, from_west, from_east, by_x, by_d, after, mine):
    del after
    levels, height, width, chans = g.shape
    edge, line, wide = levels * height, levels * width, chans // 2
    many = from_west.shape[0] - 2 * edge
    mine[:, 1 : height + 1, 0:width, :] = g[...]

    def columns(message, first, at, rows):
        for half in range(2):
            rim = message[first + half * edge : first + (half + 1) * edge, :].reshape(levels, height, wide)
            for row, to in rows:
                mine[:, to, at : at + 8, half * wide : (half + 1) * wide] = jnp.broadcast_to(
                    rim[:, row : row + 1], (levels, 8, wide)
                )

    inner = [(row, row + 1) for row in range(height)]
    columns(from_west, many, width, inner)
    columns(from_east, many, width + 8, inner)

    def lines(message, row, to):
        first = 4 * many
        for half in range(2):
            strip = message[first + half * line : first + (half + 1) * line, :]
            mine[:, to, 0:width, half * wide : (half + 1) * wide] = strip.reshape(levels, width, wide)
        columns(message, first + 2 * line, width, [(row, to)])
        columns(message, first + 2 * line + 2 * edge, width + 8, [(row, to)])

    lat = pos[1]
    odd = lax.rem(lat, 2)

    @pl.when(odd == 1)
    def _():
        lines(by_x, height - 1, 0)
        lines(by_d, 0, height + 1)

    @pl.when(odd == 0)
    def _():
        lines(by_d, height - 1, 0)
        lines(by_x, 0, height + 1)

    @pl.when(lat == 0)
    def _():
        mine[:, 0] = jnp.zeros_like(mine[:, 0])

    @pl.when(lat == 3)
    def _():
        mine[:, height + 1] = jnp.zeros_like(mine[:, height + 1])


def lines_kernel(pos, x_own, x_x, x_y, x_d, xs, blank):
    del blank
    lat = pos[1]
    levels, rows, circle, lanes = xs.shape
    rows, width, span, half = rows - 2, circle // 4, lanes // 4, levels // 2
    height = rows // 4
    many = half * height * width
    xs[:, 0] = jnp.zeros_like(xs[:, 0])
    xs[:, rows + 1] = jnp.zeros_like(xs[:, rows + 1])
    low = lax.broadcasted_iota(jnp.int32, (circle, 2 * span), 1) < span
    for tag, ref in enumerate((x_own, x_x, x_y, x_d)):
        start = (lat ^ tag) * height
        strips = [
            ref.at[pl.ds((4 - at) % 4 * many, many)].reshape(half, height, width, 2 * span) for at in range(4)
        ]

        @pl.loop(0, half * height)
        def _(step, strips=strips, start=start):
            lev, row = step // height, lax.rem(step, height)
            line = jnp.concatenate([s[lev, row] for s in strips], axis=0).astype(jnp.float32)
            turned = pltpu.roll(line, span, 1)
            for upper in range(2):
                same = jnp.where(low, turned, line) if upper else jnp.where(low, line, turned)
                before = pltpu.roll(same, 1, 0)
                after = pltpu.roll(same, circle - 1, 0)
                at = upper * half + lev
                xs[at, 1 + start + row, :, 0 : 2 * span] = jnp.where(low, before, same).astype(xs.dtype)
                xs[at, 1 + start + row, :, 2 * span : 4 * span] = after.astype(xs.dtype)


def turn(gt, slot, core, first, second, levels):
    many, filters = first.shape
    line = many // levels
    for lev in range(levels):
        block = jnp.concatenate([first[lev * line : (lev + 1) * line], second[lev * line : (lev + 1) * line]], axis=0)
        gt[
            lev * filters : (lev + 1) * filters,
            pl.ds(pl.multiple_of((2 * slot + core) * 2 * line, 2 * line), 2 * line),
        ] = block.T


def add_taps(acc, gt, xs, places):
    levels, rows, circle, lanes = xs.shape
    rows, width = rows - 2, circle // 4
    filters = gt.shape[0] // levels
    deep = rows * width

    @pl.loop(0, 3)
    def _(lat_by):
        for lev in range(levels):
            first, last = max(lev - 1, 0), min(lev + 1, levels - 1)
            to = (first - lev + 1) * filters
            many = (last - first + 1) * filters
            total = acc[lat_by, to : to + many, :]
            for slot, place in enumerate(places):
                total += jnp.dot(
                    gt[first * filters : (last + 1) * filters, slot * deep : (slot + 1) * deep],
                    xs[lev, pl.ds(lat_by, rows), place * width : (place + 1) * width].reshape(deep, lanes),
                    preferred_element_type=jnp.float32,
                )
            acc[lat_by, to : to + many, :] = total


def near_kernel(pos, xs, g, s, acc, gt):
    levels = xs.shape[0]
    right = lax.rem(pos[1], 2)
    for core, parts in ((pos[0], g), (1 - pos[0], s)):
        for slot, at in enumerate((0, 4, 2)):
            turn(gt, slot, core, parts[at + right], parts[at + 1 - right], levels)
    acc[...] = jnp.zeros_like(acc)
    add_taps(acc, gt, xs, (0, 1, 3))


def far_kernel(pos, xs, part, g2a, g2b, s2a, s2b, after, out, gt, acc):
    del after
    levels, rows, circle, lanes = xs.shape
    span = lanes // 4
    filters = out.shape[1]
    right = lax.rem(pos[1], 2) == 0
    for core, same, other in ((pos[0], g2a, g2b), (1 - pos[0], s2a, s2b)):
        one, two = same[...], other[...]
        turn(gt, 0, core, jnp.where(right, one, two), jnp.where(right, two, one), levels)
    acc[...] = part[...]
    add_taps(acc, gt, xs, (2,))
    scale = 1.0 / math.sqrt(levels * (rows - 2) * circle)

    most = jnp.zeros((span, filters), jnp.float32)
    for lat_by in range(3):
        for lev_at in range(3):
            block = acc[lat_by, lev_at * filters : (lev_at + 1) * filters, :].T * scale
            for lon_at in range(3):
                at = ((2 - lev_at) * 9 + lat_by * 3 + lon_at) * span
                value = block[lon_at * span : (lon_at + 1) * span]
                out[at : at + span, :] = value
                most = jnp.maximum(most, jnp.abs(value))
    top = jnp.maximum(jnp.max(most, axis=(0, 1), keepdims=True), 1e-30)
    power = jnp.broadcast_to(jnp.ceil(jnp.log(top) * (1.0 / math.log(2.0))), (16, filters))
    out[27 * span :, :] = power
    out[0 : 27 * span, :] = out[0 : 27 * span, :] * jnp.exp2(14.0 - power[0:1])


def field_kernel(pos, after, mine, theirs, w, out, copies, acc):
    del after
    step = pl.program_id(0)
    levels, height, width, chans = out.shape
    many = mine.shape[-1]

    @pl.when(step == 0)
    def _():
        copies[:, 0] = jnp.zeros_like(copies[:, 0])
        copies[:, levels + 1] = jnp.zeros_like(copies[:, levels + 1])
        line_at = lax.broadcasted_iota(jnp.int32, (width, many), 0)
        for which, field in ((pos[0], mine), (1 - pos[0], theirs)):
            lanes = pl.ds(pl.multiple_of(which * many, many), many)
            for lev in range(levels):
                for row in range(height + 2):
                    line = field[lev, row, 0:width].astype(jnp.float32)
                    west = field[lev, row, width : width + 1].astype(jnp.float32)
                    east = field[lev, row, width + 8 : width + 9].astype(jnp.float32)
                    before = jnp.where(line_at == 0, west, pltpu.roll(line, 1, 0))
                    later = jnp.where(line_at == width - 1, east, pltpu.roll(line, width - 1, 0))
                    copies[0, lev + 1, row, :, lanes] = later.astype(copies.dtype)
                    copies[1, lev + 1, row, :, lanes] = field[lev, row, 0:width]
                    copies[2, lev + 1, row, :, lanes] = before.astype(copies.dtype)
        acc[...] = jnp.zeros_like(acc)

    lev_by, lat_by = step // 3, lax.rem(step, 3)
    cells = [
        copies[at, pl.ds(2 - lev_by, levels), pl.ds(2 - lat_by, height)].reshape(
            levels * height * width, 2 * many
        )
        for at in range(3)
    ]
    acc[...] += lax.dot_general(
        jnp.concatenate(cells, axis=1),
        jnp.concatenate([w[at] for at in range(3)], axis=1),
        (((1,), (1,)), ((), ())),
        preferred_element_type=jnp.float32,
    )

    @pl.when(step == 8)
    def _():
        out[...] = acc[...].reshape(out.shape).astype(out.dtype)


def blocked_body(inputs, weights, out_grad):
    chans, levels, height, width = inputs.shape
    filters = weights.shape[2]
    bf16, f32 = jnp.bfloat16, jnp.float32
    lat, lon = lax.axis_index("lat"), lax.axis_index("lon")
    pos = jnp.stack([lax.axis_index("ch"), lat, lon]).astype(jnp.int32)
    x_cells = jnp.transpose(inputs, (1, 2, 3, 0))
    g_cells = jnp.transpose(out_grad, (1, 2, 3, 0))
    taps = jnp.transpose(weights, (1, 0, 2))
    cells = levels * height * width
    span, wide = chans // 4, filters // 4
    rows, circle = 4 * height, 4 * width
    edge = levels * height

    to_same = lambda c, a, o: (a // 2, 2 * c + a % 2, o)
    to_other = lambda c, a, o: (a // 2, 2 * c + 1 - a % 2, o)
    g_same, g_other = call(
        pack_grad_kernel, [jax.ShapeDtypeStruct((cells, wide), bf16)] * 2, (pos, g_cells), [], 0, "pack_grad", 16
    )
    g_s = move(g_same, to_same)
    g_o = move(g_other, to_other)
    many = cells // 2
    x0, x1, x2, x3 = call(
        pack_input_kernel,
        [jax.ShapeDtypeStruct((many + extra, 2 * span), bf16) for extra in (0, 2 * edge, 0, 2 * edge)],
        (pos, x_cells, g_cells, g_same),
        [VMEM((4, many, 2 * span), bf16)],
        0,
        "pack_input",
        16,
        held=1,
    )
    x_r1 = move(x1, lon_by(1))
    x_r3 = move(x3, lon_by(-1))
    x_r2 = move(x2, lon_by(2))
    pair = jax.ShapeDtypeStruct((2, cells, wide), bf16)
    (g0,) = call(pair_kernel, [pair], (pos, g_s, g_o), [], 0, "pair", 16)
    g1 = move(g0, lon_by(1))
    g3 = move(g0, lon_by(-1))

    inner = 4 * many
    outer = inner + 2 * levels * width + 4 * edge
    x_own, x_own_y, x_own_d = call(
        spread_kernel,
        [jax.ShapeDtypeStruct((count, 2 * span), bf16) for count in (outer, inner, outer)],
        (pos, x0, x_r1, x_r2, x_r3, g_cells),
        [],
        0,
        "spread",
        16,
    )
    x_x = move(x_own, lat_xor(1))
    x_y = move(x_own_y, lat_xor(2))
    x_d = move(x_own_d, lat_xor(3))
    block = jax.ShapeDtypeStruct((cells, wide), bf16)
    far_a, far_b, g_near = call(
        split_kernel,
        [block, block, jax.ShapeDtypeStruct((6, cells, wide), bf16)],
        (pos, g0, g1, g3),
        [],
        0,
        "split",
        16,
    )
    g2a = move(far_a, lon_by(1))
    g2b = move(far_b, lon_by(-1))
    s_near = move(g_near, sibling)
    s2a = move(g2a, sibling)
    s2b = move(g2b, sibling)

    (mine,) = call(
        rims_kernel,
        [jax.ShapeDtypeStruct((levels, height + 2, width + 16, chans), bf16)],
        (pos, g_cells, x_r1, x_r3, x_x, x_d, s_near),
        [],
        0,
        "rims",
        16,
        held=1,
    )
    theirs = move(mine, sibling)

    xs, total = pl.pallas_call(
        lines_kernel,
        out_shape=[
            jax.ShapeDtypeStruct((levels, rows + 2, circle, 4 * span), bf16),
            jax.ShapeDtypeStruct((27, chans, filters), f32),
        ],
        in_specs=[pl.BlockSpec(memory_space=SMEM)] + [pl.BlockSpec(memory_space=VMEM)] * 4,
        out_specs=[pl.BlockSpec(memory_space=VMEM), pl.BlockSpec(memory_space=pl.ANY)],
        cost_estimate=pl.CostEstimate(flops=0, bytes_accessed=12 * 2**20, transcendentals=0),
        compiler_params=pltpu.CompilerParams(vmem_limit_bytes=24 * 1024 * 1024),
        name="lines",
    )(pos, x_own, x_x, x_y, x_d)

    work = 2 * 27 * span * wide * rows * circle * levels
    (part,) = call(
        near_kernel,
        [jax.ShapeDtypeStruct((3, 3 * wide, 4 * span), f32)],
        (pos, xs, g_near, s_near),
        [VMEM((levels * wide, 3 * rows * width), bf16)],
        work,
        "near",
        28,
    )
    (grads,) = call(
        far_kernel,
        [jax.ShapeDtypeStruct((27 * span + 16, wide), f32)],
        (pos, xs, part, g2a, g2b, s2a, s2b, theirs),
        [VMEM((levels * wide, rows * width), bf16), VMEM((3, 3 * wide, 4 * span), f32)],
        work // 3,
        "far",
        28,
        held=1,
    )
    own = grads.astype(jnp.float16)

    early = 7
    cut, end = early * span, 27 * span
    size = own.shape[0] - cut
    half = size // 32 * 16
    step_rows = cut + 16

    def to_plane(share):
        return [move(share, lat_xor(tag)) for tag in (1, 2, 3)]

    late = own[cut:]
    from_3 = move(late, lon_by(1))
    from_1 = move(late, lon_by(-1))
    plane = [own] + to_plane(own)
    block = [x for p in plane for x in (p[:cut], p[end:])]
    both = to_plane(jnp.concatenate([from_3, from_1]))
    by_3 = move(jnp.concatenate([from_3[:half]] + block), lon_by(1))
    by_1 = move(jnp.concatenate([from_1[half:]] + block), lon_by(-1))
    from_2 = jnp.concatenate([by_3[:half], by_1[: size - half]])
    across = to_plane(from_2)
    early_3, early_1 = by_3[half:], by_1[size - half :]
    early_2a = move(early_3[: 2 * step_rows], lon_by(1))
    early_2b = move(early_1[2 * step_rows :], lon_by(-1))

    whole = lambda t: (0, 0, 0, 0)
    field = pl.pallas_call(
        field_kernel,
        out_shape=jax.ShapeDtypeStruct((levels, height, width, chans), bf16),
        grid=(9,),
        in_specs=[
            pl.BlockSpec(memory_space=SMEM),
            pl.BlockSpec(memory_space=pl.ANY),
            pl.BlockSpec(mine.shape, whole),
            pl.BlockSpec(mine.shape, whole),
            pl.BlockSpec((3, chans, filters), lambda t: (t, 0, 0)),
        ],
        out_specs=pl.BlockSpec((levels, height, width, chans), whole),
        scratch_shapes=[
            VMEM((3, levels + 2, height + 2, width, filters), bf16),
            VMEM((cells, chans), f32),
        ],
        cost_estimate=pl.CostEstimate(
            flops=4 * 27 * chans * filters * cells, bytes_accessed=27 * chans * filters * 2, transcendentals=0
        ),
        compiler_params=pltpu.CompilerParams(vmem_limit_bytes=56 * 1024 * 1024),
        name="field",
    )(pos, grads, mine, theirs, taps)

    def put(total, piece, power, first, last, tag, step):
        factor = jnp.exp2(power[0:1].astype(f32) - 14.0)
        value = piece.reshape(last - first, span, wide).astype(f32) * factor[None]
        at = (first, lax.rem(lon + step, 4) * span, (lat ^ tag) * wide)
        return lax.dynamic_update_slice(total, value, at)

    def put_late(total, piece, tag, step):
        return put(total, piece[: end - cut], piece[end - cut :], early, 27, tag, step)

    def put_early(total, pieces, tags, step):
        for at, tag in enumerate(tags):
            piece = pieces[at * step_rows : (at + 1) * step_rows]
            total = put(total, piece[:cut], piece[cut:], 0, early, tag, step)
        return total

    for tag, piece in enumerate(plane):
        total = put(total, piece[:end], piece[end:], 0, 27, tag, 0)
    total = put_late(total, from_3, 0, 3)
    total = put_late(total, from_1, 0, 1)
    for tag, piece in enumerate(both):
        total = put_late(total, piece[:size], tag + 1, 3)
        total = put_late(total, piece[size:], tag + 1, 1)
    total = put_early(total, early_3, (0, 1, 2, 3), 3)
    total = put_early(total, early_1, (0, 1, 2, 3), 1)
    total = put_late(total, from_2, 0, 2)
    total = put_early(total, early_2a, (0, 1), 2)
    total = put_early(total, early_2b, (2, 3), 2)
    for tag, piece in enumerate(across):
        total = put_late(total, piece, tag + 1, 2)
    return (jnp.transpose(field, (3, 0, 1, 2)), jnp.transpose(total, (1, 0, 2)))


def body(inputs, weights, out_grad):
    chans, levels, height, width = inputs.shape
    shape = tuple(lax.axis_size(axis) for axis in AXES)
    fits = (
        shape == (2, 4, 4)
        and chans == out_grad.shape[0] == 256
        and weights.shape[2] == 512
        and levels % 2 == 0
        and height % 2 == 0
        and width % 16 == 0
    )
    return (blocked_body if fits else plain_body)(inputs, weights, out_grad)


def solution(mesh):
    in_specs = (P("ch", None, "lat", "lon"), P("ch", None, None), P("ch", None, "lat", "lon"))
    out_specs = (P("ch", None, "lat", "lon"), P("ch", None, None))
    return jax.shard_map(body, mesh=mesh, in_specs=in_specs, out_specs=out_specs, check_vma=False)
```

```python
import math

import jax
import jax.numpy as jnp
from jax import lax
from jax.experimental import pallas as pl
from jax.experimental.pallas import tpu as pltpu
from jax.sharding import PartitionSpec as P

VMEM = pltpu.VMEM
SMEM = pltpu.SMEM
AXES = ("ch", "lat", "lon")


def padded_2(cells, sides, width):
    for axis, dim in sides:
        count = lax.axis_size(axis)
        head = lax.slice_in_dim(cells, 0, width, axis=dim)
        tail = lax.slice_in_dim(cells, cells.shape[dim] - width, cells.shape[dim], axis=dim)
        cells = jnp.concatenate(
            [
                lax.ppermute(tail, axis, [(i, (i + 1) % count) for i in range(count)]),
                cells,
                lax.ppermute(head, axis, [((i + 1) % count, i) for i in range(count)]),
            ],
            axis=dim,
        )
    return cells


def mask_rims(padded):
    count = lax.axis_size("lat")
    where_lat = lax.axis_index("lat")
    lines = jnp.arange(padded.shape[2])
    drop = (lines == 0) & (where_lat == 0) | (lines == padded.shape[2] - 1) & (
        where_lat == count - 1
    )
    return jnp.where(drop[None, None, :, None], jnp.zeros((), padded.dtype), padded)


def pad_levels(field):
    return jnp.pad(field, ((0, 0), (1, 1), (0, 0), (0, 0)))


def plain_body(inputs, weights, out_grad):
    chans, levels, height, width = inputs.shape
    input_pad = pad_levels(mask_rims(padded_2(inputs, (("lat", 2), ("lon", 3)), 1)))
    grad_inner = lax.all_gather(out_grad, "ch", axis=0, tiled=True)
    grad_pad = pad_levels(mask_rims(padded_2(grad_inner, (("lat", 2), ("lon", 3)), 1)))
    filters = grad_pad.shape[0]
    products = jnp.dot(
        weights.reshape(chans * 27, filters),
        grad_pad.reshape(filters, -1),
        preferred_element_type=jnp.float32,
    )
    products = products.reshape((chans, 27) + tuple(grad_pad.shape[1:]))
    total = jnp.zeros((chans, levels, height, width), jnp.float32)
    pieces = []
    for tap in range(27):
        lev, lat, lon = tap // 9 - 1, tap // 3 % 3 - 1, tap % 3 - 1
        total = (
            total
            + products[
                :,
                tap,
                1 - lev : 1 - lev + levels,
                1 - lat : 1 - lat + height,
                1 - lon : 1 - lon + width,
            ]
        )
        pieces.append(
            input_pad[
                :,
                1 + lev : 1 + lev + levels,
                1 + lat : 1 + lat + height,
                1 + lon : 1 + lon + width,
            ]
        )
    columns = jnp.stack(pieces, axis=1).reshape(chans * 27, -1)
    partial_grad = lax.dot_general(
        columns,
        grad_inner.reshape(filters, -1),
        (((1,), (1,)), ((), ())),
        preferred_element_type=jnp.float32,
    )
    summed = lax.psum(partial_grad, ("lat", "lon"))
    cells = levels * height * width * lax.axis_size("lat") * lax.axis_size("lon")
    weight_grad = (summed * (1.0 / math.sqrt(cells))).reshape(chans, 27, filters)
    return (total.astype(jnp.bfloat16), weight_grad)


def move(x, target):
    pairs = []
    for i in range(32):
        to = target(i // 16, i // 4 % 4, i % 4)
        if to is not None:
            pairs.append((i, (to[0] * 4 + to[1]) * 4 + to[2]))
    return lax.ppermute(x, AXES, pairs)


def lon_by(step):
    return lambda c, a, o: (c, a, (o + step) % 4)


def lat_xor(mask):
    return lambda c, a, o: (c, a ^ mask, o)


def sibling(c, a, o):
    return (1 - c, a, o)


def call(kernel, outs, ins, scratch, flops, name, limit, held=0):
    read = len(ins) - 1 - held
    moved = sum(math.prod(x.shape) * x.dtype.itemsize for x in list(ins[1 : 1 + read]) + list(outs))
    return pl.pallas_call(
        kernel,
        out_shape=outs,
        in_specs=[pl.BlockSpec(memory_space=SMEM)]
        + [pl.BlockSpec(memory_space=VMEM)] * read
        + [pl.BlockSpec(memory_space=pl.ANY)] * held,
        out_specs=[pl.BlockSpec(memory_space=VMEM)] * len(outs),
        scratch_shapes=scratch,
        cost_estimate=pl.CostEstimate(flops=flops, bytes_accessed=moved, transcendentals=0),
        compiler_params=pltpu.CompilerParams(vmem_limit_bytes=limit * 1024 * 1024),
        name=name,
    )(*ins)


def pack_kernel(pos, x, g, g_same, g_other, x0, x1, x2, x3, held):
    levels, height, width, chans = x.shape
    half, wide = levels // 2, chans // 2
    right = lax.rem(pos[1], 2)
    for out, at in ((g_same, right), (g_other, 1 - right)):
        out[...] = g[:, :, :, pl.ds(pl.multiple_of(at * wide, wide), wide)].reshape(out.shape)
    many = x0.shape[0]
    for block in range(4):
        at = block * (chans // 4)
        lo = x[0:half, :, :, at : at + chans // 4]
        hi = x[half:levels, :, :, at : at + chans // 4]
        held[block] = jnp.concatenate([lo, hi], axis=-1).reshape(held.shape[1:])
    lon = pos[2]
    for step, out in enumerate((x0, x1, x2, x3)):
        out[0:many, :] = held[lax.rem(lon + step, 4)]
    for out, column in ((x1, width - 1), (x3, 0)):
        rim = g[:, :, column, :].reshape(levels * height, chans)
        out[many : many + levels * height, :] = rim[:, 0:wide]
        out[many + levels * height :, :] = rim[:, wide:]


def split_kernel(pos, here, west, east, after1, after2, after3, first, second, near):
    del pos, after1, after2, after3
    first[...] = west[0]
    second[...] = east[1]
    for at, part in enumerate((here, west, east)):
        near[2 * at : 2 * at + 2] = part[...]


def spread_kernel(pos, x0, x1, x2, x3, g, one, two, both, by_x, by_y, by_d):
    both[0] = one[...]
    both[1] = two[...]
    levels, height, width, chans = g.shape
    many, wide = x0.shape[0], chans // 2
    line, edge = levels * width, levels * height
    for out in (by_x, by_y, by_d):
        for at, piece in enumerate((x0, x1, x2, x3)):
            out[at * many : (at + 1) * many, :] = piece[0:many, :]
    even = lax.rem(pos[1], 2) == 0
    low, high = g[:, 0], g[:, height - 1]
    for out, upward in ((by_x, even), (by_d, jnp.logical_not(even))):
        facing = jnp.where(upward, high, low).reshape(line, chans)
        for half in range(2):
            first = 4 * many + half * line
            out[first : first + line, :] = facing[:, half * wide : (half + 1) * wide]
        first = 4 * many + 2 * line
        out[first : first + 2 * edge, :] = x1[many : many + 2 * edge, :]
        out[first + 2 * edge : first + 4 * edge, :] = x3[many : many + 2 * edge, :]


def rims_kernel(pos, g, from_west, from_east, by_x, by_d, after, mine):
    del after
    levels, height, width, chans = g.shape
    edge, line, wide = levels * height, levels * width, chans // 2
    many = from_west.shape[0] - 2 * edge
    mine[:, 1 : height + 1, 0:width, :] = g[...]

    def columns(message, first, at, rows):
        for half in range(2):
            rim = message[first + half * edge : first + (half + 1) * edge, :].reshape(levels, height, wide)
            for row, to in rows:
                mine[:, to, at : at + 8, half * wide : (half + 1) * wide] = jnp.broadcast_to(
                    rim[:, row : row + 1], (levels, 8, wide)
                )

    inner = [(row, row + 1) for row in range(height)]
    columns(from_west, many, width, inner)
    columns(from_east, many, width + 8, inner)

    def lines(message, row, to):
        first = 4 * many
        for half in range(2):
            strip = message[first + half * line : first + (half + 1) * line, :]
            mine[:, to, 0:width, half * wide : (half + 1) * wide] = strip.reshape(levels, width, wide)
        columns(message, first + 2 * line, width, [(row, to)])
        columns(message, first + 2 * line + 2 * edge, width + 8, [(row, to)])

    lat = pos[1]
    odd = lax.rem(lat, 2)

    @pl.when(odd == 1)
    def _():
        lines(by_x, height - 1, 0)
        lines(by_d, 0, height + 1)

    @pl.when(odd == 0)
    def _():
        lines(by_d, height - 1, 0)
        lines(by_x, 0, height + 1)

    @pl.when(lat == 0)
    def _():
        mine[:, 0] = jnp.zeros_like(mine[:, 0])

    @pl.when(lat == 3)
    def _():
        mine[:, height + 1] = jnp.zeros_like(mine[:, height + 1])


def lines_kernel(pos, x_own, x_x, x_y, x_d, xs, blank):
    del blank
    lat = pos[1]
    levels, rows, circle, lanes = xs.shape
    rows, width, span, half = rows - 2, circle // 4, lanes // 4, levels // 2
    height = rows // 4
    many = half * height * width
    xs[:, 0] = jnp.zeros_like(xs[:, 0])
    xs[:, rows + 1] = jnp.zeros_like(xs[:, rows + 1])
    low = lax.broadcasted_iota(jnp.int32, (circle, 2 * span), 1) < span
    for tag, ref in enumerate((x_own, x_x, x_y, x_d)):
        start = (lat ^ tag) * height
        strips = [
            ref.at[pl.ds((4 - at) % 4 * many, many)].reshape(half, height, width, 2 * span) for at in range(4)
        ]

        @pl.loop(0, half * height)
        def _(step, strips=strips, start=start):
            lev, row = step // height, lax.rem(step, height)
            line = jnp.concatenate([s[lev, row] for s in strips], axis=0).astype(jnp.float32)
            turned = pltpu.roll(line, span, 1)
            for upper in range(2):
                same = jnp.where(low, turned, line) if upper else jnp.where(low, line, turned)
                before = pltpu.roll(same, 1, 0)
                after = pltpu.roll(same, circle - 1, 0)
                at = upper * half + lev
                xs[at, 1 + start + row, :, 0 : 2 * span] = jnp.where(low, before, same).astype(xs.dtype)
                xs[at, 1 + start + row, :, 2 * span : 4 * span] = after.astype(xs.dtype)


def turn(gt, slot, core, first, second, levels):
    many, filters = first.shape
    line = many // levels
    for lev in range(levels):
        block = jnp.concatenate([first[lev * line : (lev + 1) * line], second[lev * line : (lev + 1) * line]], axis=0)
        gt[
            lev * filters : (lev + 1) * filters,
            pl.ds(pl.multiple_of((2 * slot + core) * 2 * line, 2 * line), 2 * line),
        ] = block.T


def add_taps(acc, gt, xs, places):
    levels, rows, circle, lanes = xs.shape
    rows, width = rows - 2, circle // 4
    filters = gt.shape[0] // levels
    deep = rows * width

    @pl.loop(0, 3)
    def _(lat_by):
        for lev in range(levels):
            first, last = max(lev - 1, 0), min(lev + 1, levels - 1)
            to = (first - lev + 1) * filters
            many = (last - first + 1) * filters
            total = acc[lat_by, to : to + many, :]
            for slot, place in enumerate(places):
                total += jnp.dot(
                    gt[first * filters : (last + 1) * filters, slot * deep : (slot + 1) * deep],
                    xs[lev, pl.ds(lat_by, rows), place * width : (place + 1) * width].reshape(deep, lanes),
                    preferred_element_type=jnp.float32,
                )
            acc[lat_by, to : to + many, :] = total


def near_kernel(pos, xs, g, s, acc, gt):
    levels = xs.shape[0]
    right = lax.rem(pos[1], 2)
    for core, parts in ((pos[0], g), (1 - pos[0], s)):
        for slot, at in enumerate((0, 4, 2)):
            turn(gt, slot, core, parts[at + right], parts[at + 1 - right], levels)
    acc[...] = jnp.zeros_like(acc)
    add_taps(acc, gt, xs, (0, 1, 3))


def far_kernel(pos, xs, part, g2a, g2b, s2a, s2b, after, out, gt, acc):
    del after
    levels, rows, circle, lanes = xs.shape
    span = lanes // 4
    filters = out.shape[1]
    right = lax.rem(pos[1], 2) == 0
    for core, same, other in ((pos[0], g2a, g2b), (1 - pos[0], s2a, s2b)):
        one, two = same[...], other[...]
        turn(gt, 0, core, jnp.where(right, one, two), jnp.where(right, two, one), levels)
    acc[...] = part[...]
    add_taps(acc, gt, xs, (2,))
    scale = 1.0 / math.sqrt(levels * (rows - 2) * circle)

    most = jnp.zeros((span, filters), jnp.float32)
    for lat_by in range(3):
        for lev_at in range(3):
            block = acc[lat_by, lev_at * filters : (lev_at + 1) * filters, :].T * scale
            for lon_at in range(3):
                at = ((2 - lev_at) * 9 + lat_by * 3 + lon_at) * span
                value = block[lon_at * span : (lon_at + 1) * span]
                out[at : at + span, :] = value
                most = jnp.maximum(most, jnp.abs(value))
    top = jnp.maximum(jnp.max(most, axis=(0, 1), keepdims=True), 1e-30)
    power = jnp.broadcast_to(jnp.ceil(jnp.log(top) * (1.0 / math.log(2.0))), (16, filters))
    out[27 * span :, :] = power
    out[0 : 27 * span, :] = out[0 : 27 * span, :] * jnp.exp2(14.0 - power[0:1])


def field_kernel(pos, after, mine, theirs, w, out, copies, acc):
    del after
    step = pl.program_id(0)
    levels, height, width, chans = out.shape
    many = mine.shape[-1]

    @pl.when(step == 0)
    def _():
        copies[:, 0] = jnp.zeros_like(copies[:, 0])
        copies[:, levels + 1] = jnp.zeros_like(copies[:, levels + 1])
        line_at = lax.broadcasted_iota(jnp.int32, (width, many), 0)
        for which, field in ((pos[0], mine), (1 - pos[0], theirs)):
            lanes = pl.ds(pl.multiple_of(which * many, many), many)
            for lev in range(levels):
                for row in range(height + 2):
                    line = field[lev, row, 0:width].astype(jnp.float32)
                    west = field[lev, row, width : width + 1].astype(jnp.float32)
                    east = field[lev, row, width + 8 : width + 9].astype(jnp.float32)
                    before = jnp.where(line_at == 0, west, pltpu.roll(line, 1, 0))
                    later = jnp.where(line_at == width - 1, east, pltpu.roll(line, width - 1, 0))
                    copies[0, lev + 1, row, :, lanes] = later.astype(copies.dtype)
                    copies[1, lev + 1, row, :, lanes] = field[lev, row, 0:width]
                    copies[2, lev + 1, row, :, lanes] = before.astype(copies.dtype)
        acc[...] = jnp.zeros_like(acc)

    lev_by, lat_by = step // 3, lax.rem(step, 3)
    cells = [
        copies[at, pl.ds(2 - lev_by, levels), pl.ds(2 - lat_by, height)].reshape(
            levels * height * width, 2 * many
        )
        for at in range(3)
    ]
    acc[...] += lax.dot_general(
        jnp.concatenate(cells, axis=1),
        jnp.concatenate([w[at] for at in range(3)], axis=1),
        (((1,), (1,)), ((), ())),
        preferred_element_type=jnp.float32,
    )

    @pl.when(step == 8)
    def _():
        out[...] = acc[...].reshape(out.shape).astype(out.dtype)


def blocked_body(inputs, weights, out_grad):
    chans, levels, height, width = inputs.shape
    filters = weights.shape[2]
    bf16, f32 = jnp.bfloat16, jnp.float32
    lat, lon = lax.axis_index("lat"), lax.axis_index("lon")
    pos = jnp.stack([lax.axis_index("ch"), lat, lon]).astype(jnp.int32)
    x_cells = jnp.transpose(inputs, (1, 2, 3, 0))
    g_cells = jnp.transpose(out_grad, (1, 2, 3, 0))
    taps = jnp.transpose(weights, (1, 0, 2))
    cells = levels * height * width
    span, wide = chans // 4, filters // 4
    rows, circle = 4 * height, 4 * width
    edge = levels * height

    to_same = lambda c, a, o: (a // 2, 2 * c + a % 2, o)
    to_other = lambda c, a, o: (a // 2, 2 * c + 1 - a % 2, o)
    many = cells // 2
    block = jax.ShapeDtypeStruct((cells, wide), bf16)
    g_same, g_other, x0, x1, x2, x3 = call(
        pack_kernel,
        [block, block]
        + [jax.ShapeDtypeStruct((many + extra, 2 * span), bf16) for extra in (0, 2 * edge, 0, 2 * edge)],
        (pos, x_cells, g_cells),
        [VMEM((4, many, 2 * span), bf16)],
        0,
        "pack",
        16,
    )
    g_s = move(g_same, to_same)
    g_o = move(g_other, to_other)
    x_r1 = move(x1, lon_by(1))
    x_r3 = move(x3, lon_by(-1))
    x_r2 = move(x2, lon_by(2))

    inner = 4 * many
    outer = inner + 2 * levels * width + 4 * edge
    g0, x_own, x_own_y, x_own_d = call(
        spread_kernel,
        [jax.ShapeDtypeStruct((2, cells, wide), bf16)]
        + [jax.ShapeDtypeStruct((count, 2 * span), bf16) for count in (outer, inner, outer)],
        (pos, x0, x_r1, x_r2, x_r3, g_cells, g_s, g_o),
        [],
        0,
        "spread",
        16,
    )
    g1 = move(g0, lon_by(1))
    g3 = move(g0, lon_by(-1))
    x_x = move(x_own, lat_xor(1))
    x_y = move(x_own_y, lat_xor(2))
    x_d = move(x_own_d, lat_xor(3))
    far_a, far_b, g_near = call(
        split_kernel,
        [block, block, jax.ShapeDtypeStruct((6, cells, wide), bf16)],
        (pos, g0, g1, g3, x_x, x_y, x_d),
        [],
        0,
        "split",
        16,
        held=3,
    )
    g2a = move(far_a, lon_by(1))
    g2b = move(far_b, lon_by(-1))
    s_near = move(g_near, sibling)
    s2a = move(g2a, sibling)
    s2b = move(g2b, sibling)

    (mine,) = call(
        rims_kernel,
        [jax.ShapeDtypeStruct((levels, height + 2, width + 16, chans), bf16)],
        (pos, g_cells, x_r1, x_r3, x_x, x_d, far_a),
        [],
        0,
        "rims",
        16,
        held=1,
    )
    theirs = move(mine, sibling)

    xs, total = pl.pallas_call(
        lines_kernel,
        out_shape=[
            jax.ShapeDtypeStruct((levels, rows + 2, circle, 4 * span), bf16),
            jax.ShapeDtypeStruct((27, chans, filters), f32),
        ],
        in_specs=[pl.BlockSpec(memory_space=SMEM)] + [pl.BlockSpec(memory_space=VMEM)] * 4,
        out_specs=[pl.BlockSpec(memory_space=VMEM), pl.BlockSpec(memory_space=pl.ANY)],
        cost_estimate=pl.CostEstimate(flops=0, bytes_accessed=2**20, transcendentals=0),
        compiler_params=pltpu.CompilerParams(vmem_limit_bytes=24 * 1024 * 1024),
        name="lines",
    )(pos, x_own, x_x, x_y, x_d)

    work = 2 * 27 * span * wide * rows * circle * levels
    (part,) = call(
        near_kernel,
        [jax.ShapeDtypeStruct((3, 3 * wide, 4 * span), f32)],
        (pos, xs, g_near, s_near),
        [VMEM((levels * wide, 3 * rows * width), bf16)],
        work,
        "near",
        28,
    )
    (grads,) = call(
        far_kernel,
        [jax.ShapeDtypeStruct((27 * span + 16, wide), f32)],
        (pos, xs, part, g2a, g2b, s2a, s2b, theirs),
        [VMEM((levels * wide, rows * width), bf16), VMEM((3, 3 * wide, 4 * span), f32)],
        work // 3,
        "far",
        28,
        held=1,
    )
    own = grads.astype(jnp.float16)

    early = 7
    cut, end = early * span, 27 * span
    size = own.shape[0] - cut
    half = size // 32 * 16
    step_rows = cut + 16

    def to_plane(share):
        return [move(share, lat_xor(tag)) for tag in (1, 2, 3)]

    late = own[cut:]
    from_3 = move(late, lon_by(1))
    from_1 = move(late, lon_by(-1))
    plane = [own] + to_plane(own)
    block = [x for p in plane for x in (p[:cut], p[end:])]
    both = to_plane(jnp.concatenate([from_3, from_1]))
    by_3 = move(jnp.concatenate([from_3[:half]] + block), lon_by(1))
    by_1 = move(jnp.concatenate([from_1[half:]] + block), lon_by(-1))
    from_2 = jnp.concatenate([by_3[:half], by_1[: size - half]])
    across = to_plane(from_2)
    early_3, early_1 = by_3[half:], by_1[size - half :]
    early_2a = move(early_3[: 2 * step_rows], lon_by(1))
    early_2b = move(early_1[2 * step_rows :], lon_by(-1))

    whole = lambda t: (0, 0, 0, 0)
    field = pl.pallas_call(
        field_kernel,
        out_shape=jax.ShapeDtypeStruct((levels, height, width, chans), bf16),
        grid=(9,),
        in_specs=[
            pl.BlockSpec(memory_space=SMEM),
            pl.BlockSpec(memory_space=pl.ANY),
            pl.BlockSpec(mine.shape, whole),
            pl.BlockSpec(mine.shape, whole),
            pl.BlockSpec((3, chans, filters), lambda t: (t, 0, 0)),
        ],
        out_specs=pl.BlockSpec((levels, height, width, chans), whole),
        scratch_shapes=[
            VMEM((3, levels + 2, height + 2, width, filters), bf16),
            VMEM((cells, chans), f32),
        ],
        cost_estimate=pl.CostEstimate(
            flops=4 * 27 * chans * filters * cells, bytes_accessed=27 * chans * filters * 2, transcendentals=0
        ),
        compiler_params=pltpu.CompilerParams(vmem_limit_bytes=56 * 1024 * 1024),
        name="field",
    )(pos, grads, mine, theirs, taps)

    def put(total, piece, power, first, last, tag, step):
        factor = jnp.exp2(power[0:1].astype(f32) - 14.0)
        value = piece.reshape(last - first, span, wide).astype(f32) * factor[None]
        at = (first, lax.rem(lon + step, 4) * span, (lat ^ tag) * wide)
        return lax.dynamic_update_slice(total, value, at)

    def put_late(total, piece, tag, step):
        return put(total, piece[: end - cut], piece[end - cut :], early, 27, tag, step)

    def put_early(total, pieces, tags, step):
        for at, tag in enumerate(tags):
            piece = pieces[at * step_rows : (at + 1) * step_rows]
            total = put(total, piece[:cut], piece[cut:], 0, early, tag, step)
        return total

    for tag, piece in enumerate(plane):
        total = put(total, piece[:end], piece[end:], 0, 27, tag, 0)
    total = put_late(total, from_3, 0, 3)
    total = put_late(total, from_1, 0, 1)
    for tag, piece in enumerate(both):
        total = put_late(total, piece[:size], tag + 1, 3)
        total = put_late(total, piece[size:], tag + 1, 1)
    total = put_early(total, early_3, (0, 1, 2, 3), 3)
    total = put_early(total, early_1, (0, 1, 2, 3), 1)
    total = put_late(total, from_2, 0, 2)
    total = put_early(total, early_2a, (0, 1), 2)
    total = put_early(total, early_2b, (2, 3), 2)
    for tag, piece in enumerate(across):
        total = put_late(total, piece, tag + 1, 2)
    return (jnp.transpose(field, (3, 0, 1, 2)), jnp.transpose(total, (1, 0, 2)))


def body(inputs, weights, out_grad):
    chans, levels, height, width = inputs.shape
    shape = tuple(lax.axis_size(axis) for axis in AXES)
    fits = (
        shape == (2, 4, 4)
        and chans == out_grad.shape[0] == 256
        and weights.shape[2] == 512
        and levels % 2 == 0
        and height % 2 == 0
        and width % 16 == 0
    )
    return (blocked_body if fits else plain_body)(inputs, weights, out_grad)


def solution(mesh):
    in_specs = (P("ch", None, "lat", "lon"), P("ch", None, None), P("ch", None, "lat", "lon"))
    out_specs = (P("ch", None, "lat", "lon"), P("ch", None, None))
    return jax.shard_map(body, mesh=mesh, in_specs=in_specs, out_specs=out_specs, check_vma=False)
```

```python
import math

import jax
import jax.numpy as jnp
from jax import lax
from jax.experimental import pallas as pl
from jax.experimental.pallas import tpu as pltpu
from jax.sharding import PartitionSpec as P

VMEM = pltpu.VMEM
SMEM = pltpu.SMEM
AXES = ("ch", "lat", "lon")


def padded_2(cells, sides, width):
    for axis, dim in sides:
        count = lax.axis_size(axis)
        head = lax.slice_in_dim(cells, 0, width, axis=dim)
        tail = lax.slice_in_dim(cells, cells.shape[dim] - width, cells.shape[dim], axis=dim)
        cells = jnp.concatenate(
            [
                lax.ppermute(tail, axis, [(i, (i + 1) % count) for i in range(count)]),
                cells,
                lax.ppermute(head, axis, [((i + 1) % count, i) for i in range(count)]),
            ],
            axis=dim,
        )
    return cells


def mask_rims(padded):
    count = lax.axis_size("lat")
    where_lat = lax.axis_index("lat")
    lines = jnp.arange(padded.shape[2])
    drop = (lines == 0) & (where_lat == 0) | (lines == padded.shape[2] - 1) & (
        where_lat == count - 1
    )
    return jnp.where(drop[None, None, :, None], jnp.zeros((), padded.dtype), padded)


def pad_levels(field):
    return jnp.pad(field, ((0, 0), (1, 1), (0, 0), (0, 0)))


def plain_body(inputs, weights, out_grad):
    chans, levels, height, width = inputs.shape
    input_pad = pad_levels(mask_rims(padded_2(inputs, (("lat", 2), ("lon", 3)), 1)))
    grad_inner = lax.all_gather(out_grad, "ch", axis=0, tiled=True)
    grad_pad = pad_levels(mask_rims(padded_2(grad_inner, (("lat", 2), ("lon", 3)), 1)))
    filters = grad_pad.shape[0]
    products = jnp.dot(
        weights.reshape(chans * 27, filters),
        grad_pad.reshape(filters, -1),
        preferred_element_type=jnp.float32,
    )
    products = products.reshape((chans, 27) + tuple(grad_pad.shape[1:]))
    total = jnp.zeros((chans, levels, height, width), jnp.float32)
    pieces = []
    for tap in range(27):
        lev, lat, lon = tap // 9 - 1, tap // 3 % 3 - 1, tap % 3 - 1
        total = (
            total
            + products[
                :,
                tap,
                1 - lev : 1 - lev + levels,
                1 - lat : 1 - lat + height,
                1 - lon : 1 - lon + width,
            ]
        )
        pieces.append(
            input_pad[
                :,
                1 + lev : 1 + lev + levels,
                1 + lat : 1 + lat + height,
                1 + lon : 1 + lon + width,
            ]
        )
    columns = jnp.stack(pieces, axis=1).reshape(chans * 27, -1)
    partial_grad = lax.dot_general(
        columns,
        grad_inner.reshape(filters, -1),
        (((1,), (1,)), ((), ())),
        preferred_element_type=jnp.float32,
    )
    summed = lax.psum(partial_grad, ("lat", "lon"))
    cells = levels * height * width * lax.axis_size("lat") * lax.axis_size("lon")
    weight_grad = (summed * (1.0 / math.sqrt(cells))).reshape(chans, 27, filters)
    return (total.astype(jnp.bfloat16), weight_grad)


def move(x, target):
    pairs = []
    for i in range(32):
        to = target(i // 16, i // 4 % 4, i % 4)
        if to is not None:
            pairs.append((i, (to[0] * 4 + to[1]) * 4 + to[2]))
    return lax.ppermute(x, AXES, pairs)


def lon_by(step):
    return lambda c, a, o: (c, a, (o + step) % 4)


def lat_xor(mask):
    return lambda c, a, o: (c, a ^ mask, o)


def sibling(c, a, o):
    return (1 - c, a, o)


def call(kernel, outs, ins, scratch, flops, name, limit, held=0):
    read = len(ins) - 1 - held
    moved = sum(math.prod(x.shape) * x.dtype.itemsize for x in list(ins[1 : 1 + read]) + list(outs))
    return pl.pallas_call(
        kernel,
        out_shape=outs,
        in_specs=[pl.BlockSpec(memory_space=SMEM)]
        + [pl.BlockSpec(memory_space=VMEM)] * read
        + [pl.BlockSpec(memory_space=pl.ANY)] * held,
        out_specs=[pl.BlockSpec(memory_space=VMEM)] * len(outs),
        scratch_shapes=scratch,
        cost_estimate=pl.CostEstimate(flops=flops, bytes_accessed=moved, transcendentals=0),
        compiler_params=pltpu.CompilerParams(vmem_limit_bytes=limit * 1024 * 1024),
        name=name,
    )(*ins)


def pack_kernel(pos, x, g, g_same, g_other, x0, x1, x2, x3, held):
    levels, height, width, chans = x.shape
    half, wide = levels // 2, chans // 2
    right = lax.rem(pos[1], 2)
    for out, at in ((g_same, right), (g_other, 1 - right)):
        out[...] = g[:, :, :, pl.ds(pl.multiple_of(at * wide, wide), wide)].reshape(out.shape)
    many = x0.shape[0]
    for block in range(4):
        at = block * (chans // 4)
        lo = x[0:half, :, :, at : at + chans // 4]
        hi = x[half:levels, :, :, at : at + chans // 4]
        held[block] = jnp.concatenate([lo, hi], axis=-1).reshape(held.shape[1:])
    lon = pos[2]
    for step, out in enumerate((x0, x1, x2, x3)):
        out[0:many, :] = held[lax.rem(lon + step, 4)]
    for out, column in ((x1, width - 1), (x3, 0)):
        rim = g[:, :, column, :].reshape(levels * height, chans)
        out[many : many + levels * height, :] = rim[:, 0:wide]
        out[many + levels * height :, :] = rim[:, wide:]


def split_kernel(pos, here, west, east, after1, after2, after3, first, second, near):
    del pos, after1, after2, after3
    first[...] = west[0]
    second[...] = east[1]
    for at, part in enumerate((here, west, east)):
        near[2 * at : 2 * at + 2] = part[...]


def spread_kernel(pos, x0, x1, x2, x3, g, one, two, both, own, rim_x, rim_d):
    levels, height, width, chans = g.shape
    many, wide = x0.shape[0], chans // 2
    line, edge = levels * width, levels * height
    both[0] = one[...]
    both[1] = two[...]
    for at, piece in enumerate((x0, x1, x2, x3)):
        own[at] = piece[0:many, :]
    even = lax.rem(pos[1], 2) == 0
    low, high = g[:, 0], g[:, height - 1]
    for out, upward in ((rim_x, even), (rim_d, jnp.logical_not(even))):
        facing = jnp.where(upward, high, low).reshape(line, chans)
        for half in range(2):
            out[half * line : (half + 1) * line, :] = facing[:, half * wide : (half + 1) * wide]
        first = 2 * line
        out[first : first + 2 * edge, :] = x1[many : many + 2 * edge, :]
        out[first + 2 * edge : first + 4 * edge, :] = x3[many : many + 2 * edge, :]


def hand_kernel(pos, rim_x, rim_d, one, two, after, to_x, to_d, both):
    del pos, after
    to_x[...] = rim_x[...]
    to_d[...] = rim_d[...]
    both[0] = one[...]
    both[1] = two[...]


def rims_kernel(pos, g, from_west, from_east, by_x, by_d, mine):
    levels, height, width, chans = g.shape
    edge, line, wide = levels * height, levels * width, chans // 2
    many = from_west.shape[0] - 2 * edge
    mine[:, 1 : height + 1, 0:width, :] = g[...]

    def columns(message, first, at, rows):
        for half in range(2):
            rim = message[first + half * edge : first + (half + 1) * edge, :].reshape(levels, height, wide)
            for row, to in rows:
                mine[:, to, at : at + 8, half * wide : (half + 1) * wide] = jnp.broadcast_to(
                    rim[:, row : row + 1], (levels, 8, wide)
                )

    inner = [(row, row + 1) for row in range(height)]
    columns(from_west, many, width, inner)
    columns(from_east, many, width + 8, inner)

    def lines(message, row, to):
        for half in range(2):
            strip = message[half * line : (half + 1) * line, :]
            mine[:, to, 0:width, half * wide : (half + 1) * wide] = strip.reshape(levels, width, wide)
        columns(message, 2 * line, width, [(row, to)])
        columns(message, 2 * line + 2 * edge, width + 8, [(row, to)])

    lat = pos[1]
    odd = lax.rem(lat, 2)

    @pl.when(odd == 1)
    def _():
        lines(by_x, height - 1, 0)
        lines(by_d, 0, height + 1)

    @pl.when(odd == 0)
    def _():
        lines(by_d, height - 1, 0)
        lines(by_x, 0, height + 1)

    @pl.when(lat == 0)
    def _():
        mine[:, 0] = jnp.zeros_like(mine[:, 0])

    @pl.when(lat == 3)
    def _():
        mine[:, height + 1] = jnp.zeros_like(mine[:, height + 1])


def lines_kernel(pos, x_own, x_x, x_y, x_d, after, xs, blank):
    del after, blank
    lat = pos[1]
    levels, rows, circle, lanes = xs.shape
    rows, width, span, half = rows - 2, circle // 4, lanes // 4, levels // 2
    height = rows // 4
    xs[:, 0] = jnp.zeros_like(xs[:, 0])
    xs[:, rows + 1] = jnp.zeros_like(xs[:, rows + 1])
    low = lax.broadcasted_iota(jnp.int32, (circle, 2 * span), 1) < span
    for tag, ref in enumerate((x_own, x_x, x_y, x_d)):
        start = (lat ^ tag) * height
        strips = [ref.at[(4 - at) % 4].reshape(half, height, width, 2 * span) for at in range(4)]

        @pl.loop(0, half * height)
        def _(step, strips=strips, start=start):
            lev, row = step // height, lax.rem(step, height)
            line = jnp.concatenate([s[lev, row] for s in strips], axis=0).astype(jnp.float32)
            turned = pltpu.roll(line, span, 1)
            for upper in range(2):
                same = jnp.where(low, turned, line) if upper else jnp.where(low, line, turned)
                before = pltpu.roll(same, 1, 0)
                after = pltpu.roll(same, circle - 1, 0)
                at = upper * half + lev
                xs[at, 1 + start + row, :, 0 : 2 * span] = jnp.where(low, before, same).astype(xs.dtype)
                xs[at, 1 + start + row, :, 2 * span : 4 * span] = after.astype(xs.dtype)


def turn(gt, slot, core, first, second, levels):
    many, filters = first.shape
    line = many // levels
    for lev in range(levels):
        block = jnp.concatenate([first[lev * line : (lev + 1) * line], second[lev * line : (lev + 1) * line]], axis=0)
        gt[
            lev * filters : (lev + 1) * filters,
            pl.ds(pl.multiple_of((2 * slot + core) * 2 * line, 2 * line), 2 * line),
        ] = block.T


def taps_kernel(pos, xs, g, s, g2, s2, out, gt, acc):
    levels, rows, circle, lanes = xs.shape
    rows, width, span = rows - 2, circle // 4, lanes // 4
    filters = gt.shape[0] // levels
    deep = rows * width
    right = lax.rem(pos[1], 2)
    for core, parts, last in ((pos[0], g, g2), (1 - pos[0], s, s2)):
        for slot, (ref, at) in enumerate(((parts, 0), (parts, 4), (last, 0), (parts, 2))):
            turn(gt, slot, core, ref[at + right], ref[at + 1 - right], levels)
    acc[...] = jnp.zeros_like(acc)

    @pl.loop(0, 3)
    def _(lat_by):
        for lev in range(levels):
            first, last = max(lev - 1, 0), min(lev + 1, levels - 1)
            to = (first - lev + 1) * filters
            many = (last - first + 1) * filters
            total = acc[lat_by, to : to + many, :]
            for place in range(4):
                total += jnp.dot(
                    gt[first * filters : (last + 1) * filters, place * deep : (place + 1) * deep],
                    xs[lev, pl.ds(lat_by, rows), place * width : (place + 1) * width].reshape(deep, lanes),
                    preferred_element_type=jnp.float32,
                )
            acc[lat_by, to : to + many, :] = total

    scale = 1.0 / math.sqrt(levels * rows * circle)
    for lat_by in range(3):
        for lev_at in range(3):
            block = acc[lat_by, lev_at * filters : (lev_at + 1) * filters, :].T * scale
            for lon_at in range(3):
                out[(2 - lev_at) * 9 + lat_by * 3 + lon_at] = block[lon_at * span : (lon_at + 1) * span]


def code_kernel(pos, held, after, out, late):
    del pos, after
    taps, span, filters = held.shape
    most = jnp.abs(held[0])
    for tap in range(1, taps):
        most = jnp.maximum(most, jnp.abs(held[tap]))
    top = jnp.maximum(jnp.max(most, axis=(0, 1), keepdims=True), 1e-30)
    power = jnp.ceil(jnp.log(top) * (1.0 / math.log(2.0))) - 15.0
    unit = jnp.broadcast_to(jnp.exp2(power), (16, filters)).astype(out.dtype).astype(jnp.float32)
    shrink = 1.0 / unit[0:1]
    skip = out.shape[0] - late.shape[0]
    for tap in range(27):
        value = held[tap] * shrink
        square = value * value
        code = (square * square * square * value * jnp.abs(value)).astype(out.dtype)
        out[tap * span : (tap + 1) * span, :] = code
        if tap * span >= skip:
            late[tap * span - skip : (tap + 1) * span - skip, :] = code
    out[27 * span :, :] = unit.astype(out.dtype)
    late[27 * span - skip :, :] = unit.astype(out.dtype)


def join_kernel(pos, own, x, y, d, west, east, after, both, by_3, by_1):
    del pos, after
    size = west.shape[0]
    cut = own.shape[0] - size
    end = own.shape[0] - 16
    half = by_3.shape[0] - 4 * (cut + 16)
    both[0:size, :] = west[...]
    both[size:, :] = east[...]
    by_3[0:half, :] = west[0:half, :]
    by_1[0 : size - half, :] = east[half:, :]
    for out, at in ((by_3, half), (by_1, size - half)):
        for piece in (own, x, y, d):
            out[at : at + cut, :] = piece[0:cut, :]
            out[at + cut : at + cut + 16, :] = piece[end:, :]
            at += cut + 16


def across_kernel(pos, by_3, by_1, after, late, early_3, early_1):
    del pos, after
    size, many = late.shape[0], early_3.shape[0]
    half = by_3.shape[0] - 2 * many
    late[0:half, :] = by_3[0:half, :]
    late[half:, :] = by_1[0 : size - half, :]
    early_3[...] = by_3[half : half + many, :]
    early_1[...] = by_1[size - half + many :, :]


def unpack_kernel(pos, *refs, pieces, span):
    count = 1 + max(piece[0] for piece in pieces)
    sources = refs[:count]
    total, buffers, sems = refs[-3:]
    wide = buffers.shape[-1]

    def target(piece):
        _, _, _, first, many, tag, step = piece
        lon_at = lax.rem(pos[2] + step, 4) * span
        lat_at = (pos[1] ^ tag) * wide
        return total.at[
            pl.ds(first, many),
            pl.ds(pl.multiple_of(lon_at, span), span),
            pl.ds(pl.multiple_of(lat_at, wide), wide),
        ]

    def copy(at):
        piece = pieces[at]
        return pltpu.make_async_copy(buffers.at[at % 2, pl.ds(0, piece[4])], target(piece), sems.at[at % 2])

    for at, (which, row, power_row, _, many, _, _) in enumerate(pieces):
        if at >= 2:
            copy(at - 2).wait()
        source = sources[which]
        unit = source[power_row : power_row + 16, :].astype(jnp.float32)[0:1]

        @pl.loop(0, many)
        def _(tap, source=source, row=row, unit=unit, at=at):
            code = source[pl.ds(pl.multiple_of(row + tap * span, 16), span), :].astype(jnp.float32)
            root = jnp.sqrt(jnp.sqrt(jnp.sqrt(jnp.abs(code)))) * unit
            buffers[at % 2, tap] = jnp.where(code < 0, -root, root)

        copy(at).start()
    for at in range(max(len(pieces) - 2, 0), len(pieces)):
        copy(at).wait()


def unpack(pos, total, sources, after, pieces, span, name):
    most = max(piece[4] for piece in pieces)
    wide = sources[0].shape[-1]
    ins = (pos, *sources, *after, total)
    return pl.pallas_call(
        lambda *refs: unpack_kernel(*refs, pieces=pieces, span=span),
        out_shape=jax.ShapeDtypeStruct(total.shape, total.dtype),
        in_specs=[pl.BlockSpec(memory_space=SMEM)]
        + [pl.BlockSpec(memory_space=VMEM)] * len(sources)
        + [pl.BlockSpec(memory_space=pl.ANY)] * (len(after) + 1),
        out_specs=pl.BlockSpec(memory_space=pl.ANY),
        scratch_shapes=[VMEM((2, most, span, wide), jnp.float32), pltpu.SemaphoreType.DMA((2,))],
        input_output_aliases={len(ins) - 1: 0},
        cost_estimate=pl.CostEstimate(flops=0, bytes_accessed=4 * 2**20, transcendentals=0),
        compiler_params=pltpu.CompilerParams(vmem_limit_bytes=24 * 1024 * 1024),
        name=name,
    )(*ins)


def field_kernel(pos, after, mine, theirs, w, out, copies, acc):
    del after
    step = pl.program_id(0)
    levels, height, width, chans = out.shape
    many = mine.shape[-1]

    @pl.when(step == 0)
    def _():
        copies[:, 0] = jnp.zeros_like(copies[:, 0])
        copies[:, levels + 1] = jnp.zeros_like(copies[:, levels + 1])
        line_at = lax.broadcasted_iota(jnp.int32, (width, many), 0)
        for which, field in ((pos[0], mine), (1 - pos[0], theirs)):
            lanes = pl.ds(pl.multiple_of(which * many, many), many)
            for lev in range(levels):
                for row in range(height + 2):
                    line = field[lev, row, 0:width].astype(jnp.float32)
                    west = field[lev, row, width : width + 1].astype(jnp.float32)
                    east = field[lev, row, width + 8 : width + 9].astype(jnp.float32)
                    before = jnp.where(line_at == 0, west, pltpu.roll(line, 1, 0))
                    later = jnp.where(line_at == width - 1, east, pltpu.roll(line, width - 1, 0))
                    copies[0, lev + 1, row, :, lanes] = later.astype(copies.dtype)
                    copies[1, lev + 1, row, :, lanes] = field[lev, row, 0:width]
                    copies[2, lev + 1, row, :, lanes] = before.astype(copies.dtype)
        acc[...] = jnp.zeros_like(acc)

    lev_by, lat_by = step // 3, lax.rem(step, 3)
    cells = [
        copies[at, pl.ds(2 - lev_by, levels), pl.ds(2 - lat_by, height)].reshape(
            levels * height * width, 2 * many
        )
        for at in range(3)
    ]
    acc[...] += lax.dot_general(
        jnp.concatenate(cells, axis=1),
        jnp.concatenate([w[at] for at in range(3)], axis=1),
        (((1,), (1,)), ((), ())),
        preferred_element_type=jnp.float32,
    )

    @pl.when(step == 8)
    def _():
        out[...] = acc[...].reshape(out.shape).astype(out.dtype)


def blocked_body(inputs, weights, out_grad):
    chans, levels, height, width = inputs.shape
    filters = weights.shape[2]
    bf16, f32 = jnp.bfloat16, jnp.float32
    lat, lon = lax.axis_index("lat"), lax.axis_index("lon")
    pos = jnp.stack([lax.axis_index("ch"), lat, lon]).astype(jnp.int32)
    x_cells = jnp.transpose(inputs, (1, 2, 3, 0))
    g_cells = jnp.transpose(out_grad, (1, 2, 3, 0))
    taps = jnp.transpose(weights, (1, 0, 2))
    cells = levels * height * width
    span, wide = chans // 4, filters // 4
    rows, circle = 4 * height, 4 * width
    edge = levels * height

    to_same = lambda c, a, o: (a // 2, 2 * c + a % 2, o)
    to_other = lambda c, a, o: (a // 2, 2 * c + 1 - a % 2, o)
    many = cells // 2
    block = jax.ShapeDtypeStruct((cells, wide), bf16)
    g_same, g_other, x0, x1, x2, x3 = call(
        pack_kernel,
        [block, block]
        + [jax.ShapeDtypeStruct((many + extra, 2 * span), bf16) for extra in (0, 2 * edge, 0, 2 * edge)],
        (pos, x_cells, g_cells),
        [VMEM((4, many, 2 * span), bf16)],
        0,
        "pack",
        16,
    )
    g_s = move(g_same, to_same)
    g_o = move(g_other, to_other)
    x_r1 = move(x1, lon_by(1))
    x_r3 = move(x3, lon_by(-1))
    x_r2 = move(x2, lon_by(2))

    rim = jax.ShapeDtypeStruct((2 * levels * width + 4 * edge, 2 * span), bf16)
    g0, x_own, rim_x, rim_d = call(
        spread_kernel,
        [jax.ShapeDtypeStruct((2, cells, wide), bf16), jax.ShapeDtypeStruct((4, many, 2 * span), bf16), rim, rim],
        (pos, x0, x_r1, x_r2, x_r3, g_cells, g_s, g_o),
        [],
        0,
        "spread",
        16,
    )
    g1 = move(g0, lon_by(1))
    g3 = move(g0, lon_by(-1))
    x_x = move(x_own, lat_xor(1))
    x_y = move(x_own, lat_xor(2))
    x_d = move(x_own, lat_xor(3))
    far_a, far_b, g_near = call(
        split_kernel,
        [block, block, jax.ShapeDtypeStruct((6, cells, wide), bf16)],
        (pos, g0, g1, g3, x_x, x_y, x_d),
        [],
        0,
        "split",
        16,
        held=3,
    )
    g2a = move(far_a, lon_by(1))
    g2b = move(far_b, lon_by(-1))
    s_near = move(g_near, sibling)

    xs, total = pl.pallas_call(
        lines_kernel,
        out_shape=[
            jax.ShapeDtypeStruct((levels, rows + 2, circle, 4 * span), bf16),
            jax.ShapeDtypeStruct((27, chans, filters), f32),
        ],
        in_specs=[pl.BlockSpec(memory_space=SMEM)]
        + [pl.BlockSpec(memory_space=VMEM)] * 4
        + [pl.BlockSpec(memory_space=pl.ANY)],
        out_specs=[pl.BlockSpec(memory_space=VMEM)] + [pl.BlockSpec(memory_space=pl.ANY)],
        cost_estimate=pl.CostEstimate(flops=0, bytes_accessed=2**20, transcendentals=0),
        compiler_params=pltpu.CompilerParams(vmem_limit_bytes=24 * 1024 * 1024),
        name="lines",
    )(pos, x_own, x_x, x_y, x_d, far_a)
    rim_x, rim_d, g2 = call(
        hand_kernel,
        [rim, rim, jax.ShapeDtypeStruct((2, cells, wide), bf16)],
        (pos, rim_x, rim_d, g2a, g2b, xs),
        [],
        0,
        "hand",
        16,
        held=1,
    )
    s2 = move(g2, sibling)
    by_x = move(rim_x, lat_xor(1))
    by_d = move(rim_d, lat_xor(3))

    (mine,) = call(
        rims_kernel,
        [jax.ShapeDtypeStruct((levels, height + 2, width + 16, chans), bf16)],
        (pos, g_cells, x_r1, x_r3, by_x, by_d),
        [],
        0,
        "rims",
        16,
    )
    theirs = move(mine, sibling)

    early = 7
    cut, end = early * span, 27 * span
    size = end + 16 - cut
    half = size // 32 * 16
    first_rows = cut + 16
    slab = lambda count: jax.ShapeDtypeStruct((count, wide), bf16)
    (grads,) = call(
        taps_kernel,
        [jax.ShapeDtypeStruct((27, span, wide), f32)],
        (pos, xs, g_near, s_near, g2, s2),
        [VMEM((levels * wide, rows * circle), bf16), VMEM((3, 3 * wide, 4 * span), f32)],
        2 * 27 * span * wide * rows * circle * levels,
        "taps",
        28,
    )
    own, late = call(code_kernel, [slab(end + 16), slab(size)], (pos, grads, theirs), [], 0, "code", 16, held=1)

    whole = lambda t: (0, 0, 0, 0)
    field = pl.pallas_call(
        field_kernel,
        out_shape=jax.ShapeDtypeStruct((levels, height, width, chans), bf16),
        grid=(9,),
        in_specs=[
            pl.BlockSpec(memory_space=SMEM),
            pl.BlockSpec(memory_space=pl.ANY),
            pl.BlockSpec(mine.shape, whole),
            pl.BlockSpec(mine.shape, whole),
            pl.BlockSpec((3, chans, filters), lambda t: (t, 0, 0)),
        ],
        out_specs=pl.BlockSpec((levels, height, width, chans), whole),
        scratch_shapes=[
            VMEM((3, levels + 2, height + 2, width, filters), bf16),
            VMEM((cells, chans), f32),
        ],
        cost_estimate=pl.CostEstimate(
            flops=4 * 27 * chans * filters * cells, bytes_accessed=27 * chans * filters * 2, transcendentals=0
        ),
        compiler_params=pltpu.CompilerParams(vmem_limit_bytes=56 * 1024 * 1024),
        name="field",
    )(pos, own, mine, theirs, taps)

    def to_plane(share):
        return [move(share, lat_xor(tag)) for tag in (1, 2, 3)]

    from_3 = move(late, lon_by(1))
    from_1 = move(late, lon_by(-1))
    plane = [own] + to_plane(own)
    pair, z_3, z_1 = call(
        join_kernel,
        [slab(2 * size), slab(half + 4 * first_rows), slab(size - half + 4 * first_rows)],
        (pos, *plane, from_3, from_1, field),
        [],
        0,
        "join",
        16,
        held=1,
    )
    both = to_plane(pair)
    by_3 = move(z_3, lon_by(1))
    by_1 = move(z_1, lon_by(-1))
    def late_piece(which, tag, step, row=0):
        return (which, row, row + size - 16, early, 27 - early, tag, step)

    def early_pieces(which, row, tags, step):
        return [
            (which, row + at * first_rows, row + at * first_rows + cut, 0, early, tag, step)
            for at, tag in enumerate(tags)
        ]

    pieces = [(tag, 0, end, 0, 27, tag, 0) for tag in range(4)]
    pieces += [late_piece(4, 0, 3), late_piece(5, 0, 1)]
    total = unpack(pos, total, plane + [from_3, from_1], [pair], pieces, span, "unpack_1")
    from_2, early_3, early_1 = call(
        across_kernel,
        [slab(size), slab(2 * first_rows), slab(2 * first_rows)],
        (pos, by_3, by_1, total),
        [],
        0,
        "across",
        16,
        held=1,
    )
    across = to_plane(from_2)
    early_2a = move(early_3, lon_by(1))
    early_2b = move(early_1, lon_by(-1))

    pieces = [late_piece(tag - 1, tag, 3) for tag in (1, 2, 3)]
    pieces += [late_piece(tag - 1, tag, 1, size) for tag in (1, 2, 3)]
    pieces += early_pieces(3, half, (0, 1, 2, 3), 3) + early_pieces(4, size - half, (0, 1, 2, 3), 1)
    pieces += [late_piece(5, 0, 2)]
    total = unpack(pos, total, both + [by_3, by_1, from_2], [], pieces, span, "unpack_2")
    pieces = early_pieces(0, 0, (0, 1), 2) + early_pieces(1, 0, (2, 3), 2)
    pieces += [late_piece(tag + 1, tag, 2) for tag in (1, 2, 3)]
    total = unpack(pos, total, [early_2a, early_2b] + across, [], pieces, span, "unpack_3")
    return (jnp.transpose(field, (3, 0, 1, 2)), jnp.transpose(total, (1, 0, 2)))


def body(inputs, weights, out_grad):
    chans, levels, height, width = inputs.shape
    shape = tuple(lax.axis_size(axis) for axis in AXES)
    fits = (
        shape == (2, 4, 4)
        and chans == out_grad.shape[0] == 256
        and weights.shape[2] == 512
        and levels % 2 == 0
        and height % 2 == 0
        and width % 16 == 0
    )
    return (blocked_body if fits else plain_body)(inputs, weights, out_grad)


def solution(mesh):
    in_specs = (P("ch", None, "lat", "lon"), P("ch", None, None), P("ch", None, "lat", "lon"))
    out_specs = (P("ch", None, "lat", "lon"), P("ch", None, None))
    return jax.shard_map(body, mesh=mesh, in_specs=in_specs, out_specs=out_specs, check_vma=False)
```

```python
import math

import jax
import jax.numpy as jnp
from jax import lax
from jax.experimental import pallas as pl
from jax.experimental.pallas import tpu as pltpu
from jax.sharding import PartitionSpec as P

VMEM = pltpu.VMEM
SMEM = pltpu.SMEM
AXES = ("ch", "lat", "lon")


def padded_2(cells, sides, width):
    for axis, dim in sides:
        count = lax.axis_size(axis)
        head = lax.slice_in_dim(cells, 0, width, axis=dim)
        tail = lax.slice_in_dim(cells, cells.shape[dim] - width, cells.shape[dim], axis=dim)
        cells = jnp.concatenate(
            [
                lax.ppermute(tail, axis, [(i, (i + 1) % count) for i in range(count)]),
                cells,
                lax.ppermute(head, axis, [((i + 1) % count, i) for i in range(count)]),
            ],
            axis=dim,
        )
    return cells


def mask_rims(padded):
    count = lax.axis_size("lat")
    where_lat = lax.axis_index("lat")
    lines = jnp.arange(padded.shape[2])
    drop = (lines == 0) & (where_lat == 0) | (lines == padded.shape[2] - 1) & (
        where_lat == count - 1
    )
    return jnp.where(drop[None, None, :, None], jnp.zeros((), padded.dtype), padded)


def pad_levels(field):
    return jnp.pad(field, ((0, 0), (1, 1), (0, 0), (0, 0)))


def plain_body(inputs, weights, out_grad):
    chans, levels, height, width = inputs.shape
    input_pad = pad_levels(mask_rims(padded_2(inputs, (("lat", 2), ("lon", 3)), 1)))
    grad_inner = lax.all_gather(out_grad, "ch", axis=0, tiled=True)
    grad_pad = pad_levels(mask_rims(padded_2(grad_inner, (("lat", 2), ("lon", 3)), 1)))
    filters = grad_pad.shape[0]
    products = jnp.dot(
        weights.reshape(chans * 27, filters),
        grad_pad.reshape(filters, -1),
        preferred_element_type=jnp.float32,
    )
    products = products.reshape((chans, 27) + tuple(grad_pad.shape[1:]))
    total = jnp.zeros((chans, levels, height, width), jnp.float32)
    pieces = []
    for tap in range(27):
        lev, lat, lon = tap // 9 - 1, tap // 3 % 3 - 1, tap % 3 - 1
        total = (
            total
            + products[
                :,
                tap,
                1 - lev : 1 - lev + levels,
                1 - lat : 1 - lat + height,
                1 - lon : 1 - lon + width,
            ]
        )
        pieces.append(
            input_pad[
                :,
                1 + lev : 1 + lev + levels,
                1 + lat : 1 + lat + height,
                1 + lon : 1 + lon + width,
            ]
        )
    columns = jnp.stack(pieces, axis=1).reshape(chans * 27, -1)
    partial_grad = lax.dot_general(
        columns,
        grad_inner.reshape(filters, -1),
        (((1,), (1,)), ((), ())),
        preferred_element_type=jnp.float32,
    )
    summed = lax.psum(partial_grad, ("lat", "lon"))
    cells = levels * height * width * lax.axis_size("lat") * lax.axis_size("lon")
    weight_grad = (summed * (1.0 / math.sqrt(cells))).reshape(chans, 27, filters)
    return (total.astype(jnp.bfloat16), weight_grad)


def move(x, target):
    pairs = []
    for i in range(32):
        to = target(i // 16, i // 4 % 4, i % 4)
        if to is not None:
            pairs.append((i, (to[0] * 4 + to[1]) * 4 + to[2]))
    return lax.ppermute(x, AXES, pairs)


def lon_by(step):
    return lambda c, a, o: (c, a, (o + step) % 4)


def lat_xor(mask):
    return lambda c, a, o: (c, a ^ mask, o)


def sibling(c, a, o):
    return (1 - c, a, o)


def call(kernel, outs, ins, scratch, flops, name, limit, held=0):
    read = len(ins) - 1 - held
    moved = sum(math.prod(x.shape) * x.dtype.itemsize for x in list(ins[1 : 1 + read]) + list(outs))
    return pl.pallas_call(
        kernel,
        out_shape=outs,
        in_specs=[pl.BlockSpec(memory_space=SMEM)]
        + [pl.BlockSpec(memory_space=VMEM)] * read
        + [pl.BlockSpec(memory_space=pl.ANY)] * held,
        out_specs=[pl.BlockSpec(memory_space=VMEM)] * len(outs),
        scratch_shapes=scratch,
        cost_estimate=pl.CostEstimate(flops=flops, bytes_accessed=moved, transcendentals=0),
        compiler_params=pltpu.CompilerParams(vmem_limit_bytes=limit * 1024 * 1024),
        name=name,
    )(*ins)


def pack_kernel(pos, x, g, g_same, g_other, x0, x1, x2, x3, rim_x, rim_d, held):
    levels, height, width, chans = x.shape
    half, wide = levels // 2, chans // 2
    right = lax.rem(pos[1], 2)
    for out, at in ((g_same, right), (g_other, 1 - right)):
        out[...] = g[:, :, :, pl.ds(pl.multiple_of(at * wide, wide), wide)].reshape(out.shape)
    many = x0.shape[0]
    for block in range(4):
        at = block * (chans // 4)
        lo = x[0:half, :, :, at : at + chans // 4]
        hi = x[half:levels, :, :, at : at + chans // 4]
        held[block] = jnp.concatenate([lo, hi], axis=-1).reshape(held.shape[1:])
    lon = pos[2]
    for step, out in enumerate((x0, x1, x2, x3)):
        out[0:many, :] = held[lax.rem(lon + step, 4)]
    for out, column in ((x1, width - 1), (x3, 0)):
        rim = g[:, :, column, :].reshape(levels * height, chans)
        out[many : many + levels * height, :] = rim[:, 0:wide]
        out[many + levels * height :, :] = rim[:, wide:]
    even = right == 0
    low, high = g[:, 0], g[:, height - 1]
    line = levels * width
    for out, upward in ((rim_x, even), (rim_d, jnp.logical_not(even))):
        facing = jnp.where(upward, high, low).reshape(line, chans)
        for at in range(2):
            out[at * line : (at + 1) * line, :] = facing[:, at * wide : (at + 1) * wide]


def spread_kernel(pos, x0, x1, x2, x3, one, two, both, own, own_y):
    del pos
    many = x0.shape[0]
    both[0] = one[...]
    both[1] = two[...]
    for at, piece in enumerate((x0, x1, x2, x3)):
        own[at * many : (at + 1) * many, :] = piece[0:many, :]
        own_y[at * many : (at + 1) * many, :] = piece[0:many, :]
    extra = x1.shape[0] - many
    own[4 * many : 4 * many + extra, :] = x1[many:, :]
    own[4 * many + extra :, :] = x3[many:, :]


def split_kernel(
    pos, here, west, east, g, own, x_x, x_d, by_x, by_d, after, first, second, near, mine
):
    del after
    first[...] = west[0]
    second[...] = east[1]
    for at, part in enumerate((here, west, east)):
        near[2 * at : 2 * at + 2] = part[...]

    levels, height, width, chans = g.shape
    edge, line, wide = levels * height, levels * width, chans // 2
    inner = own.shape[0] - 4 * edge
    mine[:, 1 : height + 1, 0:width, :] = g[...]

    def columns(message, rows):
        for side in range(2):
            for half in range(2):
                start = inner + (2 * side + half) * edge
                rim = message[start : start + edge, :].reshape(levels, height, wide)
                at = width + 8 * side
                for row, to in rows:
                    mine[:, to, at : at + 8, half * wide : (half + 1) * wide] = jnp.broadcast_to(
                        rim[:, row : row + 1], (levels, 8, wide)
                    )

    columns(own, [(row, row + 1) for row in range(height)])

    def lines(strip, message, row, to):
        for half in range(2):
            part = strip[half * line : (half + 1) * line, :]
            mine[:, to, 0:width, half * wide : (half + 1) * wide] = part.reshape(levels, width, wide)
        columns(message, [(row, to)])

    lat = pos[1]
    odd = lax.rem(lat, 2)

    @pl.when(odd == 1)
    def _():
        lines(by_x, x_x, height - 1, 0)
        lines(by_d, x_d, 0, height + 1)

    @pl.when(odd == 0)
    def _():
        lines(by_d, x_d, height - 1, 0)
        lines(by_x, x_x, 0, height + 1)

    @pl.when(lat == 0)
    def _():
        mine[:, 0] = jnp.zeros_like(mine[:, 0])

    @pl.when(lat == 3)
    def _():
        mine[:, height + 1] = jnp.zeros_like(mine[:, height + 1])


def pair_kernel(pos, one, two, after, both):
    del pos, after
    both[0] = one[...]
    both[1] = two[...]


def lines_kernel(pos, x_own, x_x, x_y, x_d, after, xs, blank):
    del after, blank
    lat = pos[1]
    levels, rows, circle, lanes = xs.shape
    rows, width, span, half = rows - 2, circle // 4, lanes // 4, levels // 2
    height = rows // 4
    many = half * height * width
    xs[:, 0] = jnp.zeros_like(xs[:, 0])
    xs[:, rows + 1] = jnp.zeros_like(xs[:, rows + 1])
    low = lax.broadcasted_iota(jnp.int32, (circle, 2 * span), 1) < span
    for tag, ref in enumerate((x_own, x_x, x_y, x_d)):
        start = (lat ^ tag) * height
        strips = [
            ref.at[pl.ds((4 - at) % 4 * many, many)].reshape(half, height, width, 2 * span) for at in range(4)
        ]

        @pl.loop(0, half * height)
        def _(step, strips=strips, start=start):
            lev, row = step // height, lax.rem(step, height)
            line = jnp.concatenate([s[lev, row] for s in strips], axis=0).astype(jnp.float32)
            turned = pltpu.roll(line, span, 1)
            for upper in range(2):
                same = jnp.where(low, turned, line) if upper else jnp.where(low, line, turned)
                before = pltpu.roll(same, 1, 0)
                after = pltpu.roll(same, circle - 1, 0)
                at = upper * half + lev
                xs[at, 1 + start + row, :, 0 : 2 * span] = jnp.where(low, before, same).astype(xs.dtype)
                xs[at, 1 + start + row, :, 2 * span : 4 * span] = after.astype(xs.dtype)


def turn(gt, slot, core, first, second, levels):
    many, filters = first.shape
    line = many // levels
    for lev in range(levels):
        block = jnp.concatenate([first[lev * line : (lev + 1) * line], second[lev * line : (lev + 1) * line]], axis=0)
        gt[
            lev * filters : (lev + 1) * filters,
            pl.ds(pl.multiple_of((2 * slot + core) * 2 * line, 2 * line), 2 * line),
        ] = block.T


def taps_kernel(pos, xs, g, s, g2, s2, out, gt, acc):
    levels, rows, circle, lanes = xs.shape
    rows, width, span = rows - 2, circle // 4, lanes // 4
    filters = gt.shape[0] // levels
    deep = rows * width
    right = lax.rem(pos[1], 2)
    for core, parts, last in ((pos[0], g, g2), (1 - pos[0], s, s2)):
        for slot, (ref, at) in enumerate(((parts, 0), (parts, 4), (last, 0), (parts, 2))):
            turn(gt, slot, core, ref[at + right], ref[at + 1 - right], levels)
    acc[...] = jnp.zeros_like(acc)

    @pl.loop(0, 3)
    def _(lat_by):
        for lev in range(levels):
            first, last = max(lev - 1, 0), min(lev + 1, levels - 1)
            to = (first - lev + 1) * filters
            many = (last - first + 1) * filters
            total = acc[lat_by, to : to + many, :]
            for place in range(4):
                total += jnp.dot(
                    gt[first * filters : (last + 1) * filters, place * deep : (place + 1) * deep],
                    xs[lev, pl.ds(lat_by, rows), place * width : (place + 1) * width].reshape(deep, lanes),
                    preferred_element_type=jnp.float32,
                )
            acc[lat_by, to : to + many, :] = total

    scale = 1.0 / math.sqrt(levels * rows * circle)
    for lat_by in range(3):
        for lev_at in range(3):
            block = acc[lat_by, lev_at * filters : (lev_at + 1) * filters, :].T * scale
            for lon_at in range(3):
                out[(2 - lev_at) * 9 + lat_by * 3 + lon_at] = block[lon_at * span : (lon_at + 1) * span]


def code_kernel(pos, held, after, out, late):
    del pos, after
    taps, span, filters = held.shape
    most = jnp.abs(held[0])
    for tap in range(1, taps):
        most = jnp.maximum(most, jnp.abs(held[tap]))
    top = jnp.maximum(jnp.max(most, axis=(0, 1), keepdims=True), 1e-30)
    power = jnp.ceil(jnp.log(top) * (1.0 / math.log(2.0))) - 15.0
    unit = jnp.broadcast_to(jnp.exp2(power), (16, filters)).astype(out.dtype).astype(jnp.float32)
    shrink = 1.0 / unit[0:1]
    skip = out.shape[0] - late.shape[0]
    for tap in range(27):
        value = held[tap] * shrink
        square = value * value
        code = (square * square * square * value * jnp.abs(value)).astype(out.dtype)
        out[tap * span : (tap + 1) * span, :] = code
        if tap * span >= skip:
            late[tap * span - skip : (tap + 1) * span - skip, :] = code
    out[27 * span :, :] = unit.astype(out.dtype)
    late[27 * span - skip :, :] = unit.astype(out.dtype)


def join_kernel(pos, own, x, y, d, west, east, after, both, by_3, by_1):
    del pos, after
    size = west.shape[0]
    cut = own.shape[0] - size
    end = own.shape[0] - 16
    half = by_3.shape[0] - 4 * (cut + 16)
    both[0:size, :] = west[...]
    both[size:, :] = east[...]
    by_3[0:half, :] = west[0:half, :]
    by_1[0 : size - half, :] = east[half:, :]
    for out, at in ((by_3, half), (by_1, size - half)):
        for piece in (own, x, y, d):
            out[at : at + cut, :] = piece[0:cut, :]
            out[at + cut : at + cut + 16, :] = piece[end:, :]
            at += cut + 16


def across_kernel(pos, by_3, by_1, after, late, early_3, early_1):
    del pos, after
    size, many = late.shape[0], early_3.shape[0]
    half = by_3.shape[0] - 2 * many
    late[0:half, :] = by_3[0:half, :]
    late[half:, :] = by_1[0 : size - half, :]
    early_3[...] = by_3[half : half + many, :]
    early_1[...] = by_1[size - half + many :, :]


def unpack_kernel(pos, *refs, pieces, span):
    count = 1 + max(piece[0] for piece in pieces)
    sources = refs[:count]
    total, buffers, sems = refs[-3:]
    wide = buffers.shape[-1]

    def target(piece):
        _, _, _, first, many, tag, step = piece
        lon_at = lax.rem(pos[2] + step, 4) * span
        lat_at = (pos[1] ^ tag) * wide
        return total.at[
            pl.ds(first, many),
            pl.ds(pl.multiple_of(lon_at, span), span),
            pl.ds(pl.multiple_of(lat_at, wide), wide),
        ]

    def copy(at):
        piece = pieces[at]
        return pltpu.make_async_copy(buffers.at[at % 2, pl.ds(0, piece[4])], target(piece), sems.at[at % 2])

    for at, (which, row, power_row, _, many, _, _) in enumerate(pieces):
        if at >= 2:
            copy(at - 2).wait()
        source = sources[which]
        unit = source[power_row : power_row + 16, :].astype(jnp.float32)[0:1]

        @pl.loop(0, many)
        def _(tap, source=source, row=row, unit=unit, at=at):
            code = source[pl.ds(pl.multiple_of(row + tap * span, 16), span), :].astype(jnp.float32)
            root = lax.rsqrt(lax.rsqrt(jnp.abs(code)))
            root = root * lax.rsqrt(jnp.maximum(root, 1e-30)) * unit
            buffers[at % 2, tap] = jnp.where(code < 0, -root, root)

        copy(at).start()
    for at in range(max(len(pieces) - 2, 0), len(pieces)):
        copy(at).wait()


def unpack(pos, total, sources, after, pieces, span, name):
    most = max(piece[4] for piece in pieces)
    wide = sources[0].shape[-1]
    ins = (pos, *sources, *after, total)
    return pl.pallas_call(
        lambda *refs: unpack_kernel(*refs, pieces=pieces, span=span),
        out_shape=jax.ShapeDtypeStruct(total.shape, total.dtype),
        in_specs=[pl.BlockSpec(memory_space=SMEM)]
        + [pl.BlockSpec(memory_space=VMEM)] * len(sources)
        + [pl.BlockSpec(memory_space=pl.ANY)] * (len(after) + 1),
        out_specs=pl.BlockSpec(memory_space=pl.ANY),
        scratch_shapes=[VMEM((2, most, span, wide), jnp.float32), pltpu.SemaphoreType.DMA((2,))],
        input_output_aliases={len(ins) - 1: 0},
        cost_estimate=pl.CostEstimate(flops=0, bytes_accessed=4 * 2**20, transcendentals=0),
        compiler_params=pltpu.CompilerParams(vmem_limit_bytes=54 * 1024 * 1024),
        name=name,
    )(*ins)


def field_kernel(pos, after, mine, theirs, w, out, copies, acc):
    del after
    step = pl.program_id(0)
    levels, height, width, chans = out.shape
    many = mine.shape[-1]

    @pl.when(step == 0)
    def _():
        copies[:, 0] = jnp.zeros_like(copies[:, 0])
        copies[:, levels + 1] = jnp.zeros_like(copies[:, levels + 1])
        line_at = lax.broadcasted_iota(jnp.int32, (width, many), 0)
        for which, field in ((pos[0], mine), (1 - pos[0], theirs)):
            lanes = pl.ds(pl.multiple_of(which * many, many), many)
            for lev in range(levels):
                for row in range(height + 2):
                    line = field[lev, row, 0:width].astype(jnp.float32)
                    west = field[lev, row, width : width + 1].astype(jnp.float32)
                    east = field[lev, row, width + 8 : width + 9].astype(jnp.float32)
                    before = jnp.where(line_at == 0, west, pltpu.roll(line, 1, 0))
                    later = jnp.where(line_at == width - 1, east, pltpu.roll(line, width - 1, 0))
                    copies[0, lev + 1, row, :, lanes] = later.astype(copies.dtype)
                    copies[1, lev + 1, row, :, lanes] = field[lev, row, 0:width]
                    copies[2, lev + 1, row, :, lanes] = before.astype(copies.dtype)
        acc[...] = jnp.zeros_like(acc)

    lev_by, lat_by = step // 3, lax.rem(step, 3)
    cells = [
        copies[at, pl.ds(2 - lev_by, levels), pl.ds(2 - lat_by, height)].reshape(
            levels * height * width, 2 * many
        )
        for at in range(3)
    ]
    acc[...] += lax.dot_general(
        jnp.concatenate(cells, axis=1),
        jnp.concatenate([w[at] for at in range(3)], axis=1),
        (((1,), (1,)), ((), ())),
        preferred_element_type=jnp.float32,
    )

    @pl.when(step == 8)
    def _():
        out[...] = acc[...].reshape(out.shape).astype(out.dtype)


def blocked_body(inputs, weights, out_grad):
    chans, levels, height, width = inputs.shape
    filters = weights.shape[2]
    bf16, f32 = jnp.bfloat16, jnp.float32
    lat, lon = lax.axis_index("lat"), lax.axis_index("lon")
    pos = jnp.stack([lax.axis_index("ch"), lat, lon]).astype(jnp.int32)
    x_cells = jnp.transpose(inputs, (1, 2, 3, 0))
    g_cells = jnp.transpose(out_grad, (1, 2, 3, 0))
    taps = jnp.transpose(weights, (1, 0, 2))
    cells = levels * height * width
    span, wide = chans // 4, filters // 4
    rows, circle = 4 * height, 4 * width
    edge = levels * height

    to_same = lambda c, a, o: (a // 2, 2 * c + a % 2, o)
    to_other = lambda c, a, o: (a // 2, 2 * c + 1 - a % 2, o)
    many = cells // 2
    block = jax.ShapeDtypeStruct((cells, wide), bf16)
    strip = jax.ShapeDtypeStruct((2 * levels * width, 2 * span), bf16)
    g_same, g_other, x0, x1, x2, x3, rim_x, rim_d = call(
        pack_kernel,
        [block, block]
        + [jax.ShapeDtypeStruct((many + extra, 2 * span), bf16) for extra in (0, 2 * edge, 0, 2 * edge)]
        + [strip, strip],
        (pos, x_cells, g_cells),
        [VMEM((4, many, 2 * span), bf16)],
        0,
        "pack",
        16,
    )
    g_s = move(g_same, to_same)
    g_o = move(g_other, to_other)
    x_r1 = move(x1, lon_by(1))
    x_r3 = move(x3, lon_by(-1))
    x_r2 = move(x2, lon_by(2))
    by_x = move(rim_x, lat_xor(1))
    by_d = move(rim_d, lat_xor(3))

    inner = 4 * many
    g0, x_own, x_own_y = call(
        spread_kernel,
        [jax.ShapeDtypeStruct((2, cells, wide), bf16)]
        + [jax.ShapeDtypeStruct((count, 2 * span), bf16) for count in (inner + 4 * edge, inner)],
        (pos, x0, x_r1, x_r2, x_r3, g_s, g_o),
        [],
        0,
        "spread",
        16,
    )
    x_x = move(x_own, lat_xor(1))
    x_d = move(x_own, lat_xor(3))
    x_y = move(x_own_y, lat_xor(2))
    g1 = move(g0, lon_by(1))
    g3 = move(g0, lon_by(-1))
    far_a, far_b, g_near, mine = call(
        split_kernel,
        [
            block,
            block,
            jax.ShapeDtypeStruct((6, cells, wide), bf16),
            jax.ShapeDtypeStruct((levels, height + 2, width + 16, chans), bf16),
        ],
        (pos, g0, g1, g3, g_cells, x_own, x_x, x_d, by_x, by_d, x_y),
        [],
        0,
        "split",
        16,
        held=1,
    )
    g2a = move(far_a, lon_by(1))
    g2b = move(far_b, lon_by(-1))
    s_near = move(g_near, sibling)
    theirs = move(mine, sibling)
    xs, total = pl.pallas_call(
        lines_kernel,
        out_shape=[
            jax.ShapeDtypeStruct((levels, rows + 2, circle, 4 * span), bf16),
            jax.ShapeDtypeStruct((27, chans, filters), f32),
        ],
        in_specs=[pl.BlockSpec(memory_space=SMEM)]
        + [pl.BlockSpec(memory_space=VMEM)] * 4
        + [pl.BlockSpec(memory_space=pl.ANY)],
        out_specs=[pl.BlockSpec(memory_space=VMEM)] + [pl.BlockSpec(memory_space=pl.ANY)],
        cost_estimate=pl.CostEstimate(flops=0, bytes_accessed=2**20, transcendentals=0),
        compiler_params=pltpu.CompilerParams(vmem_limit_bytes=24 * 1024 * 1024),
        name="lines",
    )(pos, x_own, x_x, x_y, x_d, far_a)
    (g2,) = call(
        pair_kernel, [jax.ShapeDtypeStruct((2, cells, wide), bf16)], (pos, g2a, g2b, xs), [], 0, "pair", 16, held=1
    )
    s2 = move(g2, sibling)
    early = 7
    cut, end = early * span, 27 * span
    size = end + 16 - cut
    half = size // 32 * 16
    first_rows = cut + 16
    slab = lambda count: jax.ShapeDtypeStruct((count, wide), bf16)
    (grads,) = call(
        taps_kernel,
        [jax.ShapeDtypeStruct((27, span, wide), f32)],
        (pos, xs, g_near, s_near, g2, s2),
        [VMEM((levels * wide, rows * circle), bf16), VMEM((3, 3 * wide, 4 * span), f32)],
        2 * 27 * span * wide * rows * circle * levels,
        "taps",
        28,
    )
    own, late = call(code_kernel, [slab(end + 16), slab(size)], (pos, grads, theirs), [], 0, "code", 16, held=1)

    whole = lambda t: (0, 0, 0, 0)
    field = pl.pallas_call(
        field_kernel,
        out_shape=jax.ShapeDtypeStruct((levels, height, width, chans), bf16),
        grid=(9,),
        in_specs=[
            pl.BlockSpec(memory_space=SMEM),
            pl.BlockSpec(memory_space=pl.ANY),
            pl.BlockSpec(mine.shape, whole),
            pl.BlockSpec(mine.shape, whole),
            pl.BlockSpec((3, chans, filters), lambda t: (t, 0, 0)),
        ],
        out_specs=pl.BlockSpec((levels, height, width, chans), whole),
        scratch_shapes=[
            VMEM((3, levels + 2, height + 2, width, filters), bf16),
            VMEM((cells, chans), f32),
        ],
        cost_estimate=pl.CostEstimate(
            flops=4 * 27 * chans * filters * cells, bytes_accessed=27 * chans * filters * 2, transcendentals=0
        ),
        compiler_params=pltpu.CompilerParams(vmem_limit_bytes=52 * 1024 * 1024),
        name="field",
    )(pos, own, mine, theirs, taps)

    def to_plane(share):
        return [move(share, lat_xor(tag)) for tag in (1, 2, 3)]

    from_3 = move(late, lon_by(1))
    from_1 = move(late, lon_by(-1))
    plane = [own] + to_plane(own)
    pair, z_3, z_1 = call(
        join_kernel,
        [slab(2 * size), slab(half + 4 * first_rows), slab(size - half + 4 * first_rows)],
        (pos, *plane, from_3, from_1, field),
        [],
        0,
        "join",
        16,
        held=1,
    )
    both = to_plane(pair)
    by_3 = move(z_3, lon_by(1))
    by_1 = move(z_1, lon_by(-1))
    def late_piece(which, tag, step, row=0):
        return (which, row, row + size - 16, early, 27 - early, tag, step)

    def early_pieces(which, row, tags, step):
        return [
            (which, row + at * first_rows, row + at * first_rows + cut, 0, early, tag, step)
            for at, tag in enumerate(tags)
        ]

    pieces = [(tag, 0, end, 0, 27, tag, 0) for tag in range(4)]
    pieces += [late_piece(4, 0, 3), late_piece(5, 0, 1)]
    total = unpack(pos, total, plane + [from_3, from_1], [pair], pieces, span, "unpack_1")
    from_2, early_3, early_1 = call(
        across_kernel,
        [slab(size), slab(2 * first_rows), slab(2 * first_rows)],
        (pos, by_3, by_1, total),
        [],
        0,
        "across",
        16,
        held=1,
    )
    across = to_plane(from_2)
    early_2a = move(early_3, lon_by(1))
    early_2b = move(early_1, lon_by(-1))

    pieces = [late_piece(tag - 1, tag, 3) for tag in (1, 2, 3)]
    pieces += [late_piece(tag - 1, tag, 1, size) for tag in (1, 2, 3)]
    pieces += early_pieces(3, half, (0, 1, 2, 3), 3) + early_pieces(4, size - half, (0, 1, 2, 3), 1)
    pieces += [late_piece(5, 0, 2)]
    total = unpack(pos, total, both + [by_3, by_1, from_2], [], pieces, span, "unpack_2")
    pieces = early_pieces(0, 0, (0, 1), 2) + early_pieces(1, 0, (2, 3), 2)
    pieces += [late_piece(tag + 1, tag, 2) for tag in (1, 2, 3)]
    total = unpack(pos, total, [early_2a, early_2b] + across, [], pieces, span, "unpack_3")
    return (jnp.transpose(field, (3, 0, 1, 2)), jnp.transpose(total, (1, 0, 2)))


def body(inputs, weights, out_grad):
    chans, levels, height, width = inputs.shape
    shape = tuple(lax.axis_size(axis) for axis in AXES)
    fits = (
        shape == (2, 4, 4)
        and chans == out_grad.shape[0] == 256
        and weights.shape[2] == 512
        and levels % 2 == 0
        and height % 2 == 0
        and width % 16 == 0
    )
    return (blocked_body if fits else plain_body)(inputs, weights, out_grad)


def solution(mesh):
    in_specs = (P("ch", None, "lat", "lon"), P("ch", None, None), P("ch", None, "lat", "lon"))
    out_specs = (P("ch", None, "lat", "lon"), P("ch", None, None))
    return jax.shard_map(body, mesh=mesh, in_specs=in_specs, out_specs=out_specs, check_vma=False)
```

```python
import math

import jax
import jax.numpy as jnp
from jax import lax
from jax.experimental import pallas as pl
from jax.experimental.pallas import tpu as pltpu
from jax.sharding import PartitionSpec as P

VMEM = pltpu.VMEM
SMEM = pltpu.SMEM
AXES = ("ch", "lat", "lon")


def padded_2(cells, sides, width):
    for axis, dim in sides:
        count = lax.axis_size(axis)
        head = lax.slice_in_dim(cells, 0, width, axis=dim)
        tail = lax.slice_in_dim(cells, cells.shape[dim] - width, cells.shape[dim], axis=dim)
        cells = jnp.concatenate(
            [
                lax.ppermute(tail, axis, [(i, (i + 1) % count) for i in range(count)]),
                cells,
                lax.ppermute(head, axis, [((i + 1) % count, i) for i in range(count)]),
            ],
            axis=dim,
        )
    return cells


def mask_rims(padded):
    count = lax.axis_size("lat")
    where_lat = lax.axis_index("lat")
    lines = jnp.arange(padded.shape[2])
    drop = (lines == 0) & (where_lat == 0) | (lines == padded.shape[2] - 1) & (
        where_lat == count - 1
    )
    return jnp.where(drop[None, None, :, None], jnp.zeros((), padded.dtype), padded)


def pad_levels(field):
    return jnp.pad(field, ((0, 0), (1, 1), (0, 0), (0, 0)))


def plain_body(inputs, weights, out_grad):
    chans, levels, height, width = inputs.shape
    input_pad = pad_levels(mask_rims(padded_2(inputs, (("lat", 2), ("lon", 3)), 1)))
    grad_inner = lax.all_gather(out_grad, "ch", axis=0, tiled=True)
    grad_pad = pad_levels(mask_rims(padded_2(grad_inner, (("lat", 2), ("lon", 3)), 1)))
    filters = grad_pad.shape[0]
    products = jnp.dot(
        weights.reshape(chans * 27, filters),
        grad_pad.reshape(filters, -1),
        preferred_element_type=jnp.float32,
    )
    products = products.reshape((chans, 27) + tuple(grad_pad.shape[1:]))
    total = jnp.zeros((chans, levels, height, width), jnp.float32)
    pieces = []
    for tap in range(27):
        lev, lat, lon = tap // 9 - 1, tap // 3 % 3 - 1, tap % 3 - 1
        total = (
            total
            + products[
                :,
                tap,
                1 - lev : 1 - lev + levels,
                1 - lat : 1 - lat + height,
                1 - lon : 1 - lon + width,
            ]
        )
        pieces.append(
            input_pad[
                :,
                1 + lev : 1 + lev + levels,
                1 + lat : 1 + lat + height,
                1 + lon : 1 + lon + width,
            ]
        )
    columns = jnp.stack(pieces, axis=1).reshape(chans * 27, -1)
    partial_grad = lax.dot_general(
        columns,
        grad_inner.reshape(filters, -1),
        (((1,), (1,)), ((), ())),
        preferred_element_type=jnp.float32,
    )
    summed = lax.psum(partial_grad, ("lat", "lon"))
    cells = levels * height * width * lax.axis_size("lat") * lax.axis_size("lon")
    weight_grad = (summed * (1.0 / math.sqrt(cells))).reshape(chans, 27, filters)
    return (total.astype(jnp.bfloat16), weight_grad)


def move(x, target):
    pairs = []
    for i in range(32):
        to = target(i // 16, i // 4 % 4, i % 4)
        if to is not None:
            pairs.append((i, (to[0] * 4 + to[1]) * 4 + to[2]))
    return lax.ppermute(x, AXES, pairs)


def lon_by(step):
    return lambda c, a, o: (c, a, (o + step) % 4)


def lat_xor(mask):
    return lambda c, a, o: (c, a ^ mask, o)


def sibling(c, a, o):
    return (1 - c, a, o)


def call(kernel, outs, ins, scratch, flops, name, limit, held=0):
    read = len(ins) - 1 - held
    moved = sum(math.prod(x.shape) * x.dtype.itemsize for x in list(ins[1 : 1 + read]) + list(outs))
    return pl.pallas_call(
        kernel,
        out_shape=outs,
        in_specs=[pl.BlockSpec(memory_space=SMEM)]
        + [pl.BlockSpec(memory_space=VMEM)] * read
        + [pl.BlockSpec(memory_space=pl.ANY)] * held,
        out_specs=[pl.BlockSpec(memory_space=VMEM)] * len(outs),
        scratch_shapes=scratch,
        cost_estimate=pl.CostEstimate(flops=flops, bytes_accessed=moved, transcendentals=0),
        compiler_params=pltpu.CompilerParams(vmem_limit_bytes=limit * 1024 * 1024),
        name=name,
    )(*ins)


def pack_kernel(pos, x, g, g_same, g_other, x0, x1, x2, x3, rim_x, rim_d, held):
    levels, height, width, chans = x.shape
    half, wide = levels // 2, chans // 2
    right = lax.rem(pos[1], 2)
    for out, at in ((g_same, right), (g_other, 1 - right)):
        out[...] = g[:, :, :, pl.ds(pl.multiple_of(at * wide, wide), wide)].reshape(out.shape)
    many = x0.shape[0]
    for block in range(4):
        at = block * (chans // 4)
        lo = x[0:half, :, :, at : at + chans // 4]
        hi = x[half:levels, :, :, at : at + chans // 4]
        held[block] = jnp.concatenate([lo, hi], axis=-1).reshape(held.shape[1:])
    lon = pos[2]
    for step, out in enumerate((x0, x1, x2, x3)):
        out[0:many, :] = held[lax.rem(lon + step, 4)]
    for out, column in ((x1, width - 1), (x3, 0)):
        rim = g[:, :, column, :].reshape(levels * height, chans)
        out[many : many + levels * height, :] = rim[:, 0:wide]
        out[many + levels * height :, :] = rim[:, wide:]
    even = right == 0
    low, high = g[:, 0], g[:, height - 1]
    line = levels * width
    for out, upward in ((rim_x, even), (rim_d, jnp.logical_not(even))):
        facing = jnp.where(upward, high, low).reshape(line, chans)
        for at in range(2):
            out[at * line : (at + 1) * line, :] = facing[:, at * wide : (at + 1) * wide]


def spread_kernel(pos, x0, x1, x2, x3, one, two, both, own, own_y):
    del pos
    many = x0.shape[0]
    both[0] = one[...]
    both[1] = two[...]
    for at, piece in enumerate((x0, x1, x2, x3)):
        own[at * many : (at + 1) * many, :] = piece[0:many, :]
        own_y[at * many : (at + 1) * many, :] = piece[0:many, :]
    extra = x1.shape[0] - many
    own[4 * many : 4 * many + extra, :] = x1[many:, :]
    own[4 * many + extra :, :] = x3[many:, :]


def split_kernel(
    pos, here, west, east, g, own, x_x, x_d, by_x, by_d, after, first, second, near, mine
):
    del after
    first[...] = west[0]
    second[...] = east[1]
    for at, part in enumerate((here, west, east)):
        near[2 * at : 2 * at + 2] = part[...]

    levels, height, width, chans = g.shape
    edge, line, wide = levels * height, levels * width, chans // 2
    inner = own.shape[0] - 4 * edge
    mine[:, 1 : height + 1, 0:width, :] = g[...]

    def columns(message, rows):
        for side in range(2):
            for half in range(2):
                start = inner + (2 * side + half) * edge
                rim = message[start : start + edge, :].reshape(levels, height, wide)
                at = width + 8 * side
                for row, to in rows:
                    mine[:, to, at : at + 8, half * wide : (half + 1) * wide] = jnp.broadcast_to(
                        rim[:, row : row + 1], (levels, 8, wide)
                    )

    columns(own, [(row, row + 1) for row in range(height)])

    def lines(strip, message, row, to):
        for half in range(2):
            part = strip[half * line : (half + 1) * line, :]
            mine[:, to, 0:width, half * wide : (half + 1) * wide] = part.reshape(levels, width, wide)
        columns(message, [(row, to)])

    lat = pos[1]
    odd = lax.rem(lat, 2)

    @pl.when(odd == 1)
    def _():
        lines(by_x, x_x, height - 1, 0)
        lines(by_d, x_d, 0, height + 1)

    @pl.when(odd == 0)
    def _():
        lines(by_d, x_d, height - 1, 0)
        lines(by_x, x_x, 0, height + 1)

    @pl.when(lat == 0)
    def _():
        mine[:, 0] = jnp.zeros_like(mine[:, 0])

    @pl.when(lat == 3)
    def _():
        mine[:, height + 1] = jnp.zeros_like(mine[:, height + 1])


def pair_kernel(pos, one, two, after, both):
    del pos, after
    both[0] = one[...]
    both[1] = two[...]


def lines_kernel(pos, x_own, x_x, x_y, x_d, after, xs, blank):
    del after, blank
    lat = pos[1]
    levels, rows, circle, lanes = xs.shape
    rows, width, span, half = rows - 2, circle // 4, lanes // 4, levels // 2
    height = rows // 4
    many = half * height * width
    xs[:, 0] = jnp.zeros_like(xs[:, 0])
    xs[:, rows + 1] = jnp.zeros_like(xs[:, rows + 1])
    low = lax.broadcasted_iota(jnp.int32, (circle, 2 * span), 1) < span
    for tag, ref in enumerate((x_own, x_x, x_y, x_d)):
        start = (lat ^ tag) * height
        strips = [
            ref.at[pl.ds((4 - at) % 4 * many, many)].reshape(half, height, width, 2 * span) for at in range(4)
        ]

        @pl.loop(0, half * height)
        def _(step, strips=strips, start=start):
            lev, row = step // height, lax.rem(step, height)
            line = jnp.concatenate([s[lev, row] for s in strips], axis=0).astype(jnp.float32)
            turned = pltpu.roll(line, span, 1)
            for upper in range(2):
                same = jnp.where(low, turned, line) if upper else jnp.where(low, line, turned)
                before = pltpu.roll(same, 1, 0)
                after = pltpu.roll(same, circle - 1, 0)
                at = upper * half + lev
                xs[at, 1 + start + row, :, 0 : 2 * span] = jnp.where(low, before, same).astype(xs.dtype)
                xs[at, 1 + start + row, :, 2 * span : 4 * span] = after.astype(xs.dtype)


def turn(gt, slot, core, first, second, levels):
    many, filters = first.shape
    line = many // levels
    for lev in range(levels):
        block = jnp.concatenate([first[lev * line : (lev + 1) * line], second[lev * line : (lev + 1) * line]], axis=0)
        gt[
            lev * filters : (lev + 1) * filters,
            pl.ds(pl.multiple_of((2 * slot + core) * 2 * line, 2 * line), 2 * line),
        ] = block.T


def taps_kernel(pos, xs, g, s, g2, s2, out, gt, acc):
    levels, rows, circle, lanes = xs.shape
    rows, width, span = rows - 2, circle // 4, lanes // 4
    filters = gt.shape[0] // levels
    deep = rows * width
    right = lax.rem(pos[1], 2)
    for core, parts, last in ((pos[0], g, g2), (1 - pos[0], s, s2)):
        for slot, (ref, at) in enumerate(((parts, 0), (parts, 4), (last, 0), (parts, 2))):
            turn(gt, slot, core, ref[at + right], ref[at + 1 - right], levels)
    acc[...] = jnp.zeros_like(acc)

    @pl.loop(0, 3)
    def _(lat_by):
        for lev in range(levels):
            first, last = max(lev - 1, 0), min(lev + 1, levels - 1)
            to = (first - lev + 1) * filters
            many = (last - first + 1) * filters
            total = acc[lat_by, to : to + many, :]
            for place in range(4):
                total += jnp.dot(
                    gt[first * filters : (last + 1) * filters, place * deep : (place + 1) * deep],
                    xs[lev, pl.ds(lat_by, rows), place * width : (place + 1) * width].reshape(deep, lanes),
                    preferred_element_type=jnp.float32,
                )
            acc[lat_by, to : to + many, :] = total

    scale = 1.0 / math.sqrt(levels * rows * circle)
    for lat_by in range(3):
        for lev_at in range(3):
            block = acc[lat_by, lev_at * filters : (lev_at + 1) * filters, :].T * scale
            for lon_at in range(3):
                out[(2 - lev_at) * 9 + lat_by * 3 + lon_at] = block[lon_at * span : (lon_at + 1) * span]


def code_kernel(pos, held, after, out, late):
    del pos, after
    taps, span, filters = held.shape
    most = jnp.abs(held[0])
    for tap in range(1, taps):
        most = jnp.maximum(most, jnp.abs(held[tap]))
    top = jnp.maximum(jnp.max(most, axis=(0, 1), keepdims=True), 1e-30)
    power = jnp.ceil(jnp.log(top) * (1.0 / math.log(2.0))) - 15.0
    unit = jnp.broadcast_to(jnp.exp2(power), (16, filters)).astype(out.dtype).astype(jnp.float32)
    shrink = 1.0 / unit[0:1]
    skip = out.shape[0] - late.shape[0]
    for tap in range(27):
        value = held[tap] * shrink
        square = value * value
        code = (square * square * square * value * jnp.abs(value)).astype(out.dtype)
        out[tap * span : (tap + 1) * span, :] = code
        if tap * span >= skip:
            late[tap * span - skip : (tap + 1) * span - skip, :] = code
    out[27 * span :, :] = unit.astype(out.dtype)
    late[27 * span - skip :, :] = unit.astype(out.dtype)


def join_kernel(pos, west, east, own, x, y, d, after, both, by_3, by_1):
    del pos, after
    size = west.shape[0]
    cut = own.shape[0] - size
    end = own.shape[0] - 16
    half = by_3.shape[0] - 4 * (cut + 16)
    both[0:size, :] = west[...]
    both[size:, :] = east[...]
    by_3[0:half, :] = west[0:half, :]
    by_1[0 : size - half, :] = east[half:, :]
    for out, at in ((by_3, half), (by_1, size - half)):
        for piece in (own, x, y, d):
            out[at : at + cut, :] = piece[0:cut, :]
            out[at + cut : at + cut + 16, :] = piece[end:, :]
            at += cut + 16


def across_kernel(pos, by_3, by_1, after, late, early_3, early_1):
    del pos, after
    size, many = late.shape[0], early_3.shape[0]
    half = by_3.shape[0] - 2 * many
    late[0:half, :] = by_3[0:half, :]
    late[half:, :] = by_1[0 : size - half, :]
    early_3[...] = by_3[half : half + many, :]
    early_1[...] = by_1[size - half + many :, :]


def unpack_kernel(pos, *refs, slabs, count, span, group):
    sources = refs[:count]
    total, token, buffers, sems = refs[-4:]
    wide = buffers.shape[-1] // 4
    token[...] = jnp.zeros_like(token)
    parts = []
    for step, first, taps, pieces in slabs:
        for at in range(0, taps, group):
            parts.append((step, first + at, min(group, taps - at), at, pieces))

    def copy(at):
        step, first, many, _, _ = parts[at]
        lon_at = pl.multiple_of(lax.rem(pos[2] + step, 4) * span, span)
        return pltpu.make_async_copy(
            buffers.at[at % 2, pl.ds(0, many)], total.at[pl.ds(first, many), pl.ds(lon_at, span)], sems.at[at % 2]
        )

    for at, (_, _, many, skip, pieces) in enumerate(parts):
        if at >= 2:
            copy(at - 2).wait()
        for tag, (which, row, power_row) in enumerate(pieces):
            source = sources[which]
            unit = source[power_row : power_row + 16, :].astype(jnp.float32)[0:1]
            lanes = pl.ds(pl.multiple_of((pos[1] ^ tag) * wide, wide), wide)

            @pl.loop(0, many)
            def _(tap, source=source, start=row + skip * span, unit=unit, lanes=lanes, at=at):
                code = source[pl.ds(pl.multiple_of(start + tap * span, 16), span), :].astype(jnp.float32)
                root = lax.rsqrt(lax.rsqrt(jnp.abs(code)))
                root = root * lax.rsqrt(jnp.maximum(root, 1e-30)) * unit
                buffers[at % 2, tap, :, lanes] = jnp.where(code < 0, -root, root)

        copy(at).start()
    for at in range(max(len(parts) - 2, 0), len(parts)):
        copy(at).wait()


def unpack(pos, total, sources, after, slabs, span, name):
    group = 7
    wide = total.shape[2]
    ins = (pos, *sources, *after, total)
    token = jax.ShapeDtypeStruct((8, 128), jnp.float32)
    return pl.pallas_call(
        lambda *refs: unpack_kernel(*refs, slabs=slabs, count=len(sources), span=span, group=group),
        out_shape=[jax.ShapeDtypeStruct(total.shape, total.dtype), token],
        in_specs=[pl.BlockSpec(memory_space=SMEM)]
        + [pl.BlockSpec(memory_space=VMEM)] * len(sources)
        + [pl.BlockSpec(memory_space=pl.ANY)] * (len(after) + 1),
        out_specs=[pl.BlockSpec(memory_space=pl.ANY), pl.BlockSpec(memory_space=VMEM)],
        scratch_shapes=[VMEM((2, group, span, wide), jnp.float32), pltpu.SemaphoreType.DMA((2,))],
        input_output_aliases={len(ins) - 1: 0},
        cost_estimate=pl.CostEstimate(flops=0, bytes_accessed=4 * 2**20, transcendentals=0),
        compiler_params=pltpu.CompilerParams(vmem_limit_bytes=54 * 1024 * 1024),
        name=name,
    )(*ins)


def field_kernel(pos, after, mine, theirs, w, out, copies, acc):
    del after
    step = pl.program_id(0)
    levels, height, width, chans = out.shape
    many = mine.shape[-1]

    @pl.when(step == 0)
    def _():
        copies[:, 0] = jnp.zeros_like(copies[:, 0])
        copies[:, levels + 1] = jnp.zeros_like(copies[:, levels + 1])
        line_at = lax.broadcasted_iota(jnp.int32, (width, many), 0)
        for which, field in ((pos[0], mine), (1 - pos[0], theirs)):
            lanes = pl.ds(pl.multiple_of(which * many, many), many)
            for lev in range(levels):
                for row in range(height + 2):
                    line = field[lev, row, 0:width].astype(jnp.float32)
                    west = field[lev, row, width : width + 1].astype(jnp.float32)
                    east = field[lev, row, width + 8 : width + 9].astype(jnp.float32)
                    before = jnp.where(line_at == 0, west, pltpu.roll(line, 1, 0))
                    later = jnp.where(line_at == width - 1, east, pltpu.roll(line, width - 1, 0))
                    copies[0, lev + 1, row, :, lanes] = later.astype(copies.dtype)
                    copies[1, lev + 1, row, :, lanes] = field[lev, row, 0:width]
                    copies[2, lev + 1, row, :, lanes] = before.astype(copies.dtype)
        acc[...] = jnp.zeros_like(acc)

    lev_by, lat_by = step // 3, lax.rem(step, 3)
    cells = [
        copies[at, pl.ds(2 - lev_by, levels), pl.ds(2 - lat_by, height)].reshape(
            levels * height * width, 2 * many
        )
        for at in range(3)
    ]
    acc[...] += lax.dot_general(
        jnp.concatenate(cells, axis=1),
        jnp.concatenate([w[at] for at in range(3)], axis=1),
        (((1,), (1,)), ((), ())),
        preferred_element_type=jnp.float32,
    )

    @pl.when(step == 8)
    def _():
        out[...] = acc[...].reshape(out.shape).astype(out.dtype)


def blocked_body(inputs, weights, out_grad):
    chans, levels, height, width = inputs.shape
    filters = weights.shape[2]
    bf16, f32 = jnp.bfloat16, jnp.float32
    lat, lon = lax.axis_index("lat"), lax.axis_index("lon")
    pos = jnp.stack([lax.axis_index("ch"), lat, lon]).astype(jnp.int32)
    x_cells = jnp.transpose(inputs, (1, 2, 3, 0))
    g_cells = jnp.transpose(out_grad, (1, 2, 3, 0))
    taps = jnp.transpose(weights, (1, 0, 2))
    cells = levels * height * width
    span, wide = chans // 4, filters // 4
    rows, circle = 4 * height, 4 * width
    edge = levels * height

    to_same = lambda c, a, o: (a // 2, 2 * c + a % 2, o)
    to_other = lambda c, a, o: (a // 2, 2 * c + 1 - a % 2, o)
    many = cells // 2
    block = jax.ShapeDtypeStruct((cells, wide), bf16)
    strip = jax.ShapeDtypeStruct((2 * levels * width, 2 * span), bf16)
    g_same, g_other, x0, x1, x2, x3, rim_x, rim_d = call(
        pack_kernel,
        [block, block]
        + [jax.ShapeDtypeStruct((many + extra, 2 * span), bf16) for extra in (0, 2 * edge, 0, 2 * edge)]
        + [strip, strip],
        (pos, x_cells, g_cells),
        [VMEM((4, many, 2 * span), bf16)],
        0,
        "pack",
        16,
    )
    g_s = move(g_same, to_same)
    g_o = move(g_other, to_other)
    x_r1 = move(x1, lon_by(1))
    x_r3 = move(x3, lon_by(-1))
    x_r2 = move(x2, lon_by(2))
    by_x = move(rim_x, lat_xor(1))
    by_d = move(rim_d, lat_xor(3))

    inner = 4 * many
    g0, x_own, x_own_y = call(
        spread_kernel,
        [jax.ShapeDtypeStruct((2, cells, wide), bf16)]
        + [jax.ShapeDtypeStruct((count, 2 * span), bf16) for count in (inner + 4 * edge, inner)],
        (pos, x0, x_r1, x_r2, x_r3, g_s, g_o),
        [],
        0,
        "spread",
        16,
    )
    x_x = move(x_own, lat_xor(1))
    x_d = move(x_own, lat_xor(3))
    x_y = move(x_own_y, lat_xor(2))
    g1 = move(g0, lon_by(1))
    g3 = move(g0, lon_by(-1))
    far_a, far_b, g_near, mine = call(
        split_kernel,
        [
            block,
            block,
            jax.ShapeDtypeStruct((6, cells, wide), bf16),
            jax.ShapeDtypeStruct((levels, height + 2, width + 16, chans), bf16),
        ],
        (pos, g0, g1, g3, g_cells, x_own, x_x, x_d, by_x, by_d, x_y),
        [],
        0,
        "split",
        16,
        held=1,
    )
    g2a = move(far_a, lon_by(1))
    g2b = move(far_b, lon_by(-1))
    s_near = move(g_near, sibling)
    theirs = move(mine, sibling)
    xs, total = pl.pallas_call(
        lines_kernel,
        out_shape=[
            jax.ShapeDtypeStruct((levels, rows + 2, circle, 4 * span), bf16),
            jax.ShapeDtypeStruct((27, chans, filters), f32),
        ],
        in_specs=[pl.BlockSpec(memory_space=SMEM)]
        + [pl.BlockSpec(memory_space=VMEM)] * 4
        + [pl.BlockSpec(memory_space=pl.ANY)],
        out_specs=[pl.BlockSpec(memory_space=VMEM)] + [pl.BlockSpec(memory_space=pl.ANY)],
        cost_estimate=pl.CostEstimate(flops=0, bytes_accessed=2**20, transcendentals=0),
        compiler_params=pltpu.CompilerParams(vmem_limit_bytes=24 * 1024 * 1024),
        name="lines",
    )(pos, x_own, x_x, x_y, x_d, far_a)
    (g2,) = call(
        pair_kernel, [jax.ShapeDtypeStruct((2, cells, wide), bf16)], (pos, g2a, g2b, xs), [], 0, "pair", 16, held=1
    )
    s2 = move(g2, sibling)
    early = 7
    cut, end = early * span, 27 * span
    size = end + 16 - cut
    half = size // 32 * 16
    first_rows = cut + 16
    slab = lambda count: jax.ShapeDtypeStruct((count, wide), bf16)
    (grads,) = call(
        taps_kernel,
        [jax.ShapeDtypeStruct((27, span, wide), f32)],
        (pos, xs, g_near, s_near, g2, s2),
        [VMEM((levels * wide, rows * circle), bf16), VMEM((3, 3 * wide, 4 * span), f32)],
        2 * 27 * span * wide * rows * circle * levels,
        "taps",
        28,
    )
    own, late = call(code_kernel, [slab(end + 16), slab(size)], (pos, grads, theirs), [], 0, "code", 16, held=1)

    whole = lambda t: (0, 0, 0, 0)
    field = pl.pallas_call(
        field_kernel,
        out_shape=jax.ShapeDtypeStruct((levels, height, width, chans), bf16),
        grid=(9,),
        in_specs=[
            pl.BlockSpec(memory_space=SMEM),
            pl.BlockSpec(memory_space=pl.ANY),
            pl.BlockSpec(mine.shape, whole),
            pl.BlockSpec(mine.shape, whole),
            pl.BlockSpec((3, chans, filters), lambda t: (t, 0, 0)),
        ],
        out_specs=pl.BlockSpec((levels, height, width, chans), whole),
        scratch_shapes=[
            VMEM((3, levels + 2, height + 2, width, filters), bf16),
            VMEM((cells, chans), f32),
        ],
        cost_estimate=pl.CostEstimate(
            flops=4 * 27 * chans * filters * cells, bytes_accessed=27 * chans * filters * 2, transcendentals=0
        ),
        compiler_params=pltpu.CompilerParams(vmem_limit_bytes=52 * 1024 * 1024),
        name="field",
    )(pos, own, mine, theirs, taps)

    def to_plane(share):
        return [move(share, lat_xor(tag)) for tag in (1, 2, 3)]

    from_3 = move(late, lon_by(1))
    from_1 = move(late, lon_by(-1))
    plane = [own] + to_plane(own)
    pair, z_3, z_1 = call(
        join_kernel,
        [slab(2 * size), slab(half + 4 * first_rows), slab(size - half + 4 * first_rows)],
        (pos, from_3, from_1, *plane, field),
        [],
        0,
        "join",
        16,
        held=1,
    )
    both = to_plane(pair)
    by_3 = move(z_3, lon_by(1))
    by_1 = move(z_1, lon_by(-1))
    def late_piece(which, row=0):
        return (which, row, row + size - 16)

    def early_piece(which, row):
        return (which, row, row + cut)

    slabs = [(0, 0, 27, [(tag, 0, end) for tag in range(4)])]
    total, token = unpack(pos, total, plane, [pair], slabs, span, "unpack_1")
    from_2, early_3, early_1 = call(
        across_kernel,
        [slab(size), slab(2 * first_rows), slab(2 * first_rows)],
        (pos, by_3, by_1, token),
        [],
        0,
        "across",
        16,
        held=1,
    )
    across = to_plane(from_2)
    early_2a = move(early_3, lon_by(1))
    early_2b = move(early_1, lon_by(-1))

    slabs = [
        (3, early, 27 - early, [late_piece(5)] + [late_piece(at) for at in range(3)]),
        (1, early, 27 - early, [late_piece(6)] + [late_piece(at, size) for at in range(3)]),
        (3, 0, early, [early_piece(3, half + tag * first_rows) for tag in range(4)]),
        (1, 0, early, [early_piece(4, size - half + tag * first_rows) for tag in range(4)]),
    ]
    total, _ = unpack(pos, total, both + [by_3, by_1, from_3, from_1], [from_2], slabs, span, "unpack_2")
    slabs = [
        (2, 0, early, [early_piece(tag // 2, tag % 2 * first_rows) for tag in range(4)]),
        (2, early, 27 - early, [late_piece(2 + tag) for tag in range(4)]),
    ]
    total, _ = unpack(pos, total, [early_2a, early_2b, from_2] + across, [], slabs, span, "unpack_3")
    return (jnp.transpose(field, (3, 0, 1, 2)), jnp.transpose(total, (1, 0, 2)))


def body(inputs, weights, out_grad):
    chans, levels, height, width = inputs.shape
    shape = tuple(lax.axis_size(axis) for axis in AXES)
    fits = (
        shape == (2, 4, 4)
        and chans == out_grad.shape[0] == 256
        and weights.shape[2] == 512
        and levels % 2 == 0
        and height % 2 == 0
        and width % 16 == 0
    )
    return (blocked_body if fits else plain_body)(inputs, weights, out_grad)


def solution(mesh):
    in_specs = (P("ch", None, "lat", "lon"), P("ch", None, None), P("ch", None, "lat", "lon"))
    out_specs = (P("ch", None, "lat", "lon"), P("ch", None, None))
    return jax.shard_map(body, mesh=mesh, in_specs=in_specs, out_specs=out_specs, check_vma=False)
```

```python
import math

import jax
import jax.numpy as jnp
from jax import lax
from jax.experimental import pallas as pl
from jax.experimental.pallas import tpu as pltpu
from jax.sharding import PartitionSpec as P

VMEM = pltpu.VMEM
SMEM = pltpu.SMEM
AXES = ("ch", "lat", "lon")


def padded_2(cells, sides, width):
    for axis, dim in sides:
        count = lax.axis_size(axis)
        head = lax.slice_in_dim(cells, 0, width, axis=dim)
        tail = lax.slice_in_dim(cells, cells.shape[dim] - width, cells.shape[dim], axis=dim)
        cells = jnp.concatenate(
            [
                lax.ppermute(tail, axis, [(i, (i + 1) % count) for i in range(count)]),
                cells,
                lax.ppermute(head, axis, [((i + 1) % count, i) for i in range(count)]),
            ],
            axis=dim,
        )
    return cells


def mask_rims(padded):
    count = lax.axis_size("lat")
    where_lat = lax.axis_index("lat")
    lines = jnp.arange(padded.shape[2])
    drop = (lines == 0) & (where_lat == 0) | (lines == padded.shape[2] - 1) & (
        where_lat == count - 1
    )
    return jnp.where(drop[None, None, :, None], jnp.zeros((), padded.dtype), padded)


def pad_levels(field):
    return jnp.pad(field, ((0, 0), (1, 1), (0, 0), (0, 0)))


def plain_body(inputs, weights, out_grad):
    chans, levels, height, width = inputs.shape
    input_pad = pad_levels(mask_rims(padded_2(inputs, (("lat", 2), ("lon", 3)), 1)))
    grad_inner = lax.all_gather(out_grad, "ch", axis=0, tiled=True)
    grad_pad = pad_levels(mask_rims(padded_2(grad_inner, (("lat", 2), ("lon", 3)), 1)))
    filters = grad_pad.shape[0]
    products = jnp.dot(
        weights.reshape(chans * 27, filters),
        grad_pad.reshape(filters, -1),
        preferred_element_type=jnp.float32,
    )
    products = products.reshape((chans, 27) + tuple(grad_pad.shape[1:]))
    total = jnp.zeros((chans, levels, height, width), jnp.float32)
    pieces = []
    for tap in range(27):
        lev, lat, lon = tap // 9 - 1, tap // 3 % 3 - 1, tap % 3 - 1
        total = (
            total
            + products[
                :,
                tap,
                1 - lev : 1 - lev + levels,
                1 - lat : 1 - lat + height,
                1 - lon : 1 - lon + width,
            ]
        )
        pieces.append(
            input_pad[
                :,
                1 + lev : 1 + lev + levels,
                1 + lat : 1 + lat + height,
                1 + lon : 1 + lon + width,
            ]
        )
    columns = jnp.stack(pieces, axis=1).reshape(chans * 27, -1)
    partial_grad = lax.dot_general(
        columns,
        grad_inner.reshape(filters, -1),
        (((1,), (1,)), ((), ())),
        preferred_element_type=jnp.float32,
    )
    summed = lax.psum(partial_grad, ("lat", "lon"))
    cells = levels * height * width * lax.axis_size("lat") * lax.axis_size("lon")
    weight_grad = (summed * (1.0 / math.sqrt(cells))).reshape(chans, 27, filters)
    return (total.astype(jnp.bfloat16), weight_grad)


def move(x, target):
    pairs = []
    for i in range(32):
        to = target(i // 16, i // 4 % 4, i % 4)
        if to is not None:
            pairs.append((i, (to[0] * 4 + to[1]) * 4 + to[2]))
    return lax.ppermute(x, AXES, pairs)


def lon_by(step):
    return lambda c, a, o: (c, a, (o + step) % 4)


def lat_xor(mask):
    return lambda c, a, o: (c, a ^ mask, o)


def sibling(c, a, o):
    return (1 - c, a, o)


def call(kernel, outs, ins, scratch, flops, name, limit, held=0):
    read = len(ins) - 1 - held
    moved = sum(math.prod(x.shape) * x.dtype.itemsize for x in list(ins[1 : 1 + read]) + list(outs))
    return pl.pallas_call(
        kernel,
        out_shape=outs,
        in_specs=[pl.BlockSpec(memory_space=SMEM)]
        + [pl.BlockSpec(memory_space=VMEM)] * read
        + [pl.BlockSpec(memory_space=pl.ANY)] * held,
        out_specs=[pl.BlockSpec(memory_space=VMEM)] * len(outs),
        scratch_shapes=scratch,
        cost_estimate=pl.CostEstimate(flops=flops, bytes_accessed=moved, transcendentals=0),
        compiler_params=pltpu.CompilerParams(vmem_limit_bytes=limit * 1024 * 1024),
        name=name,
    )(*ins)


def pack_kernel(pos, x, g, g_same, g_other, x0, x1, x2, x3, rim_x, rim_d, held):
    levels, height, width, chans = x.shape
    half, wide = levels // 2, chans // 2
    right = lax.rem(pos[1], 2)
    for out, at in ((g_same, right), (g_other, 1 - right)):
        out[...] = g[:, :, :, pl.ds(pl.multiple_of(at * wide, wide), wide)].reshape(out.shape)
    many = x0.shape[0]
    for block in range(4):
        at = block * (chans // 4)
        lo = x[0:half, :, :, at : at + chans // 4]
        hi = x[half:levels, :, :, at : at + chans // 4]
        held[block] = jnp.concatenate([lo, hi], axis=-1).reshape(held.shape[1:])
    lon = pos[2]
    for step, out in enumerate((x0, x1, x2, x3)):
        out[0:many, :] = held[lax.rem(lon + step, 4)]
    for out, column in ((x1, width - 1), (x3, 0)):
        rim = g[:, :, column, :].reshape(levels * height, chans)
        out[many : many + levels * height, :] = rim[:, 0:wide]
        out[many + levels * height :, :] = rim[:, wide:]
    even = right == 0
    low, high = g[:, 0], g[:, height - 1]
    line = levels * width
    for out, upward in ((rim_x, even), (rim_d, jnp.logical_not(even))):
        facing = jnp.where(upward, high, low).reshape(line, chans)
        for at in range(2):
            out[at * line : (at + 1) * line, :] = facing[:, at * wide : (at + 1) * wide]


def spread_kernel(pos, x0, x1, x2, x3, one, two, both, own, own_y):
    del pos
    many = x0.shape[0]
    both[0] = one[...]
    both[1] = two[...]
    for at, piece in enumerate((x0, x1, x2, x3)):
        own[at * many : (at + 1) * many, :] = piece[0:many, :]
        own_y[at * many : (at + 1) * many, :] = piece[0:many, :]
    extra = x1.shape[0] - many
    own[4 * many : 4 * many + extra, :] = x1[many:, :]
    own[4 * many + extra :, :] = x3[many:, :]


def split_kernel(
    pos, here, west, east, g, own, x_x, x_d, by_x, by_d, after, first, second, near, mine
):
    del after
    first[...] = west[0]
    second[...] = east[1]
    for at, part in enumerate((here, west, east)):
        near[2 * at : 2 * at + 2] = part[...]

    levels, height, width, chans = g.shape
    edge, line, wide = levels * height, levels * width, chans // 2
    inner = own.shape[0] - 4 * edge
    mine[:, 1 : height + 1, 0:width, :] = g[...]

    def columns(message, rows):
        for side in range(2):
            for half in range(2):
                start = inner + (2 * side + half) * edge
                rim = message[start : start + edge, :].reshape(levels, height, wide)
                at = width + 8 * side
                for row, to in rows:
                    mine[:, to, at : at + 8, half * wide : (half + 1) * wide] = jnp.broadcast_to(
                        rim[:, row : row + 1], (levels, 8, wide)
                    )

    columns(own, [(row, row + 1) for row in range(height)])

    def lines(strip, message, row, to):
        for half in range(2):
            part = strip[half * line : (half + 1) * line, :]
            mine[:, to, 0:width, half * wide : (half + 1) * wide] = part.reshape(levels, width, wide)
        columns(message, [(row, to)])

    lat = pos[1]
    odd = lax.rem(lat, 2)

    @pl.when(odd == 1)
    def _():
        lines(by_x, x_x, height - 1, 0)
        lines(by_d, x_d, 0, height + 1)

    @pl.when(odd == 0)
    def _():
        lines(by_d, x_d, height - 1, 0)
        lines(by_x, x_x, 0, height + 1)

    @pl.when(lat == 0)
    def _():
        mine[:, 0] = jnp.zeros_like(mine[:, 0])

    @pl.when(lat == 3)
    def _():
        mine[:, height + 1] = jnp.zeros_like(mine[:, height + 1])


def pair_kernel(pos, one, two, after, both):
    del pos, after
    both[0] = one[...]
    both[1] = two[...]


def lines_kernel(pos, x_own, x_x, x_y, x_d, after, xs, blank):
    del after, blank
    lat = pos[1]
    levels, rows, circle, lanes = xs.shape
    rows, width, span, half = rows - 2, circle // 4, lanes // 4, levels // 2
    height = rows // 4
    many = half * height * width
    xs[:, 0] = jnp.zeros_like(xs[:, 0])
    xs[:, rows + 1] = jnp.zeros_like(xs[:, rows + 1])
    low = lax.broadcasted_iota(jnp.int32, (circle, 2 * span), 1) < span
    for tag, ref in enumerate((x_own, x_x, x_y, x_d)):
        start = (lat ^ tag) * height
        strips = [
            ref.at[pl.ds((4 - at) % 4 * many, many)].reshape(half, height, width, 2 * span) for at in range(4)
        ]

        @pl.loop(0, half * height)
        def _(step, strips=strips, start=start):
            lev, row = step // height, lax.rem(step, height)
            line = jnp.concatenate([s[lev, row] for s in strips], axis=0).astype(jnp.float32)
            turned = pltpu.roll(line, span, 1)
            for upper in range(2):
                same = jnp.where(low, turned, line) if upper else jnp.where(low, line, turned)
                before = pltpu.roll(same, 1, 0)
                after = pltpu.roll(same, circle - 1, 0)
                at = upper * half + lev
                xs[at, 1 + start + row, :, 0 : 2 * span] = jnp.where(low, before, same).astype(xs.dtype)
                xs[at, 1 + start + row, :, 2 * span : 4 * span] = after.astype(xs.dtype)


def turn(gt, slot, core, first, second, levels):
    many, filters = first.shape
    line = many // levels
    for lev in range(levels):
        block = jnp.concatenate([first[lev * line : (lev + 1) * line], second[lev * line : (lev + 1) * line]], axis=0)
        gt[
            lev * filters : (lev + 1) * filters,
            pl.ds(pl.multiple_of((2 * slot + core) * 2 * line, 2 * line), 2 * line),
        ] = block.T


def taps_kernel(pos, xs, g, s, g2, s2, out, gt, acc):
    levels, rows, circle, lanes = xs.shape
    rows, width, span = rows - 2, circle // 4, lanes // 4
    filters = gt.shape[0] // levels
    deep = rows * width
    right = lax.rem(pos[1], 2)
    for core, parts, last in ((pos[0], g, g2), (1 - pos[0], s, s2)):
        for slot, (ref, at) in enumerate(((parts, 0), (parts, 4), (last, 0), (parts, 2))):
            turn(gt, slot, core, ref[at + right], ref[at + 1 - right], levels)
    acc[...] = jnp.zeros_like(acc)

    @pl.loop(0, 3)
    def _(lat_by):
        for lev in range(levels):
            first, last = max(lev - 1, 0), min(lev + 1, levels - 1)
            to = (first - lev + 1) * filters
            many = (last - first + 1) * filters
            total = acc[lat_by, to : to + many, :]
            for place in range(4):
                total += jnp.dot(
                    gt[first * filters : (last + 1) * filters, place * deep : (place + 1) * deep],
                    xs[lev, pl.ds(lat_by, rows), place * width : (place + 1) * width].reshape(deep, lanes),
                    preferred_element_type=jnp.float32,
                )
            acc[lat_by, to : to + many, :] = total

    scale = 1.0 / math.sqrt(levels * rows * circle)
    for lat_by in range(3):
        for lev_at in range(3):
            block = acc[lat_by, lev_at * filters : (lev_at + 1) * filters, :].T * scale
            for lon_at in range(3):
                out[(2 - lev_at) * 9 + lat_by * 3 + lon_at] = block[lon_at * span : (lon_at + 1) * span]


def code_kernel(pos, held, after, out, late):
    del pos, after
    taps, span, filters = held.shape
    most = jnp.abs(held[0])
    for tap in range(1, taps):
        most = jnp.maximum(most, jnp.abs(held[tap]))
    top = jnp.maximum(jnp.max(most, axis=(0, 1), keepdims=True), 1e-30)
    power = jnp.ceil(jnp.log(top) * (1.0 / math.log(2.0))) - 15.0
    unit = jnp.broadcast_to(jnp.exp2(power), (16, filters)).astype(out.dtype).astype(jnp.float32)
    shrink = 1.0 / unit[0:1]
    skip = out.shape[0] - late.shape[0]
    for tap in range(27):
        value = held[tap] * shrink
        square = value * value
        code = (square * square * square * value * jnp.abs(value)).astype(out.dtype)
        out[tap * span : (tap + 1) * span, :] = code
        if tap * span >= skip:
            late[tap * span - skip : (tap + 1) * span - skip, :] = code
    out[27 * span :, :] = unit.astype(out.dtype)
    late[27 * span - skip :, :] = unit.astype(out.dtype)


def join_kernel(pos, west, east, plane, after, both, by_3, by_1):
    del pos, after
    size = west.shape[0]
    rows = plane.shape[0] // 4
    cut, end = rows - size, rows - 16
    half = by_3.shape[0] - 4 * (cut + 16)
    both[0:size, :] = west[...]
    both[size:, :] = east[...]
    by_3[0:half, :] = west[0:half, :]
    by_1[0 : size - half, :] = east[half:, :]
    for out, at in ((by_3, half), (by_1, size - half)):
        for lat in range(4):
            out[at : at + cut, :] = plane[lat * rows : lat * rows + cut, :]
            out[at + cut : at + cut + 16, :] = plane[lat * rows + end : (lat + 1) * rows, :]
            at += cut + 16


def across_kernel(pos, by_3, by_1, after, late, early_3, early_1):
    del pos, after
    size, many = late.shape[0], early_3.shape[0]
    half = by_3.shape[0] - 2 * many
    late[0:half, :] = by_3[0:half, :]
    late[half:, :] = by_1[0 : size - half, :]
    early_3[...] = by_3[half : half + many, :]
    early_1[...] = by_1[size - half + many :, :]


def unpack_kernel(pos, *refs, slabs, count, span, group):
    sources = refs[:count]
    total, token, buffers, sems = refs[-4:]
    wide = buffers.shape[-1] // 4
    token[...] = jnp.zeros_like(token)
    parts = []
    for step, first, taps, pieces in slabs:
        for at in range(0, taps, group):
            parts.append((step, first + at, min(group, taps - at), at, pieces))

    def copy(at):
        step, first, many, _, _ = parts[at]
        lon_at = pl.multiple_of(lax.rem(pos[2] + step, 4) * span, span)
        return pltpu.make_async_copy(
            buffers.at[at % 2, pl.ds(0, many)], total.at[pl.ds(first, many), pl.ds(lon_at, span)], sems.at[at % 2]
        )

    for at, (_, _, many, skip, pieces) in enumerate(parts):
        if at >= 2:
            copy(at - 2).wait()
        units = [sources[i][j : j + 16, :].astype(jnp.float32)[0:1] for i, _, j in pieces]

        @pl.loop(0, many)
        def _(tap, pieces=pieces, skip=skip, units=units, at=at):
            for lat, (which, row, _) in enumerate(pieces):
                start = pl.multiple_of(row + (skip + tap) * span, 16)
                code = sources[which][pl.ds(start, span), :].astype(jnp.float32)
                root = lax.rsqrt(lax.rsqrt(jnp.abs(code)))
                root = root * lax.rsqrt(jnp.maximum(root, 1e-30)) * units[lat]
                buffers[at % 2, tap, :, lat * wide : (lat + 1) * wide] = jnp.where(code < 0, -root, root)

        copy(at).start()
    for at in range(max(len(parts) - 2, 0), len(parts)):
        copy(at).wait()


def unpack(pos, total, sources, after, slabs, span, name):
    group = 7
    wide = total.shape[2]
    ins = (pos, *sources, *after, total)
    token = jax.ShapeDtypeStruct((8, 128), jnp.float32)
    return pl.pallas_call(
        lambda *refs: unpack_kernel(*refs, slabs=slabs, count=len(sources), span=span, group=group),
        out_shape=[jax.ShapeDtypeStruct(total.shape, total.dtype), token],
        in_specs=[pl.BlockSpec(memory_space=SMEM)]
        + [pl.BlockSpec(memory_space=VMEM)] * len(sources)
        + [pl.BlockSpec(memory_space=pl.ANY)] * (len(after) + 1),
        out_specs=[pl.BlockSpec(memory_space=pl.ANY), pl.BlockSpec(memory_space=VMEM)],
        scratch_shapes=[VMEM((2, group, span, wide), jnp.float32), pltpu.SemaphoreType.DMA((2,))],
        input_output_aliases={len(ins) - 1: 0},
        cost_estimate=pl.CostEstimate(flops=0, bytes_accessed=4 * 2**20, transcendentals=0),
        compiler_params=pltpu.CompilerParams(vmem_limit_bytes=54 * 1024 * 1024),
        name=name,
    )(*ins)


def field_kernel(pos, after, mine, theirs, w, out, copies, acc):
    del after
    step = pl.program_id(0)
    levels, height, width, chans = out.shape
    many = mine.shape[-1]

    @pl.when(step == 0)
    def _():
        copies[:, 0] = jnp.zeros_like(copies[:, 0])
        copies[:, levels + 1] = jnp.zeros_like(copies[:, levels + 1])
        line_at = lax.broadcasted_iota(jnp.int32, (width, many), 0)
        for which, field in ((pos[0], mine), (1 - pos[0], theirs)):
            lanes = pl.ds(pl.multiple_of(which * many, many), many)
            for lev in range(levels):
                for row in range(height + 2):
                    line = field[lev, row, 0:width].astype(jnp.float32)
                    west = field[lev, row, width : width + 1].astype(jnp.float32)
                    east = field[lev, row, width + 8 : width + 9].astype(jnp.float32)
                    before = jnp.where(line_at == 0, west, pltpu.roll(line, 1, 0))
                    later = jnp.where(line_at == width - 1, east, pltpu.roll(line, width - 1, 0))
                    copies[0, lev + 1, row, :, lanes] = later.astype(copies.dtype)
                    copies[1, lev + 1, row, :, lanes] = field[lev, row, 0:width]
                    copies[2, lev + 1, row, :, lanes] = before.astype(copies.dtype)
        acc[...] = jnp.zeros_like(acc)

    lev_by, lat_by = step // 3, lax.rem(step, 3)
    cells = [
        copies[at, pl.ds(2 - lev_by, levels), pl.ds(2 - lat_by, height)].reshape(
            levels * height * width, 2 * many
        )
        for at in range(3)
    ]
    acc[...] += lax.dot_general(
        jnp.concatenate(cells, axis=1),
        jnp.concatenate([w[at] for at in range(3)], axis=1),
        (((1,), (1,)), ((), ())),
        preferred_element_type=jnp.float32,
    )

    @pl.when(step == 8)
    def _():
        out[...] = acc[...].reshape(out.shape).astype(out.dtype)


def blocked_body(inputs, weights, out_grad):
    chans, levels, height, width = inputs.shape
    filters = weights.shape[2]
    bf16, f32 = jnp.bfloat16, jnp.float32
    lat, lon = lax.axis_index("lat"), lax.axis_index("lon")
    pos = jnp.stack([lax.axis_index("ch"), lat, lon]).astype(jnp.int32)
    x_cells = jnp.transpose(inputs, (1, 2, 3, 0))
    g_cells = jnp.transpose(out_grad, (1, 2, 3, 0))
    taps = jnp.transpose(weights, (1, 0, 2))
    cells = levels * height * width
    span, wide = chans // 4, filters // 4
    rows, circle = 4 * height, 4 * width
    edge = levels * height

    to_same = lambda c, a, o: (a // 2, 2 * c + a % 2, o)
    to_other = lambda c, a, o: (a // 2, 2 * c + 1 - a % 2, o)
    many = cells // 2
    block = jax.ShapeDtypeStruct((cells, wide), bf16)
    strip = jax.ShapeDtypeStruct((2 * levels * width, 2 * span), bf16)
    g_same, g_other, x0, x1, x2, x3, rim_x, rim_d = call(
        pack_kernel,
        [block, block]
        + [jax.ShapeDtypeStruct((many + extra, 2 * span), bf16) for extra in (0, 2 * edge, 0, 2 * edge)]
        + [strip, strip],
        (pos, x_cells, g_cells),
        [VMEM((4, many, 2 * span), bf16)],
        0,
        "pack",
        16,
    )
    g_s = move(g_same, to_same)
    g_o = move(g_other, to_other)
    x_r1 = move(x1, lon_by(1))
    x_r3 = move(x3, lon_by(-1))
    x_r2 = move(x2, lon_by(2))
    by_x = move(rim_x, lat_xor(1))
    by_d = move(rim_d, lat_xor(3))

    inner = 4 * many
    g0, x_own, x_own_y = call(
        spread_kernel,
        [jax.ShapeDtypeStruct((2, cells, wide), bf16)]
        + [jax.ShapeDtypeStruct((count, 2 * span), bf16) for count in (inner + 4 * edge, inner)],
        (pos, x0, x_r1, x_r2, x_r3, g_s, g_o),
        [],
        0,
        "spread",
        16,
    )
    x_x = move(x_own, lat_xor(1))
    x_d = move(x_own, lat_xor(3))
    x_y = move(x_own_y, lat_xor(2))
    g1 = move(g0, lon_by(1))
    g3 = move(g0, lon_by(-1))
    far_a, far_b, g_near, mine = call(
        split_kernel,
        [
            block,
            block,
            jax.ShapeDtypeStruct((6, cells, wide), bf16),
            jax.ShapeDtypeStruct((levels, height + 2, width + 16, chans), bf16),
        ],
        (pos, g0, g1, g3, g_cells, x_own, x_x, x_d, by_x, by_d, x_y),
        [],
        0,
        "split",
        16,
        held=1,
    )
    g2a = move(far_a, lon_by(1))
    g2b = move(far_b, lon_by(-1))
    s_near = move(g_near, sibling)
    theirs = move(mine, sibling)
    xs, total = pl.pallas_call(
        lines_kernel,
        out_shape=[
            jax.ShapeDtypeStruct((levels, rows + 2, circle, 4 * span), bf16),
            jax.ShapeDtypeStruct((27, chans, filters), f32),
        ],
        in_specs=[pl.BlockSpec(memory_space=SMEM)]
        + [pl.BlockSpec(memory_space=VMEM)] * 4
        + [pl.BlockSpec(memory_space=pl.ANY)],
        out_specs=[pl.BlockSpec(memory_space=VMEM)] + [pl.BlockSpec(memory_space=pl.ANY)],
        cost_estimate=pl.CostEstimate(flops=0, bytes_accessed=2**20, transcendentals=0),
        compiler_params=pltpu.CompilerParams(vmem_limit_bytes=24 * 1024 * 1024),
        name="lines",
    )(pos, x_own, x_x, x_y, x_d, far_a)
    (g2,) = call(
        pair_kernel, [jax.ShapeDtypeStruct((2, cells, wide), bf16)], (pos, g2a, g2b, xs), [], 0, "pair", 16, held=1
    )
    s2 = move(g2, sibling)
    early = 7
    cut, end = early * span, 27 * span
    size = end + 16 - cut
    half = size // 32 * 16
    first_rows = cut + 16
    slab = lambda count: jax.ShapeDtypeStruct((count, wide), bf16)
    (grads,) = call(
        taps_kernel,
        [jax.ShapeDtypeStruct((27, span, wide), f32)],
        (pos, xs, g_near, s_near, g2, s2),
        [VMEM((levels * wide, rows * circle), bf16), VMEM((3, 3 * wide, 4 * span), f32)],
        2 * 27 * span * wide * rows * circle * levels,
        "taps",
        28,
    )
    own, late = call(code_kernel, [slab(end + 16), slab(size)], (pos, grads, theirs), [], 0, "code", 16, held=1)

    whole = lambda t: (0, 0, 0, 0)
    field = pl.pallas_call(
        field_kernel,
        out_shape=jax.ShapeDtypeStruct((levels, height, width, chans), bf16),
        grid=(9,),
        in_specs=[
            pl.BlockSpec(memory_space=SMEM),
            pl.BlockSpec(memory_space=pl.ANY),
            pl.BlockSpec(mine.shape, whole),
            pl.BlockSpec(mine.shape, whole),
            pl.BlockSpec((3, chans, filters), lambda t: (t, 0, 0)),
        ],
        out_specs=pl.BlockSpec((levels, height, width, chans), whole),
        scratch_shapes=[
            VMEM((3, levels + 2, height + 2, width, filters), bf16),
            VMEM((cells, chans), f32),
        ],
        cost_estimate=pl.CostEstimate(
            flops=4 * 27 * chans * filters * cells, bytes_accessed=27 * chans * filters * 2, transcendentals=0
        ),
        compiler_params=pltpu.CompilerParams(vmem_limit_bytes=52 * 1024 * 1024),
        name="field",
    )(pos, own, mine, theirs, taps)

    def to_plane(share):
        return lax.all_gather(share, "lat", axis=0, tiled=True)

    from_3 = move(late, lon_by(1))
    from_1 = move(late, lon_by(-1))
    plane = to_plane(own)
    pair, z_3, z_1 = call(
        join_kernel,
        [slab(2 * size), slab(half + 4 * first_rows), slab(size - half + 4 * first_rows)],
        (pos, from_3, from_1, plane, field),
        [],
        0,
        "join",
        16,
        held=1,
    )
    both = to_plane(pair)
    by_3 = move(z_3, lon_by(1))
    by_1 = move(z_1, lon_by(-1))
    def late_piece(which, row=0):
        return (which, row, row + size - 16)

    def early_piece(which, row):
        return (which, row, row + cut)

    slabs = [(0, 0, 27, [(0, at * (end + 16), at * (end + 16) + end) for at in range(4)])]
    total, token = unpack(pos, total, [plane], [pair], slabs, span, "unpack_1")
    from_2, early_3, early_1 = call(
        across_kernel,
        [slab(size), slab(2 * first_rows), slab(2 * first_rows)],
        (pos, by_3, by_1, token),
        [],
        0,
        "across",
        16,
        held=1,
    )
    across = to_plane(from_2)
    early_2a = move(early_3, lon_by(1))
    early_2b = move(early_1, lon_by(-1))

    slabs = [
        (3, early, 27 - early, [late_piece(0, 2 * size * at) for at in range(4)]),
        (1, early, 27 - early, [late_piece(0, 2 * size * at + size) for at in range(4)]),
        (3, 0, early, [early_piece(1, half + at * first_rows) for at in range(4)]),
        (1, 0, early, [early_piece(2, size - half + at * first_rows) for at in range(4)]),
    ]
    total, _ = unpack(pos, total, [both, by_3, by_1], [from_2], slabs, span, "unpack_2")
    slabs = [
        (2, 0, early, [early_piece(at // 2, at % 2 * first_rows) for at in range(4)]),
        (2, early, 27 - early, [late_piece(2, size * at) for at in range(4)]),
    ]
    total, _ = unpack(pos, total, [early_2a, early_2b, across], [], slabs, span, "unpack_3")
    return (jnp.transpose(field, (3, 0, 1, 2)), jnp.transpose(total, (1, 0, 2)))


def body(inputs, weights, out_grad):
    chans, levels, height, width = inputs.shape
    shape = tuple(lax.axis_size(axis) for axis in AXES)
    fits = (
        shape == (2, 4, 4)
        and chans == out_grad.shape[0] == 256
        and weights.shape[2] == 512
        and levels % 2 == 0
        and height % 2 == 0
        and width % 16 == 0
    )
    return (blocked_body if fits else plain_body)(inputs, weights, out_grad)


def solution(mesh):
    in_specs = (P("ch", None, "lat", "lon"), P("ch", None, None), P("ch", None, "lat", "lon"))
    out_specs = (P("ch", None, "lat", "lon"), P("ch", None, None))
    return jax.shard_map(body, mesh=mesh, in_specs=in_specs, out_specs=out_specs, check_vma=False)
```

```python
import math

import jax
import jax.numpy as jnp
from jax import lax
from jax.experimental import pallas as pl
from jax.experimental.pallas import tpu as pltpu
from jax.sharding import PartitionSpec as P

VMEM = pltpu.VMEM
SMEM = pltpu.SMEM
AXES = ("ch", "lat", "lon")


def padded_2(cells, sides, width):
    for axis, dim in sides:
        count = lax.axis_size(axis)
        head = lax.slice_in_dim(cells, 0, width, axis=dim)
        tail = lax.slice_in_dim(cells, cells.shape[dim] - width, cells.shape[dim], axis=dim)
        cells = jnp.concatenate(
            [
                lax.ppermute(tail, axis, [(i, (i + 1) % count) for i in range(count)]),
                cells,
                lax.ppermute(head, axis, [((i + 1) % count, i) for i in range(count)]),
            ],
            axis=dim,
        )
    return cells


def mask_rims(padded):
    count = lax.axis_size("lat")
    where_lat = lax.axis_index("lat")
    lines = jnp.arange(padded.shape[2])
    drop = (lines == 0) & (where_lat == 0) | (lines == padded.shape[2] - 1) & (
        where_lat == count - 1
    )
    return jnp.where(drop[None, None, :, None], jnp.zeros((), padded.dtype), padded)


def pad_levels(field):
    return jnp.pad(field, ((0, 0), (1, 1), (0, 0), (0, 0)))


def plain_body(inputs, weights, out_grad):
    chans, levels, height, width = inputs.shape
    input_pad = pad_levels(mask_rims(padded_2(inputs, (("lat", 2), ("lon", 3)), 1)))
    grad_inner = lax.all_gather(out_grad, "ch", axis=0, tiled=True)
    grad_pad = pad_levels(mask_rims(padded_2(grad_inner, (("lat", 2), ("lon", 3)), 1)))
    filters = grad_pad.shape[0]
    products = jnp.dot(
        weights.reshape(chans * 27, filters),
        grad_pad.reshape(filters, -1),
        preferred_element_type=jnp.float32,
    )
    products = products.reshape((chans, 27) + tuple(grad_pad.shape[1:]))
    total = jnp.zeros((chans, levels, height, width), jnp.float32)
    pieces = []
    for tap in range(27):
        lev, lat, lon = tap // 9 - 1, tap // 3 % 3 - 1, tap % 3 - 1
        total = (
            total
            + products[
                :,
                tap,
                1 - lev : 1 - lev + levels,
                1 - lat : 1 - lat + height,
                1 - lon : 1 - lon + width,
            ]
        )
        pieces.append(
            input_pad[
                :,
                1 + lev : 1 + lev + levels,
                1 + lat : 1 + lat + height,
                1 + lon : 1 + lon + width,
            ]
        )
    columns = jnp.stack(pieces, axis=1).reshape(chans * 27, -1)
    partial_grad = lax.dot_general(
        columns,
        grad_inner.reshape(filters, -1),
        (((1,), (1,)), ((), ())),
        preferred_element_type=jnp.float32,
    )
    summed = lax.psum(partial_grad, ("lat", "lon"))
    cells = levels * height * width * lax.axis_size("lat") * lax.axis_size("lon")
    weight_grad = (summed * (1.0 / math.sqrt(cells))).reshape(chans, 27, filters)
    return (total.astype(jnp.bfloat16), weight_grad)


def move(x, target):
    pairs = []
    for i in range(32):
        to = target(i // 16, i // 4 % 4, i % 4)
        if to is not None:
            pairs.append((i, (to[0] * 4 + to[1]) * 4 + to[2]))
    return lax.ppermute(x, AXES, pairs)


def lon_by(step):
    return lambda c, a, o: (c, a, (o + step) % 4)


def lat_xor(mask):
    return lambda c, a, o: (c, a ^ mask, o)


def sibling(c, a, o):
    return (1 - c, a, o)


def call(kernel, outs, ins, scratch, flops, name, limit, held=0):
    read = len(ins) - 1 - held
    moved = sum(math.prod(x.shape) * x.dtype.itemsize for x in list(ins[1 : 1 + read]) + list(outs))
    return pl.pallas_call(
        kernel,
        out_shape=outs,
        in_specs=[pl.BlockSpec(memory_space=SMEM)]
        + [pl.BlockSpec(memory_space=VMEM)] * read
        + [pl.BlockSpec(memory_space=pl.ANY)] * held,
        out_specs=[pl.BlockSpec(memory_space=VMEM)] * len(outs),
        scratch_shapes=scratch,
        cost_estimate=pl.CostEstimate(flops=flops, bytes_accessed=moved, transcendentals=0),
        compiler_params=pltpu.CompilerParams(vmem_limit_bytes=limit * 1024 * 1024),
        name=name,
    )(*ins)


def pack_kernel(pos, x, g, g_same, g_other, x0, x1, x2, x3, rim_x, rim_d, held):
    levels, height, width, chans = x.shape
    half, wide = levels // 2, chans // 2
    right = lax.rem(pos[1], 2)
    for out, at in ((g_same, right), (g_other, 1 - right)):
        out[...] = g[:, :, :, pl.ds(pl.multiple_of(at * wide, wide), wide)].reshape(out.shape)
    many = x0.shape[0]
    for block in range(4):
        at = block * (chans // 4)
        lo = x[0:half, :, :, at : at + chans // 4]
        hi = x[half:levels, :, :, at : at + chans // 4]
        held[block] = jnp.concatenate([lo, hi], axis=-1).reshape(held.shape[1:])
    lon = pos[2]
    for step, out in enumerate((x0, x1, x2, x3)):
        out[0:many, :] = held[lax.rem(lon + step, 4)]
    for out, column in ((x1, width - 1), (x3, 0)):
        rim = g[:, :, column, :].reshape(levels * height, chans)
        out[many : many + levels * height, :] = rim[:, 0:wide]
        out[many + levels * height :, :] = rim[:, wide:]
    even = right == 0
    low, high = g[:, 0], g[:, height - 1]
    line = levels * width
    for out, upward in ((rim_x, even), (rim_d, jnp.logical_not(even))):
        facing = jnp.where(upward, high, low).reshape(line, chans)
        for at in range(2):
            out[at * line : (at + 1) * line, :] = facing[:, at * wide : (at + 1) * wide]


def spread_kernel(pos, x0, x1, x2, x3, one, two, both, own, own_y):
    del pos
    many = x0.shape[0]
    both[0] = one[...]
    both[1] = two[...]
    for at, piece in enumerate((x0, x1, x2, x3)):
        own[at * many : (at + 1) * many, :] = piece[0:many, :]
        own_y[at * many : (at + 1) * many, :] = piece[0:many, :]
    extra = x1.shape[0] - many
    own[4 * many : 4 * many + extra, :] = x1[many:, :]
    own[4 * many + extra :, :] = x3[many:, :]


def split_kernel(
    pos, here, west, east, g, own, x_x, x_d, by_x, by_d, after, first, second, near, mine
):
    del after
    first[...] = west[0]
    second[...] = east[1]
    for at, part in enumerate((here, west, east)):
        near[2 * at : 2 * at + 2] = part[...]

    levels, height, width, chans = g.shape
    edge, line, wide = levels * height, levels * width, chans // 2
    inner = own.shape[0] - 4 * edge
    mine[:, 1 : height + 1, 0:width, :] = g[...]

    def columns(message, rows):
        for side in range(2):
            for half in range(2):
                start = inner + (2 * side + half) * edge
                rim = message[start : start + edge, :].reshape(levels, height, wide)
                at = width + 8 * side
                for row, to in rows:
                    mine[:, to, at : at + 8, half * wide : (half + 1) * wide] = jnp.broadcast_to(
                        rim[:, row : row + 1], (levels, 8, wide)
                    )

    columns(own, [(row, row + 1) for row in range(height)])

    def lines(strip, message, row, to):
        for half in range(2):
            part = strip[half * line : (half + 1) * line, :]
            mine[:, to, 0:width, half * wide : (half + 1) * wide] = part.reshape(levels, width, wide)
        columns(message, [(row, to)])

    lat = pos[1]
    odd = lax.rem(lat, 2)

    @pl.when(odd == 1)
    def _():
        lines(by_x, x_x, height - 1, 0)
        lines(by_d, x_d, 0, height + 1)

    @pl.when(odd == 0)
    def _():
        lines(by_d, x_d, height - 1, 0)
        lines(by_x, x_x, 0, height + 1)

    @pl.when(lat == 0)
    def _():
        mine[:, 0] = jnp.zeros_like(mine[:, 0])

    @pl.when(lat == 3)
    def _():
        mine[:, height + 1] = jnp.zeros_like(mine[:, height + 1])


def pair_kernel(pos, one, two, after, both):
    del pos, after
    both[0] = one[...]
    both[1] = two[...]


def lines_kernel(pos, x_own, x_x, x_y, x_d, after, xs, blank):
    del after, blank
    lat = pos[1]
    levels, rows, circle, lanes = xs.shape
    rows, width, span, half = rows - 2, circle // 4, lanes // 4, levels // 2
    height = rows // 4
    many = half * height * width
    xs[:, 0] = jnp.zeros_like(xs[:, 0])
    xs[:, rows + 1] = jnp.zeros_like(xs[:, rows + 1])
    low = lax.broadcasted_iota(jnp.int32, (circle, 2 * span), 1) < span
    for tag, ref in enumerate((x_own, x_x, x_y, x_d)):
        start = (lat ^ tag) * height
        strips = [
            ref.at[pl.ds((4 - at) % 4 * many, many)].reshape(half, height, width, 2 * span) for at in range(4)
        ]

        @pl.loop(0, half * height)
        def _(step, strips=strips, start=start):
            lev, row = step // height, lax.rem(step, height)
            line = jnp.concatenate([s[lev, row] for s in strips], axis=0).astype(jnp.float32)
            turned = pltpu.roll(line, span, 1)
            for upper in range(2):
                same = jnp.where(low, turned, line) if upper else jnp.where(low, line, turned)
                before = pltpu.roll(same, 1, 0)
                after = pltpu.roll(same, circle - 1, 0)
                at = upper * half + lev
                xs[at, 1 + start + row, :, 0 : 2 * span] = jnp.where(low, before, same).astype(xs.dtype)
                xs[at, 1 + start + row, :, 2 * span : 4 * span] = after.astype(xs.dtype)


def turn(gt, slot, core, first, second, levels):
    many, filters = first.shape
    line = many // levels
    for lev in range(levels):
        block = jnp.concatenate([first[lev * line : (lev + 1) * line], second[lev * line : (lev + 1) * line]], axis=0)
        gt[
            lev * filters : (lev + 1) * filters,
            pl.ds(pl.multiple_of((2 * slot + core) * 2 * line, 2 * line), 2 * line),
        ] = block.T


def taps_kernel(pos, xs, g, s, g2, s2, out, gt, acc):
    levels, rows, circle, lanes = xs.shape
    rows, width, span = rows - 2, circle // 4, lanes // 4
    filters = gt.shape[0] // levels
    deep = rows * width
    right = lax.rem(pos[1], 2)
    for core, parts, last in ((pos[0], g, g2), (1 - pos[0], s, s2)):
        for slot, (ref, at) in enumerate(((parts, 0), (parts, 4), (last, 0), (parts, 2))):
            turn(gt, slot, core, ref[at + right], ref[at + 1 - right], levels)
    acc[...] = jnp.zeros_like(acc)

    @pl.loop(0, 3)
    def _(lat_by):
        for lev in range(levels):
            first, last = max(lev - 1, 0), min(lev + 1, levels - 1)
            to = (first - lev + 1) * filters
            many = (last - first + 1) * filters
            total = acc[lat_by, to : to + many, :]
            for place in range(4):
                total += jnp.dot(
                    gt[first * filters : (last + 1) * filters, place * deep : (place + 1) * deep],
                    xs[lev, pl.ds(lat_by, rows), place * width : (place + 1) * width].reshape(deep, lanes),
                    preferred_element_type=jnp.float32,
                )
            acc[lat_by, to : to + many, :] = total

    scale = 1.0 / math.sqrt(levels * rows * circle)
    for lat_by in range(3):
        for lev_at in range(3):
            block = acc[lat_by, lev_at * filters : (lev_at + 1) * filters, :].T * scale
            for lon_at in range(3):
                out[(2 - lev_at) * 9 + lat_by * 3 + lon_at] = block[lon_at * span : (lon_at + 1) * span]


def code_kernel(pos, held, after, out, late):
    del pos, after
    taps, span, filters = held.shape
    most = jnp.abs(held[0])
    for tap in range(1, taps):
        most = jnp.maximum(most, jnp.abs(held[tap]))
    top = jnp.maximum(jnp.max(most, axis=(0, 1), keepdims=True), 1e-30)
    power = jnp.ceil(jnp.log(top) * (1.0 / math.log(2.0))) - 15.0
    unit = jnp.broadcast_to(jnp.exp2(power), (16, filters)).astype(out.dtype).astype(jnp.float32)
    shrink = 1.0 / unit[0:1]
    skip = out.shape[0] - late.shape[0]
    for tap in range(27):
        value = held[tap] * shrink
        square = value * value
        code = (square * value * jnp.abs(value)).astype(out.dtype)
        out[tap * span : (tap + 1) * span, :] = code
        if tap * span >= skip:
            late[tap * span - skip : (tap + 1) * span - skip, :] = code
    out[27 * span :, :] = unit.astype(out.dtype)
    late[27 * span - skip :, :] = unit.astype(out.dtype)


def both_kernel(pos, west, east, after, both):
    del pos, after
    size = west.shape[0]
    both[0:size, :] = west[...]
    both[size:, :] = east[...]


def join_kernel(pos, west, east, own, x, y, d, after, by_3, by_1):
    del pos, after
    size = west.shape[0]
    cut = own.shape[0] - size
    end = own.shape[0] - 16
    half = by_3.shape[0] - 4 * (cut + 16)
    by_3[0:half, :] = west[0:half, :]
    by_1[0 : size - half, :] = east[half:, :]
    for out, at in ((by_3, half), (by_1, size - half)):
        for piece in (own, x, y, d):
            out[at : at + cut, :] = piece[0:cut, :]
            out[at + cut : at + cut + 16, :] = piece[end:, :]
            at += cut + 16


def across_kernel(pos, by_3, by_1, after, late, early_3, early_1):
    del pos, after
    size, many = late.shape[0], early_3.shape[0]
    half = by_3.shape[0] - 2 * many
    late[0:half, :] = by_3[0:half, :]
    late[half:, :] = by_1[0 : size - half, :]
    early_3[...] = by_3[half : half + many, :]
    early_1[...] = by_1[size - half + many :, :]


def unpack_kernel(pos, *refs, slabs, count, span, group):
    sources = refs[:count]
    total, token, buffers, sems = refs[-4:]
    wide = buffers.shape[-1] // 4
    token[...] = jnp.zeros_like(token)
    parts = []
    for step, first, taps, pieces in slabs:
        for at in range(0, taps, group):
            parts.append((step, first + at, min(group, taps - at), at, pieces))

    def copy(at):
        step, first, many, _, _ = parts[at]
        lon_at = pl.multiple_of(lax.rem(pos[2] + step, 4) * span, span)
        return pltpu.make_async_copy(
            buffers.at[at % 2, pl.ds(0, many)], total.at[pl.ds(first, many), pl.ds(lon_at, span)], sems.at[at % 2]
        )

    for at, (_, _, many, skip, pieces) in enumerate(parts):
        if at >= 2:
            copy(at - 2).wait()
        units = [sources[i][j : j + 16, :].astype(jnp.float32)[0:1] for i, _, j in pieces]

        @pl.loop(0, many)
        def _(tap, pieces=pieces, skip=skip, units=units, at=at):
            for tag, (which, row, _) in enumerate(pieces):
                start = pl.multiple_of(row + (skip + tap) * span, 16)
                code = sources[which][pl.ds(start, span), :].astype(jnp.float32)
                root = lax.rsqrt(lax.rsqrt(jnp.abs(code))) * units[tag]
                lanes = pl.ds(pl.multiple_of((pos[1] ^ tag) * wide, wide), wide)
                buffers[at % 2, tap, :, lanes] = jnp.where(code < 0, -root, root)

        copy(at).start()
    for at in range(max(len(parts) - 2, 0), len(parts)):
        copy(at).wait()


def unpack(pos, total, sources, after, slabs, span, name):
    group = 7
    wide = total.shape[2]
    ins = (pos, *sources, *after, total)
    token = jax.ShapeDtypeStruct((8, 128), jnp.float32)
    return pl.pallas_call(
        lambda *refs: unpack_kernel(*refs, slabs=slabs, count=len(sources), span=span, group=group),
        out_shape=[jax.ShapeDtypeStruct(total.shape, total.dtype), token],
        in_specs=[pl.BlockSpec(memory_space=SMEM)]
        + [pl.BlockSpec(memory_space=VMEM)] * len(sources)
        + [pl.BlockSpec(memory_space=pl.ANY)] * (len(after) + 1),
        out_specs=[pl.BlockSpec(memory_space=pl.ANY), pl.BlockSpec(memory_space=VMEM)],
        scratch_shapes=[VMEM((2, group, span, wide), jnp.float32), pltpu.SemaphoreType.DMA((2,))],
        input_output_aliases={len(ins) - 1: 0},
        cost_estimate=pl.CostEstimate(flops=0, bytes_accessed=4 * 2**20, transcendentals=0),
        compiler_params=pltpu.CompilerParams(vmem_limit_bytes=54 * 1024 * 1024),
        name=name,
    )(*ins)


def field_kernel(pos, after, mine, theirs, w, out, copies, acc):
    del after
    step = pl.program_id(0)
    levels, height, width, chans = out.shape
    many = mine.shape[-1]

    @pl.when(step == 0)
    def _():
        copies[:, 0] = jnp.zeros_like(copies[:, 0])
        copies[:, levels + 1] = jnp.zeros_like(copies[:, levels + 1])
        line_at = lax.broadcasted_iota(jnp.int32, (width, many), 0)
        for which, field in ((pos[0], mine), (1 - pos[0], theirs)):
            lanes = pl.ds(pl.multiple_of(which * many, many), many)
            for lev in range(levels):
                for row in range(height + 2):
                    line = field[lev, row, 0:width].astype(jnp.float32)
                    west = field[lev, row, width : width + 1].astype(jnp.float32)
                    east = field[lev, row, width + 8 : width + 9].astype(jnp.float32)
                    before = jnp.where(line_at == 0, west, pltpu.roll(line, 1, 0))
                    later = jnp.where(line_at == width - 1, east, pltpu.roll(line, width - 1, 0))
                    copies[0, lev + 1, row, :, lanes] = later.astype(copies.dtype)
                    copies[1, lev + 1, row, :, lanes] = field[lev, row, 0:width]
                    copies[2, lev + 1, row, :, lanes] = before.astype(copies.dtype)
        acc[...] = jnp.zeros_like(acc)

    lev_by, lat_by = step // 3, lax.rem(step, 3)
    cells = [
        copies[at, pl.ds(2 - lev_by, levels), pl.ds(2 - lat_by, height)].reshape(
            levels * height * width, 2 * many
        )
        for at in range(3)
    ]
    acc[...] += lax.dot_general(
        jnp.concatenate(cells, axis=1),
        jnp.concatenate([w[at] for at in range(3)], axis=1),
        (((1,), (1,)), ((), ())),
        preferred_element_type=jnp.float32,
    )

    @pl.when(step == 8)
    def _():
        out[...] = acc[...].reshape(out.shape).astype(out.dtype)


def blocked_body(inputs, weights, out_grad):
    chans, levels, height, width = inputs.shape
    filters = weights.shape[2]
    bf16, f32 = jnp.bfloat16, jnp.float32
    lat, lon = lax.axis_index("lat"), lax.axis_index("lon")
    pos = jnp.stack([lax.axis_index("ch"), lat, lon]).astype(jnp.int32)
    x_cells = jnp.transpose(inputs, (1, 2, 3, 0))
    g_cells = jnp.transpose(out_grad, (1, 2, 3, 0))
    taps = jnp.transpose(weights, (1, 0, 2))
    cells = levels * height * width
    span, wide = chans // 4, filters // 4
    rows, circle = 4 * height, 4 * width
    edge = levels * height

    to_same = lambda c, a, o: (a // 2, 2 * c + a % 2, o)
    to_other = lambda c, a, o: (a // 2, 2 * c + 1 - a % 2, o)
    many = cells // 2
    block = jax.ShapeDtypeStruct((cells, wide), bf16)
    strip = jax.ShapeDtypeStruct((2 * levels * width, 2 * span), bf16)
    g_same, g_other, x0, x1, x2, x3, rim_x, rim_d = call(
        pack_kernel,
        [block, block]
        + [jax.ShapeDtypeStruct((many + extra, 2 * span), bf16) for extra in (0, 2 * edge, 0, 2 * edge)]
        + [strip, strip],
        (pos, x_cells, g_cells),
        [VMEM((4, many, 2 * span), bf16)],
        0,
        "pack",
        16,
    )
    g_s = move(g_same, to_same)
    g_o = move(g_other, to_other)
    x_r1 = move(x1, lon_by(1))
    x_r3 = move(x3, lon_by(-1))
    x_r2 = move(x2, lon_by(2))
    by_x = move(rim_x, lat_xor(1))
    by_d = move(rim_d, lat_xor(3))

    inner = 4 * many
    g0, x_own, x_own_y = call(
        spread_kernel,
        [jax.ShapeDtypeStruct((2, cells, wide), bf16)]
        + [jax.ShapeDtypeStruct((count, 2 * span), bf16) for count in (inner + 4 * edge, inner)],
        (pos, x0, x_r1, x_r2, x_r3, g_s, g_o),
        [],
        0,
        "spread",
        16,
    )
    x_x = move(x_own, lat_xor(1))
    x_d = move(x_own, lat_xor(3))
    x_y = move(x_own_y, lat_xor(2))
    g1 = move(g0, lon_by(1))
    g3 = move(g0, lon_by(-1))
    far_a, far_b, g_near, mine = call(
        split_kernel,
        [
            block,
            block,
            jax.ShapeDtypeStruct((6, cells, wide), bf16),
            jax.ShapeDtypeStruct((levels, height + 2, width + 16, chans), bf16),
        ],
        (pos, g0, g1, g3, g_cells, x_own, x_x, x_d, by_x, by_d, x_y),
        [],
        0,
        "split",
        16,
        held=1,
    )
    g2a = move(far_a, lon_by(1))
    g2b = move(far_b, lon_by(-1))
    s_near = move(g_near, sibling)
    theirs = move(mine, sibling)
    xs, total = pl.pallas_call(
        lines_kernel,
        out_shape=[
            jax.ShapeDtypeStruct((levels, rows + 2, circle, 4 * span), bf16),
            jax.ShapeDtypeStruct((27, chans, filters), f32),
        ],
        in_specs=[pl.BlockSpec(memory_space=SMEM)]
        + [pl.BlockSpec(memory_space=VMEM)] * 4
        + [pl.BlockSpec(memory_space=pl.ANY)],
        out_specs=[pl.BlockSpec(memory_space=VMEM)] + [pl.BlockSpec(memory_space=pl.ANY)],
        cost_estimate=pl.CostEstimate(flops=0, bytes_accessed=2**20, transcendentals=0),
        compiler_params=pltpu.CompilerParams(vmem_limit_bytes=24 * 1024 * 1024),
        name="lines",
    )(pos, x_own, x_x, x_y, x_d, far_a)
    (g2,) = call(
        pair_kernel, [jax.ShapeDtypeStruct((2, cells, wide), bf16)], (pos, g2a, g2b, xs), [], 0, "pair", 16, held=1
    )
    s2 = move(g2, sibling)
    early = 6
    cut, end = early * span, 27 * span
    size = end + 16 - cut
    half = size // 32 * 16
    first_rows = cut + 16
    slab = lambda count: jax.ShapeDtypeStruct((count, wide), bf16)
    (grads,) = call(
        taps_kernel,
        [jax.ShapeDtypeStruct((27, span, wide), f32)],
        (pos, xs, g_near, s_near, g2, s2),
        [VMEM((levels * wide, rows * circle), bf16), VMEM((3, 3 * wide, 4 * span), f32)],
        2 * 27 * span * wide * rows * circle * levels,
        "taps",
        28,
    )
    own, late = call(code_kernel, [slab(end + 16), slab(size)], (pos, grads, theirs), [], 0, "code", 16, held=1)

    whole = lambda t: (0, 0, 0, 0)
    field = pl.pallas_call(
        field_kernel,
        out_shape=jax.ShapeDtypeStruct((levels, height, width, chans), bf16),
        grid=(9,),
        in_specs=[
            pl.BlockSpec(memory_space=SMEM),
            pl.BlockSpec(memory_space=pl.ANY),
            pl.BlockSpec(mine.shape, whole),
            pl.BlockSpec(mine.shape, whole),
            pl.BlockSpec((3, chans, filters), lambda t: (t, 0, 0)),
        ],
        out_specs=pl.BlockSpec((levels, height, width, chans), whole),
        scratch_shapes=[
            VMEM((3, levels + 2, height + 2, width, filters), bf16),
            VMEM((cells, chans), f32),
        ],
        cost_estimate=pl.CostEstimate(
            flops=4 * 27 * chans * filters * cells, bytes_accessed=27 * chans * filters * 2, transcendentals=0
        ),
        compiler_params=pltpu.CompilerParams(vmem_limit_bytes=52 * 1024 * 1024),
        name="field",
    )(pos, own, mine, theirs, taps)

    def to_plane(share):
        return [move(share, lat_xor(tag)) for tag in (1, 2, 3)]

    from_3 = move(late, lon_by(1))
    from_1 = move(late, lon_by(-1))
    plane = [own] + to_plane(own)
    (pair,) = call(both_kernel, [slab(2 * size)], (pos, from_3, from_1, field), [], 0, "both", 16, held=1)
    z_3, z_1 = call(
        join_kernel,
        [slab(half + 4 * first_rows), slab(size - half + 4 * first_rows)],
        (pos, from_3, from_1, *plane, pair),
        [],
        0,
        "join",
        16,
        held=1,
    )
    both = to_plane(pair)
    by_3 = move(z_3, lon_by(1))
    by_1 = move(z_1, lon_by(-1))
    def late_piece(which, row=0):
        return (which, row, row + size - 16)

    def early_piece(which, row):
        return (which, row, row + cut)

    slabs = [(0, 0, 27, [(tag, 0, end) for tag in range(4)])]
    total, token = unpack(pos, total, plane, [pair], slabs, span, "unpack_1")
    from_2, early_3, early_1 = call(
        across_kernel,
        [slab(size), slab(2 * first_rows), slab(2 * first_rows)],
        (pos, by_3, by_1, token),
        [],
        0,
        "across",
        16,
        held=1,
    )
    across = to_plane(from_2)
    early_2a = move(early_3, lon_by(1))
    early_2b = move(early_1, lon_by(-1))

    slabs = [
        (3, early, 27 - early, [late_piece(5)] + [late_piece(at) for at in range(3)]),
        (1, early, 27 - early, [late_piece(6)] + [late_piece(at, size) for at in range(3)]),
        (3, 0, early, [early_piece(3, half + tag * first_rows) for tag in range(4)]),
        (1, 0, early, [early_piece(4, size - half + tag * first_rows) for tag in range(4)]),
    ]
    total, _ = unpack(pos, total, both + [by_3, by_1, from_3, from_1], [from_2], slabs, span, "unpack_2")
    slabs = [
        (2, 0, early, [early_piece(tag // 2, tag % 2 * first_rows) for tag in range(4)]),
        (2, early, 27 - early, [late_piece(2 + tag) for tag in range(4)]),
    ]
    total, _ = unpack(pos, total, [early_2a, early_2b, from_2] + across, [], slabs, span, "unpack_3")
    return (jnp.transpose(field, (3, 0, 1, 2)), jnp.transpose(total, (1, 0, 2)))


def body(inputs, weights, out_grad):
    chans, levels, height, width = inputs.shape
    shape = tuple(lax.axis_size(axis) for axis in AXES)
    fits = (
        shape == (2, 4, 4)
        and chans == out_grad.shape[0] == 256
        and weights.shape[2] == 512
        and levels % 2 == 0
        and height % 2 == 0
        and width % 16 == 0
    )
    return (blocked_body if fits else plain_body)(inputs, weights, out_grad)


def solution(mesh):
    in_specs = (P("ch", None, "lat", "lon"), P("ch", None, None), P("ch", None, "lat", "lon"))
    out_specs = (P("ch", None, "lat", "lon"), P("ch", None, None))
    return jax.shard_map(body, mesh=mesh, in_specs=in_specs, out_specs=out_specs, check_vma=False)
```

```python
import math

import jax
import jax.numpy as jnp
from jax import lax
from jax.experimental import pallas as pl
from jax.experimental.pallas import tpu as pltpu
from jax.sharding import PartitionSpec as P

VMEM = pltpu.VMEM
SMEM = pltpu.SMEM
AXES = ("ch", "lat", "lon")


def padded_2(cells, sides, width):
    for axis, dim in sides:
        count = lax.axis_size(axis)
        head = lax.slice_in_dim(cells, 0, width, axis=dim)
        tail = lax.slice_in_dim(cells, cells.shape[dim] - width, cells.shape[dim], axis=dim)
        cells = jnp.concatenate(
            [
                lax.ppermute(tail, axis, [(i, (i + 1) % count) for i in range(count)]),
                cells,
                lax.ppermute(head, axis, [((i + 1) % count, i) for i in range(count)]),
            ],
            axis=dim,
        )
    return cells


def mask_rims(padded):
    count = lax.axis_size("lat")
    where_lat = lax.axis_index("lat")
    lines = jnp.arange(padded.shape[2])
    drop = (lines == 0) & (where_lat == 0) | (lines == padded.shape[2] - 1) & (
        where_lat == count - 1
    )
    return jnp.where(drop[None, None, :, None], jnp.zeros((), padded.dtype), padded)


def pad_levels(field):
    return jnp.pad(field, ((0, 0), (1, 1), (0, 0), (0, 0)))


def plain_body(inputs, weights, out_grad):
    chans, levels, height, width = inputs.shape
    input_pad = pad_levels(mask_rims(padded_2(inputs, (("lat", 2), ("lon", 3)), 1)))
    grad_inner = lax.all_gather(out_grad, "ch", axis=0, tiled=True)
    grad_pad = pad_levels(mask_rims(padded_2(grad_inner, (("lat", 2), ("lon", 3)), 1)))
    filters = grad_pad.shape[0]
    products = jnp.dot(
        weights.reshape(chans * 27, filters),
        grad_pad.reshape(filters, -1),
        preferred_element_type=jnp.float32,
    )
    products = products.reshape((chans, 27) + tuple(grad_pad.shape[1:]))
    total = jnp.zeros((chans, levels, height, width), jnp.float32)
    pieces = []
    for tap in range(27):
        lev, lat, lon = tap // 9 - 1, tap // 3 % 3 - 1, tap % 3 - 1
        total = (
            total
            + products[
                :,
                tap,
                1 - lev : 1 - lev + levels,
                1 - lat : 1 - lat + height,
                1 - lon : 1 - lon + width,
            ]
        )
        pieces.append(
            input_pad[
                :,
                1 + lev : 1 + lev + levels,
                1 + lat : 1 + lat + height,
                1 + lon : 1 + lon + width,
            ]
        )
    columns = jnp.stack(pieces, axis=1).reshape(chans * 27, -1)
    partial_grad = lax.dot_general(
        columns,
        grad_inner.reshape(filters, -1),
        (((1,), (1,)), ((), ())),
        preferred_element_type=jnp.float32,
    )
    summed = lax.psum(partial_grad, ("lat", "lon"))
    cells = levels * height * width * lax.axis_size("lat") * lax.axis_size("lon")
    weight_grad = (summed * (1.0 / math.sqrt(cells))).reshape(chans, 27, filters)
    return (total.astype(jnp.bfloat16), weight_grad)


def move(x, target):
    pairs = []
    for i in range(32):
        to = target(i // 16, i // 4 % 4, i % 4)
        if to is not None:
            pairs.append((i, (to[0] * 4 + to[1]) * 4 + to[2]))
    return lax.ppermute(x, AXES, pairs)


def lon_by(step):
    return lambda c, a, o: (c, a, (o + step) % 4)


def lat_xor(mask):
    return lambda c, a, o: (c, a ^ mask, o)


def sibling(c, a, o):
    return (1 - c, a, o)


def call(kernel, outs, ins, scratch, flops, name, limit, held=0):
    read = len(ins) - 1 - held
    moved = sum(math.prod(x.shape) * x.dtype.itemsize for x in list(ins[1 : 1 + read]) + list(outs))
    return pl.pallas_call(
        kernel,
        out_shape=outs,
        in_specs=[pl.BlockSpec(memory_space=SMEM)]
        + [pl.BlockSpec(memory_space=VMEM)] * read
        + [pl.BlockSpec(memory_space=pl.ANY)] * held,
        out_specs=[pl.BlockSpec(memory_space=VMEM)] * len(outs),
        scratch_shapes=scratch,
        cost_estimate=pl.CostEstimate(flops=flops, bytes_accessed=moved, transcendentals=0),
        compiler_params=pltpu.CompilerParams(vmem_limit_bytes=limit * 1024 * 1024),
        name=name,
    )(*ins)


def pack_kernel(pos, x, g, g_same, g_other, x0, x1, x2, x3, rim_x, rim_d, held):
    levels, height, width, chans = x.shape
    half, wide = levels // 2, chans // 2
    right = lax.rem(pos[1], 2)
    for out, at in ((g_same, right), (g_other, 1 - right)):
        out[...] = g[:, :, :, pl.ds(pl.multiple_of(at * wide, wide), wide)].reshape(out.shape)
    many = x0.shape[0]
    for block in range(4):
        at = block * (chans // 4)
        lo = x[0:half, :, :, at : at + chans // 4]
        hi = x[half:levels, :, :, at : at + chans // 4]
        held[block] = jnp.concatenate([lo, hi], axis=-1).reshape(held.shape[1:])
    lon = pos[2]
    for step, out in enumerate((x0, x1, x2, x3)):
        out[0:many, :] = held[lax.rem(lon + step, 4)]
    for out, column in ((x1, width - 1), (x3, 0)):
        rim = g[:, :, column, :].reshape(levels * height, chans)
        out[many : many + levels * height, :] = rim[:, 0:wide]
        out[many + levels * height :, :] = rim[:, wide:]
    even = right == 0
    low, high = g[:, 0], g[:, height - 1]
    line = levels * width
    for out, upward in ((rim_x, even), (rim_d, jnp.logical_not(even))):
        facing = jnp.where(upward, high, low).reshape(line, chans)
        for at in range(2):
            out[at * line : (at + 1) * line, :] = facing[:, at * wide : (at + 1) * wide]


def spread_kernel(pos, x0, x1, x2, x3, own, own_y):
    del pos
    many = x0.shape[0]
    for at, piece in enumerate((x0, x1, x2, x3)):
        own[at * many : (at + 1) * many, :] = piece[0:many, :]
        own_y[at * many : (at + 1) * many, :] = piece[0:many, :]
    extra = x1.shape[0] - many
    own[4 * many : 4 * many + extra, :] = x1[many:, :]
    own[4 * many + extra :, :] = x3[many:, :]


def split_kernel(
    pos, here, west, east, g, own, x_x, x_d, by_x, by_d, after, first, second, near, mine
):
    del after
    first[...] = west[0]
    second[...] = east[1]
    for at, part in enumerate((here, west, east)):
        near[2 * at : 2 * at + 2] = part[...]

    levels, height, width, chans = g.shape
    edge, line, wide = levels * height, levels * width, chans // 2
    inner = own.shape[0] - 4 * edge
    mine[:, 1 : height + 1, 0:width, :] = g[...]

    def columns(message, rows):
        for side in range(2):
            for half in range(2):
                start = inner + (2 * side + half) * edge
                rim = message[start : start + edge, :].reshape(levels, height, wide)
                at = width + 8 * side
                for row, to in rows:
                    mine[:, to, at : at + 8, half * wide : (half + 1) * wide] = jnp.broadcast_to(
                        rim[:, row : row + 1], (levels, 8, wide)
                    )

    columns(own, [(row, row + 1) for row in range(height)])

    def lines(strip, message, row, to):
        for half in range(2):
            part = strip[half * line : (half + 1) * line, :]
            mine[:, to, 0:width, half * wide : (half + 1) * wide] = part.reshape(levels, width, wide)
        columns(message, [(row, to)])

    lat = pos[1]
    odd = lax.rem(lat, 2)

    @pl.when(odd == 1)
    def _():
        lines(by_x, x_x, height - 1, 0)
        lines(by_d, x_d, 0, height + 1)

    @pl.when(odd == 0)
    def _():
        lines(by_d, x_d, height - 1, 0)
        lines(by_x, x_x, 0, height + 1)

    @pl.when(lat == 0)
    def _():
        mine[:, 0] = jnp.zeros_like(mine[:, 0])

    @pl.when(lat == 3)
    def _():
        mine[:, height + 1] = jnp.zeros_like(mine[:, height + 1])


def pair_kernel(pos, one, two, after, both):
    del pos, after
    both[0] = one[...]
    both[1] = two[...]


def lines_kernel(pos, x_own, x_x, x_y, x_d, after, xs, blank):
    del after, blank
    lat = pos[1]
    levels, rows, circle, lanes = xs.shape
    rows, width, span, half = rows - 2, circle // 4, lanes // 4, levels // 2
    height = rows // 4
    many = half * height * width
    xs[:, 0] = jnp.zeros_like(xs[:, 0])
    xs[:, rows + 1] = jnp.zeros_like(xs[:, rows + 1])
    low = lax.broadcasted_iota(jnp.int32, (circle, 2 * span), 1) < span
    for tag, ref in enumerate((x_own, x_x, x_y, x_d)):
        start = (lat ^ tag) * height
        strips = [
            ref.at[pl.ds((4 - at) % 4 * many, many)].reshape(half, height, width, 2 * span) for at in range(4)
        ]

        @pl.loop(0, half * height)
        def _(step, strips=strips, start=start):
            lev, row = step // height, lax.rem(step, height)
            line = jnp.concatenate([s[lev, row] for s in strips], axis=0).astype(jnp.float32)
            turned = pltpu.roll(line, span, 1)
            for upper in range(2):
                same = jnp.where(low, turned, line) if upper else jnp.where(low, line, turned)
                before = pltpu.roll(same, 1, 0)
                after = pltpu.roll(same, circle - 1, 0)
                at = upper * half + lev
                xs[at, 1 + start + row, :, 0 : 2 * span] = jnp.where(low, before, same).astype(xs.dtype)
                xs[at, 1 + start + row, :, 2 * span : 4 * span] = after.astype(xs.dtype)


def turn(gt, slot, core, first, second, levels):
    many, filters = first.shape
    line = many // levels
    for lev in range(levels):
        block = jnp.concatenate([first[lev * line : (lev + 1) * line], second[lev * line : (lev + 1) * line]], axis=0)
        gt[
            lev * filters : (lev + 1) * filters,
            pl.ds(pl.multiple_of((2 * slot + core) * 2 * line, 2 * line), 2 * line),
        ] = block.T


def taps_kernel(pos, xs, g, s, g2, s2, out, gt, acc):
    levels, rows, circle, lanes = xs.shape
    rows, width, span = rows - 2, circle // 4, lanes // 4
    filters = gt.shape[0] // levels
    deep = rows * width
    right = lax.rem(pos[1], 2)
    for core, parts, last in ((pos[0], g, g2), (1 - pos[0], s, s2)):
        for slot, (ref, at) in enumerate(((parts, 0), (parts, 4), (last, 0), (parts, 2))):
            turn(gt, slot, core, ref[at + right], ref[at + 1 - right], levels)
    acc[...] = jnp.zeros_like(acc)

    @pl.loop(0, 3)
    def _(lat_by):
        for lev in range(levels):
            first, last = max(lev - 1, 0), min(lev + 1, levels - 1)
            to = (first - lev + 1) * filters
            many = (last - first + 1) * filters
            total = acc[lat_by, to : to + many, :]
            for place in range(4):
                total += jnp.dot(
                    gt[first * filters : (last + 1) * filters, place * deep : (place + 1) * deep],
                    xs[lev, pl.ds(lat_by, rows), place * width : (place + 1) * width].reshape(deep, lanes),
                    preferred_element_type=jnp.float32,
                )
            acc[lat_by, to : to + many, :] = total

    scale = 1.0 / math.sqrt(levels * rows * circle)
    for lat_by in range(3):
        for lev_at in range(3):
            block = acc[lat_by, lev_at * filters : (lev_at + 1) * filters, :].T * scale
            for lon_at in range(3):
                out[(2 - lev_at) * 9 + lat_by * 3 + lon_at] = block[lon_at * span : (lon_at + 1) * span]


def code_kernel(pos, held, after, out, late, rest):
    del pos, after
    taps, span, filters = held.shape
    most = jnp.abs(held[0])
    for tap in range(1, taps):
        most = jnp.maximum(most, jnp.abs(held[tap]))
    top = jnp.maximum(jnp.max(most, axis=(0, 1), keepdims=True), 1e-30)
    power = jnp.ceil(jnp.log(top) * (1.0 / math.log(2.0))) - 15.0
    unit = jnp.broadcast_to(jnp.exp2(power), (16, filters)).astype(out.dtype).astype(jnp.float32)
    shrink = 1.0 / unit[0:1]
    unit = unit.astype(out.dtype)
    for tap in range(taps):
        value = held[tap] * shrink
        square = value * value
        code = (square * value * jnp.abs(value)).astype(out.dtype)
        for ref, many in ((out, out.shape[0] - 16), (late, late.shape[0] - 16), (rest, rest.shape[0])):
            at = tap * span if ref is out else tap * span - (taps * span - many)
            if 0 <= at < many:
                ref[at : at + span, :] = code
    out[out.shape[0] - 16 :, :] = unit
    late[late.shape[0] - 16 :, :] = unit


def both_kernel(pos, west, east, rest, after, both):
    del pos, after
    size = west.shape[0]
    both[0:size, :] = west[...]
    both[size : 2 * size, :] = east[...]
    both[2 * size :, :] = rest[...]


def join_kernel(pos, west, east, own, x, y, d, after, by_3, by_1, *, cut):
    del pos, after
    size = west.shape[0]
    end = own.shape[0] - 16
    half = by_3.shape[0] - 4 * (cut + 16)
    by_3[0:half, :] = west[0:half, :]
    by_1[0 : size - half, :] = east[half:, :]
    for out, at in ((by_3, half), (by_1, size - half)):
        for piece in (own, x, y, d):
            out[at : at + cut, :] = piece[0:cut, :]
            out[at + cut : at + cut + 16, :] = piece[end:, :]
            at += cut + 16


def across_kernel(pos, by_3, by_1, after, late, early_3, early_1):
    del pos, after
    size, many = late.shape[0], early_3.shape[0]
    half = by_3.shape[0] - 2 * many
    late[0:half, :] = by_3[0:half, :]
    late[half:, :] = by_1[0 : size - half, :]
    early_3[...] = by_3[half : half + many, :]
    early_1[...] = by_1[size - half + many :, :]


def unpack_kernel(pos, *refs, slabs, count, span):
    sources = refs[:count]
    total, token, buffers, sems = refs[-4:]
    slots, group = buffers.shape[:2]
    wide = buffers.shape[-1] // 4
    token[...] = jnp.zeros_like(token)
    parts = []
    for step, first, taps, pieces in slabs:
        for at in range(0, taps, group):
            parts.append((step, first + at, min(group, taps - at), at, pieces))

    def copy(at):
        step, first, many, _, _ = parts[at]
        lon_at = pl.multiple_of(lax.rem(pos[2] + step, 4) * span, span)
        return pltpu.make_async_copy(
            buffers.at[at % slots, pl.ds(0, many)],
            total.at[pl.ds(first, many), pl.ds(lon_at, span)],
            sems.at[at % slots],
        )

    for at, (_, _, many, skip, pieces) in enumerate(parts):
        if at >= slots:
            copy(at - slots).wait()
        for tag, (which, row, (power_in, power_row)) in enumerate(pieces):
            unit = sources[power_in][power_row : power_row + 16, :].astype(jnp.float32)[0:1]
            lanes = pl.ds(pl.multiple_of((pos[1] ^ tag) * wide, wide), wide)
            for tap in range(many):
                start = row + (skip + tap) * span
                code = sources[which][start : start + span, :].astype(jnp.float32)
                root = lax.rsqrt(lax.rsqrt(jnp.abs(code))) * unit
                buffers[at % slots, tap, :, lanes] = jnp.where(code < 0, -root, root)
        copy(at).start()
    for at in range(max(len(parts) - slots, 0), len(parts)):
        copy(at).wait()


def unpack(pos, total, sources, after, slabs, span, name):
    slots, group = 4, 3
    wide = total.shape[2]
    ins = (pos, *sources, *after, total)
    token = jax.ShapeDtypeStruct((8, 128), jnp.float32)
    return pl.pallas_call(
        lambda *refs: unpack_kernel(*refs, slabs=slabs, count=len(sources), span=span),
        out_shape=[jax.ShapeDtypeStruct(total.shape, total.dtype), token],
        in_specs=[pl.BlockSpec(memory_space=SMEM)]
        + [pl.BlockSpec(memory_space=VMEM)] * len(sources)
        + [pl.BlockSpec(memory_space=pl.ANY)] * (len(after) + 1),
        out_specs=[pl.BlockSpec(memory_space=pl.ANY), pl.BlockSpec(memory_space=VMEM)],
        scratch_shapes=[VMEM((slots, group, span, wide), jnp.float32), pltpu.SemaphoreType.DMA((slots,))],
        input_output_aliases={len(ins) - 1: 0},
        cost_estimate=pl.CostEstimate(flops=0, bytes_accessed=4 * 2**20, transcendentals=0),
        compiler_params=pltpu.CompilerParams(vmem_limit_bytes=54 * 1024 * 1024),
        name=name,
    )(*ins)


def field_kernel(pos, after, mine, theirs, w, out, copies, acc):
    del after
    step = pl.program_id(0)
    levels, height, width, chans = out.shape
    many = mine.shape[-1]

    @pl.when(step == 0)
    def _():
        copies[:, 0] = jnp.zeros_like(copies[:, 0])
        copies[:, levels + 1] = jnp.zeros_like(copies[:, levels + 1])
        line_at = lax.broadcasted_iota(jnp.int32, (width, many), 0)
        for which, field in ((pos[0], mine), (1 - pos[0], theirs)):
            lanes = pl.ds(pl.multiple_of(which * many, many), many)
            for lev in range(levels):
                for row in range(height + 2):
                    line = field[lev, row, 0:width].astype(jnp.float32)
                    west = field[lev, row, width : width + 1].astype(jnp.float32)
                    east = field[lev, row, width + 8 : width + 9].astype(jnp.float32)
                    before = jnp.where(line_at == 0, west, pltpu.roll(line, 1, 0))
                    later = jnp.where(line_at == width - 1, east, pltpu.roll(line, width - 1, 0))
                    copies[0, lev + 1, row, :, lanes] = later.astype(copies.dtype)
                    copies[1, lev + 1, row, :, lanes] = field[lev, row, 0:width]
                    copies[2, lev + 1, row, :, lanes] = before.astype(copies.dtype)
        acc[...] = jnp.zeros_like(acc)

    lev_by, lat_by = step // 3, lax.rem(step, 3)
    cells = [
        copies[at, pl.ds(2 - lev_by, levels), pl.ds(2 - lat_by, height)].reshape(
            levels * height * width, 2 * many
        )
        for at in range(3)
    ]
    acc[...] += lax.dot_general(
        jnp.concatenate(cells, axis=1),
        jnp.concatenate([w[at] for at in range(3)], axis=1),
        (((1,), (1,)), ((), ())),
        preferred_element_type=jnp.float32,
    )

    @pl.when(step == 8)
    def _():
        out[...] = acc[...].reshape(out.shape).astype(out.dtype)


def blocked_body(inputs, weights, out_grad):
    chans, levels, height, width = inputs.shape
    filters = weights.shape[2]
    bf16, f32 = jnp.bfloat16, jnp.float32
    lat, lon = lax.axis_index("lat"), lax.axis_index("lon")
    pos = jnp.stack([lax.axis_index("ch"), lat, lon]).astype(jnp.int32)
    x_cells = jnp.transpose(inputs, (1, 2, 3, 0))
    g_cells = jnp.transpose(out_grad, (1, 2, 3, 0))
    taps = jnp.transpose(weights, (1, 0, 2))
    cells = levels * height * width
    span, wide = chans // 4, filters // 4
    rows, circle = 4 * height, 4 * width
    edge = levels * height

    to_same = lambda c, a, o: (a // 2, 2 * c + a % 2, o)
    to_other = lambda c, a, o: (a // 2, 2 * c + 1 - a % 2, o)
    many = cells // 2
    block = jax.ShapeDtypeStruct((cells, wide), bf16)
    strip = jax.ShapeDtypeStruct((2 * levels * width, 2 * span), bf16)
    g_same, g_other, x0, x1, x2, x3, rim_x, rim_d = call(
        pack_kernel,
        [block, block]
        + [jax.ShapeDtypeStruct((many + extra, 2 * span), bf16) for extra in (0, 2 * edge, 0, 2 * edge)]
        + [strip, strip],
        (pos, x_cells, g_cells),
        [VMEM((4, many, 2 * span), bf16)],
        0,
        "pack",
        16,
    )
    g_s = move(g_same, to_same)
    g_o = move(g_other, to_other)
    x_r1 = move(x1, lon_by(1))
    x_r3 = move(x3, lon_by(-1))
    x_r2 = move(x2, lon_by(2))
    by_x = move(rim_x, lat_xor(1))
    by_d = move(rim_d, lat_xor(3))

    inner = 4 * many
    (g0,) = call(
        pair_kernel, [jax.ShapeDtypeStruct((2, cells, wide), bf16)], (pos, g_s, g_o, x0), [], 0, "pair_0", 16, held=1
    )
    x_own, x_own_y = call(
        spread_kernel,
        [jax.ShapeDtypeStruct((count, 2 * span), bf16) for count in (inner + 4 * edge, inner)],
        (pos, x0, x_r1, x_r2, x_r3),
        [],
        0,
        "spread",
        16,
    )
    x_x = move(x_own, lat_xor(1))
    x_d = move(x_own, lat_xor(3))
    x_y = move(x_own_y, lat_xor(2))
    g1 = move(g0, lon_by(1))
    g3 = move(g0, lon_by(-1))
    far_a, far_b, g_near, mine = call(
        split_kernel,
        [
            block,
            block,
            jax.ShapeDtypeStruct((6, cells, wide), bf16),
            jax.ShapeDtypeStruct((levels, height + 2, width + 16, chans), bf16),
        ],
        (pos, g0, g1, g3, g_cells, x_own, x_x, x_d, by_x, by_d, x_y),
        [],
        0,
        "split",
        16,
        held=1,
    )
    g2a = move(far_a, lon_by(1))
    g2b = move(far_b, lon_by(-1))
    s_near = move(g_near, sibling)
    theirs = move(mine, sibling)
    xs, total = pl.pallas_call(
        lines_kernel,
        out_shape=[
            jax.ShapeDtypeStruct((levels, rows + 2, circle, 4 * span), bf16),
            jax.ShapeDtypeStruct((27, chans, filters), f32),
        ],
        in_specs=[pl.BlockSpec(memory_space=SMEM)]
        + [pl.BlockSpec(memory_space=VMEM)] * 4
        + [pl.BlockSpec(memory_space=pl.ANY)],
        out_specs=[pl.BlockSpec(memory_space=VMEM)] + [pl.BlockSpec(memory_space=pl.ANY)],
        cost_estimate=pl.CostEstimate(flops=0, bytes_accessed=2**20, transcendentals=0),
        compiler_params=pltpu.CompilerParams(vmem_limit_bytes=24 * 1024 * 1024),
        name="lines",
    )(pos, x_own, x_x, x_y, x_d, far_a)
    (g2,) = call(
        pair_kernel, [jax.ShapeDtypeStruct((2, cells, wide), bf16)], (pos, g2a, g2b, xs), [], 0, "pair", 16, held=1
    )
    s2 = move(g2, sibling)
    early, middle = 9, 17
    cut, end = early * span, 27 * span
    size = end + 16 - cut
    half = size // 32 * 16
    first_rows = cut + 16
    own_rows = middle * span + 16
    slab = lambda count: jax.ShapeDtypeStruct((count, wide), bf16)
    (grads,) = call(
        taps_kernel,
        [jax.ShapeDtypeStruct((27, span, wide), f32)],
        (pos, xs, g_near, s_near, g2, s2),
        [VMEM((levels * wide, rows * circle), bf16), VMEM((3, 3 * wide, 4 * span), f32)],
        2 * 27 * span * wide * rows * circle * levels,
        "taps",
        28,
    )
    own, late, rest = call(
        code_kernel,
        [slab(own_rows), slab(size), slab(end - middle * span)],
        (pos, grads, theirs),
        [],
        0,
        "code",
        16,
        held=1,
    )

    whole = lambda t: (0, 0, 0, 0)
    field = pl.pallas_call(
        field_kernel,
        out_shape=jax.ShapeDtypeStruct((levels, height, width, chans), bf16),
        grid=(9,),
        in_specs=[
            pl.BlockSpec(memory_space=SMEM),
            pl.BlockSpec(memory_space=pl.ANY),
            pl.BlockSpec(mine.shape, whole),
            pl.BlockSpec(mine.shape, whole),
            pl.BlockSpec((3, chans, filters), lambda t: (t, 0, 0)),
        ],
        out_specs=pl.BlockSpec((levels, height, width, chans), whole),
        scratch_shapes=[
            VMEM((3, levels + 2, height + 2, width, filters), bf16),
            VMEM((cells, chans), f32),
        ],
        cost_estimate=pl.CostEstimate(
            flops=4 * 27 * chans * filters * cells, bytes_accessed=27 * chans * filters * 2, transcendentals=0
        ),
        compiler_params=pltpu.CompilerParams(vmem_limit_bytes=52 * 1024 * 1024),
        name="field",
    )(pos, own, mine, theirs, taps)

    def to_plane(share):
        return [move(share, lat_xor(tag)) for tag in (1, 2, 3)]

    from_3 = move(late, lon_by(1))
    from_1 = move(late, lon_by(-1))
    plane = [own] + to_plane(own)
    (pair,) = call(
        both_kernel,
        [slab(2 * size + end - middle * span)],
        (pos, from_3, from_1, rest, field),
        [],
        0,
        "both",
        16,
        held=1,
    )
    z_3, z_1 = call(
        lambda *refs: join_kernel(*refs, cut=cut),
        [slab(half + 4 * first_rows), slab(size - half + 4 * first_rows)],
        (pos, from_3, from_1, *plane, pair),
        [],
        0,
        "join",
        16,
        held=1,
    )
    both = to_plane(pair)
    by_3 = move(z_3, lon_by(1))
    by_1 = move(z_1, lon_by(-1))
    def late_piece(which, row=0):
        return (which, row, (which, row + size - 16))

    def early_piece(which, row):
        return (which, row, (which, row + cut))

    slabs = [(0, 0, middle, [(tag, 0, (tag, own_rows - 16)) for tag in range(4)])]
    total, token = unpack(pos, total, plane, [pair], slabs, span, "unpack_1")
    from_2, early_3, early_1 = call(
        across_kernel,
        [slab(size), slab(2 * first_rows), slab(2 * first_rows)],
        (pos, by_3, by_1, token),
        [],
        0,
        "across",
        16,
        held=1,
    )
    across = to_plane(from_2)
    early_2a = move(early_3, lon_by(1))
    early_2b = move(early_1, lon_by(-1))

    unit = own_rows - 16
    slabs = [
        (3, early, 27 - early, [late_piece(5)] + [late_piece(at) for at in range(3)]),
        (1, early, 27 - early, [late_piece(6)] + [late_piece(at, size) for at in range(3)]),
        (0, middle, 27 - middle, [(7, 0, (8, unit))] + [(at, 2 * size, (9 + at, unit)) for at in range(3)]),
        (3, 0, early, [early_piece(3, half + tag * first_rows) for tag in range(4)]),
        (1, 0, early, [early_piece(4, size - half + tag * first_rows) for tag in range(4)]),
    ]
    total, _ = unpack(
        pos, total, both + [by_3, by_1, from_3, from_1, rest] + plane, [from_2], slabs, span, "unpack_2"
    )
    slabs = [
        (2, 0, early, [early_piece(tag // 2, tag % 2 * first_rows) for tag in range(4)]),
        (2, early, 27 - early, [late_piece(2 + tag) for tag in range(4)]),
    ]
    total, _ = unpack(pos, total, [early_2a, early_2b, from_2] + across, [], slabs, span, "unpack_3")
    return (jnp.transpose(field, (3, 0, 1, 2)), jnp.transpose(total, (1, 0, 2)))


def body(inputs, weights, out_grad):
    chans, levels, height, width = inputs.shape
    shape = tuple(lax.axis_size(axis) for axis in AXES)
    fits = (
        shape == (2, 4, 4)
        and chans == out_grad.shape[0] == 256
        and weights.shape[2] == 512
        and levels % 2 == 0
        and height % 2 == 0
        and width % 16 == 0
    )
    return (blocked_body if fits else plain_body)(inputs, weights, out_grad)


def solution(mesh):
    in_specs = (P("ch", None, "lat", "lon"), P("ch", None, None), P("ch", None, "lat", "lon"))
    out_specs = (P("ch", None, "lat", "lon"), P("ch", None, None))
    return jax.shard_map(body, mesh=mesh, in_specs=in_specs, out_specs=out_specs, check_vma=False)
```

```python
import math

import jax
import jax.numpy as jnp
from jax import lax
from jax.experimental import pallas as pl
from jax.experimental.pallas import tpu as pltpu
from jax.sharding import PartitionSpec as P

VMEM = pltpu.VMEM
SMEM = pltpu.SMEM
AXES = ("ch", "lat", "lon")


def padded_2(cells, sides, width):
    for axis, dim in sides:
        count = lax.axis_size(axis)
        head = lax.slice_in_dim(cells, 0, width, axis=dim)
        tail = lax.slice_in_dim(cells, cells.shape[dim] - width, cells.shape[dim], axis=dim)
        cells = jnp.concatenate(
            [
                lax.ppermute(tail, axis, [(i, (i + 1) % count) for i in range(count)]),
                cells,
                lax.ppermute(head, axis, [((i + 1) % count, i) for i in range(count)]),
            ],
            axis=dim,
        )
    return cells


def mask_rims(padded):
    count = lax.axis_size("lat")
    where_lat = lax.axis_index("lat")
    lines = jnp.arange(padded.shape[2])
    drop = (lines == 0) & (where_lat == 0) | (lines == padded.shape[2] - 1) & (
        where_lat == count - 1
    )
    return jnp.where(drop[None, None, :, None], jnp.zeros((), padded.dtype), padded)


def pad_levels(field):
    return jnp.pad(field, ((0, 0), (1, 1), (0, 0), (0, 0)))


def plain_body(inputs, weights, out_grad):
    chans, levels, height, width = inputs.shape
    input_pad = pad_levels(mask_rims(padded_2(inputs, (("lat", 2), ("lon", 3)), 1)))
    grad_inner = lax.all_gather(out_grad, "ch", axis=0, tiled=True)
    grad_pad = pad_levels(mask_rims(padded_2(grad_inner, (("lat", 2), ("lon", 3)), 1)))
    filters = grad_pad.shape[0]
    products = jnp.dot(
        weights.reshape(chans * 27, filters),
        grad_pad.reshape(filters, -1),
        preferred_element_type=jnp.float32,
    )
    products = products.reshape((chans, 27) + tuple(grad_pad.shape[1:]))
    total = jnp.zeros((chans, levels, height, width), jnp.float32)
    pieces = []
    for tap in range(27):
        lev, lat, lon = tap // 9 - 1, tap // 3 % 3 - 1, tap % 3 - 1
        total = (
            total
            + products[
                :,
                tap,
                1 - lev : 1 - lev + levels,
                1 - lat : 1 - lat + height,
                1 - lon : 1 - lon + width,
            ]
        )
        pieces.append(
            input_pad[
                :,
                1 + lev : 1 + lev + levels,
                1 + lat : 1 + lat + height,
                1 + lon : 1 + lon + width,
            ]
        )
    columns = jnp.stack(pieces, axis=1).reshape(chans * 27, -1)
    partial_grad = lax.dot_general(
        columns,
        grad_inner.reshape(filters, -1),
        (((1,), (1,)), ((), ())),
        preferred_element_type=jnp.float32,
    )
    summed = lax.psum(partial_grad, ("lat", "lon"))
    cells = levels * height * width * lax.axis_size("lat") * lax.axis_size("lon")
    weight_grad = (summed * (1.0 / math.sqrt(cells))).reshape(chans, 27, filters)
    return (total.astype(jnp.bfloat16), weight_grad)


def move(x, target):
    pairs = []
    for i in range(32):
        to = target(i // 16, i // 4 % 4, i % 4)
        if to is not None:
            pairs.append((i, (to[0] * 4 + to[1]) * 4 + to[2]))
    return lax.ppermute(x, AXES, pairs)


def lon_by(step):
    return lambda c, a, o: (c, a, (o + step) % 4)


def lat_xor(mask):
    return lambda c, a, o: (c, a ^ mask, o)


def sibling(c, a, o):
    return (1 - c, a, o)


def call(kernel, outs, ins, scratch, flops, name, limit, held=0):
    read = len(ins) - 1 - held
    moved = sum(math.prod(x.shape) * x.dtype.itemsize for x in list(ins[1 : 1 + read]) + list(outs))
    return pl.pallas_call(
        kernel,
        out_shape=outs,
        in_specs=[pl.BlockSpec(memory_space=SMEM)]
        + [pl.BlockSpec(memory_space=VMEM)] * read
        + [pl.BlockSpec(memory_space=pl.ANY)] * held,
        out_specs=[pl.BlockSpec(memory_space=VMEM)] * len(outs),
        scratch_shapes=scratch,
        cost_estimate=pl.CostEstimate(flops=flops, bytes_accessed=moved, transcendentals=0),
        compiler_params=pltpu.CompilerParams(vmem_limit_bytes=limit * 1024 * 1024),
        name=name,
    )(*ins)


def pack_kernel(pos, x, g, g_same, g_other, x0, x1, x2, x3, rim_x, rim_d, held):
    levels, height, width, chans = x.shape
    half, wide = levels // 2, chans // 2
    right = lax.rem(pos[1], 2)
    for out, at in ((g_same, right), (g_other, 1 - right)):
        out[...] = g[:, :, :, pl.ds(pl.multiple_of(at * wide, wide), wide)].reshape(out.shape)
    many = x0.shape[0]
    for block in range(4):
        at = block * (chans // 4)
        lo = x[0:half, :, :, at : at + chans // 4]
        hi = x[half:levels, :, :, at : at + chans // 4]
        held[block] = jnp.concatenate([lo, hi], axis=-1).reshape(held.shape[1:])
    lon = pos[2]
    for step, out in enumerate((x0, x1, x2, x3)):
        out[0:many, :] = held[lax.rem(lon + step, 4)]
    for out, column in ((x1, width - 1), (x3, 0)):
        rim = g[:, :, column, :].reshape(levels * height, chans)
        out[many : many + levels * height, :] = rim[:, 0:wide]
        out[many + levels * height :, :] = rim[:, wide:]
    even = right == 0
    low, high = g[:, 0], g[:, height - 1]
    line = levels * width
    for out, upward in ((rim_x, even), (rim_d, jnp.logical_not(even))):
        facing = jnp.where(upward, high, low).reshape(line, chans)
        for at in range(2):
            out[at * line : (at + 1) * line, :] = facing[:, at * wide : (at + 1) * wide]


def spread_kernel(pos, x0, x1, x2, x3, own, own_y):
    del pos
    many = x0.shape[0]
    for at, piece in enumerate((x0, x1, x2, x3)):
        own[at * many : (at + 1) * many, :] = piece[0:many, :]
        own_y[at * many : (at + 1) * many, :] = piece[0:many, :]
    extra = x1.shape[0] - many
    own[4 * many : 4 * many + extra, :] = x1[many:, :]
    own[4 * many + extra :, :] = x3[many:, :]


def split_kernel(
    pos, here, west, east, g, own, x_x, x_d, by_x, by_d, after, first, second, near, mine
):
    del after
    first[...] = west[0]
    second[...] = east[1]
    for at, part in enumerate((here, west, east)):
        near[2 * at : 2 * at + 2] = part[...]

    levels, height, width, chans = g.shape
    edge, line, wide = levels * height, levels * width, chans // 2
    inner = own.shape[0] - 4 * edge
    mine[:, 1 : height + 1, 0:width, :] = g[...]

    def columns(message, rows):
        for side in range(2):
            for half in range(2):
                start = inner + (2 * side + half) * edge
                rim = message[start : start + edge, :].reshape(levels, height, wide)
                at = width + 8 * side
                for row, to in rows:
                    mine[:, to, at : at + 8, half * wide : (half + 1) * wide] = jnp.broadcast_to(
                        rim[:, row : row + 1], (levels, 8, wide)
                    )

    columns(own, [(row, row + 1) for row in range(height)])

    def lines(strip, message, row, to):
        for half in range(2):
            part = strip[half * line : (half + 1) * line, :]
            mine[:, to, 0:width, half * wide : (half + 1) * wide] = part.reshape(levels, width, wide)
        columns(message, [(row, to)])

    lat = pos[1]
    odd = lax.rem(lat, 2)

    @pl.when(odd == 1)
    def _():
        lines(by_x, x_x, height - 1, 0)
        lines(by_d, x_d, 0, height + 1)

    @pl.when(odd == 0)
    def _():
        lines(by_d, x_d, height - 1, 0)
        lines(by_x, x_x, 0, height + 1)

    @pl.when(lat == 0)
    def _():
        mine[:, 0] = jnp.zeros_like(mine[:, 0])

    @pl.when(lat == 3)
    def _():
        mine[:, height + 1] = jnp.zeros_like(mine[:, height + 1])


def pair_kernel(pos, one, two, after, both):
    del pos, after
    both[0] = one[...]
    both[1] = two[...]


def lines_kernel(pos, x_own, x_x, x_y, x_d, after, xs, blank):
    del after, blank
    lat = pos[1]
    levels, rows, circle, lanes = xs.shape
    rows, width, span, half = rows - 2, circle // 4, lanes // 4, levels // 2
    height = rows // 4
    many = half * height * width
    xs[:, 0] = jnp.zeros_like(xs[:, 0])
    xs[:, rows + 1] = jnp.zeros_like(xs[:, rows + 1])
    low = lax.broadcasted_iota(jnp.int32, (circle, 2 * span), 1) < span
    for tag, ref in enumerate((x_own, x_x, x_y, x_d)):
        start = (lat ^ tag) * height
        strips = [
            ref.at[pl.ds((4 - at) % 4 * many, many)].reshape(half, height, width, 2 * span) for at in range(4)
        ]

        @pl.loop(0, half * height)
        def _(step, strips=strips, start=start):
            lev, row = step // height, lax.rem(step, height)
            line = jnp.concatenate([s[lev, row] for s in strips], axis=0).astype(jnp.float32)
            turned = pltpu.roll(line, span, 1)
            for upper in range(2):
                same = jnp.where(low, turned, line) if upper else jnp.where(low, line, turned)
                before = pltpu.roll(same, 1, 0)
                after = pltpu.roll(same, circle - 1, 0)
                at = upper * half + lev
                xs[at, 1 + start + row, :, 0 : 2 * span] = jnp.where(low, before, same).astype(xs.dtype)
                xs[at, 1 + start + row, :, 2 * span : 4 * span] = after.astype(xs.dtype)


def turn(gt, slot, core, first, second, levels):
    many, filters = first.shape
    line = many // levels
    for lev in range(levels):
        block = jnp.concatenate([first[lev * line : (lev + 1) * line], second[lev * line : (lev + 1) * line]], axis=0)
        gt[
            lev * filters : (lev + 1) * filters,
            pl.ds(pl.multiple_of((2 * slot + core) * 2 * line, 2 * line), 2 * line),
        ] = block.T


def taps_kernel(pos, xs, g, s, g2, s2, out, gt, acc):
    levels, rows, circle, lanes = xs.shape
    rows, width, span = rows - 2, circle // 4, lanes // 4
    filters = gt.shape[0] // levels
    deep = rows * width
    right = lax.rem(pos[1], 2)
    for core, parts, last in ((pos[0], g, g2), (1 - pos[0], s, s2)):
        for slot, (ref, at) in enumerate(((parts, 0), (parts, 4), (last, 0), (parts, 2))):
            turn(gt, slot, core, ref[at + right], ref[at + 1 - right], levels)
    acc[...] = jnp.zeros_like(acc)

    @pl.loop(0, 3)
    def _(lat_by):
        for lev in range(levels):
            first, last = max(lev - 1, 0), min(lev + 1, levels - 1)
            to = (first - lev + 1) * filters
            many = (last - first + 1) * filters
            total = acc[lat_by, to : to + many, :]
            for place in range(4):
                total += jnp.dot(
                    gt[first * filters : (last + 1) * filters, place * deep : (place + 1) * deep],
                    xs[lev, pl.ds(lat_by, rows), place * width : (place + 1) * width].reshape(deep, lanes),
                    preferred_element_type=jnp.float32,
                )
            acc[lat_by, to : to + many, :] = total

    scale = 1.0 / math.sqrt(levels * rows * circle)
    for lat_by in range(3):
        for lev_at in range(3):
            block = acc[lat_by, lev_at * filters : (lev_at + 1) * filters, :].T * scale
            for lon_at in range(3):
                out[(2 - lev_at) * 9 + lat_by * 3 + lon_at] = block[lon_at * span : (lon_at + 1) * span]


def code_kernel(pos, held, after, out, late, rest):
    del pos, after
    taps, span, filters = held.shape
    most = jnp.abs(held[0])
    for tap in range(1, taps):
        most = jnp.maximum(most, jnp.abs(held[tap]))
    top = jnp.maximum(jnp.max(most, axis=(0, 1), keepdims=True), 1e-30)
    power = jnp.ceil(jnp.log(top) * (1.0 / math.log(2.0))) - 15.0
    unit = jnp.broadcast_to(jnp.exp2(power), (16, filters)).astype(out.dtype).astype(jnp.float32)
    shrink = 1.0 / unit[0:1]
    unit = unit.astype(out.dtype)
    for tap in range(taps):
        value = held[tap] * shrink
        square = value * value
        code = (square * value * jnp.abs(value)).astype(out.dtype)
        for ref, many in ((out, out.shape[0] - 16), (late, late.shape[0] - 16), (rest, rest.shape[0])):
            at = tap * span if ref is out else tap * span - (taps * span - many)
            if 0 <= at < many:
                ref[at : at + span, :] = code
    out[out.shape[0] - 16 :, :] = unit
    late[late.shape[0] - 16 :, :] = unit


def both_kernel(pos, west, east, rest, after, both, half_3, half_1):
    del pos, after
    size, half = west.shape[0], half_3.shape[0]
    both[0:size, :] = west[...]
    both[size : 2 * size, :] = east[...]
    both[2 * size :, :] = rest[...]
    half_3[...] = west[0:half, :]
    half_1[...] = east[half:, :]


def across_kernel(pos, half_3, half_1, own, x, y, d, late, block):
    del pos
    half = half_3.shape[0]
    late[0:half, :] = half_3[...]
    late[half:, :] = half_1[...]
    end = own.shape[0] - 16
    rows = block.shape[0] // 4
    for at, piece in enumerate((own, x, y, d)):
        block[at * rows : (at + 1) * rows - 16, :] = piece[0 : rows - 16, :]
        block[(at + 1) * rows - 16 : (at + 1) * rows, :] = piece[end:, :]


def hand_kernel(pos, block_3, block_1, after, first, second):
    del pos, after
    many = first.shape[0]
    first[...] = block_3[0:many, :]
    second[...] = block_1[many:, :]


def unpack_kernel(pos, *refs, slabs, count, span):
    sources = refs[:count]
    total, token, buffers, sems = refs[-4:]
    slots, group = buffers.shape[:2]
    wide = buffers.shape[-1] // 4
    token[...] = jnp.zeros_like(token)
    parts = []
    for step, first, taps, pieces in slabs:
        for at in range(0, taps, group):
            parts.append((step, first + at, min(group, taps - at), at, pieces))

    def copy(at):
        step, first, many, _, _ = parts[at]
        lon_at = pl.multiple_of(lax.rem(pos[2] + step, 4) * span, span)
        return pltpu.make_async_copy(
            buffers.at[at % slots, pl.ds(0, many)],
            total.at[pl.ds(first, many), pl.ds(lon_at, span)],
            sems.at[at % slots],
        )

    for at, (_, _, many, skip, pieces) in enumerate(parts):
        if at >= slots:
            copy(at - slots).wait()
        for tag, (which, row, (power_in, power_row)) in enumerate(pieces):
            unit = sources[power_in][power_row : power_row + 16, :].astype(jnp.float32)[0:1]
            lanes = pl.ds(pl.multiple_of((pos[1] ^ tag) * wide, wide), wide)
            for tap in range(many):
                start = row + (skip + tap) * span
                code = sources[which][start : start + span, :].astype(jnp.float32)
                root = lax.rsqrt(lax.rsqrt(jnp.abs(code))) * unit
                buffers[at % slots, tap, :, lanes] = jnp.where(code < 0, -root, root)
        copy(at).start()
    for at in range(max(len(parts) - slots, 0), len(parts)):
        copy(at).wait()


def unpack(pos, total, sources, after, slabs, span, name):
    slots, group = 4, 3
    wide = total.shape[2]
    ins = (pos, *sources, *after, total)
    token = jax.ShapeDtypeStruct((8, 128), jnp.float32)
    return pl.pallas_call(
        lambda *refs: unpack_kernel(*refs, slabs=slabs, count=len(sources), span=span),
        out_shape=[jax.ShapeDtypeStruct(total.shape, total.dtype), token],
        in_specs=[pl.BlockSpec(memory_space=SMEM)]
        + [pl.BlockSpec(memory_space=VMEM)] * len(sources)
        + [pl.BlockSpec(memory_space=pl.ANY)] * (len(after) + 1),
        out_specs=[pl.BlockSpec(memory_space=pl.ANY), pl.BlockSpec(memory_space=VMEM)],
        scratch_shapes=[VMEM((slots, group, span, wide), jnp.float32), pltpu.SemaphoreType.DMA((slots,))],
        input_output_aliases={len(ins) - 1: 0},
        cost_estimate=pl.CostEstimate(flops=0, bytes_accessed=4 * 2**20, transcendentals=0),
        compiler_params=pltpu.CompilerParams(vmem_limit_bytes=51 * 1024 * 1024),
        name=name,
    )(*ins)


def field_kernel(pos, after, mine, theirs, w, out, copies, acc):
    del after
    step = pl.program_id(0)
    levels, height, width, chans = out.shape
    many = mine.shape[-1]

    @pl.when(step == 0)
    def _():
        copies[:, 0] = jnp.zeros_like(copies[:, 0])
        copies[:, levels + 1] = jnp.zeros_like(copies[:, levels + 1])
        line_at = lax.broadcasted_iota(jnp.int32, (width, many), 0)
        for which, field in ((pos[0], mine), (1 - pos[0], theirs)):
            lanes = pl.ds(pl.multiple_of(which * many, many), many)
            for lev in range(levels):
                for row in range(height + 2):
                    line = field[lev, row, 0:width].astype(jnp.float32)
                    west = field[lev, row, width : width + 1].astype(jnp.float32)
                    east = field[lev, row, width + 8 : width + 9].astype(jnp.float32)
                    before = jnp.where(line_at == 0, west, pltpu.roll(line, 1, 0))
                    later = jnp.where(line_at == width - 1, east, pltpu.roll(line, width - 1, 0))
                    copies[0, lev + 1, row, :, lanes] = later.astype(copies.dtype)
                    copies[1, lev + 1, row, :, lanes] = field[lev, row, 0:width]
                    copies[2, lev + 1, row, :, lanes] = before.astype(copies.dtype)
        acc[...] = jnp.zeros_like(acc)

    lev_by, lat_by = step // 3, lax.rem(step, 3)
    cells = [
        copies[at, pl.ds(2 - lev_by, levels), pl.ds(2 - lat_by, height)].reshape(
            levels * height * width, 2 * many
        )
        for at in range(3)
    ]
    acc[...] += lax.dot_general(
        jnp.concatenate(cells, axis=1),
        jnp.concatenate([w[at] for at in range(3)], axis=1),
        (((1,), (1,)), ((), ())),
        preferred_element_type=jnp.float32,
    )

    @pl.when(step == 8)
    def _():
        out[...] = acc[...].reshape(out.shape).astype(out.dtype)


def blocked_body(inputs, weights, out_grad):
    chans, levels, height, width = inputs.shape
    filters = weights.shape[2]
    bf16, f32 = jnp.bfloat16, jnp.float32
    lat, lon = lax.axis_index("lat"), lax.axis_index("lon")
    pos = jnp.stack([lax.axis_index("ch"), lat, lon]).astype(jnp.int32)
    x_cells = jnp.transpose(inputs, (1, 2, 3, 0))
    g_cells = jnp.transpose(out_grad, (1, 2, 3, 0))
    taps = jnp.transpose(weights, (1, 0, 2))
    cells = levels * height * width
    span, wide = chans // 4, filters // 4
    rows, circle = 4 * height, 4 * width
    edge = levels * height

    to_same = lambda c, a, o: (a // 2, 2 * c + a % 2, o)
    to_other = lambda c, a, o: (a // 2, 2 * c + 1 - a % 2, o)
    many = cells // 2
    block = jax.ShapeDtypeStruct((cells, wide), bf16)
    strip = jax.ShapeDtypeStruct((2 * levels * width, 2 * span), bf16)
    g_same, g_other, x0, x1, x2, x3, rim_x, rim_d = call(
        pack_kernel,
        [block, block]
        + [jax.ShapeDtypeStruct((many + extra, 2 * span), bf16) for extra in (0, 2 * edge, 0, 2 * edge)]
        + [strip, strip],
        (pos, x_cells, g_cells),
        [VMEM((4, many, 2 * span), bf16)],
        0,
        "pack",
        16,
    )
    g_s = move(g_same, to_same)
    g_o = move(g_other, to_other)
    x_r1 = move(x1, lon_by(1))
    x_r3 = move(x3, lon_by(-1))
    x_r2 = move(x2, lon_by(2))
    by_x = move(rim_x, lat_xor(1))
    by_d = move(rim_d, lat_xor(3))

    inner = 4 * many
    (g0,) = call(
        pair_kernel, [jax.ShapeDtypeStruct((2, cells, wide), bf16)], (pos, g_s, g_o, x0), [], 0, "pair_0", 16, held=1
    )
    x_own, x_own_y = call(
        spread_kernel,
        [jax.ShapeDtypeStruct((count, 2 * span), bf16) for count in (inner + 4 * edge, inner)],
        (pos, x0, x_r1, x_r2, x_r3),
        [],
        0,
        "spread",
        16,
    )
    x_x = move(x_own, lat_xor(1))
    x_d = move(x_own, lat_xor(3))
    x_y = move(x_own_y, lat_xor(2))
    g1 = move(g0, lon_by(1))
    g3 = move(g0, lon_by(-1))
    far_a, far_b, g_near, mine = call(
        split_kernel,
        [
            block,
            block,
            jax.ShapeDtypeStruct((6, cells, wide), bf16),
            jax.ShapeDtypeStruct((levels, height + 2, width + 16, chans), bf16),
        ],
        (pos, g0, g1, g3, g_cells, x_own, x_x, x_d, by_x, by_d, x_y),
        [],
        0,
        "split",
        16,
        held=1,
    )
    g2a = move(far_a, lon_by(1))
    g2b = move(far_b, lon_by(-1))
    s_near = move(g_near, sibling)
    theirs = move(mine, sibling)
    xs, total = pl.pallas_call(
        lines_kernel,
        out_shape=[
            jax.ShapeDtypeStruct((levels, rows + 2, circle, 4 * span), bf16),
            jax.ShapeDtypeStruct((27, chans, filters), f32),
        ],
        in_specs=[pl.BlockSpec(memory_space=SMEM)]
        + [pl.BlockSpec(memory_space=VMEM)] * 4
        + [pl.BlockSpec(memory_space=pl.ANY)],
        out_specs=[pl.BlockSpec(memory_space=VMEM)] + [pl.BlockSpec(memory_space=pl.ANY)],
        cost_estimate=pl.CostEstimate(flops=0, bytes_accessed=2**20, transcendentals=0),
        compiler_params=pltpu.CompilerParams(vmem_limit_bytes=24 * 1024 * 1024),
        name="lines",
    )(pos, x_own, x_x, x_y, x_d, far_a)
    (g2,) = call(
        pair_kernel, [jax.ShapeDtypeStruct((2, cells, wide), bf16)], (pos, g2a, g2b, xs), [], 0, "pair", 16, held=1
    )
    s2 = move(g2, sibling)
    early, middle = 7, 19
    cut, end = early * span, 27 * span
    size = end + 16 - cut
    half = size // 32 * 16
    first_rows = cut + 16
    own_rows = middle * span + 16
    slab = lambda count: jax.ShapeDtypeStruct((count, wide), bf16)
    (grads,) = call(
        taps_kernel,
        [jax.ShapeDtypeStruct((27, span, wide), f32)],
        (pos, xs, g_near, s_near, g2, s2),
        [VMEM((levels * wide, rows * circle), bf16), VMEM((3, 3 * wide, 4 * span), f32)],
        2 * 27 * span * wide * rows * circle * levels,
        "taps",
        28,
    )
    own, late, rest = call(
        code_kernel,
        [slab(own_rows), slab(size), slab(end - middle * span)],
        (pos, grads, theirs),
        [],
        0,
        "code",
        16,
        held=1,
    )

    whole = lambda t: (0, 0, 0, 0)
    field = pl.pallas_call(
        field_kernel,
        out_shape=jax.ShapeDtypeStruct((levels, height, width, chans), bf16),
        grid=(9,),
        in_specs=[
            pl.BlockSpec(memory_space=SMEM),
            pl.BlockSpec(memory_space=pl.ANY),
            pl.BlockSpec(mine.shape, whole),
            pl.BlockSpec(mine.shape, whole),
            pl.BlockSpec((3, chans, filters), lambda t: (t, 0, 0)),
        ],
        out_specs=pl.BlockSpec((levels, height, width, chans), whole),
        scratch_shapes=[
            VMEM((3, levels + 2, height + 2, width, filters), bf16),
            VMEM((cells, chans), f32),
        ],
        cost_estimate=pl.CostEstimate(
            flops=4 * 27 * chans * filters * cells, bytes_accessed=27 * chans * filters * 2, transcendentals=0
        ),
        compiler_params=pltpu.CompilerParams(vmem_limit_bytes=20 * 1024 * 1024),
        name="field",
    )(pos, own, mine, theirs, taps)

    def to_plane(share):
        return [move(share, lat_xor(tag)) for tag in (1, 2, 3)]

    from_3 = move(late, lon_by(1))
    from_1 = move(late, lon_by(-1))
    plane = [own] + to_plane(own)
    pair, half_3, half_1 = call(
        both_kernel,
        [slab(2 * size + end - middle * span), slab(half), slab(size - half)],
        (pos, from_3, from_1, rest, field),
        [],
        0,
        "both",
        16,
        held=1,
    )
    half_3 = move(half_3, lon_by(1))
    half_1 = move(half_1, lon_by(-1))
    both = to_plane(pair)
    from_2, block = call(
        across_kernel, [slab(size), slab(4 * first_rows)], (pos, half_3, half_1, *plane), [], 0, "across", 16
    )
    early_3 = move(block, lon_by(1))
    early_1 = move(block, lon_by(-1))
    across = to_plane(from_2)

    def late_piece(which, row=0):
        return (which, row, (which, row + size - 16))

    def early_piece(which, row):
        return (which, row, (which, row + cut))

    slabs = [(0, 0, middle, [(tag, 0, (tag, own_rows - 16)) for tag in range(4)])]
    total, token = unpack(pos, total, plane, [block], slabs, span, "unpack_1")
    hand_3, hand_1 = call(
        hand_kernel, [slab(2 * first_rows)] * 2, (pos, early_3, early_1, token), [], 0, "hand", 16, held=1
    )
    early_2a = move(hand_3, lon_by(1))
    early_2b = move(hand_1, lon_by(-1))
    unit = own_rows - 16
    slabs = [
        (3, early, 27 - early, [late_piece(5)] + [late_piece(at) for at in range(3)]),
        (1, early, 27 - early, [late_piece(6)] + [late_piece(at, size) for at in range(3)]),
        (0, middle, 27 - middle, [(7, 0, (8, unit))] + [(at, 2 * size, (9 + at, unit)) for at in range(3)]),
        (3, 0, early, [early_piece(3, tag * first_rows) for tag in range(4)]),
        (1, 0, early, [early_piece(4, tag * first_rows) for tag in range(4)]),
    ]
    total, _ = unpack(
        pos, total, both + [early_3, early_1, from_3, from_1, rest] + plane, [hand_3], slabs, span, "unpack_2"
    )
    slabs = [
        (2, 0, early, [early_piece(tag // 2, tag % 2 * first_rows) for tag in range(4)]),
        (2, early, 27 - early, [late_piece(2 + tag) for tag in range(4)]),
    ]
    total, _ = unpack(pos, total, [early_2a, early_2b, from_2] + across, [], slabs, span, "unpack_3")
    return (jnp.transpose(field, (3, 0, 1, 2)), jnp.transpose(total, (1, 0, 2)))


def body(inputs, weights, out_grad):
    chans, levels, height, width = inputs.shape
    shape = tuple(lax.axis_size(axis) for axis in AXES)
    fits = (
        shape == (2, 4, 4)
        and chans == out_grad.shape[0] == 256
        and weights.shape[2] == 512
        and levels % 2 == 0
        and height % 2 == 0
        and width % 16 == 0
    )
    return (blocked_body if fits else plain_body)(inputs, weights, out_grad)


def solution(mesh):
    in_specs = (P("ch", None, "lat", "lon"), P("ch", None, None), P("ch", None, "lat", "lon"))
    out_specs = (P("ch", None, "lat", "lon"), P("ch", None, None))
    return jax.shard_map(body, mesh=mesh, in_specs=in_specs, out_specs=out_specs, check_vma=False)
```

```python
import math

import jax
import jax.numpy as jnp
from jax import lax
from jax.experimental import pallas as pl
from jax.experimental.pallas import tpu as pltpu
from jax.sharding import PartitionSpec as P

VMEM = pltpu.VMEM
SMEM = pltpu.SMEM
AXES = ("ch", "lat", "lon")


def padded_2(cells, sides, width):
    for axis, dim in sides:
        count = lax.axis_size(axis)
        head = lax.slice_in_dim(cells, 0, width, axis=dim)
        tail = lax.slice_in_dim(cells, cells.shape[dim] - width, cells.shape[dim], axis=dim)
        cells = jnp.concatenate(
            [
                lax.ppermute(tail, axis, [(i, (i + 1) % count) for i in range(count)]),
                cells,
                lax.ppermute(head, axis, [((i + 1) % count, i) for i in range(count)]),
            ],
            axis=dim,
        )
    return cells


def mask_rims(padded):
    count = lax.axis_size("lat")
    where_lat = lax.axis_index("lat")
    lines = jnp.arange(padded.shape[2])
    drop = (lines == 0) & (where_lat == 0) | (lines == padded.shape[2] - 1) & (
        where_lat == count - 1
    )
    return jnp.where(drop[None, None, :, None], jnp.zeros((), padded.dtype), padded)


def pad_levels(field):
    return jnp.pad(field, ((0, 0), (1, 1), (0, 0), (0, 0)))


def plain_body(inputs, weights, out_grad):
    chans, levels, height, width = inputs.shape
    input_pad = pad_levels(mask_rims(padded_2(inputs, (("lat", 2), ("lon", 3)), 1)))
    grad_inner = lax.all_gather(out_grad, "ch", axis=0, tiled=True)
    grad_pad = pad_levels(mask_rims(padded_2(grad_inner, (("lat", 2), ("lon", 3)), 1)))
    filters = grad_pad.shape[0]
    products = jnp.dot(
        weights.reshape(chans * 27, filters),
        grad_pad.reshape(filters, -1),
        preferred_element_type=jnp.float32,
    )
    products = products.reshape((chans, 27) + tuple(grad_pad.shape[1:]))
    total = jnp.zeros((chans, levels, height, width), jnp.float32)
    pieces = []
    for tap in range(27):
        lev, lat, lon = tap // 9 - 1, tap // 3 % 3 - 1, tap % 3 - 1
        total = (
            total
            + products[
                :,
                tap,
                1 - lev : 1 - lev + levels,
                1 - lat : 1 - lat + height,
                1 - lon : 1 - lon + width,
            ]
        )
        pieces.append(
            input_pad[
                :,
                1 + lev : 1 + lev + levels,
                1 + lat : 1 + lat + height,
                1 + lon : 1 + lon + width,
            ]
        )
    columns = jnp.stack(pieces, axis=1).reshape(chans * 27, -1)
    partial_grad = lax.dot_general(
        columns,
        grad_inner.reshape(filters, -1),
        (((1,), (1,)), ((), ())),
        preferred_element_type=jnp.float32,
    )
    summed = lax.psum(partial_grad, ("lat", "lon"))
    cells = levels * height * width * lax.axis_size("lat") * lax.axis_size("lon")
    weight_grad = (summed * (1.0 / math.sqrt(cells))).reshape(chans, 27, filters)
    return (total.astype(jnp.bfloat16), weight_grad)


def move(x, target):
    pairs = []
    for i in range(32):
        to = target(i // 16, i // 4 % 4, i % 4)
        if to is not None:
            pairs.append((i, (to[0] * 4 + to[1]) * 4 + to[2]))
    return lax.ppermute(x, AXES, pairs)


def lon_by(step):
    return lambda c, a, o: (c, a, (o + step) % 4)


def lat_xor(mask):
    return lambda c, a, o: (c, a ^ mask, o)


def sibling(c, a, o):
    return (1 - c, a, o)


def call(kernel, outs, ins, scratch, flops, name, limit, held=0, far=()):
    read = len(ins) - 1 - held
    spaces = [VMEM] * read + [pl.ANY] * held
    for at in far:
        spaces[at - 1] = pl.ANY
    moved = sum(math.prod(x.shape) * x.dtype.itemsize for x in list(ins[1 : 1 + read]) + list(outs))
    return pl.pallas_call(
        kernel,
        out_shape=outs,
        in_specs=[pl.BlockSpec(memory_space=space) for space in [SMEM] + spaces],
        out_specs=[pl.BlockSpec(memory_space=VMEM)] * len(outs),
        scratch_shapes=scratch,
        cost_estimate=pl.CostEstimate(flops=flops, bytes_accessed=moved, transcendentals=0),
        compiler_params=pltpu.CompilerParams(vmem_limit_bytes=limit * 1024 * 1024),
        name=name,
    )(*ins)


def pack_kernel(pos, x_far, g_far, g_same, g_other, x0, x1, x2, x3, rim_x, rim_d, x, g, held, sems):
    fetch_g = pltpu.make_async_copy(g_far, g, sems.at[0])
    fetch_x = pltpu.make_async_copy(x_far, x, sems.at[1])
    fetch_g.start()
    fetch_x.start()
    levels, height, width, chans = x.shape
    half, wide = levels // 2, chans // 2
    right = lax.rem(pos[1], 2)
    fetch_g.wait()
    for out, at in ((g_same, right), (g_other, 1 - right)):
        out[...] = g[:, :, :, pl.ds(pl.multiple_of(at * wide, wide), wide)].reshape(out.shape)
    many = x0.shape[0]
    for out, column in ((x1, width - 1), (x3, 0)):
        rim = g[:, :, column, :].reshape(levels * height, chans)
        out[many : many + levels * height, :] = rim[:, 0:wide]
        out[many + levels * height :, :] = rim[:, wide:]
    low, high = g[:, 0], g[:, height - 1]
    line = levels * width
    for out, upward in ((rim_x, right == 0), (rim_d, right == 1)):
        facing = jnp.where(upward, high, low).reshape(line, chans)
        for at in range(2):
            out[at * line : (at + 1) * line, :] = facing[:, at * wide : (at + 1) * wide]
    fetch_x.wait()
    for block in range(4):
        at = block * (chans // 4)
        lo = x[0:half, :, :, at : at + chans // 4]
        hi = x[half:levels, :, :, at : at + chans // 4]
        held[block] = jnp.concatenate([lo, hi], axis=-1).reshape(held.shape[1:])
    lon = pos[2]
    for step, out in enumerate((x0, x1, x2, x3)):
        out[0:many, :] = held[lax.rem(lon + step, 4)]


def spread_kernel(pos, x0, x1, x2, x3, rim_x, rim_d, own, own_y, to_x, to_d):
    del pos
    many = x0.shape[0]
    for at, piece in enumerate((x0, x1, x2, x3)):
        own[at * many : (at + 1) * many, :] = piece[0:many, :]
        own_y[at * many : (at + 1) * many, :] = piece[0:many, :]
    extra = x1.shape[0] - many
    own[4 * many : 4 * many + extra, :] = x1[many:, :]
    own[4 * many + extra :, :] = x3[many:, :]
    to_x[...] = rim_x[...]
    to_d[...] = rim_d[...]


def split_kernel(
    pos, here, west, east, g_far, own, x_x, x_d, by_x, by_d, after, first, second, near, mine, sems
):
    del after
    levels, height, width, chans = g_far.shape
    fetch = pltpu.make_async_copy(g_far, mine.at[:, pl.ds(1, height), pl.ds(0, width)], sems.at[0])
    fetch.start()
    first[...] = west[0]
    second[...] = east[1]
    for at, part in enumerate((here, west, east)):
        near[2 * at : 2 * at + 2] = part[...]
    edge, line, wide = levels * height, levels * width, chans // 2
    inner = own.shape[0] - 4 * edge

    def columns(message, rows):
        for side in range(2):
            for half in range(2):
                start = inner + (2 * side + half) * edge
                rim = message[start : start + edge, :].reshape(levels, height, wide)
                at = width + 8 * side
                for row, to in rows:
                    mine[:, to, at : at + 8, half * wide : (half + 1) * wide] = jnp.broadcast_to(
                        rim[:, row : row + 1], (levels, 8, wide)
                    )

    columns(own, [(row, row + 1) for row in range(height)])

    def lines(strip, message, row, to):
        for half in range(2):
            part = strip[half * line : (half + 1) * line, :]
            mine[:, to, 0:width, half * wide : (half + 1) * wide] = part.reshape(levels, width, wide)
        columns(message, [(row, to)])

    lat = pos[1]
    odd = lax.rem(lat, 2)

    @pl.when(odd == 1)
    def _():
        lines(by_x, x_x, height - 1, 0)
        lines(by_d, x_d, 0, height + 1)

    @pl.when(odd == 0)
    def _():
        lines(by_d, x_d, height - 1, 0)
        lines(by_x, x_x, 0, height + 1)

    @pl.when(lat == 0)
    def _():
        mine[:, 0] = jnp.zeros_like(mine[:, 0])

    @pl.when(lat == 3)
    def _():
        mine[:, height + 1] = jnp.zeros_like(mine[:, height + 1])

    fetch.wait()


def pair_kernel(pos, one, two, after, both):
    del pos, after
    both[0] = one[...]
    both[1] = two[...]


def lines_kernel(pos, x_own, x_x, x_y, x_d, after, xs, blank):
    del after, blank
    lat = pos[1]
    levels, rows, circle, lanes = xs.shape
    rows, width, span, half = rows - 2, circle // 4, lanes // 4, levels // 2
    height = rows // 4
    many = half * height * width
    xs[:, 0] = jnp.zeros_like(xs[:, 0])
    xs[:, rows + 1] = jnp.zeros_like(xs[:, rows + 1])
    low = lax.broadcasted_iota(jnp.int32, (circle, 2 * span), 1) < span
    for tag, ref in enumerate((x_own, x_x, x_y, x_d)):
        start = (lat ^ tag) * height
        strips = [
            ref.at[pl.ds((4 - at) % 4 * many, many)].reshape(half, height, width, 2 * span) for at in range(4)
        ]

        @pl.loop(0, half * height)
        def _(step, strips=strips, start=start):
            lev, row = step // height, lax.rem(step, height)
            line = jnp.concatenate([s[lev, row] for s in strips], axis=0).astype(jnp.float32)
            turned = pltpu.roll(line, span, 1)
            for upper in range(2):
                same = jnp.where(low, turned, line) if upper else jnp.where(low, line, turned)
                before = pltpu.roll(same, 1, 0)
                after = pltpu.roll(same, circle - 1, 0)
                at = upper * half + lev
                xs[at, 1 + start + row, :, 0 : 2 * span] = jnp.where(low, before, same).astype(xs.dtype)
                xs[at, 1 + start + row, :, 2 * span : 4 * span] = after.astype(xs.dtype)


def turn(gt, slot, core, first, second, levels):
    many, filters = first.shape
    line = many // levels
    for lev in range(levels):
        block = jnp.concatenate([first[lev * line : (lev + 1) * line], second[lev * line : (lev + 1) * line]], axis=0)
        gt[
            lev * filters : (lev + 1) * filters,
            pl.ds(pl.multiple_of((2 * slot + core) * 2 * line, 2 * line), 2 * line),
        ] = block.T


def taps_kernel(pos, xs, g, s, g2, s2, out, gt, acc):
    levels, rows, circle, lanes = xs.shape
    rows, width, span = rows - 2, circle // 4, lanes // 4
    filters = gt.shape[0] // levels
    deep = rows * width
    right = lax.rem(pos[1], 2)
    for core, parts, last in ((pos[0], g, g2), (1 - pos[0], s, s2)):
        for slot, (ref, at) in enumerate(((parts, 0), (parts, 4), (last, 0), (parts, 2))):
            turn(gt, slot, core, ref[at + right], ref[at + 1 - right], levels)
    acc[...] = jnp.zeros_like(acc)

    @pl.loop(0, 3)
    def _(lat_by):
        for lev in range(levels):
            first, last = max(lev - 1, 0), min(lev + 1, levels - 1)
            to = (first - lev + 1) * filters
            many = (last - first + 1) * filters
            total = acc[lat_by, to : to + many, :]
            for place in range(4):
                total += jnp.dot(
                    gt[first * filters : (last + 1) * filters, place * deep : (place + 1) * deep],
                    xs[lev, pl.ds(lat_by, rows), place * width : (place + 1) * width].reshape(deep, lanes),
                    preferred_element_type=jnp.float32,
                )
            acc[lat_by, to : to + many, :] = total

    scale = 1.0 / math.sqrt(levels * rows * circle)
    for lat_by in range(3):
        for lev_at in range(3):
            block = acc[lat_by, lev_at * filters : (lev_at + 1) * filters, :].T * scale
            for lon_at in range(3):
                out[(2 - lev_at) * 9 + lat_by * 3 + lon_at] = block[lon_at * span : (lon_at + 1) * span]


def code_kernel(pos, held, after, out, late, rest):
    del pos, after
    taps, span, filters = held.shape
    most = jnp.abs(held[0])
    for tap in range(1, taps):
        most = jnp.maximum(most, jnp.abs(held[tap]))
    top = jnp.maximum(jnp.max(most, axis=(0, 1), keepdims=True), 1e-30)
    power = jnp.ceil(jnp.log(top) * (1.0 / math.log(2.0))) - 15.0
    unit = jnp.broadcast_to(jnp.exp2(power), (16, filters)).astype(out.dtype).astype(jnp.float32)
    shrink = 1.0 / unit[0:1]
    unit = unit.astype(out.dtype)
    for tap in range(taps):
        value = held[tap] * shrink
        square = value * value
        code = (square * value * jnp.abs(value)).astype(out.dtype)
        for ref, many in ((out, out.shape[0] - 16), (late, late.shape[0] - 16), (rest, rest.shape[0])):
            at = tap * span if ref is out else tap * span - (taps * span - many)
            if 0 <= at < many:
                ref[at : at + span, :] = code
    out[out.shape[0] - 16 :, :] = unit
    late[late.shape[0] - 16 :, :] = unit


def both_kernel(pos, west, east, rest, after, both, half_3, half_1):
    del pos, after
    size, half = west.shape[0], half_3.shape[0]
    both[0:size, :] = west[...]
    both[size : 2 * size, :] = east[...]
    both[2 * size :, :] = rest[...]
    half_3[...] = west[0:half, :]
    half_1[...] = east[half:, :]


def across_kernel(pos, half_3, half_1, late):
    del pos
    half = half_3.shape[0]
    late[0:half, :] = half_3[...]
    late[half:, :] = half_1[...]


def block_kernel(pos, own, x, y, d, after, block):
    del pos, after
    end = own.shape[0] - 16
    rows = block.shape[0] // 4
    for at, piece in enumerate((own, x, y, d)):
        block[at * rows : (at + 1) * rows - 16, :] = piece[0 : rows - 16, :]
        block[(at + 1) * rows - 16 : (at + 1) * rows, :] = piece[end:, :]


def hand_kernel(pos, block_3, block_1, after, first, second):
    del pos, after
    many = first.shape[0]
    first[...] = block_3[0:many, :]
    second[...] = block_1[many:, :]


def unpack_kernel(pos, *refs, slabs, count, span):
    sources = refs[:count]
    total, token, buffers, sems = refs[-4:]
    slots, group = buffers.shape[:2]
    wide = buffers.shape[-1] // 4
    token[...] = jnp.zeros_like(token)
    parts = []
    for step, first, taps, pieces in slabs:
        for at in range(0, taps, group):
            parts.append((step, first + at, min(group, taps - at), at, pieces))

    def copy(at):
        step, first, many, _, _ = parts[at]
        lon_at = pl.multiple_of(lax.rem(pos[2] + step, 4) * span, span)
        return pltpu.make_async_copy(
            buffers.at[at % slots, pl.ds(0, many)],
            total.at[pl.ds(first, many), pl.ds(lon_at, span)],
            sems.at[at % slots],
        )

    for at, (_, _, many, skip, pieces) in enumerate(parts):
        if at >= slots:
            copy(at - slots).wait()
        for tag, (which, row, (power_in, power_row)) in enumerate(pieces):
            unit = sources[power_in][power_row : power_row + 16, :].astype(jnp.float32)[0:1]
            lanes = pl.ds(pl.multiple_of((pos[1] ^ tag) * wide, wide), wide)
            for tap in range(many):
                start = row + (skip + tap) * span
                code = sources[which][start : start + span, :].astype(jnp.float32)
                root = lax.rsqrt(lax.rsqrt(jnp.abs(code))) * unit
                buffers[at % slots, tap, :, lanes] = jnp.where(code < 0, -root, root)
        copy(at).start()
    for at in range(max(len(parts) - slots, 0), len(parts)):
        copy(at).wait()


def unpack(pos, total, sources, after, slabs, span, name):
    slots, group = 4, 3
    wide = total.shape[2]
    ins = (pos, *sources, *after, total)
    token = jax.ShapeDtypeStruct((8, 128), jnp.float32)
    return pl.pallas_call(
        lambda *refs: unpack_kernel(*refs, slabs=slabs, count=len(sources), span=span),
        out_shape=[jax.ShapeDtypeStruct(total.shape, total.dtype), token],
        in_specs=[pl.BlockSpec(memory_space=SMEM)]
        + [pl.BlockSpec(memory_space=VMEM)] * len(sources)
        + [pl.BlockSpec(memory_space=pl.ANY)] * (len(after) + 1),
        out_specs=[pl.BlockSpec(memory_space=pl.ANY), pl.BlockSpec(memory_space=VMEM)],
        scratch_shapes=[VMEM((slots, group, span, wide), jnp.float32), pltpu.SemaphoreType.DMA((slots,))],
        input_output_aliases={len(ins) - 1: 0},
        cost_estimate=pl.CostEstimate(flops=0, bytes_accessed=4 * 2**20, transcendentals=0),
        compiler_params=pltpu.CompilerParams(vmem_limit_bytes=51 * 1024 * 1024),
        name=name,
    )(*ins)


def field_kernel(pos, after, mine, theirs, w, out, copies, acc):
    del after
    step = pl.program_id(0)
    levels, height, width, chans = out.shape
    many = mine.shape[-1]

    @pl.when(step == 0)
    def _():
        copies[:, 0] = jnp.zeros_like(copies[:, 0])
        copies[:, levels + 1] = jnp.zeros_like(copies[:, levels + 1])
        line_at = lax.broadcasted_iota(jnp.int32, (width, many), 0)
        for which, field in ((pos[0], mine), (1 - pos[0], theirs)):
            lanes = pl.ds(pl.multiple_of(which * many, many), many)
            for lev in range(levels):
                for row in range(height + 2):
                    line = field[lev, row, 0:width].astype(jnp.float32)
                    west = field[lev, row, width : width + 1].astype(jnp.float32)
                    east = field[lev, row, width + 8 : width + 9].astype(jnp.float32)
                    before = jnp.where(line_at == 0, west, pltpu.roll(line, 1, 0))
                    later = jnp.where(line_at == width - 1, east, pltpu.roll(line, width - 1, 0))
                    copies[0, lev + 1, row, :, lanes] = later.astype(copies.dtype)
                    copies[1, lev + 1, row, :, lanes] = field[lev, row, 0:width]
                    copies[2, lev + 1, row, :, lanes] = before.astype(copies.dtype)
        acc[...] = jnp.zeros_like(acc)

    lev_by, lat_by = step // 3, lax.rem(step, 3)
    cells = [
        copies[at, pl.ds(2 - lev_by, levels), pl.ds(2 - lat_by, height)].reshape(
            levels * height * width, 2 * many
        )
        for at in range(3)
    ]
    acc[...] += lax.dot_general(
        jnp.concatenate(cells, axis=1),
        jnp.concatenate([w[at] for at in range(3)], axis=1),
        (((1,), (1,)), ((), ())),
        preferred_element_type=jnp.float32,
    )

    @pl.when(step == 8)
    def _():
        out[...] = acc[...].reshape(out.shape).astype(out.dtype)


def blocked_body(inputs, weights, out_grad):
    chans, levels, height, width = inputs.shape
    filters = weights.shape[2]
    bf16, f32 = jnp.bfloat16, jnp.float32
    lat, lon = lax.axis_index("lat"), lax.axis_index("lon")
    pos = jnp.stack([lax.axis_index("ch"), lat, lon]).astype(jnp.int32)
    x_cells = jnp.transpose(inputs, (1, 2, 3, 0))
    g_cells = jnp.transpose(out_grad, (1, 2, 3, 0))
    taps = jnp.transpose(weights, (1, 0, 2))
    cells = levels * height * width
    span, wide = chans // 4, filters // 4
    rows, circle = 4 * height, 4 * width
    edge = levels * height

    to_same = lambda c, a, o: (a // 2, 2 * c + a % 2, o)
    to_other = lambda c, a, o: (a // 2, 2 * c + 1 - a % 2, o)
    many = cells // 2
    block = jax.ShapeDtypeStruct((cells, wide), bf16)
    strip = jax.ShapeDtypeStruct((2 * levels * width, 2 * span), bf16)
    field_shape = (levels, height, width, chans)
    g_same, g_other, x0, x1, x2, x3, rim_x, rim_d = call(
        pack_kernel,
        [block, block]
        + [jax.ShapeDtypeStruct((many + extra, 2 * span), bf16) for extra in (0, 2 * edge, 0, 2 * edge)]
        + [strip, strip],
        (pos, x_cells, g_cells),
        [
            VMEM(field_shape, bf16),
            VMEM(field_shape, bf16),
            VMEM((4, many, 2 * span), bf16),
            pltpu.SemaphoreType.DMA((2,)),
        ],
        0,
        "pack",
        16,
        far=(1, 2),
    )
    g_s = move(g_same, to_same)
    g_o = move(g_other, to_other)
    x_r1 = move(x1, lon_by(1))
    x_r3 = move(x3, lon_by(-1))
    x_r2 = move(x2, lon_by(2))

    inner = 4 * many
    (g0,) = call(
        pair_kernel, [jax.ShapeDtypeStruct((2, cells, wide), bf16)], (pos, g_s, g_o, x0), [], 0, "pair_0", 16, held=1
    )
    x_own, x_own_y, rim_x, rim_d = call(
        spread_kernel,
        [jax.ShapeDtypeStruct((count, 2 * span), bf16) for count in (inner + 4 * edge, inner)] + [strip, strip],
        (pos, x0, x_r1, x_r2, x_r3, rim_x, rim_d),
        [],
        0,
        "spread",
        16,
    )
    x_x = move(x_own, lat_xor(1))
    x_d = move(x_own, lat_xor(3))
    x_y = move(x_own_y, lat_xor(2))
    g1 = move(g0, lon_by(1))
    g3 = move(g0, lon_by(-1))
    by_x = move(rim_x, lat_xor(1))
    by_d = move(rim_d, lat_xor(3))
    far_a, far_b, g_near, mine = call(
        split_kernel,
        [
            block,
            block,
            jax.ShapeDtypeStruct((6, cells, wide), bf16),
            jax.ShapeDtypeStruct((levels, height + 2, width + 16, chans), bf16),
        ],
        (pos, g0, g1, g3, g_cells, x_own, x_x, x_d, by_x, by_d, x_y),
        [pltpu.SemaphoreType.DMA((1,))],
        0,
        "split",
        16,
        held=1,
        far=(4,),
    )
    g2a = move(far_a, lon_by(1))
    g2b = move(far_b, lon_by(-1))
    s_near = move(g_near, sibling)
    theirs = move(mine, sibling)

    xs, total = pl.pallas_call(
        lines_kernel,
        out_shape=[
            jax.ShapeDtypeStruct((levels, rows + 2, circle, 4 * span), bf16),
            jax.ShapeDtypeStruct((27, chans, filters), f32),
        ],
        in_specs=[pl.BlockSpec(memory_space=SMEM)]
        + [pl.BlockSpec(memory_space=VMEM)] * 4
        + [pl.BlockSpec(memory_space=pl.ANY)],
        out_specs=[pl.BlockSpec(memory_space=VMEM)] + [pl.BlockSpec(memory_space=pl.ANY)],
        cost_estimate=pl.CostEstimate(flops=0, bytes_accessed=2**20, transcendentals=0),
        compiler_params=pltpu.CompilerParams(vmem_limit_bytes=24 * 1024 * 1024),
        name="lines",
    )(pos, x_own, x_x, x_y, x_d, far_a)
    (g2,) = call(
        pair_kernel, [jax.ShapeDtypeStruct((2, cells, wide), bf16)], (pos, g2a, g2b, xs), [], 0, "pair", 16, held=1
    )
    s2 = move(g2, sibling)
    early, middle = 6, 20
    cut, end = early * span, 27 * span
    size = end + 16 - cut
    half = size // 32 * 16
    first_rows = cut + 16
    own_rows = middle * span + 16
    slab = lambda count: jax.ShapeDtypeStruct((count, wide), bf16)
    (grads,) = call(
        taps_kernel,
        [jax.ShapeDtypeStruct((27, span, wide), f32)],
        (pos, xs, g_near, s_near, g2, s2),
        [VMEM((levels * wide, rows * circle), bf16), VMEM((3, 3 * wide, 4 * span), f32)],
        2 * 27 * span * wide * rows * circle * levels,
        "taps",
        28,
    )
    own, late, rest = call(
        code_kernel,
        [slab(own_rows), slab(size), slab(end - middle * span)],
        (pos, grads, theirs),
        [],
        0,
        "code",
        16,
        held=1,
    )

    whole = lambda t: (0, 0, 0, 0)
    field = pl.pallas_call(
        field_kernel,
        out_shape=jax.ShapeDtypeStruct((levels, height, width, chans), bf16),
        grid=(9,),
        in_specs=[
            pl.BlockSpec(memory_space=SMEM),
            pl.BlockSpec(memory_space=pl.ANY),
            pl.BlockSpec(mine.shape, whole),
            pl.BlockSpec(mine.shape, whole),
            pl.BlockSpec((3, chans, filters), lambda t: (t, 0, 0)),
        ],
        out_specs=pl.BlockSpec((levels, height, width, chans), whole),
        scratch_shapes=[
            VMEM((3, levels + 2, height + 2, width, filters), bf16),
            VMEM((cells, chans), f32),
        ],
        cost_estimate=pl.CostEstimate(
            flops=4 * 27 * chans * filters * cells, bytes_accessed=27 * chans * filters * 2, transcendentals=0
        ),
        compiler_params=pltpu.CompilerParams(vmem_limit_bytes=20 * 1024 * 1024),
        name="field",
    )(pos, own, mine, theirs, taps)

    def to_plane(share):
        return [move(share, lat_xor(tag)) for tag in (1, 2, 3)]

    from_3 = move(late, lon_by(1))
    from_1 = move(late, lon_by(-1))
    plane = [own] + to_plane(own)
    pair, half_3, half_1 = call(
        both_kernel,
        [slab(2 * size + end - middle * span), slab(half), slab(size - half)],
        (pos, from_3, from_1, rest, field),
        [],
        0,
        "both",
        16,
        held=1,
    )
    half_3 = move(half_3, lon_by(1))
    half_1 = move(half_1, lon_by(-1))
    both = to_plane(pair)
    (block,) = call(block_kernel, [slab(4 * first_rows)], (pos, *plane, pair), [], 0, "block", 16, held=1)
    (from_2,) = call(across_kernel, [slab(size)], (pos, half_3, half_1), [], 0, "across", 16)
    early_3 = move(block, lon_by(1))
    early_1 = move(block, lon_by(-1))
    across = to_plane(from_2)

    def late_piece(which, row=0):
        return (which, row, (which, row + size - 16))

    def early_piece(which, row):
        return (which, row, (which, row + cut))

    slabs = [(0, 0, middle, [(tag, 0, (tag, own_rows - 16)) for tag in range(4)])]
    total, token = unpack(pos, total, plane, [block], slabs, span, "unpack_1")
    hand_3, hand_1 = call(
        hand_kernel, [slab(2 * first_rows)] * 2, (pos, early_3, early_1, token), [], 0, "hand", 16, held=1
    )
    early_2a = move(hand_3, lon_by(1))
    early_2b = move(hand_1, lon_by(-1))
    unit = own_rows - 16
    slabs = [
        (3, early, 27 - early, [late_piece(5)] + [late_piece(at) for at in range(3)]),
        (1, early, 27 - early, [late_piece(6)] + [late_piece(at, size) for at in range(3)]),
        (0, middle, 27 - middle, [(7, 0, (8, unit))] + [(at, 2 * size, (9 + at, unit)) for at in range(3)]),
        (3, 0, early, [early_piece(3, tag * first_rows) for tag in range(4)]),
        (1, 0, early, [early_piece(4, tag * first_rows) for tag in range(4)]),
    ]
    total, _ = unpack(
        pos, total, both + [early_3, early_1, from_3, from_1, rest] + plane, [hand_3], slabs, span, "unpack_2"
    )
    slabs = [
        (2, 0, early, [early_piece(tag // 2, tag % 2 * first_rows) for tag in range(4)]),
        (2, early, 27 - early, [late_piece(2 + tag) for tag in range(4)]),
    ]
    total, _ = unpack(pos, total, [early_2a, early_2b, from_2] + across, [], slabs, span, "unpack_3")
    return (jnp.transpose(field, (3, 0, 1, 2)), jnp.transpose(total, (1, 0, 2)))


def body(inputs, weights, out_grad):
    chans, levels, height, width = inputs.shape
    shape = tuple(lax.axis_size(axis) for axis in AXES)
    fits = (
        shape == (2, 4, 4)
        and chans == out_grad.shape[0] == 256
        and weights.shape[2] == 512
        and levels % 2 == 0
        and height % 2 == 0
        and width % 16 == 0
    )
    return (blocked_body if fits else plain_body)(inputs, weights, out_grad)


def solution(mesh):
    in_specs = (P("ch", None, "lat", "lon"), P("ch", None, None), P("ch", None, "lat", "lon"))
    out_specs = (P("ch", None, "lat", "lon"), P("ch", None, None))
    return jax.shard_map(body, mesh=mesh, in_specs=in_specs, out_specs=out_specs, check_vma=False)
```

```python
import math

import jax
import jax.numpy as jnp
from jax import lax
from jax.experimental import pallas as pl
from jax.experimental.pallas import tpu as pltpu
from jax.sharding import PartitionSpec as P

VMEM = pltpu.VMEM
SMEM = pltpu.SMEM
AXES = ("ch", "lat", "lon")


def padded_2(cells, sides, width):
    for axis, dim in sides:
        count = lax.axis_size(axis)
        head = lax.slice_in_dim(cells, 0, width, axis=dim)
        tail = lax.slice_in_dim(cells, cells.shape[dim] - width, cells.shape[dim], axis=dim)
        cells = jnp.concatenate(
            [
                lax.ppermute(tail, axis, [(i, (i + 1) % count) for i in range(count)]),
                cells,
                lax.ppermute(head, axis, [((i + 1) % count, i) for i in range(count)]),
            ],
            axis=dim,
        )
    return cells


def mask_rims(padded):
    count = lax.axis_size("lat")
    where_lat = lax.axis_index("lat")
    lines = jnp.arange(padded.shape[2])
    drop = (lines == 0) & (where_lat == 0) | (lines == padded.shape[2] - 1) & (
        where_lat == count - 1
    )
    return jnp.where(drop[None, None, :, None], jnp.zeros((), padded.dtype), padded)


def pad_levels(field):
    return jnp.pad(field, ((0, 0), (1, 1), (0, 0), (0, 0)))


def plain_body(inputs, weights, out_grad):
    chans, levels, height, width = inputs.shape
    input_pad = pad_levels(mask_rims(padded_2(inputs, (("lat", 2), ("lon", 3)), 1)))
    grad_inner = lax.all_gather(out_grad, "ch", axis=0, tiled=True)
    grad_pad = pad_levels(mask_rims(padded_2(grad_inner, (("lat", 2), ("lon", 3)), 1)))
    filters = grad_pad.shape[0]
    products = jnp.dot(
        weights.reshape(chans * 27, filters),
        grad_pad.reshape(filters, -1),
        preferred_element_type=jnp.float32,
    )
    products = products.reshape((chans, 27) + tuple(grad_pad.shape[1:]))
    total = jnp.zeros((chans, levels, height, width), jnp.float32)
    pieces = []
    for tap in range(27):
        lev, lat, lon = tap // 9 - 1, tap // 3 % 3 - 1, tap % 3 - 1
        total = (
            total
            + products[
                :,
                tap,
                1 - lev : 1 - lev + levels,
                1 - lat : 1 - lat + height,
                1 - lon : 1 - lon + width,
            ]
        )
        pieces.append(
            input_pad[
                :,
                1 + lev : 1 + lev + levels,
                1 + lat : 1 + lat + height,
                1 + lon : 1 + lon + width,
            ]
        )
    columns = jnp.stack(pieces, axis=1).reshape(chans * 27, -1)
    partial_grad = lax.dot_general(
        columns,
        grad_inner.reshape(filters, -1),
        (((1,), (1,)), ((), ())),
        preferred_element_type=jnp.float32,
    )
    summed = lax.psum(partial_grad, ("lat", "lon"))
    cells = levels * height * width * lax.axis_size("lat") * lax.axis_size("lon")
    weight_grad = (summed * (1.0 / math.sqrt(cells))).reshape(chans, 27, filters)
    return (total.astype(jnp.bfloat16), weight_grad)


def move(x, target):
    pairs = []
    for i in range(32):
        to = target(i // 16, i // 4 % 4, i % 4)
        if to is not None:
            pairs.append((i, (to[0] * 4 + to[1]) * 4 + to[2]))
    return lax.ppermute(x, AXES, pairs)


def lon_by(step):
    return lambda c, a, o: (c, a, (o + step) % 4)


def lat_xor(mask):
    return lambda c, a, o: (c, a ^ mask, o)


def sibling(c, a, o):
    return (1 - c, a, o)


def call(kernel, outs, ins, scratch, flops, name, limit, held=0):
    read = len(ins) - 1 - held
    moved = sum(math.prod(x.shape) * x.dtype.itemsize for x in list(ins[1 : 1 + read]) + list(outs))
    return pl.pallas_call(
        kernel,
        out_shape=outs,
        in_specs=[pl.BlockSpec(memory_space=SMEM)]
        + [pl.BlockSpec(memory_space=VMEM)] * read
        + [pl.BlockSpec(memory_space=pl.ANY)] * held,
        out_specs=[pl.BlockSpec(memory_space=VMEM)] * len(outs),
        scratch_shapes=scratch,
        cost_estimate=pl.CostEstimate(flops=flops, bytes_accessed=moved, transcendentals=0),
        compiler_params=pltpu.CompilerParams(vmem_limit_bytes=limit * 1024 * 1024),
        name=name,
    )(*ins)


def pack_kernel(pos, x, g, g_same, g_other, x0, x1, x2, x3, rim_x, rim_d, held):
    levels, height, width, chans = x.shape
    half, wide = levels // 2, chans // 2
    right = lax.rem(pos[1], 2)
    for out, at in ((g_same, right), (g_other, 1 - right)):
        out[...] = g[:, :, :, pl.ds(pl.multiple_of(at * wide, wide), wide)].reshape(out.shape)
    many = x0.shape[0]
    for block in range(4):
        at = block * (chans // 4)
        lo = x[0:half, :, :, at : at + chans // 4]
        hi = x[half:levels, :, :, at : at + chans // 4]
        held[block] = jnp.concatenate([lo, hi], axis=-1).reshape(held.shape[1:])
    lon = pos[2]
    for step, out in enumerate((x0, x1, x2, x3)):
        out[0:many, :] = held[lax.rem(lon + step, 4)]
    for out, column in ((x1, width - 1), (x3, 0)):
        rim = g[:, :, column, :].reshape(levels * height, chans)
        out[many : many + levels * height, :] = rim[:, 0:wide]
        out[many + levels * height :, :] = rim[:, wide:]
    even = right == 0
    low, high = g[:, 0], g[:, height - 1]
    line = levels * width
    for out, upward in ((rim_x, even), (rim_d, jnp.logical_not(even))):
        facing = jnp.where(upward, high, low).reshape(line, chans)
        for at in range(2):
            out[at * line : (at + 1) * line, :] = facing[:, at * wide : (at + 1) * wide]


def spread_kernel(pos, x0, x1, x2, x3, own, own_y):
    del pos
    many = x0.shape[0]
    for at, piece in enumerate((x0, x1, x2, x3)):
        own[at * many : (at + 1) * many, :] = piece[0:many, :]
        own_y[at * many : (at + 1) * many, :] = piece[0:many, :]
    extra = x1.shape[0] - many
    own[4 * many : 4 * many + extra, :] = x1[many:, :]
    own[4 * many + extra :, :] = x3[many:, :]


def split_kernel(
    pos, here, west, east, g, own, x_x, x_d, by_x, by_d, after, first, second, near, mine
):
    del after
    first[...] = west[0]
    second[...] = east[1]
    for at, part in enumerate((here, west, east)):
        near[2 * at : 2 * at + 2] = part[...]

    levels, height, width, chans = g.shape
    edge, line, wide = levels * height, levels * width, chans // 2
    inner = own.shape[0] - 4 * edge
    mine[:, 1 : height + 1, 0:width, :] = g[...]

    def columns(message, rows):
        for side in range(2):
            for half in range(2):
                start = inner + (2 * side + half) * edge
                rim = message[start : start + edge, :].reshape(levels, height, wide)
                at = width + 8 * side
                for row, to in rows:
                    mine[:, to, at : at + 8, half * wide : (half + 1) * wide] = jnp.broadcast_to(
                        rim[:, row : row + 1], (levels, 8, wide)
                    )

    columns(own, [(row, row + 1) for row in range(height)])

    def lines(strip, message, row, to):
        for half in range(2):
            part = strip[half * line : (half + 1) * line, :]
            mine[:, to, 0:width, half * wide : (half + 1) * wide] = part.reshape(levels, width, wide)
        columns(message, [(row, to)])

    lat = pos[1]
    odd = lax.rem(lat, 2)

    @pl.when(odd == 1)
    def _():
        lines(by_x, x_x, height - 1, 0)
        lines(by_d, x_d, 0, height + 1)

    @pl.when(odd == 0)
    def _():
        lines(by_d, x_d, height - 1, 0)
        lines(by_x, x_x, 0, height + 1)

    @pl.when(lat == 0)
    def _():
        mine[:, 0] = jnp.zeros_like(mine[:, 0])

    @pl.when(lat == 3)
    def _():
        mine[:, height + 1] = jnp.zeros_like(mine[:, height + 1])


def pair_kernel(pos, one, two, after, both):
    del pos, after
    both[0] = one[...]
    both[1] = two[...]


def lines_kernel(pos, x_own, x_x, x_y, x_d, after, xs, blank):
    del after, blank
    lat = pos[1]
    levels, rows, circle, lanes = xs.shape
    rows, width, span, half = rows - 2, circle // 4, lanes // 4, levels // 2
    height = rows // 4
    many = half * height * width
    xs[:, 0] = jnp.zeros_like(xs[:, 0])
    xs[:, rows + 1] = jnp.zeros_like(xs[:, rows + 1])
    low = lax.broadcasted_iota(jnp.int32, (circle, 2 * span), 1) < span
    for tag, ref in enumerate((x_own, x_x, x_y, x_d)):
        start = (lat ^ tag) * height
        strips = [
            ref.at[pl.ds((4 - at) % 4 * many, many)].reshape(half, height, width, 2 * span) for at in range(4)
        ]

        @pl.loop(0, half * height)
        def _(step, strips=strips, start=start):
            lev, row = step // height, lax.rem(step, height)
            line = jnp.concatenate([s[lev, row] for s in strips], axis=0).astype(jnp.float32)
            turned = pltpu.roll(line, span, 1)
            for upper in range(2):
                same = jnp.where(low, turned, line) if upper else jnp.where(low, line, turned)
                before = pltpu.roll(same, 1, 0)
                after = pltpu.roll(same, circle - 1, 0)
                at = upper * half + lev
                xs[at, 1 + start + row, :, 0 : 2 * span] = jnp.where(low, before, same).astype(xs.dtype)
                xs[at, 1 + start + row, :, 2 * span : 4 * span] = after.astype(xs.dtype)


def turn(gt, slot, core, first, second, levels):
    many, filters = first.shape
    line = many // levels
    for lev in range(levels):
        block = jnp.concatenate([first[lev * line : (lev + 1) * line], second[lev * line : (lev + 1) * line]], axis=0)
        gt[
            lev * filters : (lev + 1) * filters,
            pl.ds(pl.multiple_of((2 * slot + core) * 2 * line, 2 * line), 2 * line),
        ] = block.T


def taps_kernel(pos, xs, g, s, g2, s2, out, gt, acc):
    levels, rows, circle, lanes = xs.shape
    rows, width, span = rows - 2, circle // 4, lanes // 4
    filters = gt.shape[0] // levels
    deep = rows * width
    right = lax.rem(pos[1], 2)
    for core, parts, last in ((pos[0], g, g2), (1 - pos[0], s, s2)):
        for slot, (ref, at) in enumerate(((parts, 0), (parts, 4), (last, 0), (parts, 2))):
            turn(gt, slot, core, ref[at + right], ref[at + 1 - right], levels)
    acc[...] = jnp.zeros_like(acc)

    @pl.loop(0, 3)
    def _(lat_by):
        for lev in range(levels):
            first, last = max(lev - 1, 0), min(lev + 1, levels - 1)
            to = (first - lev + 1) * filters
            many = (last - first + 1) * filters
            total = acc[lat_by, to : to + many, :]
            for place in range(4):
                total += jnp.dot(
                    gt[first * filters : (last + 1) * filters, place * deep : (place + 1) * deep],
                    xs[lev, pl.ds(lat_by, rows), place * width : (place + 1) * width].reshape(deep, lanes),
                    preferred_element_type=jnp.float32,
                )
            acc[lat_by, to : to + many, :] = total

    scale = 1.0 / math.sqrt(levels * rows * circle)
    for lat_by in range(3):
        for lev_at in range(3):
            block = acc[lat_by, lev_at * filters : (lev_at + 1) * filters, :].T * scale
            for lon_at in range(3):
                out[(2 - lev_at) * 9 + lat_by * 3 + lon_at] = block[lon_at * span : (lon_at + 1) * span]


def code_kernel(pos, held, after, out, late):
    del pos, after
    taps, span, filters = held.shape
    most = jnp.abs(held[0])
    for tap in range(1, taps):
        most = jnp.maximum(most, jnp.abs(held[tap]))
    top = jnp.maximum(jnp.max(most, axis=(0, 1), keepdims=True), 1e-30)
    power = jnp.ceil(jnp.log(top) * (1.0 / math.log(2.0))) - 15.0
    unit = jnp.broadcast_to(jnp.exp2(power), (16, filters)).astype(out.dtype).astype(jnp.float32)
    shrink = 1.0 / unit[0:1]
    unit = unit.astype(out.dtype)
    skip = out.shape[0] - late.shape[0]
    for tap in range(taps):
        value = held[tap] * shrink
        square = value * value
        code = (square * value * jnp.abs(value)).astype(out.dtype)
        out[tap * span : (tap + 1) * span, :] = code
        if tap * span >= skip:
            late[tap * span - skip : (tap + 1) * span - skip, :] = code
    out[taps * span :, :] = unit
    late[taps * span - skip :, :] = unit


def both_kernel(pos, west, east, after, both, half_3, half_1):
    del pos, after
    size, half = west.shape[0], half_3.shape[0]
    both[0:size, :] = west[...]
    both[size:, :] = east[...]
    half_3[...] = west[0:half, :]
    half_1[...] = east[half:, :]


def cross_kernel(pos, by_x, by_y, after, top, bottom):
    del pos, after
    cut = top.shape[0]
    top[...] = by_y[0:cut, :]
    bottom[...] = by_x[cut:, :]


def across_kernel(pos, half_3, half_1, late):
    del pos
    half = half_3.shape[0]
    late[0:half, :] = half_3[...]
    late[half:, :] = half_1[...]


def block_kernel(pos, own, x, y, top, bottom, block):
    del pos
    rows = block.shape[0] // 4
    for at, (piece, end) in enumerate(((own, own), (x, x), (y, y), (top, bottom))):
        block[at * rows : (at + 1) * rows - 16, :] = piece[0 : rows - 16, :]
        block[(at + 1) * rows - 16 : (at + 1) * rows, :] = end[end.shape[0] - 16 :, :]


def hand_kernel(pos, block_3, block_1, first, second):
    del pos
    many = first.shape[0]
    first[...] = block_3[0:many, :]
    second[...] = block_1[many:, :]


def unpack_kernel(pos, *refs, slabs, count, span):
    sources = refs[:count]
    total, token, buffers, sems = refs[-4:]
    slots, group = buffers.shape[:2]
    wide = buffers.shape[-1] // 4
    token[...] = jnp.zeros_like(token)
    parts = []
    for step, first, taps, pieces in slabs:
        for at in range(0, taps, group):
            parts.append((step, first + at, min(group, taps - at), at, pieces))

    def copy(at):
        step, first, many, _, _ = parts[at]
        lon_at = pl.multiple_of(lax.rem(pos[2] + step, 4) * span, span)
        return pltpu.make_async_copy(
            buffers.at[at % slots, pl.ds(0, many)],
            total.at[pl.ds(first, many), pl.ds(lon_at, span)],
            sems.at[at % slots],
        )

    for at, (_, _, many, skip, pieces) in enumerate(parts):
        if at >= slots:
            copy(at - slots).wait()
        for tag, ((power_in, power_row), *segments) in enumerate(pieces):
            unit = sources[power_in][power_row : power_row + 16, :].astype(jnp.float32)[0:1]
            lanes = pl.ds(pl.multiple_of((pos[1] ^ tag) * wide, wide), wide)
            for tap in range(many):
                begin, which, row = [segment for segment in segments if segment[0] <= skip + tap][-1]
                start = row + (skip + tap - begin) * span
                code = sources[which][start : start + span, :].astype(jnp.float32)
                root = lax.rsqrt(lax.rsqrt(jnp.abs(code))) * unit
                buffers[at % slots, tap, :, lanes] = jnp.where(code < 0, -root, root)
        copy(at).start()
    for at in range(max(len(parts) - slots, 0), len(parts)):
        copy(at).wait()


def unpack(pos, total, sources, after, slabs, span, name):
    slots, group = 4, 3
    wide = total.shape[2]
    ins = (pos, *sources, *after, total)
    token = jax.ShapeDtypeStruct((8, 128), jnp.float32)
    return pl.pallas_call(
        lambda *refs: unpack_kernel(*refs, slabs=slabs, count=len(sources), span=span),
        out_shape=[jax.ShapeDtypeStruct(total.shape, total.dtype), token],
        in_specs=[pl.BlockSpec(memory_space=SMEM)]
        + [pl.BlockSpec(memory_space=VMEM)] * len(sources)
        + [pl.BlockSpec(memory_space=pl.ANY)] * (len(after) + 1),
        out_specs=[pl.BlockSpec(memory_space=pl.ANY), pl.BlockSpec(memory_space=VMEM)],
        scratch_shapes=[VMEM((slots, group, span, wide), jnp.float32), pltpu.SemaphoreType.DMA((slots,))],
        input_output_aliases={len(ins) - 1: 0},
        cost_estimate=pl.CostEstimate(flops=0, bytes_accessed=4 * 2**20, transcendentals=0),
        compiler_params=pltpu.CompilerParams(vmem_limit_bytes=51 * 1024 * 1024),
        name=name,
    )(*ins)


def field_kernel(pos, after, mine, theirs, w, out, copies, acc):
    del after
    step = pl.program_id(0)
    levels, height, width, chans = out.shape
    many = mine.shape[-1]

    @pl.when(step == 0)
    def _():
        copies[:, 0] = jnp.zeros_like(copies[:, 0])
        copies[:, levels + 1] = jnp.zeros_like(copies[:, levels + 1])
        line_at = lax.broadcasted_iota(jnp.int32, (width, many), 0)
        for which, field in ((pos[0], mine), (1 - pos[0], theirs)):
            lanes = pl.ds(pl.multiple_of(which * many, many), many)
            for lev in range(levels):
                for row in range(height + 2):
                    line = field[lev, row, 0:width].astype(jnp.float32)
                    west = field[lev, row, width : width + 1].astype(jnp.float32)
                    east = field[lev, row, width + 8 : width + 9].astype(jnp.float32)
                    before = jnp.where(line_at == 0, west, pltpu.roll(line, 1, 0))
                    later = jnp.where(line_at == width - 1, east, pltpu.roll(line, width - 1, 0))
                    copies[0, lev + 1, row, :, lanes] = later.astype(copies.dtype)
                    copies[1, lev + 1, row, :, lanes] = field[lev, row, 0:width]
                    copies[2, lev + 1, row, :, lanes] = before.astype(copies.dtype)
        acc[...] = jnp.zeros_like(acc)

    lev_by, lat_by = step // 3, lax.rem(step, 3)
    cells = [
        copies[at, pl.ds(2 - lev_by, levels), pl.ds(2 - lat_by, height)].reshape(
            levels * height * width, 2 * many
        )
        for at in range(3)
    ]
    acc[...] += lax.dot_general(
        jnp.concatenate(cells, axis=1),
        jnp.concatenate([w[at] for at in range(3)], axis=1),
        (((1,), (1,)), ((), ())),
        preferred_element_type=jnp.float32,
    )

    @pl.when(step == 8)
    def _():
        out[...] = acc[...].reshape(out.shape).astype(out.dtype)


def blocked_body(inputs, weights, out_grad):
    chans, levels, height, width = inputs.shape
    filters = weights.shape[2]
    bf16, f32 = jnp.bfloat16, jnp.float32
    lat, lon = lax.axis_index("lat"), lax.axis_index("lon")
    pos = jnp.stack([lax.axis_index("ch"), lat, lon]).astype(jnp.int32)
    x_cells = jnp.transpose(inputs, (1, 2, 3, 0))
    g_cells = jnp.transpose(out_grad, (1, 2, 3, 0))
    taps = jnp.transpose(weights, (1, 0, 2))
    cells = levels * height * width
    span, wide = chans // 4, filters // 4
    rows, circle = 4 * height, 4 * width
    edge = levels * height

    to_same = lambda c, a, o: (a // 2, 2 * c + a % 2, o)
    to_other = lambda c, a, o: (a // 2, 2 * c + 1 - a % 2, o)
    many = cells // 2
    block = jax.ShapeDtypeStruct((cells, wide), bf16)
    strip = jax.ShapeDtypeStruct((2 * levels * width, 2 * span), bf16)
    g_same, g_other, x0, x1, x2, x3, rim_x, rim_d = call(
        pack_kernel,
        [block, block]
        + [jax.ShapeDtypeStruct((many + extra, 2 * span), bf16) for extra in (0, 2 * edge, 0, 2 * edge)]
        + [strip, strip],
        (pos, x_cells, g_cells),
        [VMEM((4, many, 2 * span), bf16)],
        0,
        "pack",
        16,
    )
    g_s = move(g_same, to_same)
    g_o = move(g_other, to_other)
    x_r1 = move(x1, lon_by(1))
    x_r3 = move(x3, lon_by(-1))
    x_r2 = move(x2, lon_by(2))
    by_x = move(rim_x, lat_xor(1))
    by_d = move(rim_d, lat_xor(3))

    inner = 4 * many
    (g0,) = call(
        pair_kernel, [jax.ShapeDtypeStruct((2, cells, wide), bf16)], (pos, g_s, g_o, x0), [], 0, "pair_0", 16, held=1
    )
    x_own, x_own_y = call(
        spread_kernel,
        [jax.ShapeDtypeStruct((count, 2 * span), bf16) for count in (inner + 4 * edge, inner)],
        (pos, x0, x_r1, x_r2, x_r3),
        [],
        0,
        "spread",
        16,
    )
    x_x = move(x_own, lat_xor(1))
    x_d = move(x_own, lat_xor(3))
    x_y = move(x_own_y, lat_xor(2))
    g1 = move(g0, lon_by(1))
    g3 = move(g0, lon_by(-1))
    far_a, far_b, g_near, mine = call(
        split_kernel,
        [
            block,
            block,
            jax.ShapeDtypeStruct((6, cells, wide), bf16),
            jax.ShapeDtypeStruct((levels, height + 2, width + 16, chans), bf16),
        ],
        (pos, g0, g1, g3, g_cells, x_own, x_x, x_d, by_x, by_d, x_y),
        [],
        0,
        "split",
        16,
        held=1,
    )
    g2a = move(far_a, lon_by(1))
    g2b = move(far_b, lon_by(-1))
    s_near = move(g_near, sibling)
    theirs = move(mine, sibling)
    xs, total = pl.pallas_call(
        lines_kernel,
        out_shape=[
            jax.ShapeDtypeStruct((levels, rows + 2, circle, 4 * span), bf16),
            jax.ShapeDtypeStruct((27, chans, filters), f32),
        ],
        in_specs=[pl.BlockSpec(memory_space=SMEM)]
        + [pl.BlockSpec(memory_space=VMEM)] * 4
        + [pl.BlockSpec(memory_space=pl.ANY)],
        out_specs=[pl.BlockSpec(memory_space=VMEM)] + [pl.BlockSpec(memory_space=pl.ANY)],
        cost_estimate=pl.CostEstimate(flops=0, bytes_accessed=2**20, transcendentals=0),
        compiler_params=pltpu.CompilerParams(vmem_limit_bytes=24 * 1024 * 1024),
        name="lines",
    )(pos, x_own, x_x, x_y, x_d, far_a)
    (g2,) = call(
        pair_kernel, [jax.ShapeDtypeStruct((2, cells, wide), bf16)], (pos, g2a, g2b, xs), [], 0, "pair", 16, held=1
    )
    s2 = move(g2, sibling)
    early = 6
    cut, end = early * span, 27 * span
    size = end + 16 - cut
    half = size // 32 * 16
    first_rows = cut + 16
    own_cut, late_cut = 14 * span, (27 - early) // 2 * span
    slab = lambda count: jax.ShapeDtypeStruct((count, wide), bf16)
    (grads,) = call(
        taps_kernel,
        [jax.ShapeDtypeStruct((27, span, wide), f32)],
        (pos, xs, g_near, s_near, g2, s2),
        [VMEM((levels * wide, rows * circle), bf16), VMEM((3, 3 * wide, 4 * span), f32)],
        2 * 27 * span * wide * rows * circle * levels,
        "taps",
        28,
    )
    own, late = call(code_kernel, [slab(end + 16), slab(size)], (pos, grads, theirs), [], 0, "code", 16, held=1)

    def to_plane(share):
        return move(share, lat_xor(1)), move(share, lat_xor(2))

    def to_diagonal(by_x, by_y, cut, after, name):
        top, bottom = call(
            cross_kernel, [slab(cut), slab(by_x.shape[0] - cut)], (pos, by_x, by_y, after), [], 0, name, 16, held=1
        )
        return move(top, lat_xor(1)), move(bottom, lat_xor(2)), top

    from_3 = move(late, lon_by(1))
    from_1 = move(late, lon_by(-1))
    own_x, own_y = to_plane(own)
    own_top, own_bottom, crossed = to_diagonal(own_x, own_y, own_cut, own, "cross_1")
    pair, half_3, half_1 = call(
        both_kernel, [slab(2 * size), slab(half), slab(size - half)], (pos, from_3, from_1, crossed), [], 0, "both", 16, held=1
    )
    whole = lambda t: (0, 0, 0, 0)
    field = pl.pallas_call(
        field_kernel,
        out_shape=jax.ShapeDtypeStruct((levels, height, width, chans), bf16),
        grid=(9,),
        in_specs=[
            pl.BlockSpec(memory_space=SMEM),
            pl.BlockSpec(memory_space=pl.ANY),
            pl.BlockSpec(mine.shape, whole),
            pl.BlockSpec(mine.shape, whole),
            pl.BlockSpec((3, chans, filters), lambda t: (t, 0, 0)),
        ],
        out_specs=pl.BlockSpec((levels, height, width, chans), whole),
        scratch_shapes=[
            VMEM((3, levels + 2, height + 2, width, filters), bf16),
            VMEM((cells, chans), f32),
        ],
        cost_estimate=pl.CostEstimate(
            flops=4 * 27 * chans * filters * cells, bytes_accessed=27 * chans * filters * 2, transcendentals=0
        ),
        compiler_params=pltpu.CompilerParams(vmem_limit_bytes=20 * 1024 * 1024),
        name="field",
    )(pos, pair, mine, theirs, taps)

    half_3 = move(half_3, lon_by(1))
    half_1 = move(half_1, lon_by(-1))
    pair_x, pair_y = to_plane(pair)
    (block,) = call(
        block_kernel, [slab(4 * first_rows)], (pos, own, own_x, own_y, own_top, own_bottom), [], 0, "block", 16
    )
    early_3 = move(block, lon_by(1))
    early_1 = move(block, lon_by(-1))
    (from_2,) = call(across_kernel, [slab(size)], (pos, half_3, half_1), [], 0, "across", 16)
    pair_top, pair_bottom, _ = to_diagonal(pair_x, pair_y, size, field, "cross_2")
    from_2x, from_2y = to_plane(from_2)
    hand_3, hand_1 = call(hand_kernel, [slab(2 * first_rows)] * 2, (pos, early_3, early_1), [], 0, "hand", 16)
    early_2a = move(hand_3, lon_by(1))
    early_2b = move(hand_1, lon_by(-1))

    def late_piece(which, row=0):
        return ((which, row + size - 16), (0, which, row))

    def early_piece(which, row):
        return ((which, row + cut), (0, which, row))

    pieces = [((which, end), (0, which, 0)) for which in range(3)]
    pieces.append(((4, end - own_cut), (0, 3, 0), (own_cut // span, 4, 0)))
    total, token = unpack(
        pos, total, [own, own_x, own_y, own_top, own_bottom], [block], [(0, 0, 27, pieces)], span, "unpack_1"
    )
    from_2top, from_2bottom, _ = to_diagonal(from_2x, from_2y, late_cut, token, "cross_3")
    slabs = [
        (3, early, 27 - early, [late_piece(0), late_piece(2), late_piece(3), late_piece(4)]),
        (1, early, 27 - early, [late_piece(1), late_piece(2, size), late_piece(3, size), late_piece(5)]),
        (3, 0, early, [early_piece(6, tag * first_rows) for tag in range(4)]),
        (1, 0, early, [early_piece(7, tag * first_rows) for tag in range(4)]),
    ]
    total, _ = unpack(
        pos,
        total,
        [from_3, from_1, pair_x, pair_y, pair_top, pair_bottom, early_3, early_1],
        [hand_3],
        slabs,
        span,
        "unpack_2",
    )
    pieces = [late_piece(2), late_piece(3), late_piece(4)]
    pieces.append(((6, size - 16 - late_cut), (0, 5, 0), (late_cut // span, 6, 0)))
    slabs = [
        (2, 0, early, [early_piece(tag // 2, tag % 2 * first_rows) for tag in range(4)]),
        (2, early, 27 - early, pieces),
    ]
    total, _ = unpack(
        pos,
        total,
        [early_2a, early_2b, from_2, from_2x, from_2y, from_2top, from_2bottom],
        [],
        slabs,
        span,
        "unpack_3",
    )
    return (jnp.transpose(field, (3, 0, 1, 2)), jnp.transpose(total, (1, 0, 2)))


def body(inputs, weights, out_grad):
    chans, levels, height, width = inputs.shape
    shape = tuple(lax.axis_size(axis) for axis in AXES)
    fits = (
        shape == (2, 4, 4)
        and chans == out_grad.shape[0] == 256
        and weights.shape[2] == 512
        and levels % 2 == 0
        and height % 2 == 0
        and width % 16 == 0
    )
    return (blocked_body if fits else plain_body)(inputs, weights, out_grad)


def solution(mesh):
    in_specs = (P("ch", None, "lat", "lon"), P("ch", None, None), P("ch", None, "lat", "lon"))
    out_specs = (P("ch", None, "lat", "lon"), P("ch", None, None))
    return jax.shard_map(body, mesh=mesh, in_specs=in_specs, out_specs=out_specs, check_vma=False)
```

```python
import math

import jax
import jax.numpy as jnp
from jax import lax
from jax.experimental import pallas as pl
from jax.experimental.pallas import tpu as pltpu
from jax.sharding import PartitionSpec as P

VMEM = pltpu.VMEM
SMEM = pltpu.SMEM
AXES = ("ch", "lat", "lon")


def padded_2(cells, sides, width):
    for axis, dim in sides:
        count = lax.axis_size(axis)
        head = lax.slice_in_dim(cells, 0, width, axis=dim)
        tail = lax.slice_in_dim(cells, cells.shape[dim] - width, cells.shape[dim], axis=dim)
        cells = jnp.concatenate(
            [
                lax.ppermute(tail, axis, [(i, (i + 1) % count) for i in range(count)]),
                cells,
                lax.ppermute(head, axis, [((i + 1) % count, i) for i in range(count)]),
            ],
            axis=dim,
        )
    return cells


def mask_rims(padded):
    count = lax.axis_size("lat")
    where_lat = lax.axis_index("lat")
    lines = jnp.arange(padded.shape[2])
    drop = (lines == 0) & (where_lat == 0) | (lines == padded.shape[2] - 1) & (
        where_lat == count - 1
    )
    return jnp.where(drop[None, None, :, None], jnp.zeros((), padded.dtype), padded)


def pad_levels(field):
    return jnp.pad(field, ((0, 0), (1, 1), (0, 0), (0, 0)))


def plain_body(inputs, weights, out_grad):
    chans, levels, height, width = inputs.shape
    input_pad = pad_levels(mask_rims(padded_2(inputs, (("lat", 2), ("lon", 3)), 1)))
    grad_inner = lax.all_gather(out_grad, "ch", axis=0, tiled=True)
    grad_pad = pad_levels(mask_rims(padded_2(grad_inner, (("lat", 2), ("lon", 3)), 1)))
    filters = grad_pad.shape[0]
    products = jnp.dot(
        weights.reshape(chans * 27, filters),
        grad_pad.reshape(filters, -1),
        preferred_element_type=jnp.float32,
    )
    products = products.reshape((chans, 27) + tuple(grad_pad.shape[1:]))
    total = jnp.zeros((chans, levels, height, width), jnp.float32)
    pieces = []
    for tap in range(27):
        lev, lat, lon = tap // 9 - 1, tap // 3 % 3 - 1, tap % 3 - 1
        total = (
            total
            + products[
                :,
                tap,
                1 - lev : 1 - lev + levels,
                1 - lat : 1 - lat + height,
                1 - lon : 1 - lon + width,
            ]
        )
        pieces.append(
            input_pad[
                :,
                1 + lev : 1 + lev + levels,
                1 + lat : 1 + lat + height,
                1 + lon : 1 + lon + width,
            ]
        )
    columns = jnp.stack(pieces, axis=1).reshape(chans * 27, -1)
    partial_grad = lax.dot_general(
        columns,
        grad_inner.reshape(filters, -1),
        (((1,), (1,)), ((), ())),
        preferred_element_type=jnp.float32,
    )
    summed = lax.psum(partial_grad, ("lat", "lon"))
    cells = levels * height * width * lax.axis_size("lat") * lax.axis_size("lon")
    weight_grad = (summed * (1.0 / math.sqrt(cells))).reshape(chans, 27, filters)
    return (total.astype(jnp.bfloat16), weight_grad)


def move(x, target):
    pairs = []
    for i in range(32):
        to = target(i // 16, i // 4 % 4, i % 4)
        if to is not None:
            pairs.append((i, (to[0] * 4 + to[1]) * 4 + to[2]))
    return lax.ppermute(x, AXES, pairs)


def lon_by(step):
    return lambda c, a, o: (c, a, (o + step) % 4)


def lat_xor(mask):
    return lambda c, a, o: (c, a ^ mask, o)


def sibling(c, a, o):
    return (1 - c, a, o)


def call(kernel, outs, ins, scratch, flops, name, limit, held=0):
    read = len(ins) - 1 - held
    moved = sum(math.prod(x.shape) * x.dtype.itemsize for x in list(ins[1 : 1 + read]) + list(outs))
    return pl.pallas_call(
        kernel,
        out_shape=outs,
        in_specs=[pl.BlockSpec(memory_space=SMEM)]
        + [pl.BlockSpec(memory_space=VMEM)] * read
        + [pl.BlockSpec(memory_space=pl.ANY)] * held,
        out_specs=[pl.BlockSpec(memory_space=VMEM)] * len(outs),
        scratch_shapes=scratch,
        cost_estimate=pl.CostEstimate(flops=flops, bytes_accessed=moved, transcendentals=0),
        compiler_params=pltpu.CompilerParams(vmem_limit_bytes=limit * 1024 * 1024),
        name=name,
    )(*ins)


def pack_kernel(pos, x, g, g_same, g_other, x0, x1, x2, x3, rim_x, rim_d, held):
    levels, height, width, chans = x.shape
    half, wide = levels // 2, chans // 2
    right = lax.rem(pos[1], 2)
    for out, at in ((g_same, right), (g_other, 1 - right)):
        out[...] = g[:, :, :, pl.ds(pl.multiple_of(at * wide, wide), wide)].reshape(out.shape)
    many = x0.shape[0]
    for block in range(4):
        at = block * (chans // 4)
        lo = x[0:half, :, :, at : at + chans // 4]
        hi = x[half:levels, :, :, at : at + chans // 4]
        held[block] = jnp.concatenate([lo, hi], axis=-1).reshape(held.shape[1:])
    lon = pos[2]
    for step, out in enumerate((x0, x1, x2, x3)):
        out[0:many, :] = held[lax.rem(lon + step, 4)]
    for out, column in ((x1, width - 1), (x3, 0)):
        rim = g[:, :, column, :].reshape(levels * height, chans)
        out[many : many + levels * height, :] = rim[:, 0:wide]
        out[many + levels * height :, :] = rim[:, wide:]
    even = right == 0
    low, high = g[:, 0], g[:, height - 1]
    line = levels * width
    for out, upward in ((rim_x, even), (rim_d, jnp.logical_not(even))):
        facing = jnp.where(upward, high, low).reshape(line, chans)
        for at in range(2):
            out[at * line : (at + 1) * line, :] = facing[:, at * wide : (at + 1) * wide]


def spread_kernel(pos, x0, x1, x2, x3, own, own_y):
    del pos
    many = x0.shape[0]
    for at, piece in enumerate((x0, x1, x2, x3)):
        own[at * many : (at + 1) * many, :] = piece[0:many, :]
        own_y[at * many : (at + 1) * many, :] = piece[0:many, :]
    extra = x1.shape[0] - many
    own[4 * many : 4 * many + extra, :] = x1[many:, :]
    own[4 * many + extra :, :] = x3[many:, :]


def split_kernel(
    pos, here, west, east, g, own, x_x, x_d, by_x, by_d, after, first, second, near, mine
):
    del after
    first[...] = west[0]
    second[...] = east[1]
    for at, part in enumerate((here, west, east)):
        near[2 * at : 2 * at + 2] = part[...]

    levels, height, width, chans = g.shape
    edge, line, wide = levels * height, levels * width, chans // 2
    inner = own.shape[0] - 4 * edge
    mine[:, 1 : height + 1, 0:width, :] = g[...]

    def columns(message, rows):
        for side in range(2):
            for half in range(2):
                start = inner + (2 * side + half) * edge
                rim = message[start : start + edge, :].reshape(levels, height, wide)
                at = width + 8 * side
                for row, to in rows:
                    mine[:, to, at : at + 8, half * wide : (half + 1) * wide] = jnp.broadcast_to(
                        rim[:, row : row + 1], (levels, 8, wide)
                    )

    columns(own, [(row, row + 1) for row in range(height)])

    def lines(strip, message, row, to):
        for half in range(2):
            part = strip[half * line : (half + 1) * line, :]
            mine[:, to, 0:width, half * wide : (half + 1) * wide] = part.reshape(levels, width, wide)
        columns(message, [(row, to)])

    lat = pos[1]
    odd = lax.rem(lat, 2)

    @pl.when(odd == 1)
    def _():
        lines(by_x, x_x, height - 1, 0)
        lines(by_d, x_d, 0, height + 1)

    @pl.when(odd == 0)
    def _():
        lines(by_d, x_d, height - 1, 0)
        lines(by_x, x_x, 0, height + 1)

    @pl.when(lat == 0)
    def _():
        mine[:, 0] = jnp.zeros_like(mine[:, 0])

    @pl.when(lat == 3)
    def _():
        mine[:, height + 1] = jnp.zeros_like(mine[:, height + 1])


def pair_kernel(pos, one, two, after, both):
    del pos, after
    both[0] = one[...]
    both[1] = two[...]


def lines_kernel(pos, x_own, x_x, x_y, x_d, after, xs, blank):
    del after, blank
    lat = pos[1]
    levels, rows, circle, lanes = xs.shape
    rows, width, span, half = rows - 2, circle // 4, lanes // 4, levels // 2
    height = rows // 4
    many = half * height * width
    xs[:, 0] = jnp.zeros_like(xs[:, 0])
    xs[:, rows + 1] = jnp.zeros_like(xs[:, rows + 1])
    low = lax.broadcasted_iota(jnp.int32, (circle, 2 * span), 1) < span
    for tag, ref in enumerate((x_own, x_x, x_y, x_d)):
        start = (lat ^ tag) * height
        strips = [
            ref.at[pl.ds((4 - at) % 4 * many, many)].reshape(half, height, width, 2 * span) for at in range(4)
        ]

        @pl.loop(0, half * height)
        def _(step, strips=strips, start=start):
            lev, row = step // height, lax.rem(step, height)
            line = jnp.concatenate([s[lev, row] for s in strips], axis=0).astype(jnp.float32)
            turned = pltpu.roll(line, span, 1)
            for upper in range(2):
                same = jnp.where(low, turned, line) if upper else jnp.where(low, line, turned)
                before = pltpu.roll(same, 1, 0)
                after = pltpu.roll(same, circle - 1, 0)
                at = upper * half + lev
                xs[at, 1 + start + row, :, 0 : 2 * span] = jnp.where(low, before, same).astype(xs.dtype)
                xs[at, 1 + start + row, :, 2 * span : 4 * span] = after.astype(xs.dtype)


def turn(gt, slot, core, first, second, levels):
    many, filters = first.shape
    line = many // levels
    for lev in range(levels):
        block = jnp.concatenate([first[lev * line : (lev + 1) * line], second[lev * line : (lev + 1) * line]], axis=0)
        gt[
            lev * filters : (lev + 1) * filters,
            pl.ds(pl.multiple_of((2 * slot + core) * 2 * line, 2 * line), 2 * line),
        ] = block.T


def taps_kernel(pos, xs, g, s, g2, s2, out, gt, acc):
    levels, rows, circle, lanes = xs.shape
    rows, width, span = rows - 2, circle // 4, lanes // 4
    filters = gt.shape[0] // levels
    deep = rows * width
    right = lax.rem(pos[1], 2)
    for core, parts, last in ((pos[0], g, g2), (1 - pos[0], s, s2)):
        for slot, (ref, at) in enumerate(((parts, 0), (parts, 4), (last, 0), (parts, 2))):
            turn(gt, slot, core, ref[at + right], ref[at + 1 - right], levels)
    acc[...] = jnp.zeros_like(acc)

    @pl.loop(0, 3)
    def _(lat_by):
        for lev in range(levels):
            first, last = max(lev - 1, 0), min(lev + 1, levels - 1)
            to = (first - lev + 1) * filters
            many = (last - first + 1) * filters
            total = acc[lat_by, to : to + many, :]
            for place in range(4):
                total += jnp.dot(
                    gt[first * filters : (last + 1) * filters, place * deep : (place + 1) * deep],
                    xs[lev, pl.ds(lat_by, rows), place * width : (place + 1) * width].reshape(deep, lanes),
                    preferred_element_type=jnp.float32,
                )
            acc[lat_by, to : to + many, :] = total

    scale = 1.0 / math.sqrt(levels * rows * circle)
    for lat_by in range(3):
        for lev_at in range(3):
            block = acc[lat_by, lev_at * filters : (lev_at + 1) * filters, :].T * scale
            for lon_at in range(3):
                out[(2 - lev_at) * 9 + lat_by * 3 + lon_at] = block[lon_at * span : (lon_at + 1) * span]


def code_kernel(pos, held, after, out, late):
    del pos, after
    taps, span, filters = held.shape
    most = jnp.abs(held[0])
    for tap in range(1, taps):
        most = jnp.maximum(most, jnp.abs(held[tap]))
    top = jnp.maximum(jnp.max(most, axis=(0, 1), keepdims=True), 1e-30)
    power = jnp.ceil(jnp.log(top) * (1.0 / math.log(2.0))) - 15.0
    unit = jnp.broadcast_to(jnp.exp2(power), (16, filters)).astype(out.dtype).astype(jnp.float32)
    shrink = 1.0 / unit[0:1]
    unit = unit.astype(out.dtype)
    skip = out.shape[0] - late.shape[0]
    for tap in range(taps):
        value = held[tap] * shrink
        square = value * value
        code = (square * value * jnp.abs(value)).astype(out.dtype)
        out[tap * span : (tap + 1) * span, :] = code
        if tap * span >= skip:
            late[tap * span - skip : (tap + 1) * span - skip, :] = code
    out[taps * span :, :] = unit
    late[taps * span - skip :, :] = unit


def both_kernel(pos, west, east, after1, after2, both, half_3, half_1):
    del pos, after1, after2
    size, half = west.shape[0], half_3.shape[0]
    both[0:size, :] = west[...]
    both[size:, :] = east[...]
    half_3[...] = west[0:half, :]
    half_1[...] = east[half:, :]


def cross_kernel(pos, by_x, by_y, after, top, bottom):
    del pos, after
    cut = top.shape[0]
    top[...] = by_y[0:cut, :]
    bottom[...] = by_x[cut:, :]


def across_kernel(pos, half_3, half_1, after, late):
    del pos, after
    half = half_3.shape[0]
    late[0:half, :] = half_3[...]
    late[half:, :] = half_1[...]


def block_kernel(pos, own, x, y, top, bottom, block):
    del pos
    rows = block.shape[0] // 4
    for at, (piece, end) in enumerate(((own, own), (x, x), (y, y), (top, bottom))):
        block[at * rows : (at + 1) * rows - 16, :] = piece[0 : rows - 16, :]
        block[(at + 1) * rows - 16 : (at + 1) * rows, :] = end[end.shape[0] - 16 :, :]


def hand_kernel(pos, block_3, block_1, first, second):
    del pos
    many = first.shape[0]
    first[...] = block_3[0:many, :]
    second[...] = block_1[many:, :]


def unpack_kernel(pos, *refs, slabs, count, span):
    sources = refs[:count]
    total, token, buffers, sems = refs[-4:]
    slots, group = buffers.shape[:2]
    wide = buffers.shape[-1] // 4
    token[...] = jnp.zeros_like(token)
    parts = []
    for step, first, taps, pieces in slabs:
        for at in range(0, taps, group):
            parts.append((step, first + at, min(group, taps - at), at, pieces))

    def copy(at):
        step, first, many, _, _ = parts[at]
        lon_at = pl.multiple_of(lax.rem(pos[2] + step, 4) * span, span)
        return pltpu.make_async_copy(
            buffers.at[at % slots, pl.ds(0, many)],
            total.at[pl.ds(first, many), pl.ds(lon_at, span)],
            sems.at[at % slots],
        )

    for at, (_, _, many, skip, pieces) in enumerate(parts):
        if at >= slots:
            copy(at - slots).wait()
        for tag, ((power_in, power_row), *segments) in enumerate(pieces):
            unit = sources[power_in][power_row : power_row + 16, :].astype(jnp.float32)[0:1]
            lanes = pl.ds(pl.multiple_of((pos[1] ^ tag) * wide, wide), wide)
            for tap in range(many):
                begin, which, row = [segment for segment in segments if segment[0] <= skip + tap][-1]
                start = row + (skip + tap - begin) * span
                code = sources[which][start : start + span, :].astype(jnp.float32)
                root = lax.rsqrt(lax.rsqrt(jnp.abs(code))) * unit
                buffers[at % slots, tap, :, lanes] = jnp.where(code < 0, -root, root)
        copy(at).start()
    for at in range(max(len(parts) - slots, 0), len(parts)):
        copy(at).wait()


def unpack(pos, total, sources, after, slabs, span, name):
    slots, group = 4, 3
    wide = total.shape[2]
    ins = (pos, *sources, *after, total)
    token = jax.ShapeDtypeStruct((8, 128), jnp.float32)
    return pl.pallas_call(
        lambda *refs: unpack_kernel(*refs, slabs=slabs, count=len(sources), span=span),
        out_shape=[jax.ShapeDtypeStruct(total.shape, total.dtype), token],
        in_specs=[pl.BlockSpec(memory_space=SMEM)]
        + [pl.BlockSpec(memory_space=VMEM)] * len(sources)
        + [pl.BlockSpec(memory_space=pl.ANY)] * (len(after) + 1),
        out_specs=[pl.BlockSpec(memory_space=pl.ANY), pl.BlockSpec(memory_space=VMEM)],
        scratch_shapes=[VMEM((slots, group, span, wide), jnp.float32), pltpu.SemaphoreType.DMA((slots,))],
        input_output_aliases={len(ins) - 1: 0},
        cost_estimate=pl.CostEstimate(flops=0, bytes_accessed=4 * 2**20, transcendentals=0),
        compiler_params=pltpu.CompilerParams(vmem_limit_bytes=51 * 1024 * 1024),
        name=name,
    )(*ins)


def field_kernel(pos, after, mine, theirs, w, out, copies, acc):
    del after
    step = pl.program_id(0)
    levels, height, width, chans = out.shape
    many = mine.shape[-1]

    @pl.when(step == 0)
    def _():
        copies[:, 0] = jnp.zeros_like(copies[:, 0])
        copies[:, levels + 1] = jnp.zeros_like(copies[:, levels + 1])
        line_at = lax.broadcasted_iota(jnp.int32, (width, many), 0)
        for which, field in ((pos[0], mine), (1 - pos[0], theirs)):
            lanes = pl.ds(pl.multiple_of(which * many, many), many)
            for lev in range(levels):
                for row in range(height + 2):
                    line = field[lev, row, 0:width].astype(jnp.float32)
                    west = field[lev, row, width : width + 1].astype(jnp.float32)
                    east = field[lev, row, width + 8 : width + 9].astype(jnp.float32)
                    before = jnp.where(line_at == 0, west, pltpu.roll(line, 1, 0))
                    later = jnp.where(line_at == width - 1, east, pltpu.roll(line, width - 1, 0))
                    copies[0, lev + 1, row, :, lanes] = later.astype(copies.dtype)
                    copies[1, lev + 1, row, :, lanes] = field[lev, row, 0:width]
                    copies[2, lev + 1, row, :, lanes] = before.astype(copies.dtype)
        acc[...] = jnp.zeros_like(acc)

    lev_by, lat_by = step // 3, lax.rem(step, 3)
    cells = [
        copies[at, pl.ds(2 - lev_by, levels), pl.ds(2 - lat_by, height)].reshape(
            levels * height * width, 2 * many
        )
        for at in range(3)
    ]
    acc[...] += lax.dot_general(
        jnp.concatenate(cells, axis=1),
        jnp.concatenate([w[at] for at in range(3)], axis=1),
        (((1,), (1,)), ((), ())),
        preferred_element_type=jnp.float32,
    )

    @pl.when(step == 8)
    def _():
        out[...] = acc[...].reshape(out.shape).astype(out.dtype)


def blocked_body(inputs, weights, out_grad):
    chans, levels, height, width = inputs.shape
    filters = weights.shape[2]
    bf16, f32 = jnp.bfloat16, jnp.float32
    lat, lon = lax.axis_index("lat"), lax.axis_index("lon")
    pos = jnp.stack([lax.axis_index("ch"), lat, lon]).astype(jnp.int32)
    x_cells = jnp.transpose(inputs, (1, 2, 3, 0))
    g_cells = jnp.transpose(out_grad, (1, 2, 3, 0))
    taps = jnp.transpose(weights, (1, 0, 2))
    cells = levels * height * width
    span, wide = chans // 4, filters // 4
    rows, circle = 4 * height, 4 * width
    edge = levels * height

    to_same = lambda c, a, o: (a // 2, 2 * c + a % 2, o)
    to_other = lambda c, a, o: (a // 2, 2 * c + 1 - a % 2, o)
    many = cells // 2
    block = jax.ShapeDtypeStruct((cells, wide), bf16)
    strip = jax.ShapeDtypeStruct((2 * levels * width, 2 * span), bf16)
    g_same, g_other, x0, x1, x2, x3, rim_x, rim_d = call(
        pack_kernel,
        [block, block]
        + [jax.ShapeDtypeStruct((many + extra, 2 * span), bf16) for extra in (0, 2 * edge, 0, 2 * edge)]
        + [strip, strip],
        (pos, x_cells, g_cells),
        [VMEM((4, many, 2 * span), bf16)],
        0,
        "pack",
        16,
    )
    g_s = move(g_same, to_same)
    g_o = move(g_other, to_other)
    x_r1 = move(x1, lon_by(1))
    x_r3 = move(x3, lon_by(-1))
    x_r2 = move(x2, lon_by(2))
    by_x = move(rim_x, lat_xor(1))
    by_d = move(rim_d, lat_xor(3))

    inner = 4 * many
    (g0,) = call(
        pair_kernel, [jax.ShapeDtypeStruct((2, cells, wide), bf16)], (pos, g_s, g_o, x0), [], 0, "pair_0", 16, held=1
    )
    x_own, x_own_y = call(
        spread_kernel,
        [jax.ShapeDtypeStruct((count, 2 * span), bf16) for count in (inner + 4 * edge, inner)],
        (pos, x0, x_r1, x_r2, x_r3),
        [],
        0,
        "spread",
        16,
    )
    x_x = move(x_own, lat_xor(1))
    x_d = move(x_own, lat_xor(3))
    x_y = move(x_own_y, lat_xor(2))
    g1 = move(g0, lon_by(1))
    g3 = move(g0, lon_by(-1))
    far_a, far_b, g_near, mine = call(
        split_kernel,
        [
            block,
            block,
            jax.ShapeDtypeStruct((6, cells, wide), bf16),
            jax.ShapeDtypeStruct((levels, height + 2, width + 16, chans), bf16),
        ],
        (pos, g0, g1, g3, g_cells, x_own, x_x, x_d, by_x, by_d, x_y),
        [],
        0,
        "split",
        16,
        held=1,
    )
    g2a = move(far_a, lon_by(1))
    g2b = move(far_b, lon_by(-1))
    s_near = move(g_near, sibling)
    theirs = move(mine, sibling)
    xs, total = pl.pallas_call(
        lines_kernel,
        out_shape=[
            jax.ShapeDtypeStruct((levels, rows + 2, circle, 4 * span), bf16),
            jax.ShapeDtypeStruct((27, chans, filters), f32),
        ],
        in_specs=[pl.BlockSpec(memory_space=SMEM)]
        + [pl.BlockSpec(memory_space=VMEM)] * 4
        + [pl.BlockSpec(memory_space=pl.ANY)],
        out_specs=[pl.BlockSpec(memory_space=VMEM)] + [pl.BlockSpec(memory_space=pl.ANY)],
        cost_estimate=pl.CostEstimate(flops=0, bytes_accessed=2**20, transcendentals=0),
        compiler_params=pltpu.CompilerParams(vmem_limit_bytes=24 * 1024 * 1024),
        name="lines",
    )(pos, x_own, x_x, x_y, x_d, far_a)
    (g2,) = call(
        pair_kernel, [jax.ShapeDtypeStruct((2, cells, wide), bf16)], (pos, g2a, g2b, xs), [], 0, "pair", 16, held=1
    )
    s2 = move(g2, sibling)
    early = 6
    cut, end = early * span, 27 * span
    size = end + 16 - cut
    half = size // 32 * 16
    first_rows = cut + 16
    own_cut, late_cut = 14 * span, (27 - early) // 2 * span
    slab = lambda count: jax.ShapeDtypeStruct((count, wide), bf16)
    (grads,) = call(
        taps_kernel,
        [jax.ShapeDtypeStruct((27, span, wide), f32)],
        (pos, xs, g_near, s_near, g2, s2),
        [VMEM((levels * wide, rows * circle), bf16), VMEM((3, 3 * wide, 4 * span), f32)],
        2 * 27 * span * wide * rows * circle * levels,
        "taps",
        28,
    )
    own, late = call(code_kernel, [slab(end + 16), slab(size)], (pos, grads, theirs), [], 0, "code", 16, held=1)

    def to_plane(share):
        return move(share, lat_xor(1)), move(share, lat_xor(2))

    def to_diagonal(by_x, by_y, cut, after, name):
        top, bottom = call(
            cross_kernel, [slab(cut), slab(by_x.shape[0] - cut)], (pos, by_x, by_y, after), [], 0, name, 16, held=1
        )
        return move(top, lat_xor(1)), move(bottom, lat_xor(2))

    from_3 = move(late, lon_by(1))
    from_1 = move(late, lon_by(-1))
    own_x, own_y = to_plane(own)
    own_top, own_bottom = to_diagonal(own_x, own_y, own_cut, own, "cross_1")
    pair, half_3, half_1 = call(
        both_kernel,
        [slab(2 * size), slab(half), slab(size - half)],
        (pos, from_3, from_1, own_top, own_bottom),
        [],
        0,
        "both",
        16,
        held=2,
    )
    half_3 = move(half_3, lon_by(1))
    half_1 = move(half_1, lon_by(-1))
    pair_x, pair_y = to_plane(pair)
    (block,) = call(
        block_kernel, [slab(4 * first_rows)], (pos, own, own_x, own_y, own_top, own_bottom), [], 0, "block", 16
    )
    early_3 = move(block, lon_by(1))
    early_1 = move(block, lon_by(-1))
    whole = lambda t: (0, 0, 0, 0)
    field = pl.pallas_call(
        field_kernel,
        out_shape=jax.ShapeDtypeStruct((levels, height, width, chans), bf16),
        grid=(9,),
        in_specs=[
            pl.BlockSpec(memory_space=SMEM),
            pl.BlockSpec(memory_space=pl.ANY),
            pl.BlockSpec(mine.shape, whole),
            pl.BlockSpec(mine.shape, whole),
            pl.BlockSpec((3, chans, filters), lambda t: (t, 0, 0)),
        ],
        out_specs=pl.BlockSpec((levels, height, width, chans), whole),
        scratch_shapes=[
            VMEM((3, levels + 2, height + 2, width, filters), bf16),
            VMEM((cells, chans), f32),
        ],
        cost_estimate=pl.CostEstimate(
            flops=4 * 27 * chans * filters * cells, bytes_accessed=27 * chans * filters * 2, transcendentals=0
        ),
        compiler_params=pltpu.CompilerParams(vmem_limit_bytes=20 * 1024 * 1024),
        name="field",
    )(pos, pair, mine, theirs, taps)

    (from_2,) = call(across_kernel, [slab(size)], (pos, half_3, half_1, field), [], 0, "across", 16, held=1)
    pair_top, pair_bottom = to_diagonal(pair_x, pair_y, size, block, "cross_2")
    from_2x, from_2y = to_plane(from_2)
    hand_3, hand_1 = call(hand_kernel, [slab(2 * first_rows)] * 2, (pos, early_3, early_1), [], 0, "hand", 16)
    early_2a = move(hand_3, lon_by(1))
    early_2b = move(hand_1, lon_by(-1))

    def late_piece(which, row=0):
        return ((which, row + size - 16), (0, which, row))

    def early_piece(which, row):
        return ((which, row + cut), (0, which, row))

    pieces = [((which, end), (0, which, 0)) for which in range(3)]
    pieces.append(((4, end - own_cut), (0, 3, 0), (own_cut // span, 4, 0)))
    total, token = unpack(
        pos, total, [own, own_x, own_y, own_top, own_bottom], [block], [(0, 0, 27, pieces)], span, "unpack_1"
    )
    from_2top, from_2bottom = to_diagonal(from_2x, from_2y, late_cut, token, "cross_3")
    slabs = [
        (3, early, 27 - early, [late_piece(0), late_piece(2), late_piece(3), late_piece(4)]),
        (1, early, 27 - early, [late_piece(1), late_piece(2, size), late_piece(3, size), late_piece(5)]),
        (3, 0, early, [early_piece(6, tag * first_rows) for tag in range(4)]),
        (1, 0, early, [early_piece(7, tag * first_rows) for tag in range(4)]),
    ]
    total, _ = unpack(
        pos,
        total,
        [from_3, from_1, pair_x, pair_y, pair_top, pair_bottom, early_3, early_1],
        [hand_3],
        slabs,
        span,
        "unpack_2",
    )
    pieces = [late_piece(2), late_piece(3), late_piece(4)]
    pieces.append(((6, size - 16 - late_cut), (0, 5, 0), (late_cut // span, 6, 0)))
    slabs = [
        (2, 0, early, [early_piece(tag // 2, tag % 2 * first_rows) for tag in range(4)]),
        (2, early, 27 - early, pieces),
    ]
    total, _ = unpack(
        pos,
        total,
        [early_2a, early_2b, from_2, from_2x, from_2y, from_2top, from_2bottom],
        [],
        slabs,
        span,
        "unpack_3",
    )
    return (jnp.transpose(field, (3, 0, 1, 2)), jnp.transpose(total, (1, 0, 2)))


def body(inputs, weights, out_grad):
    chans, levels, height, width = inputs.shape
    shape = tuple(lax.axis_size(axis) for axis in AXES)
    fits = (
        shape == (2, 4, 4)
        and chans == out_grad.shape[0] == 256
        and weights.shape[2] == 512
        and levels % 2 == 0
        and height % 2 == 0
        and width % 16 == 0
    )
    return (blocked_body if fits else plain_body)(inputs, weights, out_grad)


def solution(mesh):
    in_specs = (P("ch", None, "lat", "lon"), P("ch", None, None), P("ch", None, "lat", "lon"))
    out_specs = (P("ch", None, "lat", "lon"), P("ch", None, None))
    return jax.shard_map(body, mesh=mesh, in_specs=in_specs, out_specs=out_specs, check_vma=False)
```

```python
import math

import jax
import jax.numpy as jnp
from jax import lax
from jax.experimental import pallas as pl
from jax.experimental.pallas import tpu as pltpu
from jax.sharding import PartitionSpec as P

VMEM = pltpu.VMEM
SMEM = pltpu.SMEM
AXES = ("ch", "lat", "lon")


def padded_2(cells, sides, width):
    for axis, dim in sides:
        count = lax.axis_size(axis)
        head = lax.slice_in_dim(cells, 0, width, axis=dim)
        tail = lax.slice_in_dim(cells, cells.shape[dim] - width, cells.shape[dim], axis=dim)
        cells = jnp.concatenate(
            [
                lax.ppermute(tail, axis, [(i, (i + 1) % count) for i in range(count)]),
                cells,
                lax.ppermute(head, axis, [((i + 1) % count, i) for i in range(count)]),
            ],
            axis=dim,
        )
    return cells


def mask_rims(padded):
    count = lax.axis_size("lat")
    where_lat = lax.axis_index("lat")
    lines = jnp.arange(padded.shape[2])
    drop = (lines == 0) & (where_lat == 0) | (lines == padded.shape[2] - 1) & (
        where_lat == count - 1
    )
    return jnp.where(drop[None, None, :, None], jnp.zeros((), padded.dtype), padded)


def pad_levels(field):
    return jnp.pad(field, ((0, 0), (1, 1), (0, 0), (0, 0)))


def plain_body(inputs, weights, out_grad):
    chans, levels, height, width = inputs.shape
    input_pad = pad_levels(mask_rims(padded_2(inputs, (("lat", 2), ("lon", 3)), 1)))
    grad_inner = lax.all_gather(out_grad, "ch", axis=0, tiled=True)
    grad_pad = pad_levels(mask_rims(padded_2(grad_inner, (("lat", 2), ("lon", 3)), 1)))
    filters = grad_pad.shape[0]
    products = jnp.dot(
        weights.reshape(chans * 27, filters),
        grad_pad.reshape(filters, -1),
        preferred_element_type=jnp.float32,
    )
    products = products.reshape((chans, 27) + tuple(grad_pad.shape[1:]))
    total = jnp.zeros((chans, levels, height, width), jnp.float32)
    pieces = []
    for tap in range(27):
        lev, lat, lon = tap // 9 - 1, tap // 3 % 3 - 1, tap % 3 - 1
        total = (
            total
            + products[
                :,
                tap,
                1 - lev : 1 - lev + levels,
                1 - lat : 1 - lat + height,
                1 - lon : 1 - lon + width,
            ]
        )
        pieces.append(
            input_pad[
                :,
                1 + lev : 1 + lev + levels,
                1 + lat : 1 + lat + height,
                1 + lon : 1 + lon + width,
            ]
        )
    columns = jnp.stack(pieces, axis=1).reshape(chans * 27, -1)
    partial_grad = lax.dot_general(
        columns,
        grad_inner.reshape(filters, -1),
        (((1,), (1,)), ((), ())),
        preferred_element_type=jnp.float32,
    )
    summed = lax.psum(partial_grad, ("lat", "lon"))
    cells = levels * height * width * lax.axis_size("lat") * lax.axis_size("lon")
    weight_grad = (summed * (1.0 / math.sqrt(cells))).reshape(chans, 27, filters)
    return (total.astype(jnp.bfloat16), weight_grad)


def move(x, target):
    pairs = []
    for i in range(32):
        to = target(i // 16, i // 4 % 4, i % 4)
        if to is not None:
            pairs.append((i, (to[0] * 4 + to[1]) * 4 + to[2]))
    return lax.ppermute(x, AXES, pairs)


def lon_by(step):
    return lambda c, a, o: (c, a, (o + step) % 4)


def lat_xor(mask):
    return lambda c, a, o: (c, a ^ mask, o)


def sibling(c, a, o):
    return (1 - c, a, o)


def call(kernel, outs, ins, scratch, flops, name, limit, held=0):
    read = len(ins) - 1 - held
    moved = sum(math.prod(x.shape) * x.dtype.itemsize for x in list(ins[1 : 1 + read]) + list(outs))
    return pl.pallas_call(
        kernel,
        out_shape=outs,
        in_specs=[pl.BlockSpec(memory_space=SMEM)]
        + [pl.BlockSpec(memory_space=VMEM)] * read
        + [pl.BlockSpec(memory_space=pl.ANY)] * held,
        out_specs=[pl.BlockSpec(memory_space=VMEM)] * len(outs),
        scratch_shapes=scratch,
        cost_estimate=pl.CostEstimate(flops=flops, bytes_accessed=moved, transcendentals=0),
        compiler_params=pltpu.CompilerParams(vmem_limit_bytes=limit * 1024 * 1024),
        name=name,
    )(*ins)


def pack_kernel(pos, x, g, g_same, g_other, x0, x1, x2, x3, rim_x, rim_d, held):
    levels, height, width, chans = x.shape
    half, wide = levels // 2, chans // 2
    right = lax.rem(pos[1], 2)
    for out, at in ((g_same, right), (g_other, 1 - right)):
        out[...] = g[:, :, :, pl.ds(pl.multiple_of(at * wide, wide), wide)].reshape(out.shape)
    many = x0.shape[0]
    for block in range(4):
        at = block * (chans // 4)
        lo = x[0:half, :, :, at : at + chans // 4]
        hi = x[half:levels, :, :, at : at + chans // 4]
        held[block] = jnp.concatenate([lo, hi], axis=-1).reshape(held.shape[1:])
    lon = pos[2]
    for step, out in enumerate((x0, x1, x2, x3)):
        out[0:many, :] = held[lax.rem(lon + step, 4)]
    for out, column in ((x1, width - 1), (x3, 0)):
        rim = g[:, :, column, :].reshape(levels * height, chans)
        out[many : many + levels * height, :] = rim[:, 0:wide]
        out[many + levels * height :, :] = rim[:, wide:]
    even = right == 0
    low, high = g[:, 0], g[:, height - 1]
    line = levels * width
    for out, upward in ((rim_x, even), (rim_d, jnp.logical_not(even))):
        facing = jnp.where(upward, high, low).reshape(line, chans)
        for at in range(2):
            out[at * line : (at + 1) * line, :] = facing[:, at * wide : (at + 1) * wide]


def spread_kernel(pos, x0, x1, x2, x3, own, own_y):
    del pos
    many = x0.shape[0]
    for at, piece in enumerate((x0, x1, x2, x3)):
        own[at * many : (at + 1) * many, :] = piece[0:many, :]
        own_y[at * many : (at + 1) * many, :] = piece[0:many, :]
    extra = x1.shape[0] - many
    own[4 * many : 4 * many + extra, :] = x1[many:, :]
    own[4 * many + extra :, :] = x3[many:, :]


def split_kernel(
    pos, here, west, east, g, own, x_x, x_d, by_x, by_d, after, first, second, near, mine
):
    del after
    first[...] = west[0]
    second[...] = east[1]
    for at, part in enumerate((here, west, east)):
        near[2 * at : 2 * at + 2] = part[...]

    levels, height, width, chans = g.shape
    edge, line, wide = levels * height, levels * width, chans // 2
    inner = own.shape[0] - 4 * edge
    mine[:, 1 : height + 1, 0:width, :] = g[...]

    def columns(message, rows):
        for side in range(2):
            for half in range(2):
                start = inner + (2 * side + half) * edge
                rim = message[start : start + edge, :].reshape(levels, height, wide)
                at = width + 8 * side
                for row, to in rows:
                    mine[:, to, at : at + 8, half * wide : (half + 1) * wide] = jnp.broadcast_to(
                        rim[:, row : row + 1], (levels, 8, wide)
                    )

    columns(own, [(row, row + 1) for row in range(height)])

    def lines(strip, message, row, to):
        for half in range(2):
            part = strip[half * line : (half + 1) * line, :]
            mine[:, to, 0:width, half * wide : (half + 1) * wide] = part.reshape(levels, width, wide)
        columns(message, [(row, to)])

    lat = pos[1]
    odd = lax.rem(lat, 2)

    @pl.when(odd == 1)
    def _():
        lines(by_x, x_x, height - 1, 0)
        lines(by_d, x_d, 0, height + 1)

    @pl.when(odd == 0)
    def _():
        lines(by_d, x_d, height - 1, 0)
        lines(by_x, x_x, 0, height + 1)

    @pl.when(lat == 0)
    def _():
        mine[:, 0] = jnp.zeros_like(mine[:, 0])

    @pl.when(lat == 3)
    def _():
        mine[:, height + 1] = jnp.zeros_like(mine[:, height + 1])


def pair_kernel(pos, one, two, after, both):
    del pos, after
    both[0] = one[...]
    both[1] = two[...]


def lines_kernel(pos, x_own, x_x, x_y, x_d, after, xs, blank):
    del after, blank
    lat = pos[1]
    levels, rows, circle, lanes = xs.shape
    rows, width, span, half = rows - 2, circle // 4, lanes // 4, levels // 2
    height = rows // 4
    many = half * height * width
    xs[:, 0] = jnp.zeros_like(xs[:, 0])
    xs[:, rows + 1] = jnp.zeros_like(xs[:, rows + 1])
    low = lax.broadcasted_iota(jnp.int32, (circle, 2 * span), 1) < span
    for tag, ref in enumerate((x_own, x_x, x_y, x_d)):
        start = (lat ^ tag) * height
        strips = [
            ref.at[pl.ds((4 - at) % 4 * many, many)].reshape(half, height, width, 2 * span) for at in range(4)
        ]

        @pl.loop(0, half * height)
        def _(step, strips=strips, start=start):
            lev, row = step // height, lax.rem(step, height)
            line = jnp.concatenate([s[lev, row] for s in strips], axis=0).astype(jnp.float32)
            turned = pltpu.roll(line, span, 1)
            for upper in range(2):
                same = jnp.where(low, turned, line) if upper else jnp.where(low, line, turned)
                before = pltpu.roll(same, 1, 0)
                after = pltpu.roll(same, circle - 1, 0)
                at = upper * half + lev
                xs[at, 1 + start + row, :, 0 : 2 * span] = jnp.where(low, before, same).astype(xs.dtype)
                xs[at, 1 + start + row, :, 2 * span : 4 * span] = after.astype(xs.dtype)


def turn(gt, slot, core, first, second, levels):
    many, filters = first.shape
    line = many // levels
    for lev in range(levels):
        block = jnp.concatenate([first[lev * line : (lev + 1) * line], second[lev * line : (lev + 1) * line]], axis=0)
        gt[
            lev * filters : (lev + 1) * filters,
            pl.ds(pl.multiple_of((2 * slot + core) * 2 * line, 2 * line), 2 * line),
        ] = block.T


def taps_kernel(pos, xs, g, s, g2, s2, out, gt, acc):
    levels, rows, circle, lanes = xs.shape
    rows, width, span = rows - 2, circle // 4, lanes // 4
    filters = gt.shape[0] // levels
    deep = rows * width
    right = lax.rem(pos[1], 2)
    for core, parts, last in ((pos[0], g, g2), (1 - pos[0], s, s2)):
        for slot, (ref, at) in enumerate(((parts, 0), (parts, 4), (last, 0), (parts, 2))):
            turn(gt, slot, core, ref[at + right], ref[at + 1 - right], levels)
    acc[...] = jnp.zeros_like(acc)

    @pl.loop(0, 3)
    def _(lat_by):
        for lev in range(levels):
            first, last = max(lev - 1, 0), min(lev + 1, levels - 1)
            to = (first - lev + 1) * filters
            many = (last - first + 1) * filters
            total = acc[lat_by, to : to + many, :]
            for place in range(4):
                total += jnp.dot(
                    gt[first * filters : (last + 1) * filters, place * deep : (place + 1) * deep],
                    xs[lev, pl.ds(lat_by, rows), place * width : (place + 1) * width].reshape(deep, lanes),
                    preferred_element_type=jnp.float32,
                )
            acc[lat_by, to : to + many, :] = total

    scale = 1.0 / math.sqrt(levels * rows * circle)
    for lat_by in range(3):
        for lev_at in range(3):
            block = acc[lat_by, lev_at * filters : (lev_at + 1) * filters, :].T * scale
            for lon_at in range(3):
                out[(2 - lev_at) * 9 + lat_by * 3 + lon_at] = block[lon_at * span : (lon_at + 1) * span]


def code_kernel(pos, held, after, out, late):
    del pos, after
    taps, span, filters = held.shape
    most = jnp.abs(held[0])
    for tap in range(1, taps):
        most = jnp.maximum(most, jnp.abs(held[tap]))
    top = jnp.maximum(jnp.max(most, axis=(0, 1), keepdims=True), 1e-30)
    power = jnp.ceil(jnp.log(top) * (1.0 / math.log(2.0))) - 15.0
    unit = jnp.broadcast_to(jnp.exp2(power), (16, filters)).astype(out.dtype).astype(jnp.float32)
    shrink = 1.0 / unit[0:1]
    unit = unit.astype(out.dtype)
    skip = out.shape[0] - late.shape[0]
    for tap in range(taps):
        value = held[tap] * shrink
        square = value * value
        code = (square * value * jnp.abs(value)).astype(out.dtype)
        out[tap * span : (tap + 1) * span, :] = code
        if tap * span >= skip:
            late[tap * span - skip : (tap + 1) * span - skip, :] = code
    out[taps * span :, :] = unit
    late[taps * span - skip :, :] = unit


def both_kernel(pos, west, east, after1, after2, both, half_3, half_1):
    del pos, after1, after2
    size, half = west.shape[0], half_3.shape[0]
    both[0:size, :] = west[...]
    both[size:, :] = east[...]
    half_3[...] = west[0:half, :]
    half_1[...] = east[half:, :]


def cross_kernel(pos, by_x, by_y, after, top, bottom):
    del pos, after
    cut = top.shape[0]
    top[...] = by_y[0:cut, :]
    bottom[...] = by_x[cut:, :]


def across_kernel(pos, half_3, half_1, after, late):
    del pos, after
    half = half_3.shape[0]
    late[0:half, :] = half_3[...]
    late[half:, :] = half_1[...]


def block_kernel(pos, own, x, y, top, bottom, after, block):
    del pos, after
    rows = block.shape[0] // 4
    for at, (piece, end) in enumerate(((own, own), (x, x), (y, y), (top, bottom))):
        block[at * rows : (at + 1) * rows - 16, :] = piece[0 : rows - 16, :]
        block[(at + 1) * rows - 16 : (at + 1) * rows, :] = end[end.shape[0] - 16 :, :]


def hand_kernel(pos, block_3, block_1, first, second):
    del pos
    many = first.shape[0]
    first[...] = block_3[0:many, :]
    second[...] = block_1[many:, :]


def unpack_kernel(pos, *refs, slabs, count, span):
    sources = refs[:count]
    total, token, buffers, sems = refs[-4:]
    slots, group = buffers.shape[:2]
    wide = buffers.shape[-1] // 4
    token[...] = jnp.zeros_like(token)
    parts = []
    for step, first, taps, pieces in slabs:
        for at in range(0, taps, group):
            parts.append((step, first + at, min(group, taps - at), at, pieces))

    def copy(at):
        step, first, many, _, _ = parts[at]
        lon_at = pl.multiple_of(lax.rem(pos[2] + step, 4) * span, span)
        return pltpu.make_async_copy(
            buffers.at[at % slots, pl.ds(0, many)],
            total.at[pl.ds(first, many), pl.ds(lon_at, span)],
            sems.at[at % slots],
        )

    for at, (_, _, many, skip, pieces) in enumerate(parts):
        if at >= slots:
            copy(at - slots).wait()
        for tag, ((power_in, power_row), *segments) in enumerate(pieces):
            unit = sources[power_in][power_row : power_row + 16, :].astype(jnp.float32)[0:1]
            lanes = pl.ds(pl.multiple_of((pos[1] ^ tag) * wide, wide), wide)
            for tap in range(many):
                begin, which, row = [segment for segment in segments if segment[0] <= skip + tap][-1]
                start = row + (skip + tap - begin) * span
                code = sources[which][start : start + span, :].astype(jnp.float32)
                root = lax.rsqrt(lax.rsqrt(jnp.abs(code))) * unit
                buffers[at % slots, tap, :, lanes] = jnp.where(code < 0, -root, root)
        copy(at).start()
    for at in range(max(len(parts) - slots, 0), len(parts)):
        copy(at).wait()


def unpack(pos, total, sources, after, slabs, span, name):
    slots, group = 4, 3
    wide = total.shape[2]
    ins = (pos, *sources, *after, total)
    token = jax.ShapeDtypeStruct((8, 128), jnp.float32)
    return pl.pallas_call(
        lambda *refs: unpack_kernel(*refs, slabs=slabs, count=len(sources), span=span),
        out_shape=[jax.ShapeDtypeStruct(total.shape, total.dtype), token],
        in_specs=[pl.BlockSpec(memory_space=SMEM)]
        + [pl.BlockSpec(memory_space=VMEM)] * len(sources)
        + [pl.BlockSpec(memory_space=pl.ANY)] * (len(after) + 1),
        out_specs=[pl.BlockSpec(memory_space=pl.ANY), pl.BlockSpec(memory_space=VMEM)],
        scratch_shapes=[VMEM((slots, group, span, wide), jnp.float32), pltpu.SemaphoreType.DMA((slots,))],
        input_output_aliases={len(ins) - 1: 0},
        cost_estimate=pl.CostEstimate(flops=0, bytes_accessed=4 * 2**20, transcendentals=0),
        compiler_params=pltpu.CompilerParams(vmem_limit_bytes=51 * 1024 * 1024),
        name=name,
    )(*ins)


def field_kernel(pos, after, mine, theirs, w, out, copies, acc):
    del after
    step = pl.program_id(0)
    levels, height, width, chans = out.shape
    many = mine.shape[-1]

    @pl.when(step == 0)
    def _():
        copies[:, 0] = jnp.zeros_like(copies[:, 0])
        copies[:, levels + 1] = jnp.zeros_like(copies[:, levels + 1])
        line_at = lax.broadcasted_iota(jnp.int32, (width, many), 0)
        for which, field in ((pos[0], mine), (1 - pos[0], theirs)):
            lanes = pl.ds(pl.multiple_of(which * many, many), many)
            for lev in range(levels):
                for row in range(height + 2):
                    line = field[lev, row, 0:width].astype(jnp.float32)
                    west = field[lev, row, width : width + 1].astype(jnp.float32)
                    east = field[lev, row, width + 8 : width + 9].astype(jnp.float32)
                    before = jnp.where(line_at == 0, west, pltpu.roll(line, 1, 0))
                    later = jnp.where(line_at == width - 1, east, pltpu.roll(line, width - 1, 0))
                    copies[0, lev + 1, row, :, lanes] = later.astype(copies.dtype)
                    copies[1, lev + 1, row, :, lanes] = field[lev, row, 0:width]
                    copies[2, lev + 1, row, :, lanes] = before.astype(copies.dtype)
        acc[...] = jnp.zeros_like(acc)

    lev_by, lat_by = step // 3, lax.rem(step, 3)
    cells = [
        copies[at, pl.ds(2 - lev_by, levels), pl.ds(2 - lat_by, height)].reshape(
            levels * height * width, 2 * many
        )
        for at in range(3)
    ]
    acc[...] += lax.dot_general(
        jnp.concatenate(cells, axis=1),
        jnp.concatenate([w[at] for at in range(3)], axis=1),
        (((1,), (1,)), ((), ())),
        preferred_element_type=jnp.float32,
    )

    @pl.when(step == 8)
    def _():
        out[...] = acc[...].reshape(out.shape).astype(out.dtype)


def blocked_body(inputs, weights, out_grad):
    chans, levels, height, width = inputs.shape
    filters = weights.shape[2]
    bf16, f32 = jnp.bfloat16, jnp.float32
    lat, lon = lax.axis_index("lat"), lax.axis_index("lon")
    pos = jnp.stack([lax.axis_index("ch"), lat, lon]).astype(jnp.int32)
    x_cells = jnp.transpose(inputs, (1, 2, 3, 0))
    g_cells = jnp.transpose(out_grad, (1, 2, 3, 0))
    taps = jnp.transpose(weights, (1, 0, 2))
    cells = levels * height * width
    span, wide = chans // 4, filters // 4
    rows, circle = 4 * height, 4 * width
    edge = levels * height

    to_same = lambda c, a, o: (a // 2, 2 * c + a % 2, o)
    to_other = lambda c, a, o: (a // 2, 2 * c + 1 - a % 2, o)
    many = cells // 2
    block = jax.ShapeDtypeStruct((cells, wide), bf16)
    strip = jax.ShapeDtypeStruct((2 * levels * width, 2 * span), bf16)
    g_same, g_other, x0, x1, x2, x3, rim_x, rim_d = call(
        pack_kernel,
        [block, block]
        + [jax.ShapeDtypeStruct((many + extra, 2 * span), bf16) for extra in (0, 2 * edge, 0, 2 * edge)]
        + [strip, strip],
        (pos, x_cells, g_cells),
        [VMEM((4, many, 2 * span), bf16)],
        0,
        "pack",
        16,
    )
    g_s = move(g_same, to_same)
    g_o = move(g_other, to_other)
    x_r1 = move(x1, lon_by(1))
    x_r3 = move(x3, lon_by(-1))
    x_r2 = move(x2, lon_by(2))
    by_x = move(rim_x, lat_xor(1))
    by_d = move(rim_d, lat_xor(3))

    inner = 4 * many
    (g0,) = call(
        pair_kernel, [jax.ShapeDtypeStruct((2, cells, wide), bf16)], (pos, g_s, g_o, x0), [], 0, "pair_0", 16, held=1
    )
    x_own, x_own_y = call(
        spread_kernel,
        [jax.ShapeDtypeStruct((count, 2 * span), bf16) for count in (inner + 4 * edge, inner)],
        (pos, x0, x_r1, x_r2, x_r3),
        [],
        0,
        "spread",
        16,
    )
    x_x = move(x_own, lat_xor(1))
    x_d = move(x_own, lat_xor(3))
    x_y = move(x_own_y, lat_xor(2))
    g1 = move(g0, lon_by(1))
    g3 = move(g0, lon_by(-1))
    far_a, far_b, g_near, mine = call(
        split_kernel,
        [
            block,
            block,
            jax.ShapeDtypeStruct((6, cells, wide), bf16),
            jax.ShapeDtypeStruct((levels, height + 2, width + 16, chans), bf16),
        ],
        (pos, g0, g1, g3, g_cells, x_own, x_x, x_d, by_x, by_d, x_y),
        [],
        0,
        "split",
        16,
        held=1,
    )
    g2a = move(far_a, lon_by(1))
    g2b = move(far_b, lon_by(-1))
    s_near = move(g_near, sibling)
    theirs = move(mine, sibling)
    xs, total = pl.pallas_call(
        lines_kernel,
        out_shape=[
            jax.ShapeDtypeStruct((levels, rows + 2, circle, 4 * span), bf16),
            jax.ShapeDtypeStruct((27, chans, filters), f32),
        ],
        in_specs=[pl.BlockSpec(memory_space=SMEM)]
        + [pl.BlockSpec(memory_space=VMEM)] * 4
        + [pl.BlockSpec(memory_space=pl.ANY)],
        out_specs=[pl.BlockSpec(memory_space=VMEM)] + [pl.BlockSpec(memory_space=pl.ANY)],
        cost_estimate=pl.CostEstimate(flops=0, bytes_accessed=2**20, transcendentals=0),
        compiler_params=pltpu.CompilerParams(vmem_limit_bytes=24 * 1024 * 1024),
        name="lines",
    )(pos, x_own, x_x, x_y, x_d, far_a)
    (g2,) = call(
        pair_kernel, [jax.ShapeDtypeStruct((2, cells, wide), bf16)], (pos, g2a, g2b, xs), [], 0, "pair", 16, held=1
    )
    s2 = move(g2, sibling)
    early = 6
    cut, end = early * span, 27 * span
    size = end + 16 - cut
    half = size // 32 * 16
    first_rows = cut + 16
    own_cut, late_cut = 14 * span, (27 - early) // 2 * span
    slab = lambda count: jax.ShapeDtypeStruct((count, wide), bf16)
    (grads,) = call(
        taps_kernel,
        [jax.ShapeDtypeStruct((27, span, wide), f32)],
        (pos, xs, g_near, s_near, g2, s2),
        [VMEM((levels * wide, rows * circle), bf16), VMEM((3, 3 * wide, 4 * span), f32)],
        2 * 27 * span * wide * rows * circle * levels,
        "taps",
        28,
    )
    own, late = call(code_kernel, [slab(end + 16), slab(size)], (pos, grads, theirs), [], 0, "code", 16, held=1)

    whole = lambda t: (0, 0, 0, 0)
    field = pl.pallas_call(
        field_kernel,
        out_shape=jax.ShapeDtypeStruct((levels, height, width, chans), bf16),
        grid=(9,),
        in_specs=[
            pl.BlockSpec(memory_space=SMEM),
            pl.BlockSpec(memory_space=pl.ANY),
            pl.BlockSpec(mine.shape, whole),
            pl.BlockSpec(mine.shape, whole),
            pl.BlockSpec((3, chans, filters), lambda t: (t, 0, 0)),
        ],
        out_specs=pl.BlockSpec((levels, height, width, chans), whole),
        scratch_shapes=[
            VMEM((3, levels + 2, height + 2, width, filters), bf16),
            VMEM((cells, chans), f32),
        ],
        cost_estimate=pl.CostEstimate(
            flops=4 * 27 * chans * filters * cells, bytes_accessed=27 * chans * filters * 2, transcendentals=0
        ),
        compiler_params=pltpu.CompilerParams(vmem_limit_bytes=20 * 1024 * 1024),
        name="field",
    )(pos, own, mine, theirs, taps)

    def to_plane(share):
        return move(share, lat_xor(1)), move(share, lat_xor(2))

    def to_diagonal(by_x, by_y, cut, after, name):
        top, bottom = call(
            cross_kernel, [slab(cut), slab(by_x.shape[0] - cut)], (pos, by_x, by_y, after), [], 0, name, 16, held=1
        )
        return move(top, lat_xor(1)), move(bottom, lat_xor(2))

    from_3 = move(late, lon_by(1))
    from_1 = move(late, lon_by(-1))
    own_x, own_y = to_plane(own)
    own_top, own_bottom = to_diagonal(own_x, own_y, own_cut, field, "cross_1")
    pair, half_3, half_1 = call(
        both_kernel,
        [slab(2 * size), slab(half), slab(size - half)],
        (pos, from_3, from_1, own_top, own_bottom),
        [],
        0,
        "both",
        16,
        held=2,
    )
    half_3 = move(half_3, lon_by(1))
    half_1 = move(half_1, lon_by(-1))
    pair_x, pair_y = to_plane(pair)
    (block,) = call(
        block_kernel, [slab(4 * first_rows)], (pos, own, own_x, own_y, own_top, own_bottom, half_3), [], 0, "block", 16, held=1
    )
    early_3 = move(block, lon_by(1))
    early_1 = move(block, lon_by(-1))
    (from_2,) = call(across_kernel, [slab(size)], (pos, half_3, half_1, block), [], 0, "across", 16, held=1)
    pair_top, pair_bottom = to_diagonal(pair_x, pair_y, size, block, "cross_2")
    from_2x, from_2y = to_plane(from_2)
    hand_3, hand_1 = call(hand_kernel, [slab(2 * first_rows)] * 2, (pos, early_3, early_1), [], 0, "hand", 16)
    early_2a = move(hand_3, lon_by(1))
    early_2b = move(hand_1, lon_by(-1))

    def late_piece(which, row=0):
        return ((which, row + size - 16), (0, which, row))

    def early_piece(which, row):
        return ((which, row + cut), (0, which, row))

    pieces = [((which, end), (0, which, 0)) for which in range(3)]
    pieces.append(((4, end - own_cut), (0, 3, 0), (own_cut // span, 4, 0)))
    total, token = unpack(
        pos, total, [own, own_x, own_y, own_top, own_bottom], [block], [(0, 0, 27, pieces)], span, "unpack_1"
    )
    from_2top, from_2bottom = to_diagonal(from_2x, from_2y, late_cut, token, "cross_3")
    slabs = [
        (3, early, 27 - early, [late_piece(0), late_piece(2), late_piece(3), late_piece(4)]),
        (1, early, 27 - early, [late_piece(1), late_piece(2, size), late_piece(3, size), late_piece(5)]),
        (3, 0, early, [early_piece(6, tag * first_rows) for tag in range(4)]),
        (1, 0, early, [early_piece(7, tag * first_rows) for tag in range(4)]),
    ]
    total, _ = unpack(
        pos,
        total,
        [from_3, from_1, pair_x, pair_y, pair_top, pair_bottom, early_3, early_1],
        [hand_3],
        slabs,
        span,
        "unpack_2",
    )
    pieces = [late_piece(2), late_piece(3), late_piece(4)]
    pieces.append(((6, size - 16 - late_cut), (0, 5, 0), (late_cut // span, 6, 0)))
    slabs = [
        (2, 0, early, [early_piece(tag // 2, tag % 2 * first_rows) for tag in range(4)]),
        (2, early, 27 - early, pieces),
    ]
    total, _ = unpack(
        pos,
        total,
        [early_2a, early_2b, from_2, from_2x, from_2y, from_2top, from_2bottom],
        [],
        slabs,
        span,
        "unpack_3",
    )
    return (jnp.transpose(field, (3, 0, 1, 2)), jnp.transpose(total, (1, 0, 2)))


def body(inputs, weights, out_grad):
    chans, levels, height, width = inputs.shape
    shape = tuple(lax.axis_size(axis) for axis in AXES)
    fits = (
        shape == (2, 4, 4)
        and chans == out_grad.shape[0] == 256
        and weights.shape[2] == 512
        and levels % 2 == 0
        and height % 2 == 0
        and width % 16 == 0
    )
    return (blocked_body if fits else plain_body)(inputs, weights, out_grad)


def solution(mesh):
    in_specs = (P("ch", None, "lat", "lon"), P("ch", None, None), P("ch", None, "lat", "lon"))
    out_specs = (P("ch", None, "lat", "lon"), P("ch", None, None))
    return jax.shard_map(body, mesh=mesh, in_specs=in_specs, out_specs=out_specs, check_vma=False)
```

```python
import math

import jax
import jax.numpy as jnp
from jax import lax
from jax.experimental import pallas as pl
from jax.experimental.pallas import tpu as pltpu
from jax.sharding import PartitionSpec as P

VMEM = pltpu.VMEM
SMEM = pltpu.SMEM
AXES = ("ch", "lat", "lon")


def padded_2(cells, sides, width):
    for axis, dim in sides:
        count = lax.axis_size(axis)
        head = lax.slice_in_dim(cells, 0, width, axis=dim)
        tail = lax.slice_in_dim(cells, cells.shape[dim] - width, cells.shape[dim], axis=dim)
        cells = jnp.concatenate(
            [
                lax.ppermute(tail, axis, [(i, (i + 1) % count) for i in range(count)]),
                cells,
                lax.ppermute(head, axis, [((i + 1) % count, i) for i in range(count)]),
            ],
            axis=dim,
        )
    return cells


def mask_rims(padded):
    count = lax.axis_size("lat")
    where_lat = lax.axis_index("lat")
    lines = jnp.arange(padded.shape[2])
    drop = (lines == 0) & (where_lat == 0) | (lines == padded.shape[2] - 1) & (
        where_lat == count - 1
    )
    return jnp.where(drop[None, None, :, None], jnp.zeros((), padded.dtype), padded)


def pad_levels(field):
    return jnp.pad(field, ((0, 0), (1, 1), (0, 0), (0, 0)))


def plain_body(inputs, weights, out_grad):
    chans, levels, height, width = inputs.shape
    input_pad = pad_levels(mask_rims(padded_2(inputs, (("lat", 2), ("lon", 3)), 1)))
    grad_inner = lax.all_gather(out_grad, "ch", axis=0, tiled=True)
    grad_pad = pad_levels(mask_rims(padded_2(grad_inner, (("lat", 2), ("lon", 3)), 1)))
    filters = grad_pad.shape[0]
    products = jnp.dot(
        weights.reshape(chans * 27, filters),
        grad_pad.reshape(filters, -1),
        preferred_element_type=jnp.float32,
    )
    products = products.reshape((chans, 27) + tuple(grad_pad.shape[1:]))
    total = jnp.zeros((chans, levels, height, width), jnp.float32)
    pieces = []
    for tap in range(27):
        lev, lat, lon = tap // 9 - 1, tap // 3 % 3 - 1, tap % 3 - 1
        total = (
            total
            + products[
                :,
                tap,
                1 - lev : 1 - lev + levels,
                1 - lat : 1 - lat + height,
                1 - lon : 1 - lon + width,
            ]
        )
        pieces.append(
            input_pad[
                :,
                1 + lev : 1 + lev + levels,
                1 + lat : 1 + lat + height,
                1 + lon : 1 + lon + width,
            ]
        )
    columns = jnp.stack(pieces, axis=1).reshape(chans * 27, -1)
    partial_grad = lax.dot_general(
        columns,
        grad_inner.reshape(filters, -1),
        (((1,), (1,)), ((), ())),
        preferred_element_type=jnp.float32,
    )
    summed = lax.psum(partial_grad, ("lat", "lon"))
    cells = levels * height * width * lax.axis_size("lat") * lax.axis_size("lon")
    weight_grad = (summed * (1.0 / math.sqrt(cells))).reshape(chans, 27, filters)
    return (total.astype(jnp.bfloat16), weight_grad)


def move(x, target):
    pairs = []
    for i in range(32):
        to = target(i // 16, i // 4 % 4, i % 4)
        if to is not None:
            pairs.append((i, (to[0] * 4 + to[1]) * 4 + to[2]))
    return lax.ppermute(x, AXES, pairs)


def lon_by(step):
    return lambda c, a, o: (c, a, (o + step) % 4)


def lat_xor(mask):
    return lambda c, a, o: (c, a ^ mask, o)


def sibling(c, a, o):
    return (1 - c, a, o)


def call(kernel, outs, ins, scratch, flops, name, limit, held=0):
    read = len(ins) - 1 - held
    moved = sum(math.prod(x.shape) * x.dtype.itemsize for x in list(ins[1 : 1 + read]) + list(outs))
    return pl.pallas_call(
        kernel,
        out_shape=outs,
        in_specs=[pl.BlockSpec(memory_space=SMEM)]
        + [pl.BlockSpec(memory_space=VMEM)] * read
        + [pl.BlockSpec(memory_space=pl.ANY)] * held,
        out_specs=[pl.BlockSpec(memory_space=VMEM)] * len(outs),
        scratch_shapes=scratch,
        cost_estimate=pl.CostEstimate(flops=flops, bytes_accessed=moved, transcendentals=0),
        compiler_params=pltpu.CompilerParams(vmem_limit_bytes=limit * 1024 * 1024),
        name=name,
    )(*ins)


def pack_kernel(pos, x, g, g_same, g_other, x0, x1, x2, x3, rim_x, rim_d, held):
    levels, height, width, chans = x.shape
    half, wide = levels // 2, chans // 2
    right = lax.rem(pos[1], 2)
    for out, at in ((g_same, right), (g_other, 1 - right)):
        out[...] = g[:, :, :, pl.ds(pl.multiple_of(at * wide, wide), wide)].reshape(out.shape)
    many = x0.shape[0]
    for block in range(4):
        at = block * (chans // 4)
        lo = x[0:half, :, :, at : at + chans // 4]
        hi = x[half:levels, :, :, at : at + chans // 4]
        held[block] = jnp.concatenate([lo, hi], axis=-1).reshape(held.shape[1:])
    lon = pos[2]
    for step, out in enumerate((x0, x1, x2, x3)):
        out[0:many, :] = held[lax.rem(lon + step, 4)]
    for out, column in ((x1, width - 1), (x3, 0)):
        rim = g[:, :, column, :].reshape(levels * height, chans)
        out[many : many + levels * height, :] = rim[:, 0:wide]
        out[many + levels * height :, :] = rim[:, wide:]
    even = right == 0
    low, high = g[:, 0], g[:, height - 1]
    line = levels * width
    for out, upward in ((rim_x, even), (rim_d, jnp.logical_not(even))):
        facing = jnp.where(upward, high, low).reshape(line, chans)
        for at in range(2):
            out[at * line : (at + 1) * line, :] = facing[:, at * wide : (at + 1) * wide]


def spread_kernel(pos, x0, x1, x2, x3, own, own_y):
    del pos
    many = x0.shape[0]
    for at, piece in enumerate((x0, x1, x2, x3)):
        own[at * many : (at + 1) * many, :] = piece[0:many, :]
        own_y[at * many : (at + 1) * many, :] = piece[0:many, :]
    extra = x1.shape[0] - many
    own[4 * many : 4 * many + extra, :] = x1[many:, :]
    own[4 * many + extra :, :] = x3[many:, :]


def split_kernel(
    pos, here, west, east, g, own, x_x, x_d, by_x, by_d, after, first, second, near, mine
):
    del after
    first[...] = west[0]
    second[...] = east[1]
    for at, part in enumerate((here, west, east)):
        near[2 * at : 2 * at + 2] = part[...]

    levels, height, width, chans = g.shape
    edge, line, wide = levels * height, levels * width, chans // 2
    inner = own.shape[0] - 4 * edge
    mine[:, 1 : height + 1, 0:width, :] = g[...]

    def columns(message, rows):
        for side in range(2):
            for half in range(2):
                start = inner + (2 * side + half) * edge
                rim = message[start : start + edge, :].reshape(levels, height, wide)
                at = width + 8 * side
                for row, to in rows:
                    mine[:, to, at : at + 8, half * wide : (half + 1) * wide] = jnp.broadcast_to(
                        rim[:, row : row + 1], (levels, 8, wide)
                    )

    columns(own, [(row, row + 1) for row in range(height)])

    def lines(strip, message, row, to):
        for half in range(2):
            part = strip[half * line : (half + 1) * line, :]
            mine[:, to, 0:width, half * wide : (half + 1) * wide] = part.reshape(levels, width, wide)
        columns(message, [(row, to)])

    lat = pos[1]
    odd = lax.rem(lat, 2)

    @pl.when(odd == 1)
    def _():
        lines(by_x, x_x, height - 1, 0)
        lines(by_d, x_d, 0, height + 1)

    @pl.when(odd == 0)
    def _():
        lines(by_d, x_d, height - 1, 0)
        lines(by_x, x_x, 0, height + 1)

    @pl.when(lat == 0)
    def _():
        mine[:, 0] = jnp.zeros_like(mine[:, 0])

    @pl.when(lat == 3)
    def _():
        mine[:, height + 1] = jnp.zeros_like(mine[:, height + 1])


def pair_kernel(pos, one, two, after, both):
    del pos, after
    both[0] = one[...]
    both[1] = two[...]


def lines_kernel(pos, x_own, x_x, x_y, x_d, after, xs, blank):
    del after, blank
    lat = pos[1]
    levels, rows, circle, lanes = xs.shape
    rows, width, span, half = rows - 2, circle // 4, lanes // 4, levels // 2
    height = rows // 4
    many = half * height * width
    xs[:, 0] = jnp.zeros_like(xs[:, 0])
    xs[:, rows + 1] = jnp.zeros_like(xs[:, rows + 1])
    low = lax.broadcasted_iota(jnp.int32, (circle, 2 * span), 1) < span
    for tag, ref in enumerate((x_own, x_x, x_y, x_d)):
        start = (lat ^ tag) * height
        strips = [
            ref.at[pl.ds((4 - at) % 4 * many, many)].reshape(half, height, width, 2 * span) for at in range(4)
        ]

        @pl.loop(0, half * height)
        def _(step, strips=strips, start=start):
            lev, row = step // height, lax.rem(step, height)
            line = jnp.concatenate([s[lev, row] for s in strips], axis=0).astype(jnp.float32)
            turned = pltpu.roll(line, span, 1)
            for upper in range(2):
                same = jnp.where(low, turned, line) if upper else jnp.where(low, line, turned)
                before = pltpu.roll(same, 1, 0)
                after = pltpu.roll(same, circle - 1, 0)
                at = upper * half + lev
                xs[at, 1 + start + row, :, 0 : 2 * span] = jnp.where(low, before, same).astype(xs.dtype)
                xs[at, 1 + start + row, :, 2 * span : 4 * span] = after.astype(xs.dtype)


def turn(gt, slot, core, first, second, levels):
    many, filters = first.shape
    line = many // levels
    for lev in range(levels):
        block = jnp.concatenate([first[lev * line : (lev + 1) * line], second[lev * line : (lev + 1) * line]], axis=0)
        gt[
            lev * filters : (lev + 1) * filters,
            pl.ds(pl.multiple_of((2 * slot + core) * 2 * line, 2 * line), 2 * line),
        ] = block.T


def taps_kernel(pos, xs, g, s, g2, s2, out, gt, acc):
    levels, rows, circle, lanes = xs.shape
    rows, width, span = rows - 2, circle // 4, lanes // 4
    filters = gt.shape[0] // levels
    deep = rows * width
    right = lax.rem(pos[1], 2)
    for core, parts, last in ((pos[0], g, g2), (1 - pos[0], s, s2)):
        for slot, (ref, at) in enumerate(((parts, 0), (parts, 4), (last, 0), (parts, 2))):
            turn(gt, slot, core, ref[at + right], ref[at + 1 - right], levels)
    acc[...] = jnp.zeros_like(acc)

    @pl.loop(0, 3)
    def _(lat_by):
        for lev in range(levels):
            first, last = max(lev - 1, 0), min(lev + 1, levels - 1)
            to = (first - lev + 1) * filters
            many = (last - first + 1) * filters
            total = acc[lat_by, to : to + many, :]
            for place in range(4):
                total += jnp.dot(
                    gt[first * filters : (last + 1) * filters, place * deep : (place + 1) * deep],
                    xs[lev, pl.ds(lat_by, rows), place * width : (place + 1) * width].reshape(deep, lanes),
                    preferred_element_type=jnp.float32,
                )
            acc[lat_by, to : to + many, :] = total

    scale = 1.0 / math.sqrt(levels * rows * circle)
    for lat_by in range(3):
        for lev_at in range(3):
            block = acc[lat_by, lev_at * filters : (lev_at + 1) * filters, :].T * scale
            for lon_at in range(3):
                out[(2 - lev_at) * 9 + lat_by * 3 + lon_at] = block[lon_at * span : (lon_at + 1) * span]


def code_kernel(pos, held, after, out, late):
    del pos, after
    taps, span, filters = held.shape
    most = jnp.abs(held[0])
    for tap in range(1, taps):
        most = jnp.maximum(most, jnp.abs(held[tap]))
    top = jnp.maximum(jnp.max(most, axis=(0, 1), keepdims=True), 1e-30)
    power = jnp.ceil(jnp.log(top) * (1.0 / math.log(2.0))) - 15.0
    unit = jnp.broadcast_to(jnp.exp2(power), (16, filters)).astype(out.dtype).astype(jnp.float32)
    shrink = 1.0 / unit[0:1]
    unit = unit.astype(out.dtype)
    skip = out.shape[0] - late.shape[0]
    for tap in range(taps):
        value = held[tap] * shrink
        square = value * value
        code = (square * value * jnp.abs(value)).astype(out.dtype)
        out[tap * span : (tap + 1) * span, :] = code
        if tap * span >= skip:
            late[tap * span - skip : (tap + 1) * span - skip, :] = code
    out[taps * span :, :] = unit
    late[taps * span - skip :, :] = unit


def both_kernel(pos, west, east, after1, after2, both, half_3, half_1):
    del pos, after1, after2
    size, half = west.shape[0], half_3.shape[0]
    both[0:size, :] = west[...]
    both[size:, :] = east[...]
    half_3[...] = west[0:half, :]
    half_1[...] = east[half:, :]


def cross_kernel(pos, by_x, by_y, after1, after2, top, bottom):
    del pos, after1, after2
    cut = top.shape[0]
    top[...] = by_y[0:cut, :]
    bottom[...] = by_x[cut:, :]


def across_kernel(pos, half_3, half_1, after, late):
    del pos, after
    half = half_3.shape[0]
    late[0:half, :] = half_3[...]
    late[half:, :] = half_1[...]


def block_kernel(pos, own, x, y, top, bottom, block):
    del pos
    rows = block.shape[0] // 4
    for at, (piece, end) in enumerate(((own, own), (x, x), (y, y), (top, bottom))):
        block[at * rows : (at + 1) * rows - 16, :] = piece[0 : rows - 16, :]
        block[(at + 1) * rows - 16 : (at + 1) * rows, :] = end[end.shape[0] - 16 :, :]


def hand_kernel(pos, block_3, block_1, first, second):
    del pos
    many = first.shape[0]
    first[...] = block_3[0:many, :]
    second[...] = block_1[many:, :]


def unpack_kernel(pos, *refs, slabs, count, span):
    sources = refs[:count]
    total, token, buffers, sems = refs[-4:]
    slots, group = buffers.shape[:2]
    wide = buffers.shape[-1] // 4
    token[...] = jnp.zeros_like(token)
    parts = []
    for step, first, taps, pieces in slabs:
        for at in range(0, taps, group):
            parts.append((step, first + at, min(group, taps - at), at, pieces))

    def copy(at):
        step, first, many, _, _ = parts[at]
        lon_at = pl.multiple_of(lax.rem(pos[2] + step, 4) * span, span)
        return pltpu.make_async_copy(
            buffers.at[at % slots, pl.ds(0, many)],
            total.at[pl.ds(first, many), pl.ds(lon_at, span)],
            sems.at[at % slots],
        )

    for at, (_, _, many, skip, pieces) in enumerate(parts):
        if at >= slots:
            copy(at - slots).wait()
        for tag, ((power_in, power_row), *segments) in enumerate(pieces):
            unit = sources[power_in][power_row : power_row + 16, :].astype(jnp.float32)[0:1]
            lanes = pl.ds(pl.multiple_of((pos[1] ^ tag) * wide, wide), wide)
            for tap in range(many):
                begin, which, row = [segment for segment in segments if segment[0] <= skip + tap][-1]
                start = row + (skip + tap - begin) * span
                code = sources[which][start : start + span, :].astype(jnp.float32)
                root = lax.rsqrt(lax.rsqrt(jnp.abs(code))) * unit
                buffers[at % slots, tap, :, lanes] = jnp.where(code < 0, -root, root)
        copy(at).start()
    for at in range(max(len(parts) - slots, 0), len(parts)):
        copy(at).wait()


def unpack(pos, total, sources, after, slabs, span, name):
    slots, group = 4, 3
    wide = total.shape[2]
    ins = (pos, *sources, *after, total)
    token = jax.ShapeDtypeStruct((8, 128), jnp.float32)
    return pl.pallas_call(
        lambda *refs: unpack_kernel(*refs, slabs=slabs, count=len(sources), span=span),
        out_shape=[jax.ShapeDtypeStruct(total.shape, total.dtype), token],
        in_specs=[pl.BlockSpec(memory_space=SMEM)]
        + [pl.BlockSpec(memory_space=VMEM)] * len(sources)
        + [pl.BlockSpec(memory_space=pl.ANY)] * (len(after) + 1),
        out_specs=[pl.BlockSpec(memory_space=pl.ANY), pl.BlockSpec(memory_space=VMEM)],
        scratch_shapes=[VMEM((slots, group, span, wide), jnp.float32), pltpu.SemaphoreType.DMA((slots,))],
        input_output_aliases={len(ins) - 1: 0},
        cost_estimate=pl.CostEstimate(flops=0, bytes_accessed=4 * 2**20, transcendentals=0),
        compiler_params=pltpu.CompilerParams(vmem_limit_bytes=51 * 1024 * 1024),
        name=name,
    )(*ins)


def field_kernel(pos, after, mine, theirs, w, out, copies, acc):
    del after
    step = pl.program_id(0)
    levels, height, width, chans = out.shape
    many = mine.shape[-1]

    @pl.when(step == 0)
    def _():
        copies[:, 0] = jnp.zeros_like(copies[:, 0])
        copies[:, levels + 1] = jnp.zeros_like(copies[:, levels + 1])
        line_at = lax.broadcasted_iota(jnp.int32, (width, many), 0)
        for which, field in ((pos[0], mine), (1 - pos[0], theirs)):
            lanes = pl.ds(pl.multiple_of(which * many, many), many)
            for lev in range(levels):
                for row in range(height + 2):
                    line = field[lev, row, 0:width].astype(jnp.float32)
                    west = field[lev, row, width : width + 1].astype(jnp.float32)
                    east = field[lev, row, width + 8 : width + 9].astype(jnp.float32)
                    before = jnp.where(line_at == 0, west, pltpu.roll(line, 1, 0))
                    later = jnp.where(line_at == width - 1, east, pltpu.roll(line, width - 1, 0))
                    copies[0, lev + 1, row, :, lanes] = later.astype(copies.dtype)
                    copies[1, lev + 1, row, :, lanes] = field[lev, row, 0:width]
                    copies[2, lev + 1, row, :, lanes] = before.astype(copies.dtype)
        acc[...] = jnp.zeros_like(acc)

    lev_by, lat_by = step // 3, lax.rem(step, 3)
    cells = [
        copies[at, pl.ds(2 - lev_by, levels), pl.ds(2 - lat_by, height)].reshape(
            levels * height * width, 2 * many
        )
        for at in range(3)
    ]
    acc[...] += lax.dot_general(
        jnp.concatenate(cells, axis=1),
        jnp.concatenate([w[at] for at in range(3)], axis=1),
        (((1,), (1,)), ((), ())),
        preferred_element_type=jnp.float32,
    )

    @pl.when(step == 8)
    def _():
        out[...] = acc[...].reshape(out.shape).astype(out.dtype)


def blocked_body(inputs, weights, out_grad):
    chans, levels, height, width = inputs.shape
    filters = weights.shape[2]
    bf16, f32 = jnp.bfloat16, jnp.float32
    lat, lon = lax.axis_index("lat"), lax.axis_index("lon")
    pos = jnp.stack([lax.axis_index("ch"), lat, lon]).astype(jnp.int32)
    x_cells = jnp.transpose(inputs, (1, 2, 3, 0))
    g_cells = jnp.transpose(out_grad, (1, 2, 3, 0))
    taps = jnp.transpose(weights, (1, 0, 2))
    cells = levels * height * width
    span, wide = chans // 4, filters // 4
    rows, circle = 4 * height, 4 * width
    edge = levels * height

    to_same = lambda c, a, o: (a // 2, 2 * c + a % 2, o)
    to_other = lambda c, a, o: (a // 2, 2 * c + 1 - a % 2, o)
    many = cells // 2
    block = jax.ShapeDtypeStruct((cells, wide), bf16)
    strip = jax.ShapeDtypeStruct((2 * levels * width, 2 * span), bf16)
    g_same, g_other, x0, x1, x2, x3, rim_x, rim_d = call(
        pack_kernel,
        [block, block]
        + [jax.ShapeDtypeStruct((many + extra, 2 * span), bf16) for extra in (0, 2 * edge, 0, 2 * edge)]
        + [strip, strip],
        (pos, x_cells, g_cells),
        [VMEM((4, many, 2 * span), bf16)],
        0,
        "pack",
        16,
    )
    g_s = move(g_same, to_same)
    g_o = move(g_other, to_other)
    x_r1 = move(x1, lon_by(1))
    x_r3 = move(x3, lon_by(-1))
    x_r2 = move(x2, lon_by(2))
    by_x = move(rim_x, lat_xor(1))
    by_d = move(rim_d, lat_xor(3))

    inner = 4 * many
    (g0,) = call(
        pair_kernel, [jax.ShapeDtypeStruct((2, cells, wide), bf16)], (pos, g_s, g_o, x0), [], 0, "pair_0", 16, held=1
    )
    x_own, x_own_y = call(
        spread_kernel,
        [jax.ShapeDtypeStruct((count, 2 * span), bf16) for count in (inner + 4 * edge, inner)],
        (pos, x0, x_r1, x_r2, x_r3),
        [],
        0,
        "spread",
        16,
    )
    x_x = move(x_own, lat_xor(1))
    x_d = move(x_own, lat_xor(3))
    x_y = move(x_own_y, lat_xor(2))
    g1 = move(g0, lon_by(1))
    g3 = move(g0, lon_by(-1))
    far_a, far_b, g_near, mine = call(
        split_kernel,
        [
            block,
            block,
            jax.ShapeDtypeStruct((6, cells, wide), bf16),
            jax.ShapeDtypeStruct((levels, height + 2, width + 16, chans), bf16),
        ],
        (pos, g0, g1, g3, g_cells, x_own, x_x, x_d, by_x, by_d, x_y),
        [],
        0,
        "split",
        16,
        held=1,
    )
    g2a = move(far_a, lon_by(1))
    g2b = move(far_b, lon_by(-1))
    s_near = move(g_near, sibling)
    theirs = move(mine, sibling)
    xs, total = pl.pallas_call(
        lines_kernel,
        out_shape=[
            jax.ShapeDtypeStruct((levels, rows + 2, circle, 4 * span), bf16),
            jax.ShapeDtypeStruct((27, chans, filters), f32),
        ],
        in_specs=[pl.BlockSpec(memory_space=SMEM)]
        + [pl.BlockSpec(memory_space=VMEM)] * 4
        + [pl.BlockSpec(memory_space=pl.ANY)],
        out_specs=[pl.BlockSpec(memory_space=VMEM)] + [pl.BlockSpec(memory_space=pl.ANY)],
        cost_estimate=pl.CostEstimate(flops=0, bytes_accessed=2**20, transcendentals=0),
        compiler_params=pltpu.CompilerParams(vmem_limit_bytes=24 * 1024 * 1024),
        name="lines",
    )(pos, x_own, x_x, x_y, x_d, far_a)
    (g2,) = call(
        pair_kernel, [jax.ShapeDtypeStruct((2, cells, wide), bf16)], (pos, g2a, g2b, xs), [], 0, "pair", 16, held=1
    )
    s2 = move(g2, sibling)
    early = 3
    cut, end = early * span, 27 * span
    size = end + 16 - cut
    half = size // 32 * 16
    first_rows = cut + 16
    own_cut, late_cut = 14 * span, (27 - early) // 2 * span
    slab = lambda count: jax.ShapeDtypeStruct((count, wide), bf16)
    (grads,) = call(
        taps_kernel,
        [jax.ShapeDtypeStruct((27, span, wide), f32)],
        (pos, xs, g_near, s_near, g2, s2),
        [VMEM((levels * wide, rows * circle), bf16), VMEM((3, 3 * wide, 4 * span), f32)],
        2 * 27 * span * wide * rows * circle * levels,
        "taps",
        28,
    )
    own, late = call(code_kernel, [slab(end + 16), slab(size)], (pos, grads, theirs), [], 0, "code", 16, held=1)

    whole = lambda t: (0, 0, 0, 0)
    field = pl.pallas_call(
        field_kernel,
        out_shape=jax.ShapeDtypeStruct((levels, height, width, chans), bf16),
        grid=(9,),
        in_specs=[
            pl.BlockSpec(memory_space=SMEM),
            pl.BlockSpec(memory_space=pl.ANY),
            pl.BlockSpec(mine.shape, whole),
            pl.BlockSpec(mine.shape, whole),
            pl.BlockSpec((3, chans, filters), lambda t: (t, 0, 0)),
        ],
        out_specs=pl.BlockSpec((levels, height, width, chans), whole),
        scratch_shapes=[
            VMEM((3, levels + 2, height + 2, width, filters), bf16),
            VMEM((cells, chans), f32),
        ],
        cost_estimate=pl.CostEstimate(
            flops=4 * 27 * chans * filters * cells, bytes_accessed=27 * chans * filters * 2, transcendentals=0
        ),
        compiler_params=pltpu.CompilerParams(vmem_limit_bytes=20 * 1024 * 1024),
        name="field",
    )(pos, own, mine, theirs, taps)

    def to_plane(share):
        return move(share, lat_xor(1)), move(share, lat_xor(2))

    def to_diagonal(by_x, by_y, cut, after1, after2, name):
        top, bottom = call(
            cross_kernel, [slab(cut), slab(by_x.shape[0] - cut)], (pos, by_x, by_y, after1, after2), [], 0, name, 16, held=2
        )
        return move(top, lat_xor(1)), move(bottom, lat_xor(2))

    from_3 = move(late, lon_by(1))
    from_1 = move(late, lon_by(-1))
    own_x, own_y = to_plane(own)
    own_top, own_bottom = to_diagonal(own_x, own_y, own_cut, field, own, "cross_1")
    pair, half_3, half_1 = call(
        both_kernel,
        [slab(2 * size), slab(half), slab(size - half)],
        (pos, from_3, from_1, own_top, own_bottom),
        [],
        0,
        "both",
        16,
        held=2,
    )
    half_3 = move(half_3, lon_by(1))
    half_1 = move(half_1, lon_by(-1))
    pair_x, pair_y = to_plane(pair)
    (block,) = call(
        block_kernel, [slab(4 * first_rows)], (pos, own, own_x, own_y, own_top, own_bottom), [], 0, "block", 16
    )
    early_3 = move(block, lon_by(1))
    early_1 = move(block, lon_by(-1))
    (from_2,) = call(across_kernel, [slab(size)], (pos, half_3, half_1, pair), [], 0, "across", 16, held=1)
    pair_top, pair_bottom = to_diagonal(pair_x, pair_y, size, early_1, early_3, "cross_2")
    from_2x, from_2y = to_plane(from_2)
    hand_3, hand_1 = call(hand_kernel, [slab(2 * first_rows)] * 2, (pos, early_3, early_1), [], 0, "hand", 16)
    early_2a = move(hand_3, lon_by(1))
    early_2b = move(hand_1, lon_by(-1))

    def late_piece(which, row=0):
        return ((which, row + size - 16), (0, which, row))

    def early_piece(which, row):
        return ((which, row + cut), (0, which, row))

    pieces = [((which, end), (0, which, 0)) for which in range(3)]
    pieces.append(((4, end - own_cut), (0, 3, 0), (own_cut // span, 4, 0)))
    total, token = unpack(
        pos, total, [own, own_x, own_y, own_top, own_bottom], [block], [(0, 0, 27, pieces)], span, "unpack_1"
    )
    from_2top, from_2bottom = to_diagonal(from_2x, from_2y, late_cut, token, pair, "cross_3")
    slabs = [
        (3, early, 27 - early, [late_piece(0), late_piece(2), late_piece(3), late_piece(4)]),
        (1, early, 27 - early, [late_piece(1), late_piece(2, size), late_piece(3, size), late_piece(5)]),
        (3, 0, early, [early_piece(6, tag * first_rows) for tag in range(4)]),
        (1, 0, early, [early_piece(7, tag * first_rows) for tag in range(4)]),
    ]
    total, _ = unpack(
        pos,
        total,
        [from_3, from_1, pair_x, pair_y, pair_top, pair_bottom, early_3, early_1],
        [hand_3],
        slabs,
        span,
        "unpack_2",
    )
    pieces = [late_piece(2), late_piece(3), late_piece(4)]
    pieces.append(((6, size - 16 - late_cut), (0, 5, 0), (late_cut // span, 6, 0)))
    slabs = [
        (2, 0, early, [early_piece(tag // 2, tag % 2 * first_rows) for tag in range(4)]),
        (2, early, 27 - early, pieces),
    ]
    total, _ = unpack(
        pos,
        total,
        [early_2a, early_2b, from_2, from_2x, from_2y, from_2top, from_2bottom],
        [],
        slabs,
        span,
        "unpack_3",
    )
    return (jnp.transpose(field, (3, 0, 1, 2)), jnp.transpose(total, (1, 0, 2)))


def body(inputs, weights, out_grad):
    chans, levels, height, width = inputs.shape
    shape = tuple(lax.axis_size(axis) for axis in AXES)
    fits = (
        shape == (2, 4, 4)
        and chans == out_grad.shape[0] == 256
        and weights.shape[2] == 512
        and levels % 2 == 0
        and height % 2 == 0
        and width % 16 == 0
    )
    return (blocked_body if fits else plain_body)(inputs, weights, out_grad)


def solution(mesh):
    in_specs = (P("ch", None, "lat", "lon"), P("ch", None, None), P("ch", None, "lat", "lon"))
    out_specs = (P("ch", None, "lat", "lon"), P("ch", None, None))
    return jax.shard_map(body, mesh=mesh, in_specs=in_specs, out_specs=out_specs, check_vma=False)
```

```python
import math

import jax
import jax.numpy as jnp
from jax import lax
from jax.experimental import pallas as pl
from jax.experimental.pallas import tpu as pltpu
from jax.sharding import PartitionSpec as P

VMEM = pltpu.VMEM
SMEM = pltpu.SMEM
AXES = ("ch", "lat", "lon")


def padded_2(cells, sides, width):
    for axis, dim in sides:
        count = lax.axis_size(axis)
        head = lax.slice_in_dim(cells, 0, width, axis=dim)
        tail = lax.slice_in_dim(cells, cells.shape[dim] - width, cells.shape[dim], axis=dim)
        cells = jnp.concatenate(
            [
                lax.ppermute(tail, axis, [(i, (i + 1) % count) for i in range(count)]),
                cells,
                lax.ppermute(head, axis, [((i + 1) % count, i) for i in range(count)]),
            ],
            axis=dim,
        )
    return cells


def mask_rims(padded):
    count = lax.axis_size("lat")
    where_lat = lax.axis_index("lat")
    lines = jnp.arange(padded.shape[2])
    drop = (lines == 0) & (where_lat == 0) | (lines == padded.shape[2] - 1) & (
        where_lat == count - 1
    )
    return jnp.where(drop[None, None, :, None], jnp.zeros((), padded.dtype), padded)


def pad_levels(field):
    return jnp.pad(field, ((0, 0), (1, 1), (0, 0), (0, 0)))


def plain_body(inputs, weights, out_grad):
    chans, levels, height, width = inputs.shape
    input_pad = pad_levels(mask_rims(padded_2(inputs, (("lat", 2), ("lon", 3)), 1)))
    grad_inner = lax.all_gather(out_grad, "ch", axis=0, tiled=True)
    grad_pad = pad_levels(mask_rims(padded_2(grad_inner, (("lat", 2), ("lon", 3)), 1)))
    filters = grad_pad.shape[0]
    products = jnp.dot(
        weights.reshape(chans * 27, filters),
        grad_pad.reshape(filters, -1),
        preferred_element_type=jnp.float32,
    )
    products = products.reshape((chans, 27) + tuple(grad_pad.shape[1:]))
    total = jnp.zeros((chans, levels, height, width), jnp.float32)
    pieces = []
    for tap in range(27):
        lev, lat, lon = tap // 9 - 1, tap // 3 % 3 - 1, tap % 3 - 1
        total = (
            total
            + products[
                :,
                tap,
                1 - lev : 1 - lev + levels,
                1 - lat : 1 - lat + height,
                1 - lon : 1 - lon + width,
            ]
        )
        pieces.append(
            input_pad[
                :,
                1 + lev : 1 + lev + levels,
                1 + lat : 1 + lat + height,
                1 + lon : 1 + lon + width,
            ]
        )
    columns = jnp.stack(pieces, axis=1).reshape(chans * 27, -1)
    partial_grad = lax.dot_general(
        columns,
        grad_inner.reshape(filters, -1),
        (((1,), (1,)), ((), ())),
        preferred_element_type=jnp.float32,
    )
    summed = lax.psum(partial_grad, ("lat", "lon"))
    cells = levels * height * width * lax.axis_size("lat") * lax.axis_size("lon")
    weight_grad = (summed * (1.0 / math.sqrt(cells))).reshape(chans, 27, filters)
    return (total.astype(jnp.bfloat16), weight_grad)


def move(x, target):
    pairs = []
    for i in range(32):
        to = target(i // 16, i // 4 % 4, i % 4)
        if to is not None:
            pairs.append((i, (to[0] * 4 + to[1]) * 4 + to[2]))
    return lax.ppermute(x, AXES, pairs)


def lon_by(step):
    return lambda c, a, o: (c, a, (o + step) % 4)


def lat_xor(mask):
    return lambda c, a, o: (c, a ^ mask, o)


def sibling(c, a, o):
    return (1 - c, a, o)


def call(kernel, outs, ins, scratch, flops, name, limit, held=0):
    read = len(ins) - 1 - held
    moved = sum(math.prod(x.shape) * x.dtype.itemsize for x in list(ins[1 : 1 + read]) + list(outs))
    return pl.pallas_call(
        kernel,
        out_shape=outs,
        in_specs=[pl.BlockSpec(memory_space=SMEM)]
        + [pl.BlockSpec(memory_space=VMEM)] * read
        + [pl.BlockSpec(memory_space=pl.ANY)] * held,
        out_specs=[pl.BlockSpec(memory_space=VMEM)] * len(outs),
        scratch_shapes=scratch,
        cost_estimate=pl.CostEstimate(flops=flops, bytes_accessed=moved, transcendentals=0),
        compiler_params=pltpu.CompilerParams(vmem_limit_bytes=limit * 1024 * 1024),
        name=name,
    )(*ins)


def pack_kernel(pos, x, g, g_same, g_other, x0, x1, x2, x3, rim_x, rim_d, held):
    levels, height, width, chans = x.shape
    half, wide = levels // 2, chans // 2
    right = lax.rem(pos[1], 2)
    for out, at in ((g_same, right), (g_other, 1 - right)):
        out[...] = g[:, :, :, pl.ds(pl.multiple_of(at * wide, wide), wide)].reshape(out.shape)
    many = x0.shape[0]
    for block in range(4):
        at = block * (chans // 4)
        lo = x[0:half, :, :, at : at + chans // 4]
        hi = x[half:levels, :, :, at : at + chans // 4]
        held[block] = jnp.concatenate([lo, hi], axis=-1).reshape(held.shape[1:])
    lon = pos[2]
    for step, out in enumerate((x0, x1, x2, x3)):
        out[0:many, :] = held[lax.rem(lon + step, 4)]
    for out, column in ((x1, width - 1), (x3, 0)):
        rim = g[:, :, column, :].reshape(levels * height, chans)
        out[many : many + levels * height, :] = rim[:, 0:wide]
        out[many + levels * height :, :] = rim[:, wide:]
    even = right == 0
    low, high = g[:, 0], g[:, height - 1]
    line = levels * width
    for out, upward in ((rim_x, even), (rim_d, jnp.logical_not(even))):
        facing = jnp.where(upward, high, low).reshape(line, chans)
        for at in range(2):
            out[at * line : (at + 1) * line, :] = facing[:, at * wide : (at + 1) * wide]


def spread_kernel(pos, x0, x1, x2, x3, after1, after2, own, own_y):
    del pos, after1, after2
    many = x0.shape[0]
    for at, piece in enumerate((x0, x1, x2, x3)):
        own[at * many : (at + 1) * many, :] = piece[0:many, :]
        own_y[at * many : (at + 1) * many, :] = piece[0:many, :]
    extra = x1.shape[0] - many
    own[4 * many : 4 * many + extra, :] = x1[many:, :]
    own[4 * many + extra :, :] = x3[many:, :]


def split_kernel(pos, west, east, first, second):
    del pos
    many = first.shape[0]
    first[...] = west[0:many, :]
    second[...] = east[many : 2 * many, :]


def mine_kernel(pos, g, own, x_x, x_d, by_x, by_d, after, mine):
    del after
    levels, height, width, chans = g.shape
    edge, line, wide = levels * height, levels * width, chans // 2
    inner = own.shape[0] - 4 * edge
    mine[:, 1 : height + 1, 0:width, :] = g[...]

    def columns(message, rows):
        for side in range(2):
            for half in range(2):
                start = inner + (2 * side + half) * edge
                rim = message[start : start + edge, :].reshape(levels, height, wide)
                at = width + 8 * side
                for row, to in rows:
                    mine[:, to, at : at + 8, half * wide : (half + 1) * wide] = jnp.broadcast_to(
                        rim[:, row : row + 1], (levels, 8, wide)
                    )

    columns(own, [(row, row + 1) for row in range(height)])

    def lines(strip, message, row, to):
        for half in range(2):
            part = strip[half * line : (half + 1) * line, :]
            mine[:, to, 0:width, half * wide : (half + 1) * wide] = part.reshape(levels, width, wide)
        columns(message, [(row, to)])

    lat = pos[1]
    odd = lax.rem(lat, 2)

    @pl.when(odd == 1)
    def _():
        lines(by_x, x_x, height - 1, 0)
        lines(by_d, x_d, 0, height + 1)

    @pl.when(odd == 0)
    def _():
        lines(by_d, x_d, height - 1, 0)
        lines(by_x, x_x, 0, height + 1)

    @pl.when(lat == 0)
    def _():
        mine[:, 0] = jnp.zeros_like(mine[:, 0])

    @pl.when(lat == 3)
    def _():
        mine[:, height + 1] = jnp.zeros_like(mine[:, height + 1])


def pair_kernel(pos, one, two, after, both):
    del pos, after
    both[0] = one[...]
    both[1] = two[...]


def first_pair_kernel(pos, one, two, after1, after2, after3, both):
    del pos, after1, after2, after3
    many = one.shape[0]
    both[0:many, :] = one[...]
    both[many : 2 * many, :] = two[...]
    both[2 * many :, :] = jnp.zeros((both.shape[0] - 2 * many, both.shape[1]), both.dtype)


def lines_kernel(pos, x_own, x_x, x_y, x_d, after, xs, blank):
    del after, blank
    lat = pos[1]
    levels, rows, circle, lanes = xs.shape
    rows, width, span, half = rows - 2, circle // 4, lanes // 4, levels // 2
    height = rows // 4
    many = half * height * width
    xs[:, 0] = jnp.zeros_like(xs[:, 0])
    xs[:, rows + 1] = jnp.zeros_like(xs[:, rows + 1])
    low = lax.broadcasted_iota(jnp.int32, (circle, 2 * span), 1) < span
    for tag, ref in enumerate((x_own, x_x, x_y, x_d)):
        start = (lat ^ tag) * height
        strips = [
            ref.at[pl.ds((4 - at) % 4 * many, many)].reshape(half, height, width, 2 * span) for at in range(4)
        ]

        @pl.loop(0, half * height)
        def _(step, strips=strips, start=start):
            lev, row = step // height, lax.rem(step, height)
            line = jnp.concatenate([s[lev, row] for s in strips], axis=0).astype(jnp.float32)
            turned = pltpu.roll(line, span, 1)
            for upper in range(2):
                same = jnp.where(low, turned, line) if upper else jnp.where(low, line, turned)
                before = pltpu.roll(same, 1, 0)
                after = pltpu.roll(same, circle - 1, 0)
                at = upper * half + lev
                xs[at, 1 + start + row, :, 0 : 2 * span] = jnp.where(low, before, same).astype(xs.dtype)
                xs[at, 1 + start + row, :, 2 * span : 4 * span] = after.astype(xs.dtype)


def turn(gt, slot, core, first, second, levels):
    many, filters = first.shape
    line = many // levels
    for lev in range(levels):
        block = jnp.concatenate([first[lev * line : (lev + 1) * line], second[lev * line : (lev + 1) * line]], axis=0)
        gt[
            lev * filters : (lev + 1) * filters,
            pl.ds(pl.multiple_of((2 * slot + core) * 2 * line, 2 * line), 2 * line),
        ] = block.T


def taps_kernel(pos, xs, g0, g1, g3, s0, s1, s3, g2, s2, out, gt, acc):
    levels, rows, circle, lanes = xs.shape
    rows, width, span = rows - 2, circle // 4, lanes // 4
    filters = gt.shape[0] // levels
    deep = rows * width
    right = lax.rem(pos[1], 2)
    many = g2.shape[1]
    for core, parts, last in ((pos[0], (g0, g3, g1), g2), (1 - pos[0], (s0, s3, s1), s2)):
        for slot, part in zip((0, 1, 3), parts):
            first = part[pl.ds(pl.multiple_of(right * many, many), many), :]
            second = part[pl.ds(pl.multiple_of((1 - right) * many, many), many), :]
            turn(gt, slot, core, first, second, levels)
        turn(gt, 2, core, last[right], last[1 - right], levels)
    acc[...] = jnp.zeros_like(acc)

    @pl.loop(0, 3)
    def _(lat_by):
        for lev in range(levels):
            first, last = max(lev - 1, 0), min(lev + 1, levels - 1)
            to = (first - lev + 1) * filters
            many = (last - first + 1) * filters
            total = acc[lat_by, to : to + many, :]
            for place in range(4):
                total += jnp.dot(
                    gt[first * filters : (last + 1) * filters, place * deep : (place + 1) * deep],
                    xs[lev, pl.ds(lat_by, rows), place * width : (place + 1) * width].reshape(deep, lanes),
                    preferred_element_type=jnp.float32,
                )
            acc[lat_by, to : to + many, :] = total

    scale = 1.0 / math.sqrt(levels * rows * circle)
    for lat_by in range(3):
        for lev_at in range(3):
            block = acc[lat_by, lev_at * filters : (lev_at + 1) * filters, :].T * scale
            for lon_at in range(3):
                out[(2 - lev_at) * 9 + lat_by * 3 + lon_at] = block[lon_at * span : (lon_at + 1) * span]


def code_kernel(pos, held, after, out, late):
    del pos, after
    taps, span, filters = held.shape
    most = jnp.abs(held[0])
    for tap in range(1, taps):
        most = jnp.maximum(most, jnp.abs(held[tap]))
    top = jnp.maximum(jnp.max(most, axis=(0, 1), keepdims=True), 1e-30)
    power = jnp.ceil(jnp.log(top) * (1.0 / math.log(2.0))) - 15.0
    unit = jnp.broadcast_to(jnp.exp2(power), (16, filters)).astype(out.dtype).astype(jnp.float32)
    shrink = 1.0 / unit[0:1]
    unit = unit.astype(out.dtype)
    skip = out.shape[0] - late.shape[0]
    for tap in range(taps):
        value = held[tap] * shrink
        square = value * value
        code = (square * value * jnp.abs(value)).astype(out.dtype)
        out[tap * span : (tap + 1) * span, :] = code
        if tap * span >= skip:
            late[tap * span - skip : (tap + 1) * span - skip, :] = code
    out[taps * span :, :] = unit
    late[taps * span - skip :, :] = unit


def both_kernel(pos, west, east, after1, after2, both, half_3, half_1):
    del pos, after1, after2
    size, half = west.shape[0], half_3.shape[0]
    both[0:size, :] = west[...]
    both[size:, :] = east[...]
    half_3[...] = west[0:half, :]
    half_1[...] = east[half:, :]


def cross_kernel(pos, by_x, by_y, after1, after2, top, bottom):
    del pos, after1, after2
    cut = top.shape[0]
    top[...] = by_y[0:cut, :]
    bottom[...] = by_x[cut:, :]


def across_kernel(pos, half_3, half_1, after, late):
    del pos, after
    half = half_3.shape[0]
    late[0:half, :] = half_3[...]
    late[half:, :] = half_1[...]


def block_kernel(pos, own, x, y, top, bottom, block):
    del pos
    rows = block.shape[0] // 4
    for at, (piece, end) in enumerate(((own, own), (x, x), (y, y), (top, bottom))):
        block[at * rows : (at + 1) * rows - 16, :] = piece[0 : rows - 16, :]
        block[(at + 1) * rows - 16 : (at + 1) * rows, :] = end[end.shape[0] - 16 :, :]


def hand_kernel(pos, block_3, block_1, first, second):
    del pos
    many = first.shape[0]
    first[...] = block_3[0:many, :]
    second[...] = block_1[many:, :]


def unpack_kernel(pos, *refs, slabs, count, span):
    sources = refs[:count]
    total, token, buffers, sems = refs[-4:]
    slots, group = buffers.shape[:2]
    wide = buffers.shape[-1] // 4
    token[...] = jnp.zeros_like(token)
    parts = []
    for step, first, taps, pieces in slabs:
        for at in range(0, taps, group):
            parts.append((step, first + at, min(group, taps - at), at, pieces))

    def copy(at):
        step, first, many, _, _ = parts[at]
        lon_at = pl.multiple_of(lax.rem(pos[2] + step, 4) * span, span)
        return pltpu.make_async_copy(
            buffers.at[at % slots, pl.ds(0, many)],
            total.at[pl.ds(first, many), pl.ds(lon_at, span)],
            sems.at[at % slots],
        )

    for at, (_, _, many, skip, pieces) in enumerate(parts):
        if at >= slots:
            copy(at - slots).wait()
        for tag, ((power_in, power_row), *segments) in enumerate(pieces):
            unit = sources[power_in][power_row : power_row + 16, :].astype(jnp.float32)[0:1]
            lanes = pl.ds(pl.multiple_of((pos[1] ^ tag) * wide, wide), wide)
            for tap in range(many):
                begin, which, row = [segment for segment in segments if segment[0] <= skip + tap][-1]
                start = row + (skip + tap - begin) * span
                code = sources[which][start : start + span, :].astype(jnp.float32)
                root = lax.rsqrt(lax.rsqrt(jnp.abs(code))) * unit
                buffers[at % slots, tap, :, lanes] = jnp.where(code < 0, -root, root)
        copy(at).start()
    for at in range(max(len(parts) - slots, 0), len(parts)):
        copy(at).wait()


def unpack(pos, total, sources, after, slabs, span, name):
    slots, group = 4, 3
    wide = total.shape[2]
    ins = (pos, *sources, *after, total)
    token = jax.ShapeDtypeStruct((8, 128), jnp.float32)
    return pl.pallas_call(
        lambda *refs: unpack_kernel(*refs, slabs=slabs, count=len(sources), span=span),
        out_shape=[jax.ShapeDtypeStruct(total.shape, total.dtype), token],
        in_specs=[pl.BlockSpec(memory_space=SMEM)]
        + [pl.BlockSpec(memory_space=VMEM)] * len(sources)
        + [pl.BlockSpec(memory_space=pl.ANY)] * (len(after) + 1),
        out_specs=[pl.BlockSpec(memory_space=pl.ANY), pl.BlockSpec(memory_space=VMEM)],
        scratch_shapes=[VMEM((slots, group, span, wide), jnp.float32), pltpu.SemaphoreType.DMA((slots,))],
        input_output_aliases={len(ins) - 1: 0},
        cost_estimate=pl.CostEstimate(flops=0, bytes_accessed=4 * 2**20, transcendentals=0),
        compiler_params=pltpu.CompilerParams(vmem_limit_bytes=51 * 1024 * 1024),
        name=name,
    )(*ins)


def field_kernel(pos, after, mine, theirs, w, out, copies, acc):
    del after
    step = pl.program_id(0)
    levels, height, width, chans = out.shape
    many = mine.shape[-1]

    @pl.when(step == 0)
    def _():
        copies[:, 0] = jnp.zeros_like(copies[:, 0])
        copies[:, levels + 1] = jnp.zeros_like(copies[:, levels + 1])
        line_at = lax.broadcasted_iota(jnp.int32, (width, many), 0)
        for which, field in ((pos[0], mine), (1 - pos[0], theirs)):
            lanes = pl.ds(pl.multiple_of(which * many, many), many)
            for lev in range(levels):
                for row in range(height + 2):
                    line = field[lev, row, 0:width].astype(jnp.float32)
                    west = field[lev, row, width : width + 1].astype(jnp.float32)
                    east = field[lev, row, width + 8 : width + 9].astype(jnp.float32)
                    before = jnp.where(line_at == 0, west, pltpu.roll(line, 1, 0))
                    later = jnp.where(line_at == width - 1, east, pltpu.roll(line, width - 1, 0))
                    copies[0, lev + 1, row, :, lanes] = later.astype(copies.dtype)
                    copies[1, lev + 1, row, :, lanes] = field[lev, row, 0:width]
                    copies[2, lev + 1, row, :, lanes] = before.astype(copies.dtype)
        acc[...] = jnp.zeros_like(acc)

    lev_by, lat_by = step // 3, lax.rem(step, 3)
    cells = [
        copies[at, pl.ds(2 - lev_by, levels), pl.ds(2 - lat_by, height)].reshape(
            levels * height * width, 2 * many
        )
        for at in range(3)
    ]
    acc[...] += lax.dot_general(
        jnp.concatenate(cells, axis=1),
        jnp.concatenate([w[at] for at in range(3)], axis=1),
        (((1,), (1,)), ((), ())),
        preferred_element_type=jnp.float32,
    )

    @pl.when(step == 8)
    def _():
        out[...] = acc[...].reshape(out.shape).astype(out.dtype)


def blocked_body(inputs, weights, out_grad):
    chans, levels, height, width = inputs.shape
    filters = weights.shape[2]
    bf16, f32 = jnp.bfloat16, jnp.float32
    lat, lon = lax.axis_index("lat"), lax.axis_index("lon")
    pos = jnp.stack([lax.axis_index("ch"), lat, lon]).astype(jnp.int32)
    x_cells = jnp.transpose(inputs, (1, 2, 3, 0))
    g_cells = jnp.transpose(out_grad, (1, 2, 3, 0))
    taps = jnp.transpose(weights, (1, 0, 2))
    cells = levels * height * width
    span, wide = chans // 4, filters // 4
    rows, circle = 4 * height, 4 * width
    edge = levels * height

    to_same = lambda c, a, o: (a // 2, 2 * c + a % 2, o)
    to_other = lambda c, a, o: (a // 2, 2 * c + 1 - a % 2, o)
    many = cells // 2
    block = jax.ShapeDtypeStruct((cells, wide), bf16)
    strip = jax.ShapeDtypeStruct((2 * levels * width, 2 * span), bf16)
    g_same, g_other, x0, x1, x2, x3, rim_x, rim_d = call(
        pack_kernel,
        [block, block]
        + [jax.ShapeDtypeStruct((many + extra, 2 * span), bf16) for extra in (0, 2 * edge, 0, 2 * edge)]
        + [strip, strip],
        (pos, x_cells, g_cells),
        [VMEM((4, many, 2 * span), bf16)],
        0,
        "pack",
        16,
    )
    g_s = move(g_same, to_same)
    g_o = move(g_other, to_other)
    x_r1 = move(x1, lon_by(1))
    x_r3 = move(x3, lon_by(-1))
    x_r2 = move(x2, lon_by(2))
    by_x = move(rim_x, lat_xor(1))
    by_d = move(rim_d, lat_xor(3))

    inner = 4 * many
    (g0,) = call(
        first_pair_kernel,
        [jax.ShapeDtypeStruct((2 * cells + 80, wide), bf16)],
        (pos, g_s, g_o, x_r1, x_r2, x_r3),
        [],
        0,
        "pair_0",
        16,
        held=3,
    )
    x_own, x_own_y = call(
        spread_kernel,
        [jax.ShapeDtypeStruct((count, 2 * span), bf16) for count in (inner + 4 * edge, inner)],
        (pos, x0, x_r1, x_r2, x_r3, by_x, by_d),
        [],
        0,
        "spread",
        16,
        held=2,
    )
    x_x = move(x_own, lat_xor(1))
    x_d = move(x_own, lat_xor(3))
    x_y = move(x_own_y, lat_xor(2))
    g1 = move(g0, lon_by(1))
    g3 = move(g0, lon_by(-1))
    far_a, far_b = call(split_kernel, [block, block], (pos, g1, g3), [], 0, "split", 16)
    g2a = move(far_a, lon_by(1))
    g2b = move(far_b, lon_by(-1))
    s0, s1, s3 = move(g0, sibling), move(g1, sibling), move(g3, sibling)
    xs, total = pl.pallas_call(
        lines_kernel,
        out_shape=[
            jax.ShapeDtypeStruct((levels, rows + 2, circle, 4 * span), bf16),
            jax.ShapeDtypeStruct((27, chans, filters), f32),
        ],
        in_specs=[pl.BlockSpec(memory_space=SMEM)]
        + [pl.BlockSpec(memory_space=VMEM)] * 4
        + [pl.BlockSpec(memory_space=pl.ANY)],
        out_specs=[pl.BlockSpec(memory_space=VMEM)] + [pl.BlockSpec(memory_space=pl.ANY)],
        cost_estimate=pl.CostEstimate(flops=0, bytes_accessed=2**20, transcendentals=0),
        compiler_params=pltpu.CompilerParams(vmem_limit_bytes=24 * 1024 * 1024),
        name="lines",
    )(pos, x_own, x_x, x_y, x_d, far_a)
    (mine,) = call(
        mine_kernel,
        [jax.ShapeDtypeStruct((levels, height + 2, width + 16, chans), bf16)],
        (pos, g_cells, x_own, x_x, x_d, by_x, by_d, xs),
        [],
        0,
        "mine",
        16,
        held=1,
    )
    theirs = move(mine, sibling)
    (g2,) = call(
        pair_kernel, [jax.ShapeDtypeStruct((2, cells, wide), bf16)], (pos, g2a, g2b, xs), [], 0, "pair", 16, held=1
    )
    s2 = move(g2, sibling)
    early = 3
    cut, end = early * span, 27 * span
    size = end + 16 - cut
    half = size // 32 * 16
    first_rows = cut + 16
    own_cut, late_cut = 14 * span, (27 - early) // 2 * span
    slab = lambda count: jax.ShapeDtypeStruct((count, wide), bf16)
    (grads,) = call(
        taps_kernel,
        [jax.ShapeDtypeStruct((27, span, wide), f32)],
        (pos, xs, g0, g1, g3, s0, s1, s3, g2, s2),
        [VMEM((levels * wide, rows * circle), bf16), VMEM((3, 3 * wide, 4 * span), f32)],
        2 * 27 * span * wide * rows * circle * levels,
        "taps",
        28,
    )
    own, late = call(code_kernel, [slab(end + 16), slab(size)], (pos, grads, theirs), [], 0, "code", 16, held=1)

    whole = lambda t: (0, 0, 0, 0)
    field = pl.pallas_call(
        field_kernel,
        out_shape=jax.ShapeDtypeStruct((levels, height, width, chans), bf16),
        grid=(9,),
        in_specs=[
            pl.BlockSpec(memory_space=SMEM),
            pl.BlockSpec(memory_space=pl.ANY),
            pl.BlockSpec(mine.shape, whole),
            pl.BlockSpec(mine.shape, whole),
            pl.BlockSpec((3, chans, filters), lambda t: (t, 0, 0)),
        ],
        out_specs=pl.BlockSpec((levels, height, width, chans), whole),
        scratch_shapes=[
            VMEM((3, levels + 2, height + 2, width, filters), bf16),
            VMEM((cells, chans), f32),
        ],
        cost_estimate=pl.CostEstimate(
            flops=4 * 27 * chans * filters * cells, bytes_accessed=27 * chans * filters * 2, transcendentals=0
        ),
        compiler_params=pltpu.CompilerParams(vmem_limit_bytes=20 * 1024 * 1024),
        name="field",
    )(pos, own, mine, theirs, taps)

    def to_plane(share):
        return move(share, lat_xor(1)), move(share, lat_xor(2))

    def to_diagonal(by_x, by_y, cut, after1, after2, name):
        top, bottom = call(
            cross_kernel, [slab(cut), slab(by_x.shape[0] - cut)], (pos, by_x, by_y, after1, after2), [], 0, name, 16, held=2
        )
        return move(top, lat_xor(1)), move(bottom, lat_xor(2))

    from_3 = move(late, lon_by(1))
    from_1 = move(late, lon_by(-1))
    own_x, own_y = to_plane(own)
    own_top, own_bottom = to_diagonal(own_x, own_y, own_cut, field, own, "cross_1")
    pair, half_3, half_1 = call(
        both_kernel,
        [slab(2 * size), slab(half), slab(size - half)],
        (pos, from_3, from_1, own_top, own_bottom),
        [],
        0,
        "both",
        16,
        held=2,
    )
    half_3 = move(half_3, lon_by(1))
    half_1 = move(half_1, lon_by(-1))
    pair_x, pair_y = to_plane(pair)
    (block,) = call(
        block_kernel, [slab(4 * first_rows)], (pos, own, own_x, own_y, own_top, own_bottom), [], 0, "block", 16
    )
    early_3 = move(block, lon_by(1))
    early_1 = move(block, lon_by(-1))
    (from_2,) = call(across_kernel, [slab(size)], (pos, half_3, half_1, pair), [], 0, "across", 16, held=1)
    pair_top, pair_bottom = to_diagonal(pair_x, pair_y, size, early_1, early_3, "cross_2")
    from_2x, from_2y = to_plane(from_2)
    hand_3, hand_1 = call(hand_kernel, [slab(2 * first_rows)] * 2, (pos, early_3, early_1), [], 0, "hand", 16)
    early_2a = move(hand_3, lon_by(1))
    early_2b = move(hand_1, lon_by(-1))

    def late_piece(which, row=0):
        return ((which, row + size - 16), (0, which, row))

    def early_piece(which, row):
        return ((which, row + cut), (0, which, row))

    pieces = [((which, end), (0, which, 0)) for which in range(3)]
    pieces.append(((4, end - own_cut), (0, 3, 0), (own_cut // span, 4, 0)))
    total, token = unpack(
        pos, total, [own, own_x, own_y, own_top, own_bottom], [block], [(0, 0, 27, pieces)], span, "unpack_1"
    )
    from_2top, from_2bottom = to_diagonal(from_2x, from_2y, late_cut, token, pair, "cross_3")
    slabs = [
        (3, early, 27 - early, [late_piece(0), late_piece(2), late_piece(3), late_piece(4)]),
        (1, early, 27 - early, [late_piece(1), late_piece(2, size), late_piece(3, size), late_piece(5)]),
        (3, 0, early, [early_piece(6, tag * first_rows) for tag in range(4)]),
        (1, 0, early, [early_piece(7, tag * first_rows) for tag in range(4)]),
    ]
    total, _ = unpack(
        pos,
        total,
        [from_3, from_1, pair_x, pair_y, pair_top, pair_bottom, early_3, early_1],
        [hand_3],
        slabs,
        span,
        "unpack_2",
    )
    pieces = [late_piece(2), late_piece(3), late_piece(4)]
    pieces.append(((6, size - 16 - late_cut), (0, 5, 0), (late_cut // span, 6, 0)))
    slabs = [
        (2, 0, early, [early_piece(tag // 2, tag % 2 * first_rows) for tag in range(4)]),
        (2, early, 27 - early, pieces),
    ]
    total, _ = unpack(
        pos,
        total,
        [early_2a, early_2b, from_2, from_2x, from_2y, from_2top, from_2bottom],
        [],
        slabs,
        span,
        "unpack_3",
    )
    return (jnp.transpose(field, (3, 0, 1, 2)), jnp.transpose(total, (1, 0, 2)))


def body(inputs, weights, out_grad):
    chans, levels, height, width = inputs.shape
    shape = tuple(lax.axis_size(axis) for axis in AXES)
    fits = (
        shape == (2, 4, 4)
        and chans == out_grad.shape[0] == 256
        and weights.shape[2] == 512
        and levels % 2 == 0
        and height % 2 == 0
        and width % 16 == 0
    )
    return (blocked_body if fits else plain_body)(inputs, weights, out_grad)


def solution(mesh):
    in_specs = (P("ch", None, "lat", "lon"), P("ch", None, None), P("ch", None, "lat", "lon"))
    out_specs = (P("ch", None, "lat", "lon"), P("ch", None, None))
    return jax.shard_map(body, mesh=mesh, in_specs=in_specs, out_specs=out_specs, check_vma=False)
```

```python
import math

import jax
import jax.numpy as jnp
from jax import lax
from jax.experimental import pallas as pl
from jax.experimental.pallas import tpu as pltpu
from jax.sharding import PartitionSpec as P

VMEM = pltpu.VMEM
SMEM = pltpu.SMEM
AXES = ("ch", "lat", "lon")


def padded_2(cells, sides, width):
    for axis, dim in sides:
        count = lax.axis_size(axis)
        head = lax.slice_in_dim(cells, 0, width, axis=dim)
        tail = lax.slice_in_dim(cells, cells.shape[dim] - width, cells.shape[dim], axis=dim)
        cells = jnp.concatenate(
            [
                lax.ppermute(tail, axis, [(i, (i + 1) % count) for i in range(count)]),
                cells,
                lax.ppermute(head, axis, [((i + 1) % count, i) for i in range(count)]),
            ],
            axis=dim,
        )
    return cells


def mask_rims(padded):
    count = lax.axis_size("lat")
    where_lat = lax.axis_index("lat")
    lines = jnp.arange(padded.shape[2])
    drop = (lines == 0) & (where_lat == 0) | (lines == padded.shape[2] - 1) & (
        where_lat == count - 1
    )
    return jnp.where(drop[None, None, :, None], jnp.zeros((), padded.dtype), padded)


def pad_levels(field):
    return jnp.pad(field, ((0, 0), (1, 1), (0, 0), (0, 0)))


def plain_body(inputs, weights, out_grad):
    chans, levels, height, width = inputs.shape
    input_pad = pad_levels(mask_rims(padded_2(inputs, (("lat", 2), ("lon", 3)), 1)))
    grad_inner = lax.all_gather(out_grad, "ch", axis=0, tiled=True)
    grad_pad = pad_levels(mask_rims(padded_2(grad_inner, (("lat", 2), ("lon", 3)), 1)))
    filters = grad_pad.shape[0]
    products = jnp.dot(
        weights.reshape(chans * 27, filters),
        grad_pad.reshape(filters, -1),
        preferred_element_type=jnp.float32,
    )
    products = products.reshape((chans, 27) + tuple(grad_pad.shape[1:]))
    total = jnp.zeros((chans, levels, height, width), jnp.float32)
    pieces = []
    for tap in range(27):
        lev, lat, lon = tap // 9 - 1, tap // 3 % 3 - 1, tap % 3 - 1
        total = (
            total
            + products[
                :,
                tap,
                1 - lev : 1 - lev + levels,
                1 - lat : 1 - lat + height,
                1 - lon : 1 - lon + width,
            ]
        )
        pieces.append(
            input_pad[
                :,
                1 + lev : 1 + lev + levels,
                1 + lat : 1 + lat + height,
                1 + lon : 1 + lon + width,
            ]
        )
    columns = jnp.stack(pieces, axis=1).reshape(chans * 27, -1)
    partial_grad = lax.dot_general(
        columns,
        grad_inner.reshape(filters, -1),
        (((1,), (1,)), ((), ())),
        preferred_element_type=jnp.float32,
    )
    summed = lax.psum(partial_grad, ("lat", "lon"))
    cells = levels * height * width * lax.axis_size("lat") * lax.axis_size("lon")
    weight_grad = (summed * (1.0 / math.sqrt(cells))).reshape(chans, 27, filters)
    return (total.astype(jnp.bfloat16), weight_grad)


def move(x, target):
    pairs = []
    for i in range(32):
        to = target(i // 16, i // 4 % 4, i % 4)
        if to is not None:
            pairs.append((i, (to[0] * 4 + to[1]) * 4 + to[2]))
    return lax.ppermute(x, AXES, pairs)


def lon_by(step):
    return lambda c, a, o: (c, a, (o + step) % 4)


def lat_xor(mask):
    return lambda c, a, o: (c, a ^ mask, o)


def sibling(c, a, o):
    return (1 - c, a, o)


def call(kernel, outs, ins, scratch, flops, name, limit, held=0):
    read = len(ins) - 1 - held
    moved = sum(math.prod(x.shape) * x.dtype.itemsize for x in list(ins[1 : 1 + read]) + list(outs))
    return pl.pallas_call(
        kernel,
        out_shape=outs,
        in_specs=[pl.BlockSpec(memory_space=SMEM)]
        + [pl.BlockSpec(memory_space=VMEM)] * read
        + [pl.BlockSpec(memory_space=pl.ANY)] * held,
        out_specs=[pl.BlockSpec(memory_space=VMEM)] * len(outs),
        scratch_shapes=scratch,
        cost_estimate=pl.CostEstimate(flops=flops, bytes_accessed=moved, transcendentals=0),
        compiler_params=pltpu.CompilerParams(vmem_limit_bytes=limit * 1024 * 1024),
        name=name,
    )(*ins)


def pack_kernel(pos, x, g, g_same, g_other, x0, x1, x2, x3, rim_x, rim_d, held):
    levels, height, width, chans = x.shape
    half, wide = levels // 2, chans // 2
    right = lax.rem(pos[1], 2)
    for out, at in ((g_same, right), (g_other, 1 - right)):
        out[...] = g[:, :, :, pl.ds(pl.multiple_of(at * wide, wide), wide)].reshape(out.shape)
    many = x0.shape[0]
    for block in range(4):
        at = block * (chans // 4)
        lo = x[0:half, :, :, at : at + chans // 4]
        hi = x[half:levels, :, :, at : at + chans // 4]
        held[block] = jnp.concatenate([lo, hi], axis=-1).reshape(held.shape[1:])
    lon = pos[2]
    for step, out in enumerate((x0, x1, x2, x3)):
        out[0:many, :] = held[lax.rem(lon + step, 4)]
    for out, column in ((x1, width - 1), (x3, 0)):
        rim = g[:, :, column, :].reshape(levels * height, chans)
        out[many : many + levels * height, :] = rim[:, 0:wide]
        out[many + levels * height :, :] = rim[:, wide:]
    even = right == 0
    low, high = g[:, 0], g[:, height - 1]
    line = levels * width
    for out, upward in ((rim_x, even), (rim_d, jnp.logical_not(even))):
        facing = jnp.where(upward, high, low).reshape(line, chans)
        for at in range(2):
            out[at * line : (at + 1) * line, :] = facing[:, at * wide : (at + 1) * wide]


def spread_kernel(pos, x0, x1, x2, x3, after1, after2, own, own_y):
    del pos, after1, after2
    many = x0.shape[0]
    for at, piece in enumerate((x0, x1, x2, x3)):
        own[at * many : (at + 1) * many, :] = piece[0:many, :]
        own_y[at * many : (at + 1) * many, :] = piece[0:many, :]
    extra = x1.shape[0] - many
    own[4 * many : 4 * many + extra, :] = x1[many:, :]
    own[4 * many + extra :, :] = x3[many:, :]


def split_kernel(pos, west, east, first, second):
    del pos
    many = first.shape[0]
    first[...] = west[0:many, :]
    second[...] = east[many : 2 * many, :]


def mine_kernel(pos, g, own, x_x, x_d, by_x, by_d, after, mine):
    del after
    levels, height, width, chans = g.shape
    edge, line, wide = levels * height, levels * width, chans // 2
    inner = own.shape[0] - 4 * edge
    mine[:, 1 : height + 1, 0:width, :] = g[...]

    def columns(message, rows):
        for side in range(2):
            for half in range(2):
                start = inner + (2 * side + half) * edge
                rim = message[start : start + edge, :].reshape(levels, height, wide)
                at = width + 8 * side
                for row, to in rows:
                    mine[:, to, at : at + 8, half * wide : (half + 1) * wide] = jnp.broadcast_to(
                        rim[:, row : row + 1], (levels, 8, wide)
                    )

    columns(own, [(row, row + 1) for row in range(height)])

    def lines(strip, message, row, to):
        for half in range(2):
            part = strip[half * line : (half + 1) * line, :]
            mine[:, to, 0:width, half * wide : (half + 1) * wide] = part.reshape(levels, width, wide)
        columns(message, [(row, to)])

    lat = pos[1]
    odd = lax.rem(lat, 2)

    @pl.when(odd == 1)
    def _():
        lines(by_x, x_x, height - 1, 0)
        lines(by_d, x_d, 0, height + 1)

    @pl.when(odd == 0)
    def _():
        lines(by_d, x_d, height - 1, 0)
        lines(by_x, x_x, 0, height + 1)

    @pl.when(lat == 0)
    def _():
        mine[:, 0] = jnp.zeros_like(mine[:, 0])

    @pl.when(lat == 3)
    def _():
        mine[:, height + 1] = jnp.zeros_like(mine[:, height + 1])


def pair_kernel(pos, one, two, after, both):
    del pos, after
    both[0] = one[...]
    both[1] = two[...]


def first_pair_kernel(pos, one, two, after1, after2, after3, both):
    del pos, after1, after2, after3
    many = one.shape[0]
    both[0:many, :] = one[...]
    both[many : 2 * many, :] = two[...]
    both[2 * many :, :] = jnp.zeros((both.shape[0] - 2 * many, both.shape[1]), both.dtype)


def lines_kernel(pos, x_own, x_x, x_y, x_d, after, xs, blank):
    del after, blank
    lat = pos[1]
    levels, rows, circle, lanes = xs.shape
    rows, width, span, half = rows - 2, circle // 4, lanes // 4, levels // 2
    height = rows // 4
    many = half * height * width
    xs[:, 0] = jnp.zeros_like(xs[:, 0])
    xs[:, rows + 1] = jnp.zeros_like(xs[:, rows + 1])
    low = lax.broadcasted_iota(jnp.int32, (circle, 2 * span), 1) < span
    for tag, ref in enumerate((x_own, x_x, x_y, x_d)):
        start = (lat ^ tag) * height
        strips = [
            ref.at[pl.ds((4 - at) % 4 * many, many)].reshape(half, height, width, 2 * span) for at in range(4)
        ]

        @pl.loop(0, half * height)
        def _(step, strips=strips, start=start):
            lev, row = step // height, lax.rem(step, height)
            line = jnp.concatenate([s[lev, row] for s in strips], axis=0).astype(jnp.float32)
            turned = pltpu.roll(line, span, 1)
            for upper in range(2):
                same = jnp.where(low, turned, line) if upper else jnp.where(low, line, turned)
                before = pltpu.roll(same, 1, 0)
                after = pltpu.roll(same, circle - 1, 0)
                at = upper * half + lev
                xs[at, 1 + start + row, :, 0 : 2 * span] = jnp.where(low, before, same).astype(xs.dtype)
                xs[at, 1 + start + row, :, 2 * span : 4 * span] = after.astype(xs.dtype)


def turn(gt, slot, core, first, second, levels):
    many, filters = first.shape
    line = many // levels
    for lev in range(levels):
        block = jnp.concatenate([first[lev * line : (lev + 1) * line], second[lev * line : (lev + 1) * line]], axis=0)
        gt[
            lev * filters : (lev + 1) * filters,
            pl.ds(pl.multiple_of((2 * slot + core) * 2 * line, 2 * line), 2 * line),
        ] = block.T


def taps_kernel(pos, xs, g0, g1, g3, s0, s1, s3, g2, s2, out, gt, acc):
    levels, rows, circle, lanes = xs.shape
    rows, width, span = rows - 2, circle // 4, lanes // 4
    filters = gt.shape[0] // levels
    deep = rows * width
    right = lax.rem(pos[1], 2)
    many = g2.shape[1]
    for core, parts, last in ((pos[0], (g0, g3, g1), g2), (1 - pos[0], (s0, s3, s1), s2)):
        for slot, part in zip((0, 1, 3), parts):
            first = part[pl.ds(pl.multiple_of(right * many, many), many), :]
            second = part[pl.ds(pl.multiple_of((1 - right) * many, many), many), :]
            turn(gt, slot, core, first, second, levels)
        turn(gt, 2, core, last[right], last[1 - right], levels)
    acc[...] = jnp.zeros_like(acc)

    @pl.loop(0, 3)
    def _(lat_by):
        for lev in range(levels):
            first, last = max(lev - 1, 0), min(lev + 1, levels - 1)
            to = (first - lev + 1) * filters
            many = (last - first + 1) * filters
            total = acc[lat_by, to : to + many, :]
            for place in range(4):
                total += jnp.dot(
                    gt[first * filters : (last + 1) * filters, place * deep : (place + 1) * deep],
                    xs[lev, pl.ds(lat_by, rows), place * width : (place + 1) * width].reshape(deep, lanes),
                    preferred_element_type=jnp.float32,
                )
            acc[lat_by, to : to + many, :] = total

    scale = 1.0 / math.sqrt(levels * rows * circle)
    for lat_by in range(3):
        for lev_at in range(3):
            block = acc[lat_by, lev_at * filters : (lev_at + 1) * filters, :].T * scale
            for lon_at in range(3):
                out[(2 - lev_at) * 9 + lat_by * 3 + lon_at] = block[lon_at * span : (lon_at + 1) * span]


def code_kernel(pos, held, after, out):
    del pos, after
    taps, span, filters = held.shape
    most = jnp.abs(held[0])
    for tap in range(1, taps):
        most = jnp.maximum(most, jnp.abs(held[tap]))
    top = jnp.maximum(jnp.max(most, axis=(0, 1), keepdims=True), 1e-30)
    power = jnp.ceil(jnp.log(top) * (1.0 / math.log(2.0))) - 15.0
    unit = jnp.broadcast_to(jnp.exp2(power), (16, filters)).astype(out.dtype).astype(jnp.float32)
    shrink = 1.0 / unit[0:1]
    unit = unit.astype(out.dtype)
    for tap in range(taps):
        value = held[tap] * shrink
        square = value * value
        code = (square * value * jnp.abs(value)).astype(out.dtype)
        out[tap * span : (tap + 1) * span, :] = code
    out[taps * span :, :] = unit


def both_kernel(pos, west, east, after1, after2, both, half_3, half_1):
    del pos, after1, after2
    size, half = west.shape[0], half_3.shape[0]
    both[0:size, :] = west[...]
    both[size:, :] = east[...]
    half_3[...] = west[0:half, :]
    half_1[...] = east[half:, :]


def cross_kernel(pos, by_x, by_y, after1, after2, top, bottom):
    del pos, after1, after2
    cut = top.shape[0]
    top[...] = by_y[0:cut, :]
    bottom[...] = by_x[cut:, :]


def across_kernel(pos, half_3, half_1, after, late):
    del pos, after
    half = half_3.shape[0]
    late[0:half, :] = half_3[...]
    late[half:, :] = half_1[...]


def unpack_kernel(pos, *refs, slabs, count, span):
    sources = refs[:count]
    total, token, buffers, sems = refs[-4:]
    slots, group = buffers.shape[:2]
    wide = buffers.shape[-1] // 4
    token[...] = jnp.zeros_like(token)
    parts = []
    for step, first, taps, pieces in slabs:
        for at in range(0, taps, group):
            parts.append((step, first + at, min(group, taps - at), at, pieces))

    def copy(at):
        step, first, many, _, _ = parts[at]
        lon_at = pl.multiple_of(lax.rem(pos[2] + step, 4) * span, span)
        return pltpu.make_async_copy(
            buffers.at[at % slots, pl.ds(0, many)],
            total.at[pl.ds(first, many), pl.ds(lon_at, span)],
            sems.at[at % slots],
        )

    for at, (_, _, many, skip, pieces) in enumerate(parts):
        if at >= slots:
            copy(at - slots).wait()
        for tag, ((power_in, power_row), *segments) in enumerate(pieces):
            unit = sources[power_in][power_row : power_row + 16, :].astype(jnp.float32)[0:1]
            lanes = pl.ds(pl.multiple_of((pos[1] ^ tag) * wide, wide), wide)
            for tap in range(many):
                begin, which, row = [segment for segment in segments if segment[0] <= skip + tap][-1]
                start = row + (skip + tap - begin) * span
                code = sources[which][start : start + span, :].astype(jnp.float32)
                root = lax.rsqrt(lax.rsqrt(jnp.abs(code))) * unit
                buffers[at % slots, tap, :, lanes] = jnp.where(code < 0, -root, root)
        copy(at).start()
    for at in range(max(len(parts) - slots, 0), len(parts)):
        copy(at).wait()


def unpack(pos, total, sources, after, slabs, span, name):
    slots, group = 4, 3
    wide = total.shape[2]
    ins = (pos, *sources, *after, total)
    token = jax.ShapeDtypeStruct((8, 128), jnp.float32)
    return pl.pallas_call(
        lambda *refs: unpack_kernel(*refs, slabs=slabs, count=len(sources), span=span),
        out_shape=[jax.ShapeDtypeStruct(total.shape, total.dtype), token],
        in_specs=[pl.BlockSpec(memory_space=SMEM)]
        + [pl.BlockSpec(memory_space=VMEM)] * len(sources)
        + [pl.BlockSpec(memory_space=pl.ANY)] * (len(after) + 1),
        out_specs=[pl.BlockSpec(memory_space=pl.ANY), pl.BlockSpec(memory_space=VMEM)],
        scratch_shapes=[VMEM((slots, group, span, wide), jnp.float32), pltpu.SemaphoreType.DMA((slots,))],
        input_output_aliases={len(ins) - 1: 0},
        cost_estimate=pl.CostEstimate(flops=0, bytes_accessed=4 * 2**20, transcendentals=0),
        compiler_params=pltpu.CompilerParams(vmem_limit_bytes=51 * 1024 * 1024),
        name=name,
    )(*ins)


def field_kernel(pos, after, mine, theirs, w, out, copies, acc):
    del after
    step = pl.program_id(0)
    levels, height, width, chans = out.shape
    many = mine.shape[-1]

    @pl.when(step == 0)
    def _():
        copies[:, 0] = jnp.zeros_like(copies[:, 0])
        copies[:, levels + 1] = jnp.zeros_like(copies[:, levels + 1])
        line_at = lax.broadcasted_iota(jnp.int32, (width, many), 0)
        for which, field in ((pos[0], mine), (1 - pos[0], theirs)):
            lanes = pl.ds(pl.multiple_of(which * many, many), many)
            for lev in range(levels):
                for row in range(height + 2):
                    line = field[lev, row, 0:width].astype(jnp.float32)
                    west = field[lev, row, width : width + 1].astype(jnp.float32)
                    east = field[lev, row, width + 8 : width + 9].astype(jnp.float32)
                    before = jnp.where(line_at == 0, west, pltpu.roll(line, 1, 0))
                    later = jnp.where(line_at == width - 1, east, pltpu.roll(line, width - 1, 0))
                    copies[0, lev + 1, row, :, lanes] = later.astype(copies.dtype)
                    copies[1, lev + 1, row, :, lanes] = field[lev, row, 0:width]
                    copies[2, lev + 1, row, :, lanes] = before.astype(copies.dtype)
        acc[...] = jnp.zeros_like(acc)

    lev_by, lat_by = step // 3, lax.rem(step, 3)
    cells = [
        copies[at, pl.ds(2 - lev_by, levels), pl.ds(2 - lat_by, height)].reshape(
            levels * height * width, 2 * many
        )
        for at in range(3)
    ]
    acc[...] += lax.dot_general(
        jnp.concatenate(cells, axis=1),
        jnp.concatenate([w[at] for at in range(3)], axis=1),
        (((1,), (1,)), ((), ())),
        preferred_element_type=jnp.float32,
    )

    @pl.when(step == 8)
    def _():
        out[...] = acc[...].reshape(out.shape).astype(out.dtype)


def blocked_body(inputs, weights, out_grad):
    chans, levels, height, width = inputs.shape
    filters = weights.shape[2]
    bf16, f32 = jnp.bfloat16, jnp.float32
    lat, lon = lax.axis_index("lat"), lax.axis_index("lon")
    pos = jnp.stack([lax.axis_index("ch"), lat, lon]).astype(jnp.int32)
    x_cells = jnp.transpose(inputs, (1, 2, 3, 0))
    g_cells = jnp.transpose(out_grad, (1, 2, 3, 0))
    taps = jnp.transpose(weights, (1, 0, 2))
    cells = levels * height * width
    span, wide = chans // 4, filters // 4
    rows, circle = 4 * height, 4 * width
    edge = levels * height

    to_same = lambda c, a, o: (a // 2, 2 * c + a % 2, o)
    to_other = lambda c, a, o: (a // 2, 2 * c + 1 - a % 2, o)
    many = cells // 2
    block = jax.ShapeDtypeStruct((cells, wide), bf16)
    strip = jax.ShapeDtypeStruct((2 * levels * width, 2 * span), bf16)
    g_same, g_other, x0, x1, x2, x3, rim_x, rim_d = call(
        pack_kernel,
        [block, block]
        + [jax.ShapeDtypeStruct((many + extra, 2 * span), bf16) for extra in (0, 2 * edge, 0, 2 * edge)]
        + [strip, strip],
        (pos, x_cells, g_cells),
        [VMEM((4, many, 2 * span), bf16)],
        0,
        "pack",
        16,
    )
    g_s = move(g_same, to_same)
    g_o = move(g_other, to_other)
    x_r1 = move(x1, lon_by(1))
    x_r3 = move(x3, lon_by(-1))
    x_r2 = move(x2, lon_by(2))
    by_x = move(rim_x, lat_xor(1))
    by_d = move(rim_d, lat_xor(3))

    inner = 4 * many
    (g0,) = call(
        first_pair_kernel,
        [jax.ShapeDtypeStruct((2 * cells + 80, wide), bf16)],
        (pos, g_s, g_o, x_r1, x_r2, x_r3),
        [],
        0,
        "pair_0",
        16,
        held=3,
    )
    x_own, x_own_y = call(
        spread_kernel,
        [jax.ShapeDtypeStruct((count, 2 * span), bf16) for count in (inner + 4 * edge, inner)],
        (pos, x0, x_r1, x_r2, x_r3, by_x, by_d),
        [],
        0,
        "spread",
        16,
        held=2,
    )
    x_x = move(x_own, lat_xor(1))
    x_d = move(x_own, lat_xor(3))
    x_y = move(x_own_y, lat_xor(2))
    g1 = move(g0, lon_by(1))
    g3 = move(g0, lon_by(-1))
    far_a, far_b = call(split_kernel, [block, block], (pos, g1, g3), [], 0, "split", 16)
    g2a = move(far_a, lon_by(1))
    g2b = move(far_b, lon_by(-1))
    s0, s1, s3 = move(g0, sibling), move(g1, sibling), move(g3, sibling)
    xs, total = pl.pallas_call(
        lines_kernel,
        out_shape=[
            jax.ShapeDtypeStruct((levels, rows + 2, circle, 4 * span), bf16),
            jax.ShapeDtypeStruct((27, chans, filters), f32),
        ],
        in_specs=[pl.BlockSpec(memory_space=SMEM)]
        + [pl.BlockSpec(memory_space=VMEM)] * 4
        + [pl.BlockSpec(memory_space=pl.ANY)],
        out_specs=[pl.BlockSpec(memory_space=VMEM)] + [pl.BlockSpec(memory_space=pl.ANY)],
        cost_estimate=pl.CostEstimate(flops=0, bytes_accessed=2**20, transcendentals=0),
        compiler_params=pltpu.CompilerParams(vmem_limit_bytes=24 * 1024 * 1024),
        name="lines",
    )(pos, x_own, x_x, x_y, x_d, far_a)
    (mine,) = call(
        mine_kernel,
        [jax.ShapeDtypeStruct((levels, height + 2, width + 16, chans), bf16)],
        (pos, g_cells, x_own, x_x, x_d, by_x, by_d, xs),
        [],
        0,
        "mine",
        16,
        held=1,
    )
    theirs = move(mine, sibling)
    (g2,) = call(
        pair_kernel, [jax.ShapeDtypeStruct((2, cells, wide), bf16)], (pos, g2a, g2b, xs), [], 0, "pair", 16, held=1
    )
    s2 = move(g2, sibling)
    end = 27 * span
    size = end + 16
    half = size // 32 * 16
    cut = 14 * span
    slab = lambda count: jax.ShapeDtypeStruct((count, wide), bf16)
    (grads,) = call(
        taps_kernel,
        [jax.ShapeDtypeStruct((27, span, wide), f32)],
        (pos, xs, g0, g1, g3, s0, s1, s3, g2, s2),
        [VMEM((levels * wide, rows * circle), bf16), VMEM((3, 3 * wide, 4 * span), f32)],
        2 * 27 * span * wide * rows * circle * levels,
        "taps",
        28,
    )
    (own,) = call(code_kernel, [slab(size)], (pos, grads, theirs), [], 0, "code", 16, held=1)

    whole = lambda t: (0, 0, 0, 0)
    field = pl.pallas_call(
        field_kernel,
        out_shape=jax.ShapeDtypeStruct((levels, height, width, chans), bf16),
        grid=(9,),
        in_specs=[
            pl.BlockSpec(memory_space=SMEM),
            pl.BlockSpec(memory_space=pl.ANY),
            pl.BlockSpec(mine.shape, whole),
            pl.BlockSpec(mine.shape, whole),
            pl.BlockSpec((3, chans, filters), lambda t: (t, 0, 0)),
        ],
        out_specs=pl.BlockSpec((levels, height, width, chans), whole),
        scratch_shapes=[
            VMEM((3, levels + 2, height + 2, width, filters), bf16),
            VMEM((cells, chans), f32),
        ],
        cost_estimate=pl.CostEstimate(
            flops=4 * 27 * chans * filters * cells, bytes_accessed=27 * chans * filters * 2, transcendentals=0
        ),
        compiler_params=pltpu.CompilerParams(vmem_limit_bytes=20 * 1024 * 1024),
        name="field",
    )(pos, own, mine, theirs, taps)

    def to_plane(share):
        return move(share, lat_xor(1)), move(share, lat_xor(2))

    def to_diagonal(by_x, by_y, cut, after1, after2, name):
        top, bottom = call(
            cross_kernel, [slab(cut), slab(by_x.shape[0] - cut)], (pos, by_x, by_y, after1, after2), [], 0, name, 16, held=2
        )
        return move(top, lat_xor(1)), move(bottom, lat_xor(2))

    from_3 = move(own, lon_by(1))
    from_1 = move(own, lon_by(-1))
    own_x, own_y = to_plane(own)
    own_top, own_bottom = to_diagonal(own_x, own_y, cut, field, own, "cross_1")
    pair, half_3, half_1 = call(
        both_kernel,
        [slab(2 * size), slab(half), slab(size - half)],
        (pos, from_3, from_1, own_top, own_bottom),
        [],
        0,
        "both",
        16,
        held=2,
    )
    half_3 = move(half_3, lon_by(1))
    half_1 = move(half_1, lon_by(-1))
    pair_x, pair_y = to_plane(pair)
    (from_2,) = call(across_kernel, [slab(size)], (pos, half_3, half_1, pair), [], 0, "across", 16, held=1)
    pair_top, pair_bottom = to_diagonal(pair_x, pair_y, size, pair, own, "cross_2")
    from_2x, from_2y = to_plane(from_2)

    def piece(which, row=0):
        return ((which, row + end), (0, which, row))

    def split_piece(top, bottom):
        return ((bottom, end - cut), (0, top, 0), (cut // span, bottom, 0))

    slabs = [(0, 0, 27, [piece(0), piece(1), piece(2), split_piece(3, 4)])]
    total, token = unpack(pos, total, [own, own_x, own_y, own_top, own_bottom], [pair], slabs, span, "unpack_1")
    from_2top, from_2bottom = to_diagonal(from_2x, from_2y, cut, token, pair, "cross_3")
    slabs = [
        (3, 0, 27, [piece(0), piece(2), piece(3), piece(4)]),
        (1, 0, 27, [piece(1), piece(2, size), piece(3, size), piece(5)]),
    ]
    sources = [from_3, from_1, pair_x, pair_y, pair_top, pair_bottom]
    total, _ = unpack(pos, total, sources, [from_2], slabs, span, "unpack_2")
    slabs = [(2, 0, 27, [piece(0), piece(1), piece(2), split_piece(3, 4)])]
    sources = [from_2, from_2x, from_2y, from_2top, from_2bottom]
    total, _ = unpack(pos, total, sources, [], slabs, span, "unpack_3")
    return (jnp.transpose(field, (3, 0, 1, 2)), jnp.transpose(total, (1, 0, 2)))


def body(inputs, weights, out_grad):
    chans, levels, height, width = inputs.shape
    shape = tuple(lax.axis_size(axis) for axis in AXES)
    fits = (
        shape == (2, 4, 4)
        and chans == out_grad.shape[0] == 256
        and weights.shape[2] == 512
        and levels % 2 == 0
        and height % 2 == 0
        and width % 16 == 0
    )
    return (blocked_body if fits else plain_body)(inputs, weights, out_grad)


def solution(mesh):
    in_specs = (P("ch", None, "lat", "lon"), P("ch", None, None), P("ch", None, "lat", "lon"))
    out_specs = (P("ch", None, "lat", "lon"), P("ch", None, None))
    return jax.shard_map(body, mesh=mesh, in_specs=in_specs, out_specs=out_specs, check_vma=False)
```

```python
import math

import jax
import jax.numpy as jnp
from jax import lax
from jax.experimental import pallas as pl
from jax.experimental.pallas import tpu as pltpu
from jax.sharding import PartitionSpec as P

VMEM = pltpu.VMEM
SMEM = pltpu.SMEM
AXES = ("ch", "lat", "lon")


def padded_2(cells, sides, width):
    for axis, dim in sides:
        count = lax.axis_size(axis)
        head = lax.slice_in_dim(cells, 0, width, axis=dim)
        tail = lax.slice_in_dim(cells, cells.shape[dim] - width, cells.shape[dim], axis=dim)
        cells = jnp.concatenate(
            [
                lax.ppermute(tail, axis, [(i, (i + 1) % count) for i in range(count)]),
                cells,
                lax.ppermute(head, axis, [((i + 1) % count, i) for i in range(count)]),
            ],
            axis=dim,
        )
    return cells


def mask_rims(padded):
    count = lax.axis_size("lat")
    where_lat = lax.axis_index("lat")
    lines = jnp.arange(padded.shape[2])
    drop = (lines == 0) & (where_lat == 0) | (lines == padded.shape[2] - 1) & (
        where_lat == count - 1
    )
    return jnp.where(drop[None, None, :, None], jnp.zeros((), padded.dtype), padded)


def pad_levels(field):
    return jnp.pad(field, ((0, 0), (1, 1), (0, 0), (0, 0)))


def plain_body(inputs, weights, out_grad):
    chans, levels, height, width = inputs.shape
    input_pad = pad_levels(mask_rims(padded_2(inputs, (("lat", 2), ("lon", 3)), 1)))
    grad_inner = lax.all_gather(out_grad, "ch", axis=0, tiled=True)
    grad_pad = pad_levels(mask_rims(padded_2(grad_inner, (("lat", 2), ("lon", 3)), 1)))
    filters = grad_pad.shape[0]
    products = jnp.dot(
        weights.reshape(chans * 27, filters),
        grad_pad.reshape(filters, -1),
        preferred_element_type=jnp.float32,
    )
    products = products.reshape((chans, 27) + tuple(grad_pad.shape[1:]))
    total = jnp.zeros((chans, levels, height, width), jnp.float32)
    pieces = []
    for tap in range(27):
        lev, lat, lon = tap // 9 - 1, tap // 3 % 3 - 1, tap % 3 - 1
        total = (
            total
            + products[
                :,
                tap,
                1 - lev : 1 - lev + levels,
                1 - lat : 1 - lat + height,
                1 - lon : 1 - lon + width,
            ]
        )
        pieces.append(
            input_pad[
                :,
                1 + lev : 1 + lev + levels,
                1 + lat : 1 + lat + height,
                1 + lon : 1 + lon + width,
            ]
        )
    columns = jnp.stack(pieces, axis=1).reshape(chans * 27, -1)
    partial_grad = lax.dot_general(
        columns,
        grad_inner.reshape(filters, -1),
        (((1,), (1,)), ((), ())),
        preferred_element_type=jnp.float32,
    )
    summed = lax.psum(partial_grad, ("lat", "lon"))
    cells = levels * height * width * lax.axis_size("lat") * lax.axis_size("lon")
    weight_grad = (summed * (1.0 / math.sqrt(cells))).reshape(chans, 27, filters)
    return (total.astype(jnp.bfloat16), weight_grad)


def move(x, target):
    pairs = []
    for i in range(32):
        to = target(i // 16, i // 4 % 4, i % 4)
        if to is not None:
            pairs.append((i, (to[0] * 4 + to[1]) * 4 + to[2]))
    return lax.ppermute(x, AXES, pairs)


def lon_by(step):
    return lambda c, a, o: (c, a, (o + step) % 4)


def lat_xor(mask):
    return lambda c, a, o: (c, a ^ mask, o)


def sibling(c, a, o):
    return (1 - c, a, o)


def call(kernel, outs, ins, scratch, flops, name, limit, held=0):
    read = len(ins) - 1 - held
    moved = sum(math.prod(x.shape) * x.dtype.itemsize for x in list(ins[1 : 1 + read]) + list(outs))
    return pl.pallas_call(
        kernel,
        out_shape=outs,
        in_specs=[pl.BlockSpec(memory_space=SMEM)]
        + [pl.BlockSpec(memory_space=VMEM)] * read
        + [pl.BlockSpec(memory_space=pl.ANY)] * held,
        out_specs=[pl.BlockSpec(memory_space=VMEM)] * len(outs),
        scratch_shapes=scratch,
        cost_estimate=pl.CostEstimate(flops=flops, bytes_accessed=moved, transcendentals=0),
        compiler_params=pltpu.CompilerParams(vmem_limit_bytes=limit * 1024 * 1024),
        name=name,
    )(*ins)


def pack_kernel(pos, x, g, g_same, g_other, x0, x1, x2, x3, rim_x, rim_d, held):
    levels, height, width, chans = x.shape
    half, wide = levels // 2, chans // 2
    right = lax.rem(pos[1], 2)
    for out, at in ((g_same, right), (g_other, 1 - right)):
        out[...] = g[:, :, :, pl.ds(pl.multiple_of(at * wide, wide), wide)].reshape(out.shape)
    many = x0.shape[0]
    for block in range(4):
        at = block * (chans // 4)
        lo = x[0:half, :, :, at : at + chans // 4]
        hi = x[half:levels, :, :, at : at + chans // 4]
        held[block] = jnp.concatenate([lo, hi], axis=-1).reshape(held.shape[1:])
    lon = pos[2]
    for step, out in enumerate((x0, x1, x2, x3)):
        out[0:many, :] = held[lax.rem(lon + step, 4)]
    for out, column in ((x1, width - 1), (x3, 0)):
        rim = g[:, :, column, :].reshape(levels * height, chans)
        out[many : many + levels * height, :] = rim[:, 0:wide]
        out[many + levels * height :, :] = rim[:, wide:]
    even = right == 0
    low, high = g[:, 0], g[:, height - 1]
    line = levels * width
    for out, upward in ((rim_x, even), (rim_d, jnp.logical_not(even))):
        facing = jnp.where(upward, high, low).reshape(line, chans)
        for at in range(2):
            out[at * line : (at + 1) * line, :] = facing[:, at * wide : (at + 1) * wide]


def spread_kernel(pos, x0, x1, x2, x3, after1, after2, own, own_y):
    del pos, after1, after2
    many = x0.shape[0]
    for at, piece in enumerate((x0, x1, x2, x3)):
        own[at * many : (at + 1) * many, :] = piece[0:many, :]
        own_y[at * many : (at + 1) * many, :] = piece[0:many, :]
    extra = x1.shape[0] - many
    own[4 * many : 4 * many + extra, :] = x1[many:, :]
    own[4 * many + extra :, :] = x3[many:, :]


def split_kernel(pos, west, east, first, second):
    del pos
    many = first.shape[0]
    first[...] = west[0:many, :]
    second[...] = east[many : 2 * many, :]


def mine_kernel(pos, g, own, x_x, x_d, by_x, by_d, after, mine):
    del after
    levels, height, width, chans = g.shape
    edge, line, wide = levels * height, levels * width, chans // 2
    inner = own.shape[0] - 4 * edge
    mine[:, 1 : height + 1, 0:width, :] = g[...]

    def columns(message, rows):
        for side in range(2):
            for half in range(2):
                start = inner + (2 * side + half) * edge
                rim = message[start : start + edge, :].reshape(levels, height, wide)
                at = width + 8 * side
                for row, to in rows:
                    mine[:, to, at : at + 8, half * wide : (half + 1) * wide] = jnp.broadcast_to(
                        rim[:, row : row + 1], (levels, 8, wide)
                    )

    columns(own, [(row, row + 1) for row in range(height)])

    def lines(strip, message, row, to):
        for half in range(2):
            part = strip[half * line : (half + 1) * line, :]
            mine[:, to, 0:width, half * wide : (half + 1) * wide] = part.reshape(levels, width, wide)
        columns(message, [(row, to)])

    lat = pos[1]
    odd = lax.rem(lat, 2)

    @pl.when(odd == 1)
    def _():
        lines(by_x, x_x, height - 1, 0)
        lines(by_d, x_d, 0, height + 1)

    @pl.when(odd == 0)
    def _():
        lines(by_d, x_d, height - 1, 0)
        lines(by_x, x_x, 0, height + 1)

    @pl.when(lat == 0)
    def _():
        mine[:, 0] = jnp.zeros_like(mine[:, 0])

    @pl.when(lat == 3)
    def _():
        mine[:, height + 1] = jnp.zeros_like(mine[:, height + 1])


def pair_kernel(pos, one, two, after, both):
    del pos, after
    both[0] = one[...]
    both[1] = two[...]


def first_pair_kernel(pos, one, two, after1, after2, after3, both):
    del pos, after1, after2, after3
    many = one.shape[0]
    both[0:many, :] = one[...]
    both[many : 2 * many, :] = two[...]
    both[2 * many :, :] = jnp.zeros((both.shape[0] - 2 * many, both.shape[1]), both.dtype)


def lines_kernel(pos, x_own, x_x, x_y, x_d, after, xs, blank):
    del after, blank
    lat = pos[1]
    levels, rows, circle, lanes = xs.shape
    rows, width, span, half = rows - 2, circle // 4, lanes // 4, levels // 2
    height = rows // 4
    many = half * height * width
    xs[:, 0] = jnp.zeros_like(xs[:, 0])
    xs[:, rows + 1] = jnp.zeros_like(xs[:, rows + 1])
    low = lax.broadcasted_iota(jnp.int32, (circle, 2 * span), 1) < span
    for tag, ref in enumerate((x_own, x_x, x_y, x_d)):
        start = (lat ^ tag) * height
        strips = [
            ref.at[pl.ds((4 - at) % 4 * many, many)].reshape(half, height, width, 2 * span) for at in range(4)
        ]

        @pl.loop(0, half * height)
        def _(step, strips=strips, start=start):
            lev, row = step // height, lax.rem(step, height)
            line = jnp.concatenate([s[lev, row] for s in strips], axis=0).astype(jnp.float32)
            turned = pltpu.roll(line, span, 1)
            for upper in range(2):
                same = jnp.where(low, turned, line) if upper else jnp.where(low, line, turned)
                before = pltpu.roll(same, 1, 0)
                after = pltpu.roll(same, circle - 1, 0)
                at = upper * half + lev
                xs[at, 1 + start + row, :, 0 : 2 * span] = jnp.where(low, before, same).astype(xs.dtype)
                xs[at, 1 + start + row, :, 2 * span : 4 * span] = after.astype(xs.dtype)


def turn(gt, slot, core, first, second, levels):
    many, filters = first.shape
    line = many // levels
    for lev in range(levels):
        block = jnp.concatenate([first[lev * line : (lev + 1) * line], second[lev * line : (lev + 1) * line]], axis=0)
        gt[
            lev * filters : (lev + 1) * filters,
            pl.ds(pl.multiple_of((2 * slot + core) * 2 * line, 2 * line), 2 * line),
        ] = block.T


def taps_kernel(pos, xs, g0, g1, g3, s0, s1, s3, g2, s2, out, gt, acc):
    levels, rows, circle, lanes = xs.shape
    rows, width, span = rows - 2, circle // 4, lanes // 4
    filters = gt.shape[0] // levels
    deep = rows * width
    right = lax.rem(pos[1], 2)
    many = g2.shape[1]
    for core, parts, last in ((pos[0], (g0, g3, g1), g2), (1 - pos[0], (s0, s3, s1), s2)):
        for slot, part in zip((0, 1, 3), parts):
            first = part[pl.ds(pl.multiple_of(right * many, many), many), :]
            second = part[pl.ds(pl.multiple_of((1 - right) * many, many), many), :]
            turn(gt, slot, core, first, second, levels)
        turn(gt, 2, core, last[right], last[1 - right], levels)
    acc[...] = jnp.zeros_like(acc)

    @pl.loop(0, 3)
    def _(lat_by):
        for lev in range(levels):
            first, last = max(lev - 1, 0), min(lev + 1, levels - 1)
            to = (first - lev + 1) * filters
            many = (last - first + 1) * filters
            total = acc[lat_by, to : to + many, :]
            for place in range(4):
                total += jnp.dot(
                    gt[first * filters : (last + 1) * filters, place * deep : (place + 1) * deep],
                    xs[lev, pl.ds(lat_by, rows), place * width : (place + 1) * width].reshape(deep, lanes),
                    preferred_element_type=jnp.float32,
                )
            acc[lat_by, to : to + many, :] = total

    scale = 1.0 / math.sqrt(levels * rows * circle)
    for lat_by in range(3):
        for lev_at in range(3):
            block = acc[lat_by, lev_at * filters : (lev_at + 1) * filters, :].T * scale
            for lon_at in range(3):
                out[(2 - lev_at) * 9 + lat_by * 3 + lon_at] = block[lon_at * span : (lon_at + 1) * span]


def code_kernel(pos, held, after, out, late):
    del pos, after
    taps, span, filters = held.shape
    most = jnp.abs(held[0])
    for tap in range(1, taps):
        most = jnp.maximum(most, jnp.abs(held[tap]))
    top = jnp.maximum(jnp.max(most, axis=(0, 1), keepdims=True), 1e-30)
    power = jnp.ceil(jnp.log(top) * (1.0 / math.log(2.0))) - 15.0
    unit = jnp.broadcast_to(jnp.exp2(power), (16, filters)).astype(out.dtype).astype(jnp.float32)
    shrink = 1.0 / unit[0:1]
    unit = unit.astype(out.dtype)
    skip = out.shape[0] - late.shape[0]
    for tap in range(taps):
        value = held[tap] * shrink
        square = value * value
        code = (square * value * jnp.abs(value)).astype(out.dtype)
        out[tap * span : (tap + 1) * span, :] = code
        if tap * span >= skip:
            late[tap * span - skip : (tap + 1) * span - skip, :] = code
    out[taps * span :, :] = unit
    late[taps * span - skip :, :] = unit


def both_kernel(pos, west, east, after1, after2, after3, both, half_3, half_1):
    del pos, after1, after2, after3
    size, half = west.shape[0], half_3.shape[0]
    both[0:size, :] = west[...]
    both[size:, :] = east[...]
    half_3[...] = west[0:half, :]
    half_1[...] = east[half:, :]


def cross_kernel(pos, by_x, by_y, after1, after2, top, bottom):
    del pos, after1, after2
    cut = top.shape[0]
    top[...] = by_y[0:cut, :]
    bottom[...] = by_x[cut:, :]


def across_kernel(pos, half_3, half_1, after, late):
    del pos, after
    half = half_3.shape[0]
    late[0:half, :] = half_3[...]
    late[half:, :] = half_1[...]


def block_kernel(pos, own, x, y, top, bottom, block):
    del pos
    rows = block.shape[0] // 4
    for at, (piece, end) in enumerate(((own, own), (x, x), (y, y), (top, bottom))):
        block[at * rows : (at + 1) * rows - 16, :] = piece[0 : rows - 16, :]
        block[(at + 1) * rows - 16 : (at + 1) * rows, :] = end[end.shape[0] - 16 :, :]


def hand_kernel(pos, block_3, block_1, first, second):
    del pos
    many = first.shape[0]
    first[...] = block_3[0:many, :]
    second[...] = block_1[many:, :]


def unpack_kernel(pos, *refs, slabs, count, span):
    sources = refs[:count]
    total, token, buffers, sems = refs[-4:]
    slots, group = buffers.shape[:2]
    wide = buffers.shape[-1] // 4
    token[...] = jnp.zeros_like(token)
    parts = []
    for step, first, taps, pieces in slabs:
        for at in range(0, taps, group):
            parts.append((step, first + at, min(group, taps - at), at, pieces))

    def copy(at):
        step, first, many, _, _ = parts[at]
        lon_at = pl.multiple_of(lax.rem(pos[2] + step, 4) * span, span)
        return pltpu.make_async_copy(
            buffers.at[at % slots, pl.ds(0, many)],
            total.at[pl.ds(first, many), pl.ds(lon_at, span)],
            sems.at[at % slots],
        )

    for at, (_, _, many, skip, pieces) in enumerate(parts):
        if at >= slots:
            copy(at - slots).wait()
        for tag, ((power_in, power_row), *segments) in enumerate(pieces):
            unit = sources[power_in][power_row : power_row + 16, :].astype(jnp.float32)[0:1]
            lanes = pl.ds(pl.multiple_of((pos[1] ^ tag) * wide, wide), wide)
            for tap in range(many):
                begin, which, row = [segment for segment in segments if segment[0] <= skip + tap][-1]
                start = row + (skip + tap - begin) * span
                code = sources[which][start : start + span, :].astype(jnp.float32)
                root = lax.rsqrt(lax.rsqrt(jnp.abs(code))) * unit
                buffers[at % slots, tap, :, lanes] = jnp.where(code < 0, -root, root)
        copy(at).start()
    for at in range(max(len(parts) - slots, 0), len(parts)):
        copy(at).wait()


def unpack(pos, total, sources, after, slabs, span, name):
    slots, group = 4, 3
    wide = total.shape[2]
    ins = (pos, *sources, *after, total)
    token = jax.ShapeDtypeStruct((8, 128), jnp.float32)
    return pl.pallas_call(
        lambda *refs: unpack_kernel(*refs, slabs=slabs, count=len(sources), span=span),
        out_shape=[jax.ShapeDtypeStruct(total.shape, total.dtype), token],
        in_specs=[pl.BlockSpec(memory_space=SMEM)]
        + [pl.BlockSpec(memory_space=VMEM)] * len(sources)
        + [pl.BlockSpec(memory_space=pl.ANY)] * (len(after) + 1),
        out_specs=[pl.BlockSpec(memory_space=pl.ANY), pl.BlockSpec(memory_space=VMEM)],
        scratch_shapes=[VMEM((slots, group, span, wide), jnp.float32), pltpu.SemaphoreType.DMA((slots,))],
        input_output_aliases={len(ins) - 1: 0},
        cost_estimate=pl.CostEstimate(flops=0, bytes_accessed=4 * 2**20, transcendentals=0),
        compiler_params=pltpu.CompilerParams(vmem_limit_bytes=51 * 1024 * 1024),
        name=name,
    )(*ins)


def field_kernel(pos, after, mine, theirs, w, *refs, first, last):
    del after
    so_far = refs[0] if first else None
    out, copies, acc = refs[-3:]
    step = pl.program_id(0) + first
    levels, height, width, chans = mine.shape[0], mine.shape[1] - 2, mine.shape[2] - 16, mine.shape[3]
    many = mine.shape[-1]

    @pl.when(step == first)
    def _():
        copies[:, 0] = jnp.zeros_like(copies[:, 0])
        copies[:, levels + 1] = jnp.zeros_like(copies[:, levels + 1])
        line_at = lax.broadcasted_iota(jnp.int32, (width, many), 0)
        for which, field in ((pos[0], mine), (1 - pos[0], theirs)):
            lanes = pl.ds(pl.multiple_of(which * many, many), many)
            for lev in range(levels):
                for row in range(height + 2):
                    line = field[lev, row, 0:width].astype(jnp.float32)
                    west = field[lev, row, width : width + 1].astype(jnp.float32)
                    east = field[lev, row, width + 8 : width + 9].astype(jnp.float32)
                    before = jnp.where(line_at == 0, west, pltpu.roll(line, 1, 0))
                    later = jnp.where(line_at == width - 1, east, pltpu.roll(line, width - 1, 0))
                    copies[0, lev + 1, row, :, lanes] = later.astype(copies.dtype)
                    copies[1, lev + 1, row, :, lanes] = field[lev, row, 0:width]
                    copies[2, lev + 1, row, :, lanes] = before.astype(copies.dtype)
        acc[...] = so_far[...] if first else jnp.zeros_like(acc)

    lev_by, lat_by = step // 3, lax.rem(step, 3)
    cells = [
        copies[at, pl.ds(2 - lev_by, levels), pl.ds(2 - lat_by, height)].reshape(
            levels * height * width, 2 * many
        )
        for at in range(3)
    ]
    acc[...] += lax.dot_general(
        jnp.concatenate(cells, axis=1),
        jnp.concatenate([w[at] for at in range(3)], axis=1),
        (((1,), (1,)), ((), ())),
        preferred_element_type=jnp.float32,
    )

    @pl.when(step == last)
    def _():
        out[...] = acc[...].reshape(out.shape).astype(out.dtype)


def blocked_body(inputs, weights, out_grad):
    chans, levels, height, width = inputs.shape
    filters = weights.shape[2]
    bf16, f32 = jnp.bfloat16, jnp.float32
    lat, lon = lax.axis_index("lat"), lax.axis_index("lon")
    pos = jnp.stack([lax.axis_index("ch"), lat, lon]).astype(jnp.int32)
    x_cells = jnp.transpose(inputs, (1, 2, 3, 0))
    g_cells = jnp.transpose(out_grad, (1, 2, 3, 0))
    taps = jnp.transpose(weights, (1, 0, 2))
    cells = levels * height * width
    span, wide = chans // 4, filters // 4
    rows, circle = 4 * height, 4 * width
    edge = levels * height

    to_same = lambda c, a, o: (a // 2, 2 * c + a % 2, o)
    to_other = lambda c, a, o: (a // 2, 2 * c + 1 - a % 2, o)
    many = cells // 2
    block = jax.ShapeDtypeStruct((cells, wide), bf16)
    strip = jax.ShapeDtypeStruct((2 * levels * width, 2 * span), bf16)
    g_same, g_other, x0, x1, x2, x3, rim_x, rim_d = call(
        pack_kernel,
        [block, block]
        + [jax.ShapeDtypeStruct((many + extra, 2 * span), bf16) for extra in (0, 2 * edge, 0, 2 * edge)]
        + [strip, strip],
        (pos, x_cells, g_cells),
        [VMEM((4, many, 2 * span), bf16)],
        0,
        "pack",
        16,
    )
    g_s = move(g_same, to_same)
    g_o = move(g_other, to_other)
    x_r1 = move(x1, lon_by(1))
    x_r3 = move(x3, lon_by(-1))
    x_r2 = move(x2, lon_by(2))
    by_x = move(rim_x, lat_xor(1))
    by_d = move(rim_d, lat_xor(3))

    inner = 4 * many
    (g0,) = call(
        first_pair_kernel,
        [jax.ShapeDtypeStruct((2 * cells + 80, wide), bf16)],
        (pos, g_s, g_o, x_r1, x_r2, x_r3),
        [],
        0,
        "pair_0",
        16,
        held=3,
    )
    x_own, x_own_y = call(
        spread_kernel,
        [jax.ShapeDtypeStruct((count, 2 * span), bf16) for count in (inner + 4 * edge, inner)],
        (pos, x0, x_r1, x_r2, x_r3, by_x, by_d),
        [],
        0,
        "spread",
        16,
        held=2,
    )
    x_x = move(x_own, lat_xor(1))
    x_d = move(x_own, lat_xor(3))
    x_y = move(x_own_y, lat_xor(2))
    g1 = move(g0, lon_by(1))
    g3 = move(g0, lon_by(-1))
    far_a, far_b = call(split_kernel, [block, block], (pos, g1, g3), [], 0, "split", 16)
    g2a = move(far_a, lon_by(1))
    g2b = move(far_b, lon_by(-1))
    s0, s1, s3 = move(g0, sibling), move(g1, sibling), move(g3, sibling)
    xs, total = pl.pallas_call(
        lines_kernel,
        out_shape=[
            jax.ShapeDtypeStruct((levels, rows + 2, circle, 4 * span), bf16),
            jax.ShapeDtypeStruct((27, chans, filters), f32),
        ],
        in_specs=[pl.BlockSpec(memory_space=SMEM)]
        + [pl.BlockSpec(memory_space=VMEM)] * 4
        + [pl.BlockSpec(memory_space=pl.ANY)],
        out_specs=[pl.BlockSpec(memory_space=VMEM)] + [pl.BlockSpec(memory_space=pl.ANY)],
        cost_estimate=pl.CostEstimate(flops=0, bytes_accessed=2**20, transcendentals=0),
        compiler_params=pltpu.CompilerParams(vmem_limit_bytes=24 * 1024 * 1024),
        name="lines",
    )(pos, x_own, x_x, x_y, x_d, far_a)
    (mine,) = call(
        mine_kernel,
        [jax.ShapeDtypeStruct((levels, height + 2, width + 16, chans), bf16)],
        (pos, g_cells, x_own, x_x, x_d, by_x, by_d, xs),
        [],
        0,
        "mine",
        16,
        held=1,
    )
    theirs = move(mine, sibling)
    (g2,) = call(
        pair_kernel, [jax.ShapeDtypeStruct((2, cells, wide), bf16)], (pos, g2a, g2b, xs), [], 0, "pair", 16, held=1
    )
    s2 = move(g2, sibling)
    early = 3
    cut, end = early * span, 27 * span
    size = end + 16 - cut
    half = size // 32 * 16
    first_rows = cut + 16
    own_cut, late_cut = 14 * span, (27 - early) // 2 * span
    slab = lambda count: jax.ShapeDtypeStruct((count, wide), bf16)
    (grads,) = call(
        taps_kernel,
        [jax.ShapeDtypeStruct((27, span, wide), f32)],
        (pos, xs, g0, g1, g3, s0, s1, s3, g2, s2),
        [VMEM((levels * wide, rows * circle), bf16), VMEM((3, 3 * wide, 4 * span), f32)],
        2 * 27 * span * wide * rows * circle * levels,
        "taps",
        28,
    )
    own, late = call(code_kernel, [slab(end + 16), slab(size)], (pos, grads, theirs), [], 0, "code", 16, held=1)

    def part_of_field(after, first, last, so_far, out):
        whole = lambda t: (0, 0, 0, 0)
        before = [so_far] if first else []
        return pl.pallas_call(
            lambda *refs: field_kernel(*refs, first=first, last=last),
            out_shape=out,
            grid=(last - first + 1,),
            in_specs=[
                pl.BlockSpec(memory_space=SMEM),
                pl.BlockSpec(memory_space=pl.ANY),
                pl.BlockSpec(mine.shape, whole),
                pl.BlockSpec(mine.shape, whole),
                pl.BlockSpec((3, chans, filters), lambda t: (t + first, 0, 0)),
            ]
            + [pl.BlockSpec(x.shape, lambda t: (0, 0)) for x in before],
            out_specs=pl.BlockSpec(out.shape, lambda t: (0,) * len(out.shape)),
            scratch_shapes=[
                VMEM((3, levels + 2, height + 2, width, filters), bf16),
                VMEM((cells, chans), f32),
            ],
            cost_estimate=pl.CostEstimate(
                flops=2 * 27 * chans * filters * cells,
                bytes_accessed=14 * chans * filters * 2,
                transcendentals=0,
            ),
            compiler_params=pltpu.CompilerParams(vmem_limit_bytes=20 * 1024 * 1024),
            name="field",
        )(pos, after, mine, theirs, taps, *before)

    so_far = part_of_field(own, 0, 4, None, jax.ShapeDtypeStruct((cells, chans), f32))

    def to_plane(share):
        return move(share, lat_xor(1)), move(share, lat_xor(2))

    def to_diagonal(by_x, by_y, cut, after1, after2, name):
        top, bottom = call(
            cross_kernel, [slab(cut), slab(by_x.shape[0] - cut)], (pos, by_x, by_y, after1, after2), [], 0, name, 16, held=2
        )
        return move(top, lat_xor(1)), move(bottom, lat_xor(2)), top

    from_3 = move(late, lon_by(1))
    from_1 = move(late, lon_by(-1))
    own_x, own_y = to_plane(own)
    own_top, own_bottom, crossed = to_diagonal(own_x, own_y, own_cut, so_far, own, "cross_1")
    field = part_of_field(crossed, 5, 8, so_far, jax.ShapeDtypeStruct((levels, height, width, chans), bf16))
    pair, half_3, half_1 = call(
        both_kernel,
        [slab(2 * size), slab(half), slab(size - half)],
        (pos, from_3, from_1, own_top, own_bottom, field),
        [],
        0,
        "both",
        16,
        held=3,
    )
    half_3 = move(half_3, lon_by(1))
    half_1 = move(half_1, lon_by(-1))
    pair_x, pair_y = to_plane(pair)
    (block,) = call(
        block_kernel, [slab(4 * first_rows)], (pos, own, own_x, own_y, own_top, own_bottom), [], 0, "block", 16
    )
    early_3 = move(block, lon_by(1))
    early_1 = move(block, lon_by(-1))
    (from_2,) = call(across_kernel, [slab(size)], (pos, half_3, half_1, pair), [], 0, "across", 16, held=1)
    pair_top, pair_bottom, _ = to_diagonal(pair_x, pair_y, size, early_1, early_3, "cross_2")
    from_2x, from_2y = to_plane(from_2)
    hand_3, hand_1 = call(hand_kernel, [slab(2 * first_rows)] * 2, (pos, early_3, early_1), [], 0, "hand", 16)
    early_2a = move(hand_3, lon_by(1))
    early_2b = move(hand_1, lon_by(-1))

    def late_piece(which, row=0):
        return ((which, row + size - 16), (0, which, row))

    def early_piece(which, row):
        return ((which, row + cut), (0, which, row))

    pieces = [((which, end), (0, which, 0)) for which in range(3)]
    pieces.append(((4, end - own_cut), (0, 3, 0), (own_cut // span, 4, 0)))
    total, token = unpack(
        pos, total, [own, own_x, own_y, own_top, own_bottom], [block], [(0, 0, 27, pieces)], span, "unpack_1"
    )
    from_2top, from_2bottom, _ = to_diagonal(from_2x, from_2y, late_cut, token, pair, "cross_3")
    slabs = [
        (3, early, 27 - early, [late_piece(0), late_piece(2), late_piece(3), late_piece(4)]),
        (1, early, 27 - early, [late_piece(1), late_piece(2, size), late_piece(3, size), late_piece(5)]),
        (3, 0, early, [early_piece(6, tag * first_rows) for tag in range(4)]),
        (1, 0, early, [early_piece(7, tag * first_rows) for tag in range(4)]),
    ]
    total, _ = unpack(
        pos,
        total,
        [from_3, from_1, pair_x, pair_y, pair_top, pair_bottom, early_3, early_1],
        [hand_3],
        slabs,
        span,
        "unpack_2",
    )
    pieces = [late_piece(2), late_piece(3), late_piece(4)]
    pieces.append(((6, size - 16 - late_cut), (0, 5, 0), (late_cut // span, 6, 0)))
    slabs = [
        (2, 0, early, [early_piece(tag // 2, tag % 2 * first_rows) for tag in range(4)]),
        (2, early, 27 - early, pieces),
    ]
    total, _ = unpack(
        pos,
        total,
        [early_2a, early_2b, from_2, from_2x, from_2y, from_2top, from_2bottom],
        [],
        slabs,
        span,
        "unpack_3",
    )
    return (jnp.transpose(field, (3, 0, 1, 2)), jnp.transpose(total, (1, 0, 2)))


def body(inputs, weights, out_grad):
    chans, levels, height, width = inputs.shape
    shape = tuple(lax.axis_size(axis) for axis in AXES)
    fits = (
        shape == (2, 4, 4)
        and chans == out_grad.shape[0] == 256
        and weights.shape[2] == 512
        and levels % 2 == 0
        and height % 2 == 0
        and width % 16 == 0
    )
    return (blocked_body if fits else plain_body)(inputs, weights, out_grad)


def solution(mesh):
    in_specs = (P("ch", None, "lat", "lon"), P("ch", None, None), P("ch", None, "lat", "lon"))
    out_specs = (P("ch", None, "lat", "lon"), P("ch", None, None))
    return jax.shard_map(body, mesh=mesh, in_specs=in_specs, out_specs=out_specs, check_vma=False)
```

```python
import math

import jax
import jax.numpy as jnp
from jax import lax
from jax.experimental import pallas as pl
from jax.experimental.pallas import tpu as pltpu
from jax.sharding import PartitionSpec as P

VMEM = pltpu.VMEM
SMEM = pltpu.SMEM
AXES = ("ch", "lat", "lon")


def padded_2(cells, sides, width):
    for axis, dim in sides:
        count = lax.axis_size(axis)
        head = lax.slice_in_dim(cells, 0, width, axis=dim)
        tail = lax.slice_in_dim(cells, cells.shape[dim] - width, cells.shape[dim], axis=dim)
        cells = jnp.concatenate(
            [
                lax.ppermute(tail, axis, [(i, (i + 1) % count) for i in range(count)]),
                cells,
                lax.ppermute(head, axis, [((i + 1) % count, i) for i in range(count)]),
            ],
            axis=dim,
        )
    return cells


def mask_rims(padded):
    count = lax.axis_size("lat")
    where_lat = lax.axis_index("lat")
    lines = jnp.arange(padded.shape[2])
    drop = (lines == 0) & (where_lat == 0) | (lines == padded.shape[2] - 1) & (
        where_lat == count - 1
    )
    return jnp.where(drop[None, None, :, None], jnp.zeros((), padded.dtype), padded)


def pad_levels(field):
    return jnp.pad(field, ((0, 0), (1, 1), (0, 0), (0, 0)))


def plain_body(inputs, weights, out_grad):
    chans, levels, height, width = inputs.shape
    input_pad = pad_levels(mask_rims(padded_2(inputs, (("lat", 2), ("lon", 3)), 1)))
    grad_inner = lax.all_gather(out_grad, "ch", axis=0, tiled=True)
    grad_pad = pad_levels(mask_rims(padded_2(grad_inner, (("lat", 2), ("lon", 3)), 1)))
    filters = grad_pad.shape[0]
    products = jnp.dot(
        weights.reshape(chans * 27, filters),
        grad_pad.reshape(filters, -1),
        preferred_element_type=jnp.float32,
    )
    products = products.reshape((chans, 27) + tuple(grad_pad.shape[1:]))
    total = jnp.zeros((chans, levels, height, width), jnp.float32)
    pieces = []
    for tap in range(27):
        lev, lat, lon = tap // 9 - 1, tap // 3 % 3 - 1, tap % 3 - 1
        total = (
            total
            + products[
                :,
                tap,
                1 - lev : 1 - lev + levels,
                1 - lat : 1 - lat + height,
                1 - lon : 1 - lon + width,
            ]
        )
        pieces.append(
            input_pad[
                :,
                1 + lev : 1 + lev + levels,
                1 + lat : 1 + lat + height,
                1 + lon : 1 + lon + width,
            ]
        )
    columns = jnp.stack(pieces, axis=1).reshape(chans * 27, -1)
    partial_grad = lax.dot_general(
        columns,
        grad_inner.reshape(filters, -1),
        (((1,), (1,)), ((), ())),
        preferred_element_type=jnp.float32,
    )
    summed = lax.psum(partial_grad, ("lat", "lon"))
    cells = levels * height * width * lax.axis_size("lat") * lax.axis_size("lon")
    weight_grad = (summed * (1.0 / math.sqrt(cells))).reshape(chans, 27, filters)
    return (total.astype(jnp.bfloat16), weight_grad)


def move(x, target):
    pairs = []
    for i in range(32):
        to = target(i // 16, i // 4 % 4, i % 4)
        if to is not None:
            pairs.append((i, (to[0] * 4 + to[1]) * 4 + to[2]))
    return lax.ppermute(x, AXES, pairs)


def lon_by(step):
    return lambda c, a, o: (c, a, (o + step) % 4)


def lat_xor(mask):
    return lambda c, a, o: (c, a ^ mask, o)


def sibling(c, a, o):
    return (1 - c, a, o)


def call(kernel, outs, ins, scratch, flops, name, limit, held=0):
    read = len(ins) - 1 - held
    moved = sum(math.prod(x.shape) * x.dtype.itemsize for x in list(ins[1 : 1 + read]) + list(outs))
    return pl.pallas_call(
        kernel,
        out_shape=outs,
        in_specs=[pl.BlockSpec(memory_space=SMEM)]
        + [pl.BlockSpec(memory_space=VMEM)] * read
        + [pl.BlockSpec(memory_space=pl.ANY)] * held,
        out_specs=[pl.BlockSpec(memory_space=VMEM)] * len(outs),
        scratch_shapes=scratch,
        cost_estimate=pl.CostEstimate(flops=flops, bytes_accessed=moved, transcendentals=0),
        compiler_params=pltpu.CompilerParams(vmem_limit_bytes=limit * 1024 * 1024),
        name=name,
    )(*ins)


def pack_kernel(pos, x, g, g_same, g_other, x0, x1, x2, x3, rim_x, rim_d, held):
    levels, height, width, chans = x.shape
    half, wide = levels // 2, chans // 2
    right = lax.rem(pos[1], 2)
    for out, at in ((g_same, right), (g_other, 1 - right)):
        out[...] = g[:, :, :, pl.ds(pl.multiple_of(at * wide, wide), wide)].reshape(out.shape)
    many = x0.shape[0]
    for block in range(4):
        at = block * (chans // 4)
        lo = x[0:half, :, :, at : at + chans // 4]
        hi = x[half:levels, :, :, at : at + chans // 4]
        held[block] = jnp.concatenate([lo, hi], axis=-1).reshape(held.shape[1:])
    lon = pos[2]
    for step, out in enumerate((x0, x1, x2, x3)):
        out[0:many, :] = held[lax.rem(lon + step, 4)]
    for out, column in ((x1, width - 1), (x3, 0)):
        rim = g[:, :, column, :].reshape(levels * height, chans)
        out[many : many + levels * height, :] = rim[:, 0:wide]
        out[many + levels * height :, :] = rim[:, wide:]
    even = right == 0
    low, high = g[:, 0], g[:, height - 1]
    line = levels * width
    for out, upward in ((rim_x, even), (rim_d, jnp.logical_not(even))):
        facing = jnp.where(upward, high, low).reshape(line, chans)
        for at in range(2):
            out[at * line : (at + 1) * line, :] = facing[:, at * wide : (at + 1) * wide]


def spread_kernel(pos, x0, x1, x2, x3, after1, after2, own, own_y):
    del pos, after1, after2
    many = x0.shape[0]
    for at, piece in enumerate((x0, x1, x2, x3)):
        own[at * many : (at + 1) * many, :] = piece[0:many, :]
        own_y[at * many : (at + 1) * many, :] = piece[0:many, :]
    extra = x1.shape[0] - many
    own[4 * many : 4 * many + extra, :] = x1[many:, :]
    own[4 * many + extra :, :] = x3[many:, :]


def split_kernel(pos, west, east, first, second):
    del pos
    many = first.shape[0]
    first[...] = west[0:many, :]
    second[...] = east[many : 2 * many, :]


def mine_kernel(pos, g, own, x_x, x_d, by_x, by_d, after, mine):
    del after
    levels, height, width, chans = g.shape
    edge, line, wide = levels * height, levels * width, chans // 2
    inner = own.shape[0] - 4 * edge
    mine[:, 1 : height + 1, 0:width, :] = g[...]

    def columns(message, rows):
        for side in range(2):
            for half in range(2):
                start = inner + (2 * side + half) * edge
                rim = message[start : start + edge, :].reshape(levels, height, wide)
                at = width + 8 * side
                for row, to in rows:
                    mine[:, to, at : at + 8, half * wide : (half + 1) * wide] = jnp.broadcast_to(
                        rim[:, row : row + 1], (levels, 8, wide)
                    )

    columns(own, [(row, row + 1) for row in range(height)])

    def lines(strip, message, row, to):
        for half in range(2):
            part = strip[half * line : (half + 1) * line, :]
            mine[:, to, 0:width, half * wide : (half + 1) * wide] = part.reshape(levels, width, wide)
        columns(message, [(row, to)])

    lat = pos[1]
    odd = lax.rem(lat, 2)

    @pl.when(odd == 1)
    def _():
        lines(by_x, x_x, height - 1, 0)
        lines(by_d, x_d, 0, height + 1)

    @pl.when(odd == 0)
    def _():
        lines(by_d, x_d, height - 1, 0)
        lines(by_x, x_x, 0, height + 1)

    @pl.when(lat == 0)
    def _():
        mine[:, 0] = jnp.zeros_like(mine[:, 0])

    @pl.when(lat == 3)
    def _():
        mine[:, height + 1] = jnp.zeros_like(mine[:, height + 1])


def pair_kernel(pos, one, two, after, both):
    del pos, after
    both[0] = one[...]
    both[1] = two[...]


def first_pair_kernel(pos, one, two, after1, after2, after3, both):
    del pos, after1, after2, after3
    many = one.shape[0]
    both[0:many, :] = one[...]
    both[many : 2 * many, :] = two[...]
    both[2 * many :, :] = jnp.zeros((both.shape[0] - 2 * many, both.shape[1]), both.dtype)


def lines_kernel(pos, x_own, x_x, x_y, x_d, after, xs, blank):
    del after, blank
    lat = pos[1]
    levels, rows, circle, lanes = xs.shape
    rows, width, span, half = rows - 2, circle // 4, lanes // 4, levels // 2
    height = rows // 4
    many = half * height * width
    xs[:, 0] = jnp.zeros_like(xs[:, 0])
    xs[:, rows + 1] = jnp.zeros_like(xs[:, rows + 1])
    low = lax.broadcasted_iota(jnp.int32, (circle, 2 * span), 1) < span
    for tag, ref in enumerate((x_own, x_x, x_y, x_d)):
        start = (lat ^ tag) * height
        strips = [
            ref.at[pl.ds((4 - at) % 4 * many, many)].reshape(half, height, width, 2 * span) for at in range(4)
        ]

        @pl.loop(0, half * height)
        def _(step, strips=strips, start=start):
            lev, row = step // height, lax.rem(step, height)
            line = jnp.concatenate([s[lev, row] for s in strips], axis=0).astype(jnp.float32)
            turned = pltpu.roll(line, span, 1)
            for upper in range(2):
                same = jnp.where(low, turned, line) if upper else jnp.where(low, line, turned)
                before = pltpu.roll(same, 1, 0)
                after = pltpu.roll(same, circle - 1, 0)
                at = upper * half + lev
                xs[at, 1 + start + row, :, 0 : 2 * span] = jnp.where(low, before, same).astype(xs.dtype)
                xs[at, 1 + start + row, :, 2 * span : 4 * span] = after.astype(xs.dtype)


def turn(gt, slot, core, first, second, levels):
    many, filters = first.shape
    line = many // levels
    for lev in range(levels):
        block = jnp.concatenate([first[lev * line : (lev + 1) * line], second[lev * line : (lev + 1) * line]], axis=0)
        gt[
            lev * filters : (lev + 1) * filters,
            pl.ds(pl.multiple_of((2 * slot + core) * 2 * line, 2 * line), 2 * line),
        ] = block.T


def taps_kernel(pos, xs, g0, g1, g3, s0, s1, s3, g2, s2, out, gt, acc):
    levels, rows, circle, lanes = xs.shape
    rows, width, span = rows - 2, circle // 4, lanes // 4
    filters = gt.shape[0] // levels
    deep = rows * width
    right = lax.rem(pos[1], 2)
    many = g2.shape[1]
    for core, parts, last in ((pos[0], (g0, g3, g1), g2), (1 - pos[0], (s0, s3, s1), s2)):
        for slot, part in zip((0, 1, 3), parts):
            first = part[pl.ds(pl.multiple_of(right * many, many), many), :]
            second = part[pl.ds(pl.multiple_of((1 - right) * many, many), many), :]
            turn(gt, slot, core, first, second, levels)
        turn(gt, 2, core, last[right], last[1 - right], levels)
    acc[...] = jnp.zeros_like(acc)

    @pl.loop(0, 3)
    def _(lat_by):
        for lev in range(levels):
            first, last = max(lev - 1, 0), min(lev + 1, levels - 1)
            to = (first - lev + 1) * filters
            many = (last - first + 1) * filters
            total = acc[lat_by, to : to + many, :]
            for place in range(4):
                total += jnp.dot(
                    gt[first * filters : (last + 1) * filters, place * deep : (place + 1) * deep],
                    xs[lev, pl.ds(lat_by, rows), place * width : (place + 1) * width].reshape(deep, lanes),
                    preferred_element_type=jnp.float32,
                )
            acc[lat_by, to : to + many, :] = total

    scale = 1.0 / math.sqrt(levels * rows * circle)
    for lat_by in range(3):
        for lev_at in range(3):
            block = acc[lat_by, lev_at * filters : (lev_at + 1) * filters, :].T * scale
            for lon_at in range(3):
                out[(2 - lev_at) * 9 + lat_by * 3 + lon_at] = block[lon_at * span : (lon_at + 1) * span]


def code_kernel(pos, held, after, out, late):
    del pos, after
    taps, span, filters = held.shape
    most = jnp.abs(held[0])
    for tap in range(1, taps):
        most = jnp.maximum(most, jnp.abs(held[tap]))
    top = jnp.maximum(jnp.max(most, axis=(0, 1), keepdims=True), 1e-30)
    power = jnp.ceil(jnp.log(top) * (1.0 / math.log(2.0))) - 15.0
    unit = jnp.broadcast_to(jnp.exp2(power), (16, filters)).astype(out.dtype).astype(jnp.float32)
    shrink = 1.0 / unit[0:1]
    unit = unit.astype(out.dtype)
    skip = out.shape[0] - late.shape[0]
    for tap in range(taps):
        value = held[tap] * shrink
        square = value * value
        code = (square * value * jnp.abs(value)).astype(out.dtype)
        out[tap * span : (tap + 1) * span, :] = code
        if tap * span >= skip:
            late[tap * span - skip : (tap + 1) * span - skip, :] = code
    out[taps * span :, :] = unit
    late[taps * span - skip :, :] = unit


def both_kernel(pos, west, east, after1, after2, both, half_3, half_1):
    del pos, after1, after2
    size, half = west.shape[0], half_3.shape[0]
    both[0:size, :] = west[...]
    both[size:, :] = east[...]
    half_3[...] = west[0:half, :]
    half_1[...] = east[half:, :]


def cross_kernel(pos, by_x, by_y, after1, after2, after3, top, bottom):
    del pos, after1, after2, after3
    cut = top.shape[0]
    top[...] = by_y[0:cut, :]
    bottom[...] = by_x[cut:, :]


def across_kernel(pos, half_3, half_1, after, late):
    del pos, after
    half = half_3.shape[0]
    late[0:half, :] = half_3[...]
    late[half:, :] = half_1[...]


def block_kernel(pos, own, x, y, top, bottom, block):
    del pos
    rows = block.shape[0] // 4
    for at, (piece, end) in enumerate(((own, own), (x, x), (y, y), (top, bottom))):
        block[at * rows : (at + 1) * rows - 16, :] = piece[0 : rows - 16, :]
        block[(at + 1) * rows - 16 : (at + 1) * rows, :] = end[end.shape[0] - 16 :, :]


def hand_kernel(pos, block_3, block_1, first, second):
    del pos
    many = first.shape[0]
    first[...] = block_3[0:many, :]
    second[...] = block_1[many:, :]


def unpack_kernel(pos, *refs, slabs, count, span):
    sources = refs[:count]
    total, token, buffers, sems = refs[-4:]
    slots, group = buffers.shape[:2]
    wide = buffers.shape[-1] // 4
    token[...] = jnp.zeros_like(token)
    parts = []
    for step, first, taps, pieces in slabs:
        for at in range(0, taps, group):
            parts.append((step, first + at, min(group, taps - at), at, pieces))

    def copy(at):
        step, first, many, _, _ = parts[at]
        lon_at = pl.multiple_of(lax.rem(pos[2] + step, 4) * span, span)
        return pltpu.make_async_copy(
            buffers.at[at % slots, pl.ds(0, many)],
            total.at[pl.ds(first, many), pl.ds(lon_at, span)],
            sems.at[at % slots],
        )

    for at, (_, _, many, skip, pieces) in enumerate(parts):
        if at >= slots:
            copy(at - slots).wait()
        for tag, ((power_in, power_row), *segments) in enumerate(pieces):
            unit = sources[power_in][power_row : power_row + 16, :].astype(jnp.float32)[0:1]
            lanes = pl.ds(pl.multiple_of((pos[1] ^ tag) * wide, wide), wide)
            for tap in range(many):
                begin, which, row = [segment for segment in segments if segment[0] <= skip + tap][-1]
                start = row + (skip + tap - begin) * span
                code = sources[which][start : start + span, :].astype(jnp.float32)
                root = lax.rsqrt(lax.rsqrt(jnp.abs(code))) * unit
                buffers[at % slots, tap, :, lanes] = jnp.where(code < 0, -root, root)
        copy(at).start()
    for at in range(max(len(parts) - slots, 0), len(parts)):
        copy(at).wait()


def unpack(pos, total, sources, after, slabs, span, name):
    slots, group = 4, 3
    wide = total.shape[2]
    ins = (pos, *sources, *after, total)
    token = jax.ShapeDtypeStruct((8, 128), jnp.float32)
    return pl.pallas_call(
        lambda *refs: unpack_kernel(*refs, slabs=slabs, count=len(sources), span=span),
        out_shape=[jax.ShapeDtypeStruct(total.shape, total.dtype), token],
        in_specs=[pl.BlockSpec(memory_space=SMEM)]
        + [pl.BlockSpec(memory_space=VMEM)] * len(sources)
        + [pl.BlockSpec(memory_space=pl.ANY)] * (len(after) + 1),
        out_specs=[pl.BlockSpec(memory_space=pl.ANY), pl.BlockSpec(memory_space=VMEM)],
        scratch_shapes=[VMEM((slots, group, span, wide), jnp.float32), pltpu.SemaphoreType.DMA((slots,))],
        input_output_aliases={len(ins) - 1: 0},
        cost_estimate=pl.CostEstimate(flops=0, bytes_accessed=4 * 2**20, transcendentals=0),
        compiler_params=pltpu.CompilerParams(vmem_limit_bytes=51 * 1024 * 1024),
        name=name,
    )(*ins)


def field_kernel(pos, after, mine, theirs, w, out, copies, acc):
    del after
    step = pl.program_id(0)
    levels, height, width, chans = out.shape
    many = mine.shape[-1]

    @pl.when(step == 0)
    def _():
        copies[:, 0] = jnp.zeros_like(copies[:, 0])
        copies[:, levels + 1] = jnp.zeros_like(copies[:, levels + 1])
        line_at = lax.broadcasted_iota(jnp.int32, (width, many), 0)
        for which, field in ((pos[0], mine), (1 - pos[0], theirs)):
            lanes = pl.ds(pl.multiple_of(which * many, many), many)
            for lev in range(levels):
                for row in range(height + 2):
                    line = field[lev, row, 0:width].astype(jnp.float32)
                    west = field[lev, row, width : width + 1].astype(jnp.float32)
                    east = field[lev, row, width + 8 : width + 9].astype(jnp.float32)
                    before = jnp.where(line_at == 0, west, pltpu.roll(line, 1, 0))
                    later = jnp.where(line_at == width - 1, east, pltpu.roll(line, width - 1, 0))
                    copies[0, lev + 1, row, :, lanes] = later.astype(copies.dtype)
                    copies[1, lev + 1, row, :, lanes] = field[lev, row, 0:width]
                    copies[2, lev + 1, row, :, lanes] = before.astype(copies.dtype)
        acc[...] = jnp.zeros_like(acc)

    lev_by, lat_by = step // 3, lax.rem(step, 3)
    cells = [
        copies[at, pl.ds(2 - lev_by, levels), pl.ds(2 - lat_by, height)].reshape(
            levels * height * width, 2 * many
        )
        for at in range(3)
    ]
    acc[...] += lax.dot_general(
        jnp.concatenate(cells, axis=1),
        jnp.concatenate([w[at] for at in range(3)], axis=1),
        (((1,), (1,)), ((), ())),
        preferred_element_type=jnp.float32,
    )

    @pl.when(step == 8)
    def _():
        out[...] = acc[...].reshape(out.shape).astype(out.dtype)


def blocked_body(inputs, weights, out_grad):
    chans, levels, height, width = inputs.shape
    filters = weights.shape[2]
    bf16, f32 = jnp.bfloat16, jnp.float32
    lat, lon = lax.axis_index("lat"), lax.axis_index("lon")
    pos = jnp.stack([lax.axis_index("ch"), lat, lon]).astype(jnp.int32)
    x_cells = jnp.transpose(inputs, (1, 2, 3, 0))
    g_cells = jnp.transpose(out_grad, (1, 2, 3, 0))
    taps = jnp.transpose(weights, (1, 0, 2))
    cells = levels * height * width
    span, wide = chans // 4, filters // 4
    rows, circle = 4 * height, 4 * width
    edge = levels * height

    to_same = lambda c, a, o: (a // 2, 2 * c + a % 2, o)
    to_other = lambda c, a, o: (a // 2, 2 * c + 1 - a % 2, o)
    many = cells // 2
    block = jax.ShapeDtypeStruct((cells, wide), bf16)
    strip = jax.ShapeDtypeStruct((2 * levels * width, 2 * span), bf16)
    g_same, g_other, x0, x1, x2, x3, rim_x, rim_d = call(
        pack_kernel,
        [block, block]
        + [jax.ShapeDtypeStruct((many + extra, 2 * span), bf16) for extra in (0, 2 * edge, 0, 2 * edge)]
        + [strip, strip],
        (pos, x_cells, g_cells),
        [VMEM((4, many, 2 * span), bf16)],
        0,
        "pack",
        16,
    )
    g_s = move(g_same, to_same)
    g_o = move(g_other, to_other)
    x_r1 = move(x1, lon_by(1))
    x_r3 = move(x3, lon_by(-1))
    x_r2 = move(x2, lon_by(2))
    by_x = move(rim_x, lat_xor(1))
    by_d = move(rim_d, lat_xor(3))

    inner = 4 * many
    (g0,) = call(
        first_pair_kernel,
        [jax.ShapeDtypeStruct((2 * cells + 80, wide), bf16)],
        (pos, g_s, g_o, x_r1, x_r2, x_r3),
        [],
        0,
        "pair_0",
        16,
        held=3,
    )
    x_own, x_own_y = call(
        spread_kernel,
        [jax.ShapeDtypeStruct((count, 2 * span), bf16) for count in (inner + 4 * edge, inner)],
        (pos, x0, x_r1, x_r2, x_r3, by_x, by_d),
        [],
        0,
        "spread",
        16,
        held=2,
    )
    x_x = move(x_own, lat_xor(1))
    x_d = move(x_own, lat_xor(3))
    x_y = move(x_own_y, lat_xor(2))
    g1 = move(g0, lon_by(1))
    g3 = move(g0, lon_by(-1))
    far_a, far_b = call(split_kernel, [block, block], (pos, g1, g3), [], 0, "split", 16)
    g2a = move(far_a, lon_by(1))
    g2b = move(far_b, lon_by(-1))
    s0, s1, s3 = move(g0, sibling), move(g1, sibling), move(g3, sibling)
    xs, total = pl.pallas_call(
        lines_kernel,
        out_shape=[
            jax.ShapeDtypeStruct((levels, rows + 2, circle, 4 * span), bf16),
            jax.ShapeDtypeStruct((27, chans, filters), f32),
        ],
        in_specs=[pl.BlockSpec(memory_space=SMEM)]
        + [pl.BlockSpec(memory_space=VMEM)] * 4
        + [pl.BlockSpec(memory_space=pl.ANY)],
        out_specs=[pl.BlockSpec(memory_space=VMEM)] + [pl.BlockSpec(memory_space=pl.ANY)],
        cost_estimate=pl.CostEstimate(flops=0, bytes_accessed=2**20, transcendentals=0),
        compiler_params=pltpu.CompilerParams(vmem_limit_bytes=24 * 1024 * 1024),
        name="lines",
    )(pos, x_own, x_x, x_y, x_d, far_a)
    (mine,) = call(
        mine_kernel,
        [jax.ShapeDtypeStruct((levels, height + 2, width + 16, chans), bf16)],
        (pos, g_cells, x_own, x_x, x_d, by_x, by_d, xs),
        [],
        0,
        "mine",
        16,
        held=1,
    )
    theirs = move(mine, sibling)
    (g2,) = call(
        pair_kernel, [jax.ShapeDtypeStruct((2, cells, wide), bf16)], (pos, g2a, g2b, xs), [], 0, "pair", 16, held=1
    )
    s2 = move(g2, sibling)
    early = 3
    cut, end = early * span, 27 * span
    size = end + 16 - cut
    half = size // 32 * 16
    first_rows = cut + 16
    own_cut, late_cut = 14 * span, (27 - early) // 2 * span
    slab = lambda count: jax.ShapeDtypeStruct((count, wide), bf16)
    (grads,) = call(
        taps_kernel,
        [jax.ShapeDtypeStruct((27, span, wide), f32)],
        (pos, xs, g0, g1, g3, s0, s1, s3, g2, s2),
        [VMEM((levels * wide, rows * circle), bf16), VMEM((3, 3 * wide, 4 * span), f32)],
        2 * 27 * span * wide * rows * circle * levels,
        "taps",
        28,
    )
    own, late = call(code_kernel, [slab(end + 16), slab(size)], (pos, grads, theirs), [], 0, "code", 16, held=1)

    whole = lambda t: (0, 0, 0, 0)
    field = pl.pallas_call(
        field_kernel,
        out_shape=jax.ShapeDtypeStruct((levels, height, width, chans), bf16),
        grid=(9,),
        in_specs=[
            pl.BlockSpec(memory_space=SMEM),
            pl.BlockSpec(memory_space=pl.ANY),
            pl.BlockSpec(mine.shape, whole),
            pl.BlockSpec(mine.shape, whole),
            pl.BlockSpec((3, chans, filters), lambda t: (t, 0, 0)),
        ],
        out_specs=pl.BlockSpec((levels, height, width, chans), whole),
        scratch_shapes=[
            VMEM((3, levels + 2, height + 2, width, filters), bf16),
            VMEM((cells, chans), f32),
        ],
        cost_estimate=pl.CostEstimate(
            flops=4 * 27 * chans * filters * cells, bytes_accessed=27 * chans * filters * 2, transcendentals=0
        ),
        compiler_params=pltpu.CompilerParams(vmem_limit_bytes=20 * 1024 * 1024),
        name="field",
    )(pos, own, mine, theirs, taps)

    def to_plane(share):
        return move(share, lat_xor(1)), move(share, lat_xor(2))

    def to_diagonal(by_x, by_y, cut, after, name):
        top, bottom = call(
            cross_kernel, [slab(cut), slab(by_x.shape[0] - cut)], (pos, by_x, by_y, *after), [], 0, name, 16, held=3
        )
        return move(top, lat_xor(1)), move(bottom, lat_xor(2))

    from_3 = move(late, lon_by(1))
    from_1 = move(late, lon_by(-1))
    own_x, own_y = to_plane(own)
    own_top, own_bottom = to_diagonal(own_x, own_y, own_cut, (field, own, own), "cross_1")
    pair, half_3, half_1 = call(
        both_kernel,
        [slab(2 * size), slab(half), slab(size - half)],
        (pos, from_3, from_1, own_top, own_bottom),
        [],
        0,
        "both",
        16,
        held=2,
    )
    half_3 = move(half_3, lon_by(1))
    half_1 = move(half_1, lon_by(-1))
    pair_x, pair_y = to_plane(pair)
    (block,) = call(
        block_kernel, [slab(4 * first_rows)], (pos, own, own_x, own_y, own_top, own_bottom), [], 0, "block", 16
    )
    early_3 = move(block, lon_by(1))
    early_1 = move(block, lon_by(-1))
    (from_2,) = call(across_kernel, [slab(size)], (pos, half_3, half_1, pair), [], 0, "across", 16, held=1)
    pair_top, pair_bottom = to_diagonal(pair_x, pair_y, size, (early_1, early_3, pair), "cross_2")
    from_2x, from_2y = to_plane(from_2)
    hand_3, hand_1 = call(hand_kernel, [slab(2 * first_rows)] * 2, (pos, early_3, early_1), [], 0, "hand", 16)
    early_2a = move(hand_3, lon_by(1))
    early_2b = move(hand_1, lon_by(-1))

    def late_piece(which, row=0):
        return ((which, row + size - 16), (0, which, row))

    def early_piece(which, row):
        return ((which, row + cut), (0, which, row))

    pieces = [((which, end), (0, which, 0)) for which in range(3)]
    pieces.append(((4, end - own_cut), (0, 3, 0), (own_cut // span, 4, 0)))
    total, token = unpack(
        pos, total, [own, own_x, own_y, own_top, own_bottom], [block], [(0, 0, 27, pieces)], span, "unpack_1"
    )
    from_2top, from_2bottom = to_diagonal(from_2x, from_2y, late_cut, (token, early_2a, early_2b), "cross_3")
    slabs = [
        (3, early, 27 - early, [late_piece(0), late_piece(2), late_piece(3), late_piece(4)]),
        (1, early, 27 - early, [late_piece(1), late_piece(2, size), late_piece(3, size), late_piece(5)]),
        (3, 0, early, [early_piece(6, tag * first_rows) for tag in range(4)]),
        (1, 0, early, [early_piece(7, tag * first_rows) for tag in range(4)]),
    ]
    total, _ = unpack(
        pos,
        total,
        [from_3, from_1, pair_x, pair_y, pair_top, pair_bottom, early_3, early_1],
        [hand_3],
        slabs,
        span,
        "unpack_2",
    )
    pieces = [late_piece(2), late_piece(3), late_piece(4)]
    pieces.append(((6, size - 16 - late_cut), (0, 5, 0), (late_cut // span, 6, 0)))
    slabs = [
        (2, 0, early, [early_piece(tag // 2, tag % 2 * first_rows) for tag in range(4)]),
        (2, early, 27 - early, pieces),
    ]
    total, _ = unpack(
        pos,
        total,
        [early_2a, early_2b, from_2, from_2x, from_2y, from_2top, from_2bottom],
        [],
        slabs,
        span,
        "unpack_3",
    )
    return (jnp.transpose(field, (3, 0, 1, 2)), jnp.transpose(total, (1, 0, 2)))


def body(inputs, weights, out_grad):
    chans, levels, height, width = inputs.shape
    shape = tuple(lax.axis_size(axis) for axis in AXES)
    fits = (
        shape == (2, 4, 4)
        and chans == out_grad.shape[0] == 256
        and weights.shape[2] == 512
        and levels % 2 == 0
        and height % 2 == 0
        and width % 16 == 0
    )
    return (blocked_body if fits else plain_body)(inputs, weights, out_grad)


def solution(mesh):
    in_specs = (P("ch", None, "lat", "lon"), P("ch", None, None), P("ch", None, "lat", "lon"))
    out_specs = (P("ch", None, "lat", "lon"), P("ch", None, None))
    return jax.shard_map(body, mesh=mesh, in_specs=in_specs, out_specs=out_specs, check_vma=False)
```

```python
import math

import jax
import jax.numpy as jnp
from jax import lax
from jax.experimental import pallas as pl
from jax.experimental.pallas import tpu as pltpu
from jax.sharding import PartitionSpec as P

VMEM = pltpu.VMEM
SMEM = pltpu.SMEM
AXES = ("ch", "lat", "lon")


def padded_2(cells, sides, width):
    for axis, dim in sides:
        count = lax.axis_size(axis)
        head = lax.slice_in_dim(cells, 0, width, axis=dim)
        tail = lax.slice_in_dim(cells, cells.shape[dim] - width, cells.shape[dim], axis=dim)
        cells = jnp.concatenate(
            [
                lax.ppermute(tail, axis, [(i, (i + 1) % count) for i in range(count)]),
                cells,
                lax.ppermute(head, axis, [((i + 1) % count, i) for i in range(count)]),
            ],
            axis=dim,
        )
    return cells


def mask_rims(padded):
    count = lax.axis_size("lat")
    where_lat = lax.axis_index("lat")
    lines = jnp.arange(padded.shape[2])
    drop = (lines == 0) & (where_lat == 0) | (lines == padded.shape[2] - 1) & (
        where_lat == count - 1
    )
    return jnp.where(drop[None, None, :, None], jnp.zeros((), padded.dtype), padded)


def pad_levels(field):
    return jnp.pad(field, ((0, 0), (1, 1), (0, 0), (0, 0)))


def plain_body(inputs, weights, out_grad):
    chans, levels, height, width = inputs.shape
    input_pad = pad_levels(mask_rims(padded_2(inputs, (("lat", 2), ("lon", 3)), 1)))
    grad_inner = lax.all_gather(out_grad, "ch", axis=0, tiled=True)
    grad_pad = pad_levels(mask_rims(padded_2(grad_inner, (("lat", 2), ("lon", 3)), 1)))
    filters = grad_pad.shape[0]
    products = jnp.dot(
        weights.reshape(chans * 27, filters),
        grad_pad.reshape(filters, -1),
        preferred_element_type=jnp.float32,
    )
    products = products.reshape((chans, 27) + tuple(grad_pad.shape[1:]))
    total = jnp.zeros((chans, levels, height, width), jnp.float32)
    pieces = []
    for tap in range(27):
        lev, lat, lon = tap // 9 - 1, tap // 3 % 3 - 1, tap % 3 - 1
        total = (
            total
            + products[
                :,
                tap,
                1 - lev : 1 - lev + levels,
                1 - lat : 1 - lat + height,
                1 - lon : 1 - lon + width,
            ]
        )
        pieces.append(
            input_pad[
                :,
                1 + lev : 1 + lev + levels,
                1 + lat : 1 + lat + height,
                1 + lon : 1 + lon + width,
            ]
        )
    columns = jnp.stack(pieces, axis=1).reshape(chans * 27, -1)
    partial_grad = lax.dot_general(
        columns,
        grad_inner.reshape(filters, -1),
        (((1,), (1,)), ((), ())),
        preferred_element_type=jnp.float32,
    )
    summed = lax.psum(partial_grad, ("lat", "lon"))
    cells = levels * height * width * lax.axis_size("lat") * lax.axis_size("lon")
    weight_grad = (summed * (1.0 / math.sqrt(cells))).reshape(chans, 27, filters)
    return (total.astype(jnp.bfloat16), weight_grad)


def move(x, target):
    pairs = []
    for i in range(32):
        to = target(i // 16, i // 4 % 4, i % 4)
        if to is not None:
            pairs.append((i, (to[0] * 4 + to[1]) * 4 + to[2]))
    return lax.ppermute(x, AXES, pairs)


def lon_by(step):
    return lambda c, a, o: (c, a, (o + step) % 4)


def lat_xor(mask):
    return lambda c, a, o: (c, a ^ mask, o)


def sibling(c, a, o):
    return (1 - c, a, o)


def call(kernel, outs, ins, scratch, flops, name, limit, held=0):
    read = len(ins) - 1 - held
    moved = sum(math.prod(x.shape) * x.dtype.itemsize for x in list(ins[1 : 1 + read]) + list(outs))
    return pl.pallas_call(
        kernel,
        out_shape=outs,
        in_specs=[pl.BlockSpec(memory_space=SMEM)]
        + [pl.BlockSpec(memory_space=VMEM)] * read
        + [pl.BlockSpec(memory_space=pl.ANY)] * held,
        out_specs=[pl.BlockSpec(memory_space=VMEM)] * len(outs),
        scratch_shapes=scratch,
        cost_estimate=pl.CostEstimate(flops=flops, bytes_accessed=moved, transcendentals=0),
        compiler_params=pltpu.CompilerParams(vmem_limit_bytes=limit * 1024 * 1024),
        name=name,
    )(*ins)


def pack_kernel(pos, x, g, g_same, g_other, x0, x1, x2, x3, rim_x, rim_d, held):
    levels, height, width, chans = x.shape
    half, wide = levels // 2, chans // 2
    right = lax.rem(pos[1], 2)
    for out, at in ((g_same, right), (g_other, 1 - right)):
        out[...] = g[:, :, :, pl.ds(pl.multiple_of(at * wide, wide), wide)].reshape(out.shape)
    many = x0.shape[0]
    for block in range(4):
        at = block * (chans // 4)
        lo = x[0:half, :, :, at : at + chans // 4]
        hi = x[half:levels, :, :, at : at + chans // 4]
        held[block] = jnp.concatenate([lo, hi], axis=-1).reshape(held.shape[1:])
    lon = pos[2]
    for step, out in enumerate((x0, x1, x2, x3)):
        out[0:many, :] = held[lax.rem(lon + step, 4)]
    for out, column in ((x1, width - 1), (x3, 0)):
        rim = g[:, :, column, :].reshape(levels * height, chans)
        out[many : many + levels * height, :] = rim[:, 0:wide]
        out[many + levels * height :, :] = rim[:, wide:]
    even = right == 0
    low, high = g[:, 0], g[:, height - 1]
    line = levels * width
    for out, upward in ((rim_x, even), (rim_d, jnp.logical_not(even))):
        facing = jnp.where(upward, high, low).reshape(line, chans)
        for at in range(2):
            out[at * line : (at + 1) * line, :] = facing[:, at * wide : (at + 1) * wide]


def spread_kernel(pos, x0, x1, x2, x3, after1, after2, own, own_y):
    del pos, after1, after2
    many = x0.shape[0]
    for at, piece in enumerate((x0, x1, x2, x3)):
        own[at * many : (at + 1) * many, :] = piece[0:many, :]
        own_y[at * many : (at + 1) * many, :] = piece[0:many, :]
    extra = x1.shape[0] - many
    own[4 * many : 4 * many + extra, :] = x1[many:, :]
    own[4 * many + extra :, :] = x3[many:, :]


def split_kernel(pos, west, east, first, second):
    del pos
    many = first.shape[0]
    first[...] = west[0:many, :]
    second[...] = east[many : 2 * many, :]


def mine_kernel(pos, g, own, x_x, x_d, by_x, by_d, after, mine):
    del after
    levels, height, width, chans = g.shape
    edge, line, wide = levels * height, levels * width, chans // 2
    inner = own.shape[0] - 4 * edge
    mine[:, 1 : height + 1, 0:width, :] = g[...]

    def columns(message, rows):
        for side in range(2):
            for half in range(2):
                start = inner + (2 * side + half) * edge
                rim = message[start : start + edge, :].reshape(levels, height, wide)
                at = width + 8 * side
                for row, to in rows:
                    mine[:, to, at : at + 8, half * wide : (half + 1) * wide] = jnp.broadcast_to(
                        rim[:, row : row + 1], (levels, 8, wide)
                    )

    columns(own, [(row, row + 1) for row in range(height)])

    def lines(strip, message, row, to):
        for half in range(2):
            part = strip[half * line : (half + 1) * line, :]
            mine[:, to, 0:width, half * wide : (half + 1) * wide] = part.reshape(levels, width, wide)
        columns(message, [(row, to)])

    lat = pos[1]
    odd = lax.rem(lat, 2)

    @pl.when(odd == 1)
    def _():
        lines(by_x, x_x, height - 1, 0)
        lines(by_d, x_d, 0, height + 1)

    @pl.when(odd == 0)
    def _():
        lines(by_d, x_d, height - 1, 0)
        lines(by_x, x_x, 0, height + 1)

    @pl.when(lat == 0)
    def _():
        mine[:, 0] = jnp.zeros_like(mine[:, 0])

    @pl.when(lat == 3)
    def _():
        mine[:, height + 1] = jnp.zeros_like(mine[:, height + 1])


def pair_kernel(pos, one, two, after, both):
    del pos, after
    both[0] = one[...]
    both[1] = two[...]


def first_pair_kernel(pos, one, two, after1, after2, after3, both):
    del pos, after1, after2, after3
    many = one.shape[0]
    both[0:many, :] = one[...]
    both[many : 2 * many, :] = two[...]
    both[2 * many :, :] = jnp.zeros((both.shape[0] - 2 * many, both.shape[1]), both.dtype)


def lines_kernel(pos, x_own, x_x, x_y, x_d, after, xs, blank):
    del after, blank
    lat = pos[1]
    levels, rows, circle, lanes = xs.shape
    rows, width, span, half = rows - 2, circle // 4, lanes // 4, levels // 2
    height = rows // 4
    many = half * height * width
    xs[:, 0] = jnp.zeros_like(xs[:, 0])
    xs[:, rows + 1] = jnp.zeros_like(xs[:, rows + 1])
    low = lax.broadcasted_iota(jnp.int32, (circle, 2 * span), 1) < span
    for tag, ref in enumerate((x_own, x_x, x_y, x_d)):
        start = (lat ^ tag) * height
        strips = [
            ref.at[pl.ds((4 - at) % 4 * many, many)].reshape(half, height, width, 2 * span) for at in range(4)
        ]

        @pl.loop(0, half * height)
        def _(step, strips=strips, start=start):
            lev, row = step // height, lax.rem(step, height)
            line = jnp.concatenate([s[lev, row] for s in strips], axis=0).astype(jnp.float32)
            turned = pltpu.roll(line, span, 1)
            for upper in range(2):
                same = jnp.where(low, turned, line) if upper else jnp.where(low, line, turned)
                before = pltpu.roll(same, 1, 0)
                after = pltpu.roll(same, circle - 1, 0)
                at = upper * half + lev
                xs[at, 1 + start + row, :, 0 : 2 * span] = jnp.where(low, before, same).astype(xs.dtype)
                xs[at, 1 + start + row, :, 2 * span : 4 * span] = after.astype(xs.dtype)


def turn(gt, slot, core, first, second, levels):
    many, filters = first.shape
    line = many // levels
    for lev in range(levels):
        block = jnp.concatenate([first[lev * line : (lev + 1) * line], second[lev * line : (lev + 1) * line]], axis=0)
        gt[
            lev * filters : (lev + 1) * filters,
            pl.ds(pl.multiple_of((2 * slot + core) * 2 * line, 2 * line), 2 * line),
        ] = block.T


def taps_kernel(pos, xs, g0, g1, g3, s0, s1, s3, g2, s2, out, gt, acc):
    levels, rows, circle, lanes = xs.shape
    rows, width, span = rows - 2, circle // 4, lanes // 4
    filters = gt.shape[0] // levels
    deep = rows * width
    right = lax.rem(pos[1], 2)
    many = g2.shape[1]
    for core, parts, last in ((pos[0], (g0, g3, g1), g2), (1 - pos[0], (s0, s3, s1), s2)):
        for slot, part in zip((0, 1, 3), parts):
            first = part[pl.ds(pl.multiple_of(right * many, many), many), :]
            second = part[pl.ds(pl.multiple_of((1 - right) * many, many), many), :]
            turn(gt, slot, core, first, second, levels)
        turn(gt, 2, core, last[right], last[1 - right], levels)
    acc[...] = jnp.zeros_like(acc)

    @pl.loop(0, 3)
    def _(lat_by):
        for lev in range(levels):
            first, last = max(lev - 1, 0), min(lev + 1, levels - 1)
            to = (first - lev + 1) * filters
            many = (last - first + 1) * filters
            total = acc[lat_by, to : to + many, :]
            for place in range(4):
                total += jnp.dot(
                    gt[first * filters : (last + 1) * filters, place * deep : (place + 1) * deep],
                    xs[lev, pl.ds(lat_by, rows), place * width : (place + 1) * width].reshape(deep, lanes),
                    preferred_element_type=jnp.float32,
                )
            acc[lat_by, to : to + many, :] = total

    scale = 1.0 / math.sqrt(levels * rows * circle)
    for lat_by in range(3):
        for lev_at in range(3):
            block = acc[lat_by, lev_at * filters : (lev_at + 1) * filters, :].T * scale
            for lon_at in range(3):
                out[(2 - lev_at) * 9 + lat_by * 3 + lon_at] = block[lon_at * span : (lon_at + 1) * span]


def code_kernel(pos, held, after, out, late, rest):
    del pos, after
    taps, span, filters = held.shape
    most = jnp.abs(held[0])
    for tap in range(1, taps):
        most = jnp.maximum(most, jnp.abs(held[tap]))
    top = jnp.maximum(jnp.max(most, axis=(0, 1), keepdims=True), 1e-30)
    power = jnp.ceil(jnp.log(top) * (1.0 / math.log(2.0))) - 15.0
    unit = jnp.broadcast_to(jnp.exp2(power), (16, filters)).astype(out.dtype).astype(jnp.float32)
    shrink = 1.0 / unit[0:1]
    unit = unit.astype(out.dtype)
    for tap in range(taps):
        value = held[tap] * shrink
        square = value * value
        code = (square * value * jnp.abs(value)).astype(out.dtype)
        for ref, many in ((out, out.shape[0] - 16), (late, late.shape[0] - 16), (rest, rest.shape[0])):
            at = tap * span if ref is out else tap * span - (taps * span - many)
            if 0 <= at < many:
                ref[at : at + span, :] = code
    out[out.shape[0] - 16 :, :] = unit
    late[late.shape[0] - 16 :, :] = unit


def both_kernel(pos, west, east, rest, after, both, half_3, half_1):
    del pos, after
    size, half = west.shape[0], half_3.shape[0]
    both[0:size, :] = west[...]
    both[size : 2 * size, :] = east[...]
    both[2 * size :, :] = rest[...]
    half_3[...] = west[0:half, :]
    half_1[...] = east[half:, :]


def across_kernel(pos, half_3, half_1, own, x, y, d, late, block):
    del pos
    half = half_3.shape[0]
    late[0:half, :] = half_3[...]
    late[half:, :] = half_1[...]
    end = own.shape[0] - 16
    rows = block.shape[0] // 4
    for at, piece in enumerate((own, x, y, d)):
        block[at * rows : (at + 1) * rows - 16, :] = piece[0 : rows - 16, :]
        block[(at + 1) * rows - 16 : (at + 1) * rows, :] = piece[end:, :]


def hand_kernel(pos, block_3, block_1, after, first, second):
    del pos, after
    many = first.shape[0]
    first[...] = block_3[0:many, :]
    second[...] = block_1[many:, :]


def unpack_kernel(pos, *refs, slabs, count, span):
    sources = refs[:count]
    total, token, buffers, sems = refs[-4:]
    slots, group = buffers.shape[:2]
    wide = buffers.shape[-1] // 4
    token[...] = jnp.zeros_like(token)
    parts = []
    for step, first, taps, pieces in slabs:
        for at in range(0, taps, group):
            parts.append((step, first + at, min(group, taps - at), at, pieces))

    def copy(at):
        step, first, many, _, _ = parts[at]
        lon_at = pl.multiple_of(lax.rem(pos[2] + step, 4) * span, span)
        return pltpu.make_async_copy(
            buffers.at[at % slots, pl.ds(0, many)],
            total.at[pl.ds(first, many), pl.ds(lon_at, span)],
            sems.at[at % slots],
        )

    for at, (_, _, many, skip, pieces) in enumerate(parts):
        if at >= slots:
            copy(at - slots).wait()
        for tag, (which, row, (power_in, power_row)) in enumerate(pieces):
            unit = sources[power_in][power_row : power_row + 16, :].astype(jnp.float32)[0:1]
            lanes = pl.ds(pl.multiple_of((pos[1] ^ tag) * wide, wide), wide)
            for tap in range(many):
                start = row + (skip + tap) * span
                code = sources[which][start : start + span, :].astype(jnp.float32)
                root = lax.rsqrt(lax.rsqrt(jnp.abs(code))) * unit
                buffers[at % slots, tap, :, lanes] = jnp.where(code < 0, -root, root)
        copy(at).start()
    for at in range(max(len(parts) - slots, 0), len(parts)):
        copy(at).wait()


def unpack(pos, total, sources, after, slabs, span, name):
    slots, group = 4, 3
    wide = total.shape[2]
    ins = (pos, *sources, *after, total)
    token = jax.ShapeDtypeStruct((8, 128), jnp.float32)
    return pl.pallas_call(
        lambda *refs: unpack_kernel(*refs, slabs=slabs, count=len(sources), span=span),
        out_shape=[jax.ShapeDtypeStruct(total.shape, total.dtype), token],
        in_specs=[pl.BlockSpec(memory_space=SMEM)]
        + [pl.BlockSpec(memory_space=VMEM)] * len(sources)
        + [pl.BlockSpec(memory_space=pl.ANY)] * (len(after) + 1),
        out_specs=[pl.BlockSpec(memory_space=pl.ANY), pl.BlockSpec(memory_space=VMEM)],
        scratch_shapes=[VMEM((slots, group, span, wide), jnp.float32), pltpu.SemaphoreType.DMA((slots,))],
        input_output_aliases={len(ins) - 1: 0},
        cost_estimate=pl.CostEstimate(flops=0, bytes_accessed=4 * 2**20, transcendentals=0),
        compiler_params=pltpu.CompilerParams(vmem_limit_bytes=51 * 1024 * 1024),
        name=name,
    )(*ins)


def field_kernel(pos, after, mine, theirs, w, out, copies, acc):
    del after
    step = pl.program_id(0)
    levels, height, width, chans = out.shape
    many = mine.shape[-1]

    @pl.when(step == 0)
    def _():
        copies[:, 0] = jnp.zeros_like(copies[:, 0])
        copies[:, levels + 1] = jnp.zeros_like(copies[:, levels + 1])
        line_at = lax.broadcasted_iota(jnp.int32, (width, many), 0)
        for which, field in ((pos[0], mine), (1 - pos[0], theirs)):
            lanes = pl.ds(pl.multiple_of(which * many, many), many)
            for lev in range(levels):
                for row in range(height + 2):
                    line = field[lev, row, 0:width].astype(jnp.float32)
                    west = field[lev, row, width : width + 1].astype(jnp.float32)
                    east = field[lev, row, width + 8 : width + 9].astype(jnp.float32)
                    before = jnp.where(line_at == 0, west, pltpu.roll(line, 1, 0))
                    later = jnp.where(line_at == width - 1, east, pltpu.roll(line, width - 1, 0))
                    copies[0, lev + 1, row, :, lanes] = later.astype(copies.dtype)
                    copies[1, lev + 1, row, :, lanes] = field[lev, row, 0:width]
                    copies[2, lev + 1, row, :, lanes] = before.astype(copies.dtype)
        acc[...] = jnp.zeros_like(acc)

    lev_by, lat_by = step // 3, lax.rem(step, 3)
    cells = [
        copies[at, pl.ds(2 - lev_by, levels), pl.ds(2 - lat_by, height)].reshape(
            levels * height * width, 2 * many
        )
        for at in range(3)
    ]
    acc[...] += lax.dot_general(
        jnp.concatenate(cells, axis=1),
        jnp.concatenate([w[at] for at in range(3)], axis=1),
        (((1,), (1,)), ((), ())),
        preferred_element_type=jnp.float32,
    )

    @pl.when(step == 8)
    def _():
        out[...] = acc[...].reshape(out.shape).astype(out.dtype)


def blocked_body(inputs, weights, out_grad):
    chans, levels, height, width = inputs.shape
    filters = weights.shape[2]
    bf16, f32 = jnp.bfloat16, jnp.float32
    lat, lon = lax.axis_index("lat"), lax.axis_index("lon")
    pos = jnp.stack([lax.axis_index("ch"), lat, lon]).astype(jnp.int32)
    x_cells = jnp.transpose(inputs, (1, 2, 3, 0))
    g_cells = jnp.transpose(out_grad, (1, 2, 3, 0))
    taps = jnp.transpose(weights, (1, 0, 2))
    cells = levels * height * width
    span, wide = chans // 4, filters // 4
    rows, circle = 4 * height, 4 * width
    edge = levels * height

    to_same = lambda c, a, o: (a // 2, 2 * c + a % 2, o)
    to_other = lambda c, a, o: (a // 2, 2 * c + 1 - a % 2, o)
    many = cells // 2
    block = jax.ShapeDtypeStruct((cells, wide), bf16)
    strip = jax.ShapeDtypeStruct((2 * levels * width, 2 * span), bf16)
    g_same, g_other, x0, x1, x2, x3, rim_x, rim_d = call(
        pack_kernel,
        [block, block]
        + [jax.ShapeDtypeStruct((many + extra, 2 * span), bf16) for extra in (0, 2 * edge, 0, 2 * edge)]
        + [strip, strip],
        (pos, x_cells, g_cells),
        [VMEM((4, many, 2 * span), bf16)],
        0,
        "pack",
        16,
    )
    g_s = move(g_same, to_same)
    g_o = move(g_other, to_other)
    x_r1 = move(x1, lon_by(1))
    x_r3 = move(x3, lon_by(-1))
    x_r2 = move(x2, lon_by(2))
    by_x = move(rim_x, lat_xor(1))
    by_d = move(rim_d, lat_xor(3))

    inner = 4 * many
    (g0,) = call(
        first_pair_kernel,
        [jax.ShapeDtypeStruct((2 * cells + 80, wide), bf16)],
        (pos, g_s, g_o, x_r1, x_r2, x_r3),
        [],
        0,
        "pair_0",
        16,
        held=3,
    )
    x_own, x_own_y = call(
        spread_kernel,
        [jax.ShapeDtypeStruct((count, 2 * span), bf16) for count in (inner + 4 * edge, inner)],
        (pos, x0, x_r1, x_r2, x_r3, by_x, by_d),
        [],
        0,
        "spread",
        16,
        held=2,
    )
    x_x = move(x_own, lat_xor(1))
    x_d = move(x_own, lat_xor(3))
    x_y = move(x_own_y, lat_xor(2))
    g1 = move(g0, lon_by(1))
    g3 = move(g0, lon_by(-1))
    far_a, far_b = call(split_kernel, [block, block], (pos, g1, g3), [], 0, "split", 16)
    g2a = move(far_a, lon_by(1))
    g2b = move(far_b, lon_by(-1))
    s0, s1, s3 = move(g0, sibling), move(g1, sibling), move(g3, sibling)
    xs, total = pl.pallas_call(
        lines_kernel,
        out_shape=[
            jax.ShapeDtypeStruct((levels, rows + 2, circle, 4 * span), bf16),
            jax.ShapeDtypeStruct((27, chans, filters), f32),
        ],
        in_specs=[pl.BlockSpec(memory_space=SMEM)]
        + [pl.BlockSpec(memory_space=VMEM)] * 4
        + [pl.BlockSpec(memory_space=pl.ANY)],
        out_specs=[pl.BlockSpec(memory_space=VMEM)] + [pl.BlockSpec(memory_space=pl.ANY)],
        cost_estimate=pl.CostEstimate(flops=0, bytes_accessed=2**20, transcendentals=0),
        compiler_params=pltpu.CompilerParams(vmem_limit_bytes=24 * 1024 * 1024),
        name="lines",
    )(pos, x_own, x_x, x_y, x_d, far_a)
    (mine,) = call(
        mine_kernel,
        [jax.ShapeDtypeStruct((levels, height + 2, width + 16, chans), bf16)],
        (pos, g_cells, x_own, x_x, x_d, by_x, by_d, xs),
        [],
        0,
        "mine",
        16,
        held=1,
    )
    theirs = move(mine, sibling)
    (g2,) = call(
        pair_kernel, [jax.ShapeDtypeStruct((2, cells, wide), bf16)], (pos, g2a, g2b, xs), [], 0, "pair", 16, held=1
    )
    s2 = move(g2, sibling)
    early, middle = 7, 19
    cut, end = early * span, 27 * span
    size = end + 16 - cut
    half = size // 32 * 16
    first_rows = cut + 16
    own_rows = middle * span + 16
    slab = lambda count: jax.ShapeDtypeStruct((count, wide), bf16)
    (grads,) = call(
        taps_kernel,
        [jax.ShapeDtypeStruct((27, span, wide), f32)],
        (pos, xs, g0, g1, g3, s0, s1, s3, g2, s2),
        [VMEM((levels * wide, rows * circle), bf16), VMEM((3, 3 * wide, 4 * span), f32)],
        2 * 27 * span * wide * rows * circle * levels,
        "taps",
        28,
    )
    own, late, rest = call(
        code_kernel,
        [slab(own_rows), slab(size), slab(end - middle * span)],
        (pos, grads, theirs),
        [],
        0,
        "code",
        16,
        held=1,
    )

    whole = lambda t: (0, 0, 0, 0)
    field = pl.pallas_call(
        field_kernel,
        out_shape=jax.ShapeDtypeStruct((levels, height, width, chans), bf16),
        grid=(9,),
        in_specs=[
            pl.BlockSpec(memory_space=SMEM),
            pl.BlockSpec(memory_space=pl.ANY),
            pl.BlockSpec(mine.shape, whole),
            pl.BlockSpec(mine.shape, whole),
            pl.BlockSpec((3, chans, filters), lambda t: (t, 0, 0)),
        ],
        out_specs=pl.BlockSpec((levels, height, width, chans), whole),
        scratch_shapes=[
            VMEM((3, levels + 2, height + 2, width, filters), bf16),
            VMEM((cells, chans), f32),
        ],
        cost_estimate=pl.CostEstimate(
            flops=4 * 27 * chans * filters * cells, bytes_accessed=27 * chans * filters * 2, transcendentals=0
        ),
        compiler_params=pltpu.CompilerParams(vmem_limit_bytes=20 * 1024 * 1024),
        name="field",
    )(pos, own, mine, theirs, taps)

    def to_plane(share):
        return [move(share, lat_xor(tag)) for tag in (1, 2, 3)]

    from_3 = move(late, lon_by(1))
    from_1 = move(late, lon_by(-1))
    plane = [own] + to_plane(own)
    pair, half_3, half_1 = call(
        both_kernel,
        [slab(2 * size + end - middle * span), slab(half), slab(size - half)],
        (pos, from_3, from_1, rest, field),
        [],
        0,
        "both",
        16,
        held=1,
    )
    half_3 = move(half_3, lon_by(1))
    half_1 = move(half_1, lon_by(-1))
    both = to_plane(pair)
    from_2, block = call(
        across_kernel, [slab(size), slab(4 * first_rows)], (pos, half_3, half_1, *plane), [], 0, "across", 16
    )
    early_3 = move(block, lon_by(1))
    early_1 = move(block, lon_by(-1))
    across = to_plane(from_2)

    def late_piece(which, row=0):
        return (which, row, (which, row + size - 16))

    def early_piece(which, row):
        return (which, row, (which, row + cut))

    slabs = [(0, 0, middle, [(tag, 0, (tag, own_rows - 16)) for tag in range(4)])]
    total, token = unpack(pos, total, plane, [block], slabs, span, "unpack_1")
    hand_3, hand_1 = call(
        hand_kernel, [slab(2 * first_rows)] * 2, (pos, early_3, early_1, token), [], 0, "hand", 16, held=1
    )
    early_2a = move(hand_3, lon_by(1))
    early_2b = move(hand_1, lon_by(-1))
    unit = own_rows - 16
    slabs = [
        (3, early, 27 - early, [late_piece(5)] + [late_piece(at) for at in range(3)]),
        (1, early, 27 - early, [late_piece(6)] + [late_piece(at, size) for at in range(3)]),
        (0, middle, 27 - middle, [(7, 0, (8, unit))] + [(at, 2 * size, (9 + at, unit)) for at in range(3)]),
        (3, 0, early, [early_piece(3, tag * first_rows) for tag in range(4)]),
        (1, 0, early, [early_piece(4, tag * first_rows) for tag in range(4)]),
    ]
    total, _ = unpack(
        pos, total, both + [early_3, early_1, from_3, from_1, rest] + plane, [hand_3], slabs, span, "unpack_2"
    )
    slabs = [
        (2, 0, early, [early_piece(tag // 2, tag % 2 * first_rows) for tag in range(4)]),
        (2, early, 27 - early, [late_piece(2 + tag) for tag in range(4)]),
    ]
    total, _ = unpack(pos, total, [early_2a, early_2b, from_2] + across, [], slabs, span, "unpack_3")
    return (jnp.transpose(field, (3, 0, 1, 2)), jnp.transpose(total, (1, 0, 2)))


def body(inputs, weights, out_grad):
    chans, levels, height, width = inputs.shape
    shape = tuple(lax.axis_size(axis) for axis in AXES)
    fits = (
        shape == (2, 4, 4)
        and chans == out_grad.shape[0] == 256
        and weights.shape[2] == 512
        and levels % 2 == 0
        and height % 2 == 0
        and width % 16 == 0
    )
    return (blocked_body if fits else plain_body)(inputs, weights, out_grad)


def solution(mesh):
    in_specs = (P("ch", None, "lat", "lon"), P("ch", None, None), P("ch", None, "lat", "lon"))
    out_specs = (P("ch", None, "lat", "lon"), P("ch", None, None))
    return jax.shard_map(body, mesh=mesh, in_specs=in_specs, out_specs=out_specs, check_vma=False)
```

```python
import math

import jax
import jax.numpy as jnp
from jax import lax
from jax.experimental import pallas as pl
from jax.experimental.pallas import tpu as pltpu
from jax.sharding import PartitionSpec as P

VMEM = pltpu.VMEM
SMEM = pltpu.SMEM
AXES = ("ch", "lat", "lon")


def padded_2(cells, sides, width):
    for axis, dim in sides:
        count = lax.axis_size(axis)
        head = lax.slice_in_dim(cells, 0, width, axis=dim)
        tail = lax.slice_in_dim(cells, cells.shape[dim] - width, cells.shape[dim], axis=dim)
        cells = jnp.concatenate(
            [
                lax.ppermute(tail, axis, [(i, (i + 1) % count) for i in range(count)]),
                cells,
                lax.ppermute(head, axis, [((i + 1) % count, i) for i in range(count)]),
            ],
            axis=dim,
        )
    return cells


def mask_rims(padded):
    count = lax.axis_size("lat")
    where_lat = lax.axis_index("lat")
    lines = jnp.arange(padded.shape[2])
    drop = (lines == 0) & (where_lat == 0) | (lines == padded.shape[2] - 1) & (
        where_lat == count - 1
    )
    return jnp.where(drop[None, None, :, None], jnp.zeros((), padded.dtype), padded)


def pad_levels(field):
    return jnp.pad(field, ((0, 0), (1, 1), (0, 0), (0, 0)))


def plain_body(inputs, weights, out_grad):
    chans, levels, height, width = inputs.shape
    input_pad = pad_levels(mask_rims(padded_2(inputs, (("lat", 2), ("lon", 3)), 1)))
    grad_inner = lax.all_gather(out_grad, "ch", axis=0, tiled=True)
    grad_pad = pad_levels(mask_rims(padded_2(grad_inner, (("lat", 2), ("lon", 3)), 1)))
    filters = grad_pad.shape[0]
    products = jnp.dot(
        weights.reshape(chans * 27, filters),
        grad_pad.reshape(filters, -1),
        preferred_element_type=jnp.float32,
    )
    products = products.reshape((chans, 27) + tuple(grad_pad.shape[1:]))
    total = jnp.zeros((chans, levels, height, width), jnp.float32)
    pieces = []
    for tap in range(27):
        lev, lat, lon = tap // 9 - 1, tap // 3 % 3 - 1, tap % 3 - 1
        total = (
            total
            + products[
                :,
                tap,
                1 - lev : 1 - lev + levels,
                1 - lat : 1 - lat + height,
                1 - lon : 1 - lon + width,
            ]
        )
        pieces.append(
            input_pad[
                :,
                1 + lev : 1 + lev + levels,
                1 + lat : 1 + lat + height,
                1 + lon : 1 + lon + width,
            ]
        )
    columns = jnp.stack(pieces, axis=1).reshape(chans * 27, -1)
    partial_grad = lax.dot_general(
        columns,
        grad_inner.reshape(filters, -1),
        (((1,), (1,)), ((), ())),
        preferred_element_type=jnp.float32,
    )
    summed = lax.psum(partial_grad, ("lat", "lon"))
    cells = levels * height * width * lax.axis_size("lat") * lax.axis_size("lon")
    weight_grad = (summed * (1.0 / math.sqrt(cells))).reshape(chans, 27, filters)
    return (total.astype(jnp.bfloat16), weight_grad)


def move(x, target):
    pairs = []
    for i in range(32):
        to = target(i // 16, i // 4 % 4, i % 4)
        if to is not None:
            pairs.append((i, (to[0] * 4 + to[1]) * 4 + to[2]))
    return lax.ppermute(x, AXES, pairs)


def lon_by(step):
    return lambda c, a, o: (c, a, (o + step) % 4)


def lat_xor(mask):
    return lambda c, a, o: (c, a ^ mask, o)


def sibling(c, a, o):
    return (1 - c, a, o)


def call(kernel, outs, ins, scratch, flops, name, limit, held=0):
    read = len(ins) - 1 - held
    moved = sum(math.prod(x.shape) * x.dtype.itemsize for x in list(ins[1 : 1 + read]) + list(outs))
    return pl.pallas_call(
        kernel,
        out_shape=outs,
        in_specs=[pl.BlockSpec(memory_space=SMEM)]
        + [pl.BlockSpec(memory_space=VMEM)] * read
        + [pl.BlockSpec(memory_space=pl.ANY)] * held,
        out_specs=[pl.BlockSpec(memory_space=VMEM)] * len(outs),
        scratch_shapes=scratch,
        cost_estimate=pl.CostEstimate(flops=flops, bytes_accessed=moved, transcendentals=0),
        compiler_params=pltpu.CompilerParams(vmem_limit_bytes=limit * 1024 * 1024),
        name=name,
    )(*ins)


def pack_kernel(pos, x, g, g_same, g_other, x0, x1, x2, x3, rim_x, rim_d, held):
    levels, height, width, chans = x.shape
    half, wide = levels // 2, chans // 2
    right = lax.rem(pos[1], 2)
    for out, at in ((g_same, right), (g_other, 1 - right)):
        out[...] = g[:, :, :, pl.ds(pl.multiple_of(at * wide, wide), wide)].reshape(out.shape)
    many = x0.shape[0]
    for block in range(4):
        at = block * (chans // 4)
        lo = x[0:half, :, :, at : at + chans // 4]
        hi = x[half:levels, :, :, at : at + chans // 4]
        held[block] = jnp.concatenate([lo, hi], axis=-1).reshape(held.shape[1:])
    lon = pos[2]
    for step, out in enumerate((x0, x1, x2, x3)):
        out[0:many, :] = held[lax.rem(lon + step, 4)]
    for out, column in ((x1, width - 1), (x3, 0)):
        rim = g[:, :, column, :].reshape(levels * height, chans)
        out[many : many + levels * height, :] = rim[:, 0:wide]
        out[many + levels * height :, :] = rim[:, wide:]
    even = right == 0
    low, high = g[:, 0], g[:, height - 1]
    line = levels * width
    for out, upward in ((rim_x, even), (rim_d, jnp.logical_not(even))):
        facing = jnp.where(upward, high, low).reshape(line, chans)
        for at in range(2):
            out[at * line : (at + 1) * line, :] = facing[:, at * wide : (at + 1) * wide]


def spread_kernel(pos, x0, x1, x2, x3, after1, after2, own, own_y):
    del pos, after1, after2
    many = x0.shape[0]
    for at, piece in enumerate((x0, x1, x2, x3)):
        own[at * many : (at + 1) * many, :] = piece[0:many, :]
        own_y[at * many : (at + 1) * many, :] = piece[0:many, :]
    extra = x1.shape[0] - many
    own[4 * many : 4 * many + extra, :] = x1[many:, :]
    own[4 * many + extra :, :] = x3[many:, :]


def split_kernel(pos, west, east, first, second):
    del pos
    many = first.shape[0]
    first[...] = west[0:many, :]
    second[...] = east[many : 2 * many, :]


def mine_kernel(pos, g, own, x_x, x_d, by_x, by_d, after, mine):
    del after
    levels, height, width, chans = g.shape
    edge, line, wide = levels * height, levels * width, chans // 2
    inner = own.shape[0] - 4 * edge
    mine[:, 1 : height + 1, 0:width, :] = g[...]

    def columns(message, rows):
        for side in range(2):
            for half in range(2):
                start = inner + (2 * side + half) * edge
                rim = message[start : start + edge, :].reshape(levels, height, wide)
                at = width + 8 * side
                for row, to in rows:
                    mine[:, to, at : at + 8, half * wide : (half + 1) * wide] = jnp.broadcast_to(
                        rim[:, row : row + 1], (levels, 8, wide)
                    )

    columns(own, [(row, row + 1) for row in range(height)])

    def lines(strip, message, row, to):
        for half in range(2):
            part = strip[half * line : (half + 1) * line, :]
            mine[:, to, 0:width, half * wide : (half + 1) * wide] = part.reshape(levels, width, wide)
        columns(message, [(row, to)])

    lat = pos[1]
    odd = lax.rem(lat, 2)

    @pl.when(odd == 1)
    def _():
        lines(by_x, x_x, height - 1, 0)
        lines(by_d, x_d, 0, height + 1)

    @pl.when(odd == 0)
    def _():
        lines(by_d, x_d, height - 1, 0)
        lines(by_x, x_x, 0, height + 1)

    @pl.when(lat == 0)
    def _():
        mine[:, 0] = jnp.zeros_like(mine[:, 0])

    @pl.when(lat == 3)
    def _():
        mine[:, height + 1] = jnp.zeros_like(mine[:, height + 1])


def pair_kernel(pos, one, two, after, both):
    del pos, after
    both[0] = one[...]
    both[1] = two[...]


def first_pair_kernel(pos, one, two, after1, after2, after3, both):
    del pos, after1, after2, after3
    many = one.shape[0]
    both[0:many, :] = one[...]
    both[many : 2 * many, :] = two[...]
    both[2 * many :, :] = jnp.zeros((both.shape[0] - 2 * many, both.shape[1]), both.dtype)


def lines_kernel(pos, x_own, x_x, x_y, x_d, after, xs, blank):
    del after, blank
    lat = pos[1]
    levels, rows, circle, lanes = xs.shape
    rows, width, span, half = rows - 2, circle // 4, lanes // 4, levels // 2
    height = rows // 4
    many = half * height * width
    xs[:, 0] = jnp.zeros_like(xs[:, 0])
    xs[:, rows + 1] = jnp.zeros_like(xs[:, rows + 1])
    low = lax.broadcasted_iota(jnp.int32, (circle, 2 * span), 1) < span
    for tag, ref in enumerate((x_own, x_x, x_y, x_d)):
        start = (lat ^ tag) * height
        strips = [
            ref.at[pl.ds((4 - at) % 4 * many, many)].reshape(half, height, width, 2 * span) for at in range(4)
        ]

        @pl.loop(0, half * height)
        def _(step, strips=strips, start=start):
            lev, row = step // height, lax.rem(step, height)
            line = jnp.concatenate([s[lev, row] for s in strips], axis=0).astype(jnp.float32)
            turned = pltpu.roll(line, span, 1)
            for upper in range(2):
                same = jnp.where(low, turned, line) if upper else jnp.where(low, line, turned)
                before = pltpu.roll(same, 1, 0)
                after = pltpu.roll(same, circle - 1, 0)
                at = upper * half + lev
                xs[at, 1 + start + row, :, 0 : 2 * span] = jnp.where(low, before, same).astype(xs.dtype)
                xs[at, 1 + start + row, :, 2 * span : 4 * span] = after.astype(xs.dtype)


def turn(gt, slot, core, first, second, levels):
    many, filters = first.shape
    line = many // levels
    for lev in range(levels):
        block = jnp.concatenate([first[lev * line : (lev + 1) * line], second[lev * line : (lev + 1) * line]], axis=0)
        gt[
            lev * filters : (lev + 1) * filters,
            pl.ds(pl.multiple_of((2 * slot + core) * 2 * line, 2 * line), 2 * line),
        ] = block.T


def taps_kernel(pos, xs, g0, g1, g3, s0, s1, s3, g2, s2, out, gt, acc):
    levels, rows, circle, lanes = xs.shape
    rows, width, span = rows - 2, circle // 4, lanes // 4
    filters = gt.shape[0] // levels
    deep = rows * width
    right = lax.rem(pos[1], 2)
    many = g2.shape[1]
    for core, parts, last in ((pos[0], (g0, g3, g1), g2), (1 - pos[0], (s0, s3, s1), s2)):
        for slot, part in zip((0, 1, 3), parts):
            first = part[pl.ds(pl.multiple_of(right * many, many), many), :]
            second = part[pl.ds(pl.multiple_of((1 - right) * many, many), many), :]
            turn(gt, slot, core, first, second, levels)
        turn(gt, 2, core, last[right], last[1 - right], levels)
    acc[...] = jnp.zeros_like(acc)

    @pl.loop(0, 3)
    def _(lat_by):
        for lev in range(levels):
            first, last = max(lev - 1, 0), min(lev + 1, levels - 1)
            to = (first - lev + 1) * filters
            many = (last - first + 1) * filters
            total = acc[lat_by, to : to + many, :]
            for place in range(4):
                total += jnp.dot(
                    gt[first * filters : (last + 1) * filters, place * deep : (place + 1) * deep],
                    xs[lev, pl.ds(lat_by, rows), place * width : (place + 1) * width].reshape(deep, lanes),
                    preferred_element_type=jnp.float32,
                )
            acc[lat_by, to : to + many, :] = total

    scale = 1.0 / math.sqrt(levels * rows * circle)
    for lat_by in range(3):
        for lev_at in range(3):
            block = acc[lat_by, lev_at * filters : (lev_at + 1) * filters, :].T * scale
            for lon_at in range(3):
                out[(2 - lev_at) * 9 + lat_by * 3 + lon_at] = block[lon_at * span : (lon_at + 1) * span]


def code_kernel(pos, held, after, out, late):
    del pos, after
    taps, span, filters = held.shape
    most = jnp.abs(held[0])
    for tap in range(1, taps):
        most = jnp.maximum(most, jnp.abs(held[tap]))
    top = jnp.maximum(jnp.max(most, axis=(0, 1), keepdims=True), 1e-30)
    power = jnp.ceil(jnp.log(top) * (1.0 / math.log(2.0))) - 15.0
    unit = jnp.broadcast_to(jnp.exp2(power), (16, filters)).astype(out.dtype).astype(jnp.float32)
    shrink = 1.0 / unit[0:1]
    unit = unit.astype(out.dtype)
    skip = out.shape[0] - late.shape[0]
    for tap in range(taps):
        value = held[tap] * shrink
        square = value * value
        code = (square * value * jnp.abs(value)).astype(out.dtype)
        out[tap * span : (tap + 1) * span, :] = code
        if tap * span >= skip:
            late[tap * span - skip : (tap + 1) * span - skip, :] = code
    out[taps * span :, :] = unit
    late[taps * span - skip :, :] = unit


def both_kernel(pos, west, east, after1, after2, both, half_3, half_1):
    del pos, after1, after2
    size, half = west.shape[0], half_3.shape[0]
    both[0:size, :] = west[...]
    both[size:, :] = east[...]
    half_3[...] = west[0:half, :]
    half_1[...] = east[half:, :]


def cross_kernel(pos, by_x, by_y, after1, after2, after3, top, bottom):
    del pos, after1, after2, after3
    cut = top.shape[0]
    top[...] = by_y[0:cut, :]
    bottom[...] = by_x[cut:, :]


def across_kernel(pos, half_3, half_1, after, late):
    del pos, after
    half = half_3.shape[0]
    late[0:half, :] = half_3[...]
    late[half:, :] = half_1[...]


def block_kernel(pos, own, x, y, top, bottom, block):
    del pos
    rows = block.shape[0] // 4
    for at, (piece, end) in enumerate(((own, own), (x, x), (y, y), (top, bottom))):
        block[at * rows : (at + 1) * rows - 16, :] = piece[0 : rows - 16, :]
        block[(at + 1) * rows - 16 : (at + 1) * rows, :] = end[end.shape[0] - 16 :, :]


def hand_kernel(pos, block_3, block_1, first, second):
    del pos
    many = first.shape[0]
    first[...] = block_3[0:many, :]
    second[...] = block_1[many:, :]


def unpack_kernel(pos, *refs, slabs, count, span):
    sources = refs[:count]
    total, token, buffers, sems = refs[-4:]
    slots, group = buffers.shape[:2]
    wide = buffers.shape[-1] // 4
    token[...] = jnp.zeros_like(token)
    parts = []
    for step, first, taps, pieces in slabs:
        for at in range(0, taps, group):
            parts.append((step, first + at, min(group, taps - at), at, pieces))

    def copy(at):
        step, first, many, _, _ = parts[at]
        lon_at = pl.multiple_of(lax.rem(pos[2] + step, 4) * span, span)
        return pltpu.make_async_copy(
            buffers.at[at % slots, pl.ds(0, many)],
            total.at[pl.ds(first, many), pl.ds(lon_at, span)],
            sems.at[at % slots],
        )

    for at, (_, _, many, skip, pieces) in enumerate(parts):
        if at >= slots:
            copy(at - slots).wait()
        for tag, ((power_in, power_row), *segments) in enumerate(pieces):
            unit = sources[power_in][power_row : power_row + 16, :].astype(jnp.float32)[0:1]
            lanes = pl.ds(pl.multiple_of((pos[1] ^ tag) * wide, wide), wide)
            for tap in range(many):
                begin, which, row = [segment for segment in segments if segment[0] <= skip + tap][-1]
                start = row + (skip + tap - begin) * span
                code = sources[which][start : start + span, :].astype(jnp.float32)
                root = lax.rsqrt(lax.rsqrt(jnp.abs(code))) * unit
                buffers[at % slots, tap, :, lanes] = jnp.where(code < 0, -root, root)
        copy(at).start()
    for at in range(max(len(parts) - slots, 0), len(parts)):
        copy(at).wait()


def unpack(pos, total, sources, after, slabs, span, name):
    slots, group = 4, 3
    wide = total.shape[2]
    ins = (pos, *sources, *after, total)
    token = jax.ShapeDtypeStruct((8, 128), jnp.float32)
    return pl.pallas_call(
        lambda *refs: unpack_kernel(*refs, slabs=slabs, count=len(sources), span=span),
        out_shape=[jax.ShapeDtypeStruct(total.shape, total.dtype), token],
        in_specs=[pl.BlockSpec(memory_space=SMEM)]
        + [pl.BlockSpec(memory_space=VMEM)] * len(sources)
        + [pl.BlockSpec(memory_space=pl.ANY)] * (len(after) + 1),
        out_specs=[pl.BlockSpec(memory_space=pl.ANY), pl.BlockSpec(memory_space=VMEM)],
        scratch_shapes=[VMEM((slots, group, span, wide), jnp.float32), pltpu.SemaphoreType.DMA((slots,))],
        input_output_aliases={len(ins) - 1: 0},
        cost_estimate=pl.CostEstimate(flops=0, bytes_accessed=4 * 2**20, transcendentals=0),
        compiler_params=pltpu.CompilerParams(vmem_limit_bytes=51 * 1024 * 1024),
        name=name,
    )(*ins)


def field_kernel(pos, after, mine, theirs, w, out, copies, acc):
    del after
    step = pl.program_id(0)
    levels, height, width, chans = out.shape
    many = mine.shape[-1]

    @pl.when(step == 0)
    def _():
        copies[:, 0] = jnp.zeros_like(copies[:, 0])
        copies[:, levels + 1] = jnp.zeros_like(copies[:, levels + 1])
        line_at = lax.broadcasted_iota(jnp.int32, (width, many), 0)
        for which, field in ((pos[0], mine), (1 - pos[0], theirs)):
            lanes = pl.ds(pl.multiple_of(which * many, many), many)
            for lev in range(levels):
                for row in range(height + 2):
                    line = field[lev, row, 0:width].astype(jnp.float32)
                    west = field[lev, row, width : width + 1].astype(jnp.float32)
                    east = field[lev, row, width + 8 : width + 9].astype(jnp.float32)
                    before = jnp.where(line_at == 0, west, pltpu.roll(line, 1, 0))
                    later = jnp.where(line_at == width - 1, east, pltpu.roll(line, width - 1, 0))
                    copies[0, lev + 1, row, :, lanes] = later.astype(copies.dtype)
                    copies[1, lev + 1, row, :, lanes] = field[lev, row, 0:width]
                    copies[2, lev + 1, row, :, lanes] = before.astype(copies.dtype)
        acc[...] = jnp.zeros_like(acc)

    lev_by, lat_by = step // 3, lax.rem(step, 3)
    cells = [
        copies[at, pl.ds(2 - lev_by, levels), pl.ds(2 - lat_by, height)].reshape(
            levels * height * width, 2 * many
        )
        for at in range(3)
    ]
    acc[...] += lax.dot_general(
        jnp.concatenate(cells, axis=1),
        jnp.concatenate([w[at] for at in range(3)], axis=1),
        (((1,), (1,)), ((), ())),
        preferred_element_type=jnp.float32,
    )

    @pl.when(step == 8)
    def _():
        out[...] = acc[...].reshape(out.shape).astype(out.dtype)


def blocked_body(inputs, weights, out_grad):
    chans, levels, height, width = inputs.shape
    filters = weights.shape[2]
    bf16, f32 = jnp.bfloat16, jnp.float32
    lat, lon = lax.axis_index("lat"), lax.axis_index("lon")
    pos = jnp.stack([lax.axis_index("ch"), lat, lon]).astype(jnp.int32)
    x_cells = jnp.transpose(inputs, (1, 2, 3, 0))
    g_cells = jnp.transpose(out_grad, (1, 2, 3, 0))
    taps = jnp.transpose(weights, (1, 0, 2))
    cells = levels * height * width
    span, wide = chans // 4, filters // 4
    rows, circle = 4 * height, 4 * width
    edge = levels * height

    to_same = lambda c, a, o: (a // 2, 2 * c + a % 2, o)
    to_other = lambda c, a, o: (a // 2, 2 * c + 1 - a % 2, o)
    many = cells // 2
    block = jax.ShapeDtypeStruct((cells, wide), bf16)
    strip = jax.ShapeDtypeStruct((2 * levels * width, 2 * span), bf16)
    g_same, g_other, x0, x1, x2, x3, rim_x, rim_d = call(
        pack_kernel,
        [block, block]
        + [jax.ShapeDtypeStruct((many + extra, 2 * span), bf16) for extra in (0, 2 * edge, 0, 2 * edge)]
        + [strip, strip],
        (pos, x_cells, g_cells),
        [VMEM((4, many, 2 * span), bf16)],
        0,
        "pack",
        16,
    )
    g_s = move(g_same, to_same)
    g_o = move(g_other, to_other)
    x_r1 = move(x1, lon_by(1))
    x_r3 = move(x3, lon_by(-1))
    x_r2 = move(x2, lon_by(2))
    by_x = move(rim_x, lat_xor(1))
    by_d = move(rim_d, lat_xor(3))

    inner = 4 * many
    (g0,) = call(
        first_pair_kernel,
        [jax.ShapeDtypeStruct((2 * cells + 80, wide), bf16)],
        (pos, g_s, g_o, x_r1, x_r2, x_r3),
        [],
        0,
        "pair_0",
        16,
        held=3,
    )
    x_own, x_own_y = call(
        spread_kernel,
        [jax.ShapeDtypeStruct((count, 2 * span), bf16) for count in (inner + 4 * edge, inner)],
        (pos, x0, x_r1, x_r2, x_r3, by_x, by_d),
        [],
        0,
        "spread",
        16,
        held=2,
    )
    x_x = move(x_own, lat_xor(1))
    x_d = move(x_own, lat_xor(3))
    x_y = move(x_own_y, lat_xor(2))
    g1 = move(g0, lon_by(1))
    g3 = move(g0, lon_by(-1))
    far_a, far_b = call(split_kernel, [block, block], (pos, g1, g3), [], 0, "split", 16)
    g2a = move(far_a, lon_by(1))
    g2b = move(far_b, lon_by(-1))
    s0, s1, s3 = move(g0, sibling), move(g1, sibling), move(g3, sibling)
    xs, total = pl.pallas_call(
        lines_kernel,
        out_shape=[
            jax.ShapeDtypeStruct((levels, rows + 2, circle, 4 * span), bf16),
            jax.ShapeDtypeStruct((27, chans, filters), f32),
        ],
        in_specs=[pl.BlockSpec(memory_space=SMEM)]
        + [pl.BlockSpec(memory_space=VMEM)] * 4
        + [pl.BlockSpec(memory_space=pl.ANY)],
        out_specs=[pl.BlockSpec(memory_space=VMEM)] + [pl.BlockSpec(memory_space=pl.ANY)],
        cost_estimate=pl.CostEstimate(flops=0, bytes_accessed=2**20, transcendentals=0),
        compiler_params=pltpu.CompilerParams(vmem_limit_bytes=24 * 1024 * 1024),
        name="lines",
    )(pos, x_own, x_x, x_y, x_d, far_a)
    (mine,) = call(
        mine_kernel,
        [jax.ShapeDtypeStruct((levels, height + 2, width + 16, chans), bf16)],
        (pos, g_cells, x_own, x_x, x_d, by_x, by_d, xs),
        [],
        0,
        "mine",
        16,
        held=1,
    )
    theirs = move(mine, sibling)
    (g2,) = call(
        pair_kernel, [jax.ShapeDtypeStruct((2, cells, wide), bf16)], (pos, g2a, g2b, xs), [], 0, "pair", 16, held=1
    )
    s2 = move(g2, sibling)
    early = 2
    cut, end = early * span, 27 * span
    size = end + 16 - cut
    half = size // 32 * 16
    first_rows = cut + 16
    own_cut, late_cut = 14 * span, (27 - early) // 2 * span
    slab = lambda count: jax.ShapeDtypeStruct((count, wide), bf16)
    (grads,) = call(
        taps_kernel,
        [jax.ShapeDtypeStruct((27, span, wide), f32)],
        (pos, xs, g0, g1, g3, s0, s1, s3, g2, s2),
        [VMEM((levels * wide, rows * circle), bf16), VMEM((3, 3 * wide, 4 * span), f32)],
        2 * 27 * span * wide * rows * circle * levels,
        "taps",
        28,
    )
    own, late = call(code_kernel, [slab(end + 16), slab(size)], (pos, grads, theirs), [], 0, "code", 16, held=1)

    whole = lambda t: (0, 0, 0, 0)
    field = pl.pallas_call(
        field_kernel,
        out_shape=jax.ShapeDtypeStruct((levels, height, width, chans), bf16),
        grid=(9,),
        in_specs=[
            pl.BlockSpec(memory_space=SMEM),
            pl.BlockSpec(memory_space=pl.ANY),
            pl.BlockSpec(mine.shape, whole),
            pl.BlockSpec(mine.shape, whole),
            pl.BlockSpec((3, chans, filters), lambda t: (t, 0, 0)),
        ],
        out_specs=pl.BlockSpec((levels, height, width, chans), whole),
        scratch_shapes=[
            VMEM((3, levels + 2, height + 2, width, filters), bf16),
            VMEM((cells, chans), f32),
        ],
        cost_estimate=pl.CostEstimate(
            flops=4 * 27 * chans * filters * cells, bytes_accessed=27 * chans * filters * 2, transcendentals=0
        ),
        compiler_params=pltpu.CompilerParams(vmem_limit_bytes=20 * 1024 * 1024),
        name="field",
    )(pos, own, mine, theirs, taps)

    def to_plane(share):
        return move(share, lat_xor(1)), move(share, lat_xor(2))

    def to_diagonal(by_x, by_y, cut, after, name):
        top, bottom = call(
            cross_kernel, [slab(cut), slab(by_x.shape[0] - cut)], (pos, by_x, by_y, *after), [], 0, name, 16, held=3
        )
        return move(top, lat_xor(1)), move(bottom, lat_xor(2))

    from_3 = move(late, lon_by(1))
    from_1 = move(late, lon_by(-1))
    own_x, own_y = to_plane(own)
    own_top, own_bottom = to_diagonal(own_x, own_y, own_cut, (field, own, own), "cross_1")
    pair, half_3, half_1 = call(
        both_kernel,
        [slab(2 * size), slab(half), slab(size - half)],
        (pos, from_3, from_1, own_top, own_bottom),
        [],
        0,
        "both",
        16,
        held=2,
    )
    half_3 = move(half_3, lon_by(1))
    half_1 = move(half_1, lon_by(-1))
    pair_x, pair_y = to_plane(pair)
    (block,) = call(
        block_kernel, [slab(4 * first_rows)], (pos, own, own_x, own_y, own_top, own_bottom), [], 0, "block", 16
    )
    early_3 = move(block, lon_by(1))
    early_1 = move(block, lon_by(-1))
    (from_2,) = call(across_kernel, [slab(size)], (pos, half_3, half_1, pair), [], 0, "across", 16, held=1)
    pair_top, pair_bottom = to_diagonal(pair_x, pair_y, size, (early_1, early_3, pair), "cross_2")
    from_2x, from_2y = to_plane(from_2)
    hand_3, hand_1 = call(hand_kernel, [slab(2 * first_rows)] * 2, (pos, early_3, early_1), [], 0, "hand", 16)
    early_2a = move(hand_3, lon_by(1))
    early_2b = move(hand_1, lon_by(-1))

    def late_piece(which, row=0):
        return ((which, row + size - 16), (0, which, row))

    def early_piece(which, row):
        return ((which, row + cut), (0, which, row))

    pieces = [((which, end), (0, which, 0)) for which in range(3)]
    pieces.append(((4, end - own_cut), (0, 3, 0), (own_cut // span, 4, 0)))
    total, token = unpack(
        pos, total, [own, own_x, own_y, own_top, own_bottom], [block], [(0, 0, 27, pieces)], span, "unpack_1"
    )
    from_2top, from_2bottom = to_diagonal(from_2x, from_2y, late_cut, (token, early_2a, early_2b), "cross_3")
    slabs = [
        (3, early, 27 - early, [late_piece(0), late_piece(2), late_piece(3), late_piece(4)]),
        (1, early, 27 - early, [late_piece(1), late_piece(2, size), late_piece(3, size), late_piece(5)]),
        (3, 0, early, [early_piece(6, tag * first_rows) for tag in range(4)]),
        (1, 0, early, [early_piece(7, tag * first_rows) for tag in range(4)]),
    ]
    total, _ = unpack(
        pos,
        total,
        [from_3, from_1, pair_x, pair_y, pair_top, pair_bottom, early_3, early_1],
        [hand_3],
        slabs,
        span,
        "unpack_2",
    )
    pieces = [late_piece(2), late_piece(3), late_piece(4)]
    pieces.append(((6, size - 16 - late_cut), (0, 5, 0), (late_cut // span, 6, 0)))
    slabs = [
        (2, 0, early, [early_piece(tag // 2, tag % 2 * first_rows) for tag in range(4)]),
        (2, early, 27 - early, pieces),
    ]
    total, _ = unpack(
        pos,
        total,
        [early_2a, early_2b, from_2, from_2x, from_2y, from_2top, from_2bottom],
        [],
        slabs,
        span,
        "unpack_3",
    )
    return (jnp.transpose(field, (3, 0, 1, 2)), jnp.transpose(total, (1, 0, 2)))


def body(inputs, weights, out_grad):
    chans, levels, height, width = inputs.shape
    shape = tuple(lax.axis_size(axis) for axis in AXES)
    fits = (
        shape == (2, 4, 4)
        and chans == out_grad.shape[0] == 256
        and weights.shape[2] == 512
        and levels % 2 == 0
        and height % 2 == 0
        and width % 16 == 0
    )
    return (blocked_body if fits else plain_body)(inputs, weights, out_grad)


def solution(mesh):
    in_specs = (P("ch", None, "lat", "lon"), P("ch", None, None), P("ch", None, "lat", "lon"))
    out_specs = (P("ch", None, "lat", "lon"), P("ch", None, None))
    return jax.shard_map(body, mesh=mesh, in_specs=in_specs, out_specs=out_specs, check_vma=False)
```
